256 devices in a mesh: fft: 64 (over x, z, core), band: 4 (over y).
Axes of the slice: x: 4, y: 4, z: 8, core: 2. Of those that a mesh axis runs over, the one named last changes fastest.
Arguments:
- psi_g: float32 [4, 2, 192, 36864], P('band', None, 'fft'), may hold values from -24 to 24
- vloc: float32 [192, 36864], P('fft'), may hold values from -6 to 6
- beta: float32 [32768, 8, 128], P(('fft', 'band')), may hold values from -0.1875 to 0.1875
- blk_slot: int32 [32768], P(('fft', 'band')), may hold values from 0 to 192, as said below
- blk_tile: int32 [32768], P(('fft', 'band')), may hold values from 0 to 863, as said below
- dmat: float32 [4096, 8, 8], P('fft'), may hold values from -12 to 12
Outputs:
- hpsi_g: float32 [4, 2, 192, 36864], P('band', None, 'fft')
The draws below stay inside these ranges and needn't reach their ends.
Inputs may be any that keep to these rules, and one draw needn't show every extreme that they name: Blocks come slab by slab, 512 to a slab. blk_slot // 64 is 0, 1 or 2 for an atom homed on the slab below (periodically), on the block's own slab, or on the slab above; 192 marks an empty block. `blk_tile`: blocks of atoms homed on the slab below lie in their slab's first 288 tiles; those of atoms homed on the slab above in its last 288 tiles.
All inputs are finite; a program needn't handle non-finite values.
Results may differ from the reference program's by a relative error of at most 0.00007.
Values sent between devices are 32-bit elements; how exact they have to be, the bound alone decides.
No kernel may reach another device: no remote copies, remote signals or barrier semaphores. Data moves between devices by JAX's collectives and lax.ppermute only.
A program may use at most 64 MiB of HBM per device.

```python
import jax
import jax.numpy as jnp
from jax import lax

N = 192
R = 48
NPROJ = 8
ATOM_CAP = 64
ZDEV = 3
PLANE_TILES = 288
TILES = 864
PAIRS = 4
SLAB_BLOCKS = 512
BLOCKS = 32768
ATOMS = 4096
N_FFT = 64


def block_layout(key):
    base = jax.random.fold_in(key, 4711)
    slabs = BLOCKS // SLAB_BLOCKS
    keys = jax.random.split(base, 7)
    level = jax.random.randint(keys[0], (slabs,), 0, 5)
    busiest = jax.random.randint(keys[1], (), 0, slabs)
    level = jnp.where(jnp.arange(slabs) == busiest, 4, level)
    used_count = level * SLAB_BLOCKS // 4
    order = jax.vmap(lambda member: jax.random.permutation(member, SLAB_BLOCKS))(jax.random.split(keys[2], slabs))
    used = order < used_count[:, None]
    side_draw = jax.random.randint(keys[3], (slabs, SLAB_BLOCKS), 0, 4)
    home_side = jnp.where(side_draw == 0, 0, jnp.where(side_draw == 3, 2, 1))
    atom_index = jax.random.randint(keys[4], (slabs, SLAB_BLOCKS), 0, ATOM_CAP)
    slot_ids = jnp.where(used, home_side * ATOM_CAP + atom_index, 3 * ATOM_CAP)
    any_tile = jax.random.randint(keys[5], (slabs, SLAB_BLOCKS), 0, TILES)
    edge_tile = jax.random.randint(keys[6], (slabs, SLAB_BLOCKS), 0, PLANE_TILES)
    tile_ids = jnp.where(home_side == 0, edge_tile, jnp.where(home_side == 2, TILES - PLANE_TILES + edge_tile, any_tile))
    return (slot_ids.reshape(BLOCKS).astype(jnp.int32), tile_ids.reshape(BLOCKS).astype(jnp.int32))


def draw_blk_slot(key, part):
    return block_layout(key)[0]


def draw_blk_tile(key, part):
    return block_layout(key)[1]


def block_levels(key, extent, shards, least, high):
    def one(position, parts):
        steps = jax.random.uniform(jax.random.fold_in(jax.random.fold_in(key, 6), position), (parts,), jnp.float32, least / len(shards), high / len(shards))
        return jnp.repeat(jnp.exp(steps), extent[position] // parts).reshape((-1,) + (1,) * (len(extent) - position - 1))

    loudness = one(*shards[0])
    for cut in shards[1:]:
        loudness = loudness * one(*cut)
    return loudness


def noise(own_key, extent, scale, most, cuts=(), kind=jnp.bfloat16):
    level = block_levels(own_key, extent, cuts, -0.22, 0.18) if cuts else 1.0
    values = jax.random.normal(own_key, extent, jnp.float32) * scale * level
    return jnp.minimum(jnp.maximum(values, -most), most).astype(kind)


def setup_inputs(seed: int = 0) -> dict:
    seeds = jax.random.split(jax.random.key(seed), 7)
    psi_g = noise(seeds[0], (PAIRS, 2, N, N * N), 4.0, 24.0, ((0, 4), (2, 64)), jnp.float32)
    vloc = noise(seeds[1], (N, N * N), 1.0, 6.0, ((0, 64),), jnp.float32)
    beta = noise(seeds[2], (BLOCKS, NPROJ, 128), (NPROJ * 128) ** -0.5, 0.1875, ((0, 256),), jnp.float32)
    blk_slot = draw_blk_slot(jax.random.fold_in(seeds[6], 71), 0)
    blk_tile = draw_blk_tile(jax.random.fold_in(seeds[6], 71), 0)
    dmat = noise(seeds[5], (ATOMS, NPROJ, NPROJ), 2.0, 12.0, ((0, 64),), jnp.float32)
    return {"psi_g": psi_g, "vloc": vloc, "beta": beta, "blk_slot": blk_slot, "blk_tile": blk_tile, "dmat": dmat}


def signed_freq(count):
    values = jnp.arange(count, dtype=jnp.int32)
    return jnp.where(values <= count // 2, values, values - count)


def reference(psi_g, vloc, beta, blk_slot, blk_tile, dmat):
    dealt = psi_g.reshape(PAIRS, 2, N_FFT, ZDEV, N, N)
    psi_full = jnp.transpose(dealt, (0, 1, 3, 2, 4, 5)).reshape(PAIRS, 2, N, N, N)
    vloc_full = vloc.reshape(N, N, N)
    freq = signed_freq(N)
    radius = freq[:, None, None] ** 2 + freq[None, :, None] ** 2 + freq[None, None, :] ** 2
    inside = radius <= R * R
    slab_ids = jnp.arange(BLOCKS, dtype=jnp.int32) // SLAB_BLOCKS
    valid = blk_slot < 3 * ATOM_CAP
    home_slab = (slab_ids + blk_slot // ATOM_CAP - 1 + N_FFT) % N_FFT
    atom_ids = jnp.where(valid, home_slab * ATOM_CAP + blk_slot % ATOM_CAP, ATOMS).astype(jnp.int32)
    tile_ids = (slab_ids * TILES + blk_tile).astype(jnp.int32)
    highest = lax.Precision.HIGHEST

    def one_pair(field_g):
        waves = jnp.where(inside, field_g[0], 0.0) + 1j * jnp.where(inside, field_g[1], 0.0)
        real_space = jnp.fft.ifftn(waves, axes=(0, 1, 2), norm="ortho")
        field_r = jnp.transpose(jnp.stack([real_space.real, real_space.imag]), (0, 3, 2, 1))
        tiles = field_r.reshape(2, N_FFT * TILES, 128)
        block_rows = jnp.take(tiles, tile_ids, axis=1)
        partial_value = jnp.einsum("cbt,bpt->bcp", block_rows, beta, precision=highest)
        coef = jax.ops.segment_sum(partial_value, atom_ids, num_segments=ATOMS + 1)[:ATOMS]
        screened = jnp.einsum("apq,acq->acp", dmat, coef, precision=highest)
        padded = jnp.concatenate([screened, jnp.zeros((1, 2, NPROJ), screened.dtype)], axis=0)
        weights = jnp.take(padded, atom_ids, axis=0)
        spread = jnp.einsum("bcp,bpt->bct", weights, beta, precision=highest)
        nonlocal_part = jax.ops.segment_sum(spread, tile_ids, num_segments=N_FFT * TILES)
        nonlocal_field = jnp.transpose(nonlocal_part, (1, 0, 2)).reshape(2, N, N, N)
        applied = vloc_full * field_r + nonlocal_field
        in_order = jnp.transpose(applied, (0, 3, 2, 1))
        grid_g = jnp.fft.fftn(in_order[0] + 1j * in_order[1], axes=(0, 1, 2), norm="ortho")
        return jnp.stack([jnp.where(inside, grid_g.real, 0.0), jnp.where(inside, grid_g.imag, 0.0)])

    result = lax.map(one_pair, psi_full)
    undealt = jnp.transpose(result.reshape(PAIRS, 2, ZDEV, N_FFT, N, N), (0, 1, 3, 2, 4, 5))
    return undealt.reshape(PAIRS, 2, N, N * N)
```

```python
import functools

import jax
import jax.numpy as jnp
import ml_dtypes
import numpy as np
from jax import lax
from jax.experimental import pallas as pl
from jax.experimental.pallas import tpu as pltpu
from jax.sharding import PartitionSpec as P

N = 192
R2 = 48 * 48
BF = jnp.bfloat16
F32 = jnp.float32
VMEM_LIMIT = 48 * 1024 * 1024


def trig(freqs, points):
    angle = 2.0 * np.pi * (np.outer(freqs, points) % N) / N
    return np.cos(angle) / np.sqrt(N), np.sin(angle) / np.sqrt(N)


def pair_of(table):
    table = np.asarray(table, np.float32)
    high = table.astype(ml_dtypes.bfloat16)
    low = (table - high.astype(np.float32)).astype(ml_dtypes.bfloat16)
    return high, low


KZ = np.concatenate([np.arange(64), np.arange(128, 192)])
SIGNED = np.concatenate([np.arange(64), np.arange(-64, 0)])
YS = [2 * np.arange(96), 2 * np.arange(96) + 1]


@functools.cache
def tables():
    t = {}
    blocks = []
    for zi in range(3):
        c, s = trig(3 * np.arange(64) + zi, KZ)
        blocks += [np.concatenate([c, -s], 1), np.concatenate([s, c], 1)]
    t["wz"] = pair_of(np.concatenate(blocks, 0))
    c, s = trig(np.concatenate(YS), SIGNED)
    t["ey"] = pair_of(
        np.concatenate([np.concatenate([c, -s], 1), np.concatenate([s, c], 1)], 0)
    )
    c, s = trig(SIGNED, np.arange(N))
    gap = np.zeros((128, 64))
    even = [np.concatenate([v, gap], 1) for v in (c, s, -s, c)]
    odd = [np.concatenate([gap, v], 1) for v in (c, s, -s, c)]
    t["xe"] = pair_of(np.block([[even[0], even[1]], [even[2], even[3]]]))
    t["xo"] = pair_of(np.block([[odd[0], odd[1]], [odd[2], odd[3]]]))
    parts = {}
    for name, table in (("c", c), ("s", s)):
        parts[name] = (
            np.concatenate([table, gap], 1),
            np.concatenate([gap, table], 1),
        )

    def forward_x(which):
        cc, ss = parts["c"][which], parts["s"][which]
        rows = []
        for first, second in ((cc, ss), (-ss, cc)):
            rows.append(
                np.concatenate(
                    [first[:, :128], second[:, :128], first[:, 128:], second[:, 128:]], 1
                )
            )
        return np.concatenate(rows, 0)

    t["fe"] = pair_of(forward_x(0))
    t["fo"] = pair_of(forward_x(1))
    c, s = trig(np.concatenate(YS), SIGNED)
    t["fy"] = pair_of(
        np.concatenate([np.concatenate([c, -s], 1), np.concatenate([s, c], 1)], 0)
    )
    blocks = []
    for zi in range(3):
        c, s = trig(3 * np.arange(64) + zi, KZ)
        blocks += [np.concatenate([c, -s], 1), np.concatenate([s, c], 1)]
    t["fz"] = pair_of(np.concatenate(blocks, 0))
    u = np.zeros((128, 384), np.float32)
    for zi in range(3):
        for p in range(128):
            u[32 * zi + 8 * (p >= 64) + p % 8, 128 * zi + p] = 1.0
    t["u"] = u.astype(ml_dtypes.bfloat16)
    t["ut"] = np.concatenate([u[:, 128 * zi : 128 * zi + 128].T for zi in range(3)], 0).astype(
        ml_dtypes.bfloat16
    )
    return t


def split(x):
    high = x.astype(BF)
    return high, (x - high.astype(F32)).astype(BF)


def mm(a, b):
    return jnp.dot(a, b, preferred_element_type=F32)


def mm_nt(a, b):
    return lax.dot_general(a, b, (((1,), (1,)), ((), ())), preferred_element_type=F32)


def three(product, a, b):
    return product(a[0], b[0]) + (product(a[0], b[1]) + product(a[1], b[0]))


def iota(shape, dim):
    return lax.broadcasted_iota(jnp.int32, shape, dim)


def masks_sp():
    s, p = iota((64, 128), 0), iota((64, 128), 1)
    ky = jnp.where(p < 64, p, p - 128)
    away = 64 - jnp.abs(ky)
    inside = ky * ky + s * s <= R2
    clash = away * away + (64 - s) * (64 - s) <= R2
    other = (p - 64) * (p - 64) + (64 - s) * (64 - s) <= R2
    return inside & ~clash, inside & clash, other


def line_places(r, s):
    plane, rest = r // 128, r % 128
    ky = 2 * (rest % 64 - 24) + rest // 64
    here = jnp.where(plane == 0, s, 64 - s)
    away = 64 - jnp.abs(ky)
    inside = ky * ky + here * here <= R2
    clash = (away * away + (64 - s) * (64 - s) <= R2) & (plane == 0)
    place = jnp.where(plane == 0, jnp.where(ky < 0, ky + 128, ky), ky + 64)
    main = jnp.where(inside & ~clash, place, -1)
    spare = jnp.where(inside & clash, jnp.where(ky < 0, 8, 0) + (ky + 64) % 8, -1)
    return main, spare


def one_hot(condition):
    return jnp.where(condition, 1.0, 0.0).astype(BF)


def sphere_rows(plane, parity, s):
    m, lane = iota((64, 128), 0), iota((64, 128), 1)
    ky = 2 * (m - 24) + parity
    kz = jnp.where(lane < 64, lane, lane - 128)
    kx = s - 64 * plane
    return ky * ky + kz * kz + kx * kx <= R2


def kernel_z_inverse(psi, wz_h, wz_l, send, buf, sems):
    s = lax.axis_index("fft")
    copies = []
    for plane in range(2):
        base = 1152 * plane
        for k, (src, dst, rows) in enumerate(((432, 0, 144), (0, 144, 152))):
            copies.append(
                pltpu.make_async_copy(
                    psi.at[pl.ds(base + src, rows)],
                    buf.at[plane, pl.ds(dst, rows)],
                    sems.at[2 * plane + k],
                )
            )
    for copy in copies:
        copy.start()
    r = iota((1, 256), 1)
    main, spare = line_places(r, s)
    j = iota((128, 256), 0)
    pack = jnp.concatenate(
        [one_hot(j == main), one_hot((j % 32 == spare) & (j < 96))], axis=0
    )
    for copy in copies:
        copy.wait()
    lane = iota((64, 128), 1)
    rows = []
    for plane in range(2):
        lines = [[], []]
        for c in range(2):
            t = [buf[plane, pl.ds(2 * k + c, 64, stride=6), :] for k in range(3)]
            middle = pltpu.roll(t[1], 64, 1)
            even = jnp.where(lane < 64, t[0], middle)
            odd = jnp.where(lane < 64, middle, t[2])
            lines[0].append(jnp.where(sphere_rows(plane, 0, s), even, 0.0))
            lines[1].append(jnp.where(sphere_rows(plane, 1, s), odd, 0.0))
        rows += [jnp.concatenate(lines[0], 1), jnp.concatenate(lines[1], 1)]
    high, low = split(jnp.concatenate(rows, 0))
    packed = (mm(pack, high).astype(BF), mm(pack, low).astype(BF))
    out = three(mm_nt, (wz_h[...], wz_l[...]), packed)
    for c in range(2):
        block = [out[(2 * zi + c) * 64 : (2 * zi + c) * 64 + 64] for zi in range(3)]
        for zi in range(3):
            send[pl.ds(4 * c + zi, 64, stride=8), :] = block[zi][:, :128]
        send[pl.ds(4 * c + 3, 64, stride=8), :] = jnp.where(
            lane < 32, block[0][:, 128:], jnp.where(lane < 64, block[1][:, 128:], block[2][:, 128:])
        )


def block_ids(betas, row):
    return jnp.concatenate([b[1024 + row : 1025 + row, :] for b in betas], 1)


def as_column(ids):
    return jnp.broadcast_to(ids, (8, 512)).T[:, 0:1]


def slot_hot(betas):
    return one_hot(as_column(block_ids(betas, 0)).astype(jnp.int32) == iota((512, 256), 1))


def kernel_field(
    recv, ey_h, ey_l, xe_h, xe_l, xo_h, xo_l, u, vloc, dmat, b0, b1, b2, b3,
    local, near, far, rows_h, rows_l, field_rows,
):
    main, spare, other = masks_sp()
    spread = []
    for c in range(2):
        high, low = split(recv[pl.ds(4 * c + 3, 64, stride=8), :])
        spread.append(mm(high, u[...]) + mm(low, u[...]))
    lines = []
    for zi in range(3):
        first, second = [], []
        for c in range(2):
            got = recv[pl.ds(4 * c + zi, 64, stride=8), :]
            extra = spread[c][:, 128 * zi : 128 * zi + 128]
            first.append(jnp.where(main, got, jnp.where(spare, extra, 0.0)))
            second.append(pltpu.roll(jnp.where(other, got, 0.0), 64, 1))
        lines += [jnp.concatenate(first, 1), jnp.concatenate(second, 1)]
    g = three(mm_nt, (ey_h[...], ey_l[...]), split(jnp.concatenate(lines, 0)))
    out = []
    for parity, table in ((0, (xe_h, xe_l)), (1, (xo_h, xo_l))):
        a = 96 * parity
        block = jnp.concatenate(
            [
                jnp.concatenate(
                    [
                        g[a : a + 96, 128 * zi : 128 * zi + 128],
                        g[192 + a : 288 + a, 128 * zi : 128 * zi + 128],
                    ],
                    1,
                )
                for zi in range(3)
            ],
            0,
        )
        out.append(three(mm, split(block), (table[0][...], table[1][...])))
    even, odd = out
    for c in range(2):
        a = 256 * c
        kinds = (
            even[:, a : a + 128],
            even[:, a + 128 : a + 256] + odd[:, a : a + 128],
            odd[:, a + 128 : a + 256],
        )
        for k, tile in enumerate(kinds):
            span = pl.ds(288 * k, 288)
            lanes = pl.ds(128 * c, 128)
            local[span, lanes] = tile * vloc[span, :]
            high, low = split(tile)
            rows_h[span, lanes] = high
            rows_l[span, lanes] = low
    rows_h[864:896, :] = jnp.zeros((32, 256), BF)
    rows_l[864:896, :] = jnp.zeros((32, 256), BF)

    betas = (b0, b1, b2, b3)
    tile_of = as_column(block_ids(betas, 1)).astype(jnp.int32)
    pick = one_hot(tile_of == iota((512, 896), 1))
    field_rows[...] = mm(pick, rows_h[...]) + mm(pick, rows_l[...])
    lane = iota((128, 128), 1)
    sums = []
    for k, beta in enumerate(betas):
        total = jnp.zeros((128, 128), F32)
        for j in range(8):
            projector = beta[pl.ds(j, 128, stride=8), :]
            for c in range(2):
                value = field_rows[128 * k : 128 * k + 128, 128 * c : 128 * c + 128] * projector
                total = jnp.where(
                    lane == 8 * c + j, jnp.sum(value, axis=1, keepdims=True), total
                )
        sums.append(total.T[:16])
    high, low = split(jnp.concatenate(sums, 1))
    slots = slot_hot(betas)
    coef = mm(high, slots) + mm(low, slots)
    coef = jnp.where(iota((16, 256), 1) < 192, coef, 0.0)
    near[0:64, :] = jnp.concatenate([dmat[...], jnp.zeros((64, 64), F32)], 1)
    near[64:80, :] = coef[:, :128]
    near[80:96, :] = coef[:, 128:]
    far[0:16, :] = coef[:, :128]
    far[16:32, :] = coef[:, 128:]


def kernel_back(
    local, near, below, above, below2, above2, b0, b1, b2, b3,
    fe_h, fe_l, fo_h, fo_l, fy_h, fy_l, ut, send, scr, rows,
):
    lane = iota((16, 128), 1)

    def half(ref, k):
        return ref[64 + 16 * k : 80 + 16 * k, :]

    def shifted(low, high, up):
        low, high = pltpu.roll(low, 64, 1), pltpu.roll(high, 64, 1)
        if up:
            return jnp.where(lane < 64, 0.0, low), jnp.where(lane < 64, low, high)
        return jnp.where(lane < 64, low, high), jnp.where(lane < 64, high, 0.0)

    from_below = shifted(half(below, 0), half(below, 1), False)
    from_above = shifted(half(above, 0), half(above, 1), True)
    tot = [
        half(near, 0) + from_below[0] + from_above[0] + below2[16:32, :],
        half(near, 1) + from_below[1] + from_above[1] + above2[0:16, :],
    ]
    tot[1] = jnp.where(lane < 64, tot[1], 0.0)
    wide = iota((64, 128), 1)
    coupling = [
        jnp.where(wide < 64, below[0:64, :], pltpu.roll(near[0:64, :], 64, 1)),
        jnp.where(wide < 64, above[0:64, :], 0.0),
    ]
    for h in range(2):
        for c in range(2):
            coef = tot[h][8 * c : 8 * c + 8, :]
            for j in range(8):
                row = jnp.sum(coupling[h][8 * j : 8 * j + 8, :] * coef, axis=0, keepdims=True)
                scr[8 * c + j : 8 * c + j + 1, 128 * h : 128 * h + 128] = row
    betas = (b0, b1, b2, b3)
    slots = slot_hot(betas)
    high, low = split(scr[...])
    weight = mm_nt(slots, high) + mm_nt(slots, low)
    for k, beta in enumerate(betas):
        span = slice(128 * k, 128 * k + 128)
        terms = [jnp.zeros((128, 128), F32), jnp.zeros((128, 128), F32)]
        for j in range(8):
            projector = beta[pl.ds(j, 128, stride=8), :]
            for c in range(2):
                terms[c] = terms[c] + projector * weight[span, 8 * c + j : 8 * c + j + 1]
        for c in range(2):
            high, low = split(terms[c])
            rows[span, 128 * c : 128 * c + 128] = high
            rows[span, 256 + 128 * c : 384 + 128 * c] = low
    tile_of = block_ids(betas, 1).astype(jnp.int32)
    put = one_hot(iota((864, 512), 0) == tile_of)
    both = mm(put, rows[...])
    applied = local[...] + (both[:, :256] + both[:, 256:])
    app = split(applied)
    main, spare, _ = masks_sp()
    spares = [jnp.zeros((64, 128), F32), jnp.zeros((64, 128), F32)]
    for zi in range(3):
        kinds = [
            [a[288 * k + 96 * zi : 288 * k + 96 * zi + 96] for a in app] for k in range(3)
        ]
        h = jnp.zeros((128, 256), F32)
        for parity, table in ((0, (fe_h, fe_l)), (1, (fo_h, fo_l))):
            lines = [
                jnp.concatenate([kinds[parity][i], kinds[parity + 1][i]], 1) for i in range(2)
            ]
            g = split(three(mm_nt, (table[0][...], table[1][...]), lines))
            for c in range(2):
                part = [v[128 * c : 128 * c + 128] for v in g]
                at = slice(192 * c + 96 * parity, 192 * c + 96 * parity + 96)
                h = h + three(mm, part, (fy_h[at, :], fy_l[at, :]))
        for c in range(2):
            first = h[:64, 128 * c : 128 * c + 128]
            second = pltpu.roll(h[64:, 128 * c : 128 * c + 128], 64, 1)
            send[pl.ds(4 * c + zi, 64, stride=8), :] = jnp.where(main, first, second)
            high, low = split(jnp.where(spare, first, 0.0))
            move = ut[128 * zi : 128 * zi + 128, :]
            spares[c] = spares[c] + (mm(high, move) + mm(low, move))
    for c in range(2):
        send[pl.ds(4 * c + 3, 64, stride=8), :] = spares[c]


def kernel_z_forward(recv, fz_h, fz_l, out):
    s = lax.axis_index("fft")
    out[...] = jnp.zeros((1728, 128), F32)
    r = iota((256, 1), 0)
    main, spare = line_places(r, s)
    lane = iota((256, 128), 1)
    keep = one_hot(lane == main)
    highs, lows = [], []
    for zi in range(3):
        unpack = jnp.concatenate(
            [keep, one_hot((lane == spare + 32 * zi) & (spare >= 0))], 1
        )
        lines = jnp.concatenate(
            [
                jnp.concatenate(
                    [
                        recv[pl.ds(4 * c + zi, 64, stride=8), :],
                        recv[pl.ds(4 * c + 3, 64, stride=8), :],
                    ],
                    1,
                )
                for c in range(2)
            ],
            0,
        )
        high, low = split(lines)
        columns = mm_nt(unpack, jnp.concatenate([high, low], 0))
        highs.append(columns[:, :128].astype(BF))
        lows.append(columns[:, 128:].astype(BF))
    z = three(
        mm, (jnp.concatenate(highs, 1), jnp.concatenate(lows, 1)), (fz_h[...], fz_l[...])
    )
    low_lane = iota((64, 128), 1) < 64
    for plane in range(2):
        for c in range(2):
            block = z[128 * plane : 128 * plane + 128, 128 * c : 128 * c + 128]
            even = jnp.where(sphere_rows(plane, 0, s), block[:64], 0.0)
            odd = jnp.where(sphere_rows(plane, 1, s), block[64:], 0.0)
            kinds = (
                jnp.where(low_lane, even, 0.0),
                pltpu.roll(jnp.where(low_lane, odd, even), 64, 1),
                jnp.where(low_lane, 0.0, odd),
            )
            for k, tile in enumerate(kinds):
                at = 1152 * plane + 2 * k + c
                out[pl.ds(at, 32, stride=6), :] = tile[24:56]
                out[pl.ds(at + 432, 24, stride=6), :] = tile[:24]


def call(kernel, name, out_shape, args, scratch=(), anywhere=()):
    specs = [
        pl.BlockSpec(memory_space=pl.ANY if k in anywhere else pltpu.VMEM)
        for k in range(len(args))
    ]
    shapes = [jax.ShapeDtypeStruct(shape, F32) for shape in out_shape]
    out = pl.pallas_call(
        kernel,
        name=name,
        out_shape=shapes,
        in_specs=specs,
        out_specs=[pl.BlockSpec(memory_space=pltpu.VMEM)] * len(shapes),
        scratch_shapes=list(scratch),
        compiler_params=pltpu.CompilerParams(vmem_limit_bytes=VMEM_LIMIT),
    )(*args)
    return out


def body(psi_g, vloc, beta, blk_slot, blk_tile, dmat):
    t = {
        name: tuple(jnp.asarray(v) for v in value) if isinstance(value, tuple) else jnp.asarray(value)
        for name, value in tables().items()
    }
    tile_row = (blk_tile % 3) * 288 + blk_tile // 3
    ids = jnp.concatenate(
        [blk_slot[None], tile_row[None], jnp.zeros((6, 128), jnp.int32)], 0
    ).astype(F32)
    own = jnp.concatenate([beta, ids[None]], 0).reshape(1032, 128)
    betas = [own] + [
        lax.ppermute(own, "band", [(i, (i + k) % 4) for i in range(4)]) for k in (1, 3, 2)
    ]

    psi = psi_g[0].transpose(1, 0, 2).reshape(3, 2, 288, 128).transpose(0, 2, 1, 3)
    psi = psi.reshape(1728, 128)
    (send,) = call(
        kernel_z_inverse,
        "z_inverse",
        [(512, 128)],
        (psi, *t["wz"]),
        [pltpu.VMEM((2, 384, 128), F32), pltpu.SemaphoreType.DMA((4,))],
        anywhere=(0,),
    )

    def exchange(x):
        x = lax.all_to_all(x.reshape(64, 8, 128), "fft", 0, 0, tiled=True)
        return x.reshape(512, 128)

    recv = exchange(send)
    vloc_rows = vloc.reshape(3, 96, 3, 128).transpose(2, 0, 1, 3).reshape(864, 128)
    dmat_rows = dmat.transpose(1, 2, 0).reshape(64, 64)
    local, near, far = call(
        kernel_field,
        "field",
        [(864, 256), (96, 128), (32, 128)],
        (recv, *t["ey"], *t["xe"], *t["xo"], t["u"], vloc_rows, dmat_rows, *betas),
        [pltpu.VMEM((896, 256), BF), pltpu.VMEM((896, 256), BF), pltpu.VMEM((512, 256), F32)],
    )

    def moved(x, step):
        return lax.ppermute(x, "fft", [(i, (i + step) % 64) for i in range(64)])

    sides = (moved(near, 1), moved(near, -1), moved(far, 2), moved(far, -2))
    (send,) = call(
        kernel_back,
        "back",
        [(512, 128)],
        (local, near, *sides, *betas, *t["fe"], *t["fo"], *t["fy"], t["ut"]),
        [pltpu.VMEM((16, 256), F32), pltpu.VMEM((512, 512), BF)],
    )
    (out,) = call(kernel_z_forward, "z_forward", [(1728, 128)], (exchange(send), *t["fz"]))
    out = out.reshape(3, 288, 2, 128).transpose(0, 2, 1, 3).reshape(3, 2, N * N)
    return out.transpose(1, 0, 2)[None]


def solution(mesh):
    in_specs = (
        P("band", None, "fft", None),
        P("fft", None),
        P(("fft", "band"), None, None),
        P(("fft", "band")),
        P(("fft", "band")),
        P("fft", None, None),
    )
    out_specs = P("band", None, "fft", None)
    return jax.shard_map(body, mesh=mesh, in_specs=in_specs, out_specs=out_specs, check_vma=False)
```

```python
import functools

import jax
import jax.numpy as jnp
import ml_dtypes
import numpy as np
from jax import lax
from jax.experimental import pallas as pl
from jax.experimental.pallas import tpu as pltpu
from jax.sharding import PartitionSpec as P

N = 192
R2 = 48 * 48
BF = jnp.bfloat16
F32 = jnp.float32
VMEM_LIMIT = 48 * 1024 * 1024


def trig(freqs, points):
    angle = 2.0 * np.pi * (np.outer(freqs, points) % N) / N
    return np.cos(angle) / np.sqrt(N), np.sin(angle) / np.sqrt(N)


def pair_of(table):
    table = np.asarray(table, np.float32)
    high = table.astype(ml_dtypes.bfloat16)
    low = (table - high.astype(np.float32)).astype(ml_dtypes.bfloat16)
    return np.concatenate([high, low], 0)


KZ = np.concatenate([np.arange(64), np.arange(128, 192)])
SIGNED = np.concatenate([np.arange(64), np.arange(-64, 0)])
YS = [2 * np.arange(96), 2 * np.arange(96) + 1]


@functools.cache
def tables():
    t = {}
    blocks = []
    for zi in range(3):
        c, s = trig(3 * np.arange(64) + zi, KZ)
        blocks += [np.concatenate([c, -s], 1), np.concatenate([s, c], 1)]
    t["wz"] = pair_of(np.concatenate(blocks, 0))
    c, s = trig(np.concatenate(YS), SIGNED)
    t["ey"] = pair_of(
        np.concatenate([np.concatenate([c, -s], 1), np.concatenate([s, c], 1)], 0)
    )
    c, s = trig(SIGNED, np.arange(N))
    gap = np.zeros((128, 64))
    even = [np.concatenate([v, gap], 1) for v in (c, s, -s, c)]
    odd = [np.concatenate([gap, v], 1) for v in (c, s, -s, c)]
    t["ix"] = np.concatenate(
        [
            pair_of(np.block([[even[0], even[1]], [even[2], even[3]]])),
            pair_of(np.block([[odd[0], odd[1]], [odd[2], odd[3]]])),
        ],
        0,
    )
    parts = {}
    for name, table in (("c", c), ("s", s)):
        parts[name] = (
            np.concatenate([table, gap], 1),
            np.concatenate([gap, table], 1),
        )

    def forward_x(which):
        cc, ss = parts["c"][which], parts["s"][which]
        rows = []
        for first, second in ((cc, ss), (-ss, cc)):
            rows.append(
                np.concatenate(
                    [first[:, :128], second[:, :128], first[:, 128:], second[:, 128:]], 1
                )
            )
        return np.concatenate(rows, 0)

    t["fx"] = np.concatenate([pair_of(forward_x(0)), pair_of(forward_x(1))], 0)
    c, s = trig(np.concatenate(YS), SIGNED)
    t["fy"] = pair_of(
        np.concatenate([np.concatenate([c, -s], 1), np.concatenate([s, c], 1)], 0)
    )
    blocks = []
    for zi in range(3):
        c, s = trig(3 * np.arange(64) + zi, KZ)
        blocks += [np.concatenate([c, -s], 1), np.concatenate([s, c], 1)]
    t["fz"] = pair_of(np.concatenate(blocks, 0))
    u = np.zeros((128, 384), np.float32)
    for zi in range(3):
        for p in range(128):
            u[32 * zi + 8 * (p >= 64) + p % 8, 128 * zi + p] = 1.0
    t["u"] = u.astype(ml_dtypes.bfloat16)
    t["ut"] = np.concatenate([u[:, 128 * zi : 128 * zi + 128].T for zi in range(3)], 0).astype(
        ml_dtypes.bfloat16
    )
    return t


def split(x):
    high = x.astype(BF)
    return high, (x - high.astype(F32)).astype(BF)


def mm(a, b):
    return jnp.dot(a, b, preferred_element_type=F32)


def mm_nt(a, b):
    return lax.dot_general(a, b, (((1,), (1,)), ((), ())), preferred_element_type=F32)


def three(product, a, b):
    return product(a[0], b[0]) + (product(a[0], b[1]) + product(a[1], b[0]))


def iota(shape, dim):
    return lax.broadcasted_iota(jnp.int32, shape, dim)


def masks_sp():
    s, p = iota((64, 128), 0), iota((64, 128), 1)
    ky = jnp.where(p < 64, p, p - 128)
    away = 64 - jnp.abs(ky)
    inside = ky * ky + s * s <= R2
    clash = away * away + (64 - s) * (64 - s) <= R2
    other = (p - 64) * (p - 64) + (64 - s) * (64 - s) <= R2
    return inside & ~clash, inside & clash, other


def line_places(r, s):
    plane, rest = r // 128, r % 128
    ky = 2 * (rest % 64 - 24) + rest // 64
    here = jnp.where(plane == 0, s, 64 - s)
    away = 64 - jnp.abs(ky)
    inside = ky * ky + here * here <= R2
    clash = (away * away + (64 - s) * (64 - s) <= R2) & (plane == 0)
    place = jnp.where(plane == 0, jnp.where(ky < 0, ky + 128, ky), ky + 64)
    main = jnp.where(inside & ~clash, place, -1)
    spare = jnp.where(inside & clash, jnp.where(ky < 0, 8, 0) + (ky + 64) % 8, -1)
    return main, spare


def one_hot(condition):
    return jnp.where(condition, 1.0, 0.0).astype(BF)


def sphere_rows(plane, parity, s):
    m, lane = iota((64, 128), 0), iota((64, 128), 1)
    ky = 2 * (m - 24) + parity
    kz = jnp.where(lane < 64, lane, lane - 128)
    kx = s - 64 * plane
    return ky * ky + kz * kz + kx * kx <= R2


def kernel_z_inverse(psi, wz_in, beta, slot, tile, send, own, buf, wz, ids, sems):
    s = lax.axis_index("fft")
    ids[...] = jnp.zeros((8, 128), F32)
    ids[0:1, :] = slot[...].astype(F32)
    ids[1:2, :] = ((tile[...] % 3) * 288 + tile[...] // 3).astype(F32)
    later = [
        pltpu.make_async_copy(beta, own.at[pl.ds(0, 1024)], sems.at[5]),
        pltpu.make_async_copy(ids, own.at[pl.ds(1024, 8)], sems.at[6]),
    ]
    copies = [pltpu.make_async_copy(wz_in, wz, sems.at[4])]
    for plane in range(2):
        base = 1152 * plane
        for k, (src, dst, rows) in enumerate(((432, 0, 144), (0, 144, 152))):
            copies.append(
                pltpu.make_async_copy(
                    psi.at[pl.ds(base + src, rows)],
                    buf.at[plane, pl.ds(dst, rows)],
                    sems.at[2 * plane + k],
                )
            )
    for copy in copies[1:] + copies[:1] + later:
        copy.start()
    r = iota((1, 256), 1)
    main, spare = line_places(r, s)
    j = iota((128, 256), 0)
    pack = jnp.concatenate(
        [one_hot(j == main), one_hot((j % 32 == spare) & (j < 96))], axis=0
    )
    for copy in copies:
        copy.wait()
    lane = iota((64, 128), 1)
    rows = []
    for plane in range(2):
        lines = [[], []]
        for c in range(2):
            t = [buf[plane, pl.ds(2 * k + c, 64, stride=6), :] for k in range(3)]
            middle = pltpu.roll(t[1], 64, 1)
            even = jnp.where(lane < 64, t[0], middle)
            odd = jnp.where(lane < 64, middle, t[2])
            lines[0].append(jnp.where(sphere_rows(plane, 0, s), even, 0.0))
            lines[1].append(jnp.where(sphere_rows(plane, 1, s), odd, 0.0))
        rows += [jnp.concatenate(lines[0], 1), jnp.concatenate(lines[1], 1)]
    high, low = split(jnp.concatenate(rows, 0))
    packed = (mm(pack, high).astype(BF), mm(pack, low).astype(BF))
    out = three(mm_nt, (wz[0:384, :], wz[384:768, :]), packed)
    for c in range(2):
        block = [out[(2 * zi + c) * 64 : (2 * zi + c) * 64 + 64] for zi in range(3)]
        for zi in range(3):
            send[pl.ds(4 * c + zi, 64, stride=8), :] = block[zi][:, :128]
        send[pl.ds(4 * c + 3, 64, stride=8), :] = jnp.where(
            lane < 32, block[0][:, 128:], jnp.where(lane < 64, block[1][:, 128:], block[2][:, 128:])
        )
    for copy in later:
        copy.wait()


def block_ids(betas, row):
    return jnp.concatenate([b[1024 + row : 1025 + row, :] for b in betas], 1)


def as_column(ids):
    return jnp.broadcast_to(ids, (8, 512)).T[:, 0:1]


def slot_hot(betas):
    return one_hot(as_column(block_ids(betas, 0)).astype(jnp.int32) == iota((512, 256), 1))


def kernel_field(
    recv, ey, ix_in, u, dmat, b0, b1, b2, b3,
    field, near, far, rows_h, rows_l, field_rows, ix, sem,
):
    copy = pltpu.make_async_copy(ix_in, ix, sem)
    copy.start()
    main, spare, other = masks_sp()
    spread = []
    for c in range(2):
        high, low = split(recv[pl.ds(4 * c + 3, 64, stride=8), :])
        spread.append(mm(high, u[...]) + mm(low, u[...]))
    lines = []
    for zi in range(3):
        first, second = [], []
        for c in range(2):
            got = recv[pl.ds(4 * c + zi, 64, stride=8), :]
            extra = spread[c][:, 128 * zi : 128 * zi + 128]
            first.append(jnp.where(main, got, jnp.where(spare, extra, 0.0)))
            second.append(pltpu.roll(jnp.where(other, got, 0.0), 64, 1))
        lines += [jnp.concatenate(first, 1), jnp.concatenate(second, 1)]
    g = three(mm_nt, (ey[0:384, :], ey[384:768, :]), split(jnp.concatenate(lines, 0)))
    copy.wait()
    out = []
    for parity in range(2):
        a = 96 * parity
        table = [ix[512 * parity + 256 * i : 512 * parity + 256 * i + 256, :] for i in range(2)]
        block = jnp.concatenate(
            [
                jnp.concatenate(
                    [
                        g[a : a + 96, 128 * zi : 128 * zi + 128],
                        g[192 + a : 288 + a, 128 * zi : 128 * zi + 128],
                    ],
                    1,
                )
                for zi in range(3)
            ],
            0,
        )
        out.append(three(mm, split(block), table))
    even, odd = out
    for c in range(2):
        a = 256 * c
        kinds = (
            even[:, a : a + 128],
            even[:, a + 128 : a + 256] + odd[:, a : a + 128],
            odd[:, a + 128 : a + 256],
        )
        for k, tile in enumerate(kinds):
            span = pl.ds(288 * k, 288)
            lanes = pl.ds(128 * c, 128)
            field[span, lanes] = tile
            high, low = split(tile)
            rows_h[span, lanes] = high
            rows_l[span, lanes] = low
    rows_h[864:896, :] = jnp.zeros((32, 256), BF)
    rows_l[864:896, :] = jnp.zeros((32, 256), BF)

    betas = (b0, b1, b2, b3)
    tile_of = as_column(block_ids(betas, 1)).astype(jnp.int32)
    pick = one_hot(tile_of == iota((512, 896), 1))
    field_rows[...] = mm(pick, rows_h[...]) + mm(pick, rows_l[...])
    lane = iota((128, 128), 1)
    sums = []
    for k, beta in enumerate(betas):
        total = jnp.zeros((128, 128), F32)
        for j in range(8):
            projector = beta[pl.ds(j, 128, stride=8), :]
            for c in range(2):
                value = field_rows[128 * k : 128 * k + 128, 128 * c : 128 * c + 128] * projector
                total = jnp.where(
                    lane == 8 * c + j, jnp.sum(value, axis=1, keepdims=True), total
                )
        sums.append(total.T[:16])
    high, low = split(jnp.concatenate(sums, 1))
    slots = slot_hot(betas)
    coef = mm(high, slots) + mm(low, slots)
    coef = jnp.where(iota((16, 256), 1) < 192, coef, 0.0)
    near[0:64, :] = jnp.concatenate([dmat[...], jnp.zeros((64, 64), F32)], 1)
    near[64:80, :] = coef[:, :128]
    near[80:96, :] = coef[:, 128:]
    far[0:16, :] = coef[:, :128]
    far[16:32, :] = coef[:, 128:]


def kernel_back(
    field, near, below, above, below2, above2, b0, b1, b2, b3,
    vloc_in, fx_in, fy_in, ut_in, send, scr, rows, vloc, fx, fy, ut, sems,
):
    copies = [
        pltpu.make_async_copy(vloc_in.at[:, zi, :], vloc.at[zi], sems.at[zi]) for zi in range(3)
    ] + [
        pltpu.make_async_copy(fx_in, fx, sems.at[3]),
        pltpu.make_async_copy(fy_in, fy, sems.at[4]),
        pltpu.make_async_copy(ut_in, ut, sems.at[5]),
    ]
    for copy in copies:
        copy.start()
    lane = iota((16, 128), 1)

    def half(ref, k):
        return ref[64 + 16 * k : 80 + 16 * k, :]

    def shifted(low, high, up):
        low, high = pltpu.roll(low, 64, 1), pltpu.roll(high, 64, 1)
        if up:
            return jnp.where(lane < 64, 0.0, low), jnp.where(lane < 64, low, high)
        return jnp.where(lane < 64, low, high), jnp.where(lane < 64, high, 0.0)

    from_below = shifted(half(below, 0), half(below, 1), False)
    from_above = shifted(half(above, 0), half(above, 1), True)
    tot = [
        half(near, 0) + from_below[0] + from_above[0] + below2[16:32, :],
        half(near, 1) + from_below[1] + from_above[1] + above2[0:16, :],
    ]
    tot[1] = jnp.where(lane < 64, tot[1], 0.0)
    wide = iota((64, 128), 1)
    coupling = [
        jnp.where(wide < 64, below[0:64, :], pltpu.roll(near[0:64, :], 64, 1)),
        jnp.where(wide < 64, above[0:64, :], 0.0),
    ]
    for h in range(2):
        for c in range(2):
            coef = tot[h][8 * c : 8 * c + 8, :]
            for j in range(8):
                row = jnp.sum(coupling[h][8 * j : 8 * j + 8, :] * coef, axis=0, keepdims=True)
                scr[8 * c + j : 8 * c + j + 1, 128 * h : 128 * h + 128] = row
    betas = (b0, b1, b2, b3)
    slots = slot_hot(betas)
    high, low = split(scr[...])
    weight = mm_nt(slots, high) + mm_nt(slots, low)
    for k, beta in enumerate(betas):
        span = slice(128 * k, 128 * k + 128)
        terms = [jnp.zeros((128, 128), F32), jnp.zeros((128, 128), F32)]
        for j in range(8):
            projector = beta[pl.ds(j, 128, stride=8), :]
            for c in range(2):
                terms[c] = terms[c] + projector * weight[span, 8 * c + j : 8 * c + j + 1]
        for c in range(2):
            high, low = split(terms[c])
            rows[span, 128 * c : 128 * c + 128] = high
            rows[span, 256 + 128 * c : 384 + 128 * c] = low
    tile_of = block_ids(betas, 1).astype(jnp.int32)
    put = one_hot(iota((864, 512), 0) == tile_of)
    both = mm(put, rows[...])
    nonloc = both[:, :256] + both[:, 256:]
    for copy in copies:
        copy.wait()
    main, spare, _ = masks_sp()
    spares = [jnp.zeros((64, 128), F32), jnp.zeros((64, 128), F32)]
    for zi in range(3):
        kinds = []
        for k in range(3):
            at = slice(288 * k + 96 * zi, 288 * k + 96 * zi + 96)
            factor = vloc[zi, pl.ds(k, 96, stride=3), :]
            kinds.append(
                split(field[at, :] * jnp.concatenate([factor, factor], 1) + nonloc[at, :])
            )
        h = jnp.zeros((128, 256), F32)
        for parity in range(2):
            table = [fx[512 * parity + 256 * i : 512 * parity + 256 * i + 256, :] for i in range(2)]
            lines = [
                jnp.concatenate([kinds[parity][i], kinds[parity + 1][i]], 1) for i in range(2)
            ]
            g = split(three(mm_nt, table, lines))
            for c in range(2):
                part = [v[128 * c : 128 * c + 128] for v in g]
                at = 192 * c + 96 * parity
                h = h + three(mm, part, (fy[at : at + 96, :], fy[384 + at : 480 + at, :]))
        for c in range(2):
            first = h[:64, 128 * c : 128 * c + 128]
            second = pltpu.roll(h[64:, 128 * c : 128 * c + 128], 64, 1)
            send[pl.ds(4 * c + zi, 64, stride=8), :] = jnp.where(main, first, second)
            high, low = split(jnp.where(spare, first, 0.0))
            move = ut[128 * zi : 128 * zi + 128, :]
            spares[c] = spares[c] + (mm(high, move) + mm(low, move))
    for c in range(2):
        send[pl.ds(4 * c + 3, 64, stride=8), :] = spares[c]


def kernel_z_forward(recv, fz, out):
    s = lax.axis_index("fft")
    out[...] = jnp.zeros((1728, 128), F32)
    r = iota((256, 1), 0)
    main, spare = line_places(r, s)
    lane = iota((256, 128), 1)
    keep = one_hot(lane == main)
    highs, lows = [], []
    for zi in range(3):
        unpack = jnp.concatenate(
            [keep, one_hot((lane == spare + 32 * zi) & (spare >= 0))], 1
        )
        lines = jnp.concatenate(
            [
                jnp.concatenate(
                    [
                        recv[pl.ds(4 * c + zi, 64, stride=8), :],
                        recv[pl.ds(4 * c + 3, 64, stride=8), :],
                    ],
                    1,
                )
                for c in range(2)
            ],
            0,
        )
        high, low = split(lines)
        columns = mm_nt(unpack, jnp.concatenate([high, low], 0))
        highs.append(columns[:, :128].astype(BF))
        lows.append(columns[:, 128:].astype(BF))
    z = three(
        mm, (jnp.concatenate(highs, 1), jnp.concatenate(lows, 1)), (fz[0:384, :], fz[384:768, :])
    )
    low_lane = iota((64, 128), 1) < 64
    for plane in range(2):
        for c in range(2):
            block = z[128 * plane : 128 * plane + 128, 128 * c : 128 * c + 128]
            even = jnp.where(sphere_rows(plane, 0, s), block[:64], 0.0)
            odd = jnp.where(sphere_rows(plane, 1, s), block[64:], 0.0)
            kinds = (
                jnp.where(low_lane, even, 0.0),
                pltpu.roll(jnp.where(low_lane, odd, even), 64, 1),
                jnp.where(low_lane, 0.0, odd),
            )
            for k, tile in enumerate(kinds):
                at = 1152 * plane + 2 * k + c
                out[pl.ds(at, 32, stride=6), :] = tile[24:56]
                out[pl.ds(at + 432, 24, stride=6), :] = tile[:24]


def call(
    kernel, name, out_shape, args, scratch=(), anywhere=(), anywhere_out=(), limit=VMEM_LIMIT
):
    specs = [
        pl.BlockSpec(memory_space=pl.ANY if k in anywhere else pltpu.VMEM)
        for k in range(len(args))
    ]
    shapes = [jax.ShapeDtypeStruct(shape, F32) for shape in out_shape]
    out = pl.pallas_call(
        kernel,
        name=name,
        out_shape=shapes,
        in_specs=specs,
        out_specs=[
            pl.BlockSpec(memory_space=pl.ANY if k in anywhere_out else pltpu.VMEM)
            for k in range(len(shapes))
        ],
        scratch_shapes=list(scratch),
        compiler_params=pltpu.CompilerParams(vmem_limit_bytes=limit),
    )(*args)
    return out


def body(psi_g, vloc, beta, blk_slot, blk_tile, dmat):
    t = {
        name: jnp.asarray(value) for name, value in tables().items()
    }
    psi = psi_g[0].transpose(1, 0, 2).reshape(3, 2, 288, 128).transpose(0, 2, 1, 3)
    psi = psi.reshape(1728, 128)
    send, own = call(
        kernel_z_inverse,
        "z_inverse",
        [(512, 128), (1032, 128)],
        (psi, t["wz"], beta.reshape(1024, 128), blk_slot[None], blk_tile[None]),
        [
            pltpu.VMEM((2, 384, 128), F32),
            pltpu.VMEM((768, 256), BF),
            pltpu.VMEM((8, 128), F32),
            pltpu.SemaphoreType.DMA((7,)),
        ],
        anywhere=(0, 1, 2),
        anywhere_out=(1,),
        limit=60 * 1024 * 1024,
    )
    betas = [own] + [
        lax.ppermute(own, "band", [(i, (i + k) % 4) for i in range(4)]) for k in (1, 3, 2)
    ]

    def exchange(x):
        x = lax.all_to_all(x.reshape(64, 8, 128), "fft", 0, 0, tiled=True)
        return x.reshape(512, 128)

    recv = exchange(send)
    vloc_tiles = vloc.reshape(3, 288, 128).transpose(1, 0, 2)
    dmat_rows = dmat.transpose(1, 2, 0).reshape(64, 64)
    field, near, far = call(
        kernel_field,
        "field",
        [(864, 256), (96, 128), (32, 128)],
        (recv, t["ey"], t["ix"], t["u"], dmat_rows, *betas),
        [
            pltpu.VMEM((896, 256), BF),
            pltpu.VMEM((896, 256), BF),
            pltpu.VMEM((512, 256), F32),
            pltpu.VMEM((1024, 512), BF),
            pltpu.SemaphoreType.DMA,
        ],
        anywhere=(2,),
    )

    def moved(x, step):
        return lax.ppermute(x, "fft", [(i, (i + step) % 64) for i in range(64)])

    sides = (moved(near, 1), moved(near, -1), moved(far, 2), moved(far, -2))
    (send,) = call(
        kernel_back,
        "back",
        [(512, 128)],
        (field, near, *sides, *betas, vloc_tiles, t["fx"], t["fy"], t["ut"]),
        [
            pltpu.VMEM((16, 256), F32),
            pltpu.VMEM((512, 512), BF),
            pltpu.VMEM((3, 288, 128), F32),
            pltpu.VMEM((1024, 512), BF),
            pltpu.VMEM((768, 256), BF),
            pltpu.VMEM((384, 128), BF),
            pltpu.SemaphoreType.DMA((6,)),
        ],
        anywhere=(10, 11, 12, 13),
    )
    (out,) = call(kernel_z_forward, "z_forward", [(1728, 128)], (exchange(send), t["fz"]))
    out = out.reshape(3, 288, 2, 128).transpose(0, 2, 1, 3).reshape(3, 2, N * N)
    return out.transpose(1, 0, 2)[None]


def solution(mesh):
    in_specs = (
        P("band", None, "fft", None),
        P("fft", None),
        P(("fft", "band"), None, None),
        P(("fft", "band")),
        P(("fft", "band")),
        P("fft", None, None),
    )
    out_specs = P("band", None, "fft", None)
    return jax.shard_map(body, mesh=mesh, in_specs=in_specs, out_specs=out_specs, check_vma=False)
```

```python
import functools

import jax
import jax.numpy as jnp
import ml_dtypes
import numpy as np
from jax import lax
from jax.experimental import pallas as pl
from jax.experimental.pallas import tpu as pltpu
from jax.sharding import PartitionSpec as P

N = 192
R2 = 48 * 48
BF = jnp.bfloat16
F32 = jnp.float32
VMEM_LIMIT = 48 * 1024 * 1024


def trig(freqs, points):
    angle = 2.0 * np.pi * (np.outer(freqs, points) % N) / N
    return np.cos(angle) / np.sqrt(N), np.sin(angle) / np.sqrt(N)


def pair_of(table):
    table = np.asarray(table, np.float32)
    high = table.astype(ml_dtypes.bfloat16)
    low = (table - high.astype(np.float32)).astype(ml_dtypes.bfloat16)
    return np.concatenate([high, low], 0)


KZ = np.concatenate([np.arange(64), np.arange(128, 192)])
SIGNED = np.concatenate([np.arange(64), np.arange(-64, 0)])
YS = [2 * np.arange(96), 2 * np.arange(96) + 1]


@functools.cache
def tables():
    t = {}
    blocks = []
    for zi in range(3):
        c, s = trig(3 * np.arange(64) + zi, KZ)
        blocks += [np.concatenate([c, -s], 1), np.concatenate([s, c], 1)]
    t["wz"] = pair_of(np.concatenate(blocks, 0))
    c, s = trig(np.concatenate(YS), SIGNED)
    t["ey"] = pair_of(
        np.concatenate([np.concatenate([c, -s], 1), np.concatenate([s, c], 1)], 0)
    )
    c, s = trig(SIGNED, np.arange(N))
    gap = np.zeros((128, 64))
    even = [np.concatenate([v, gap], 1) for v in (c, s, -s, c)]
    odd = [np.concatenate([gap, v], 1) for v in (c, s, -s, c)]
    t["ix"] = np.concatenate(
        [
            pair_of(np.block([[even[0], even[1]], [even[2], even[3]]])),
            pair_of(np.block([[odd[0], odd[1]], [odd[2], odd[3]]])),
        ],
        0,
    )
    parts = {}
    c, s = trig(np.arange(N), SIGNED)
    gap = np.zeros((64, 128))
    for name, table in (("c", c), ("s", s)):
        parts[name] = (np.concatenate([table, gap], 0), np.concatenate([gap, table], 0))

    def forward_x(which):
        cc, ss = parts["c"][which], parts["s"][which]
        first, second = np.concatenate([cc, -ss], 1), np.concatenate([ss, cc], 1)
        return np.concatenate([first[:128], second[:128], first[128:], second[128:]], 0)

    t["fx"] = np.concatenate([pair_of(forward_x(0)), pair_of(forward_x(1))], 0)
    c, s = trig(SIGNED, np.concatenate(YS))
    t["fy"] = pair_of(
        np.concatenate([np.concatenate([c, s], 1), np.concatenate([-s, c], 1)], 0)
    )
    blocks = []
    for zi in range(3):
        c, s = trig(3 * np.arange(64) + zi, KZ)
        blocks += [np.concatenate([c, -s], 1), np.concatenate([s, c], 1)]
    t["fz"] = pair_of(np.concatenate(blocks, 0))
    u = np.zeros((128, 384), np.float32)
    for zi in range(3):
        for p in range(128):
            u[32 * zi + 8 * (p >= 64) + p % 8, 128 * zi + p] = 1.0
    t["u"] = u.astype(ml_dtypes.bfloat16)
    t["ut"] = np.concatenate([u[:, 128 * zi : 128 * zi + 128].T for zi in range(3)], 0).astype(
        ml_dtypes.bfloat16
    )
    return t


def split(x):
    high = x.astype(BF)
    return high, (x - high.astype(F32)).astype(BF)


def mm(a, b):
    return jnp.dot(a, b, preferred_element_type=F32)


def mm_nt(a, b):
    return lax.dot_general(a, b, (((1,), (1,)), ((), ())), preferred_element_type=F32)


def three(product, a, b):
    return product(a[0], b[0]) + (product(a[0], b[1]) + product(a[1], b[0]))


def iota(shape, dim):
    return lax.broadcasted_iota(jnp.int32, shape, dim)


def masks_sp():
    s, p = iota((64, 128), 0), iota((64, 128), 1)
    ky = jnp.where(p < 64, p, p - 128)
    away = 64 - jnp.abs(ky)
    inside = ky * ky + s * s <= R2
    clash = away * away + (64 - s) * (64 - s) <= R2
    other = (p - 64) * (p - 64) + (64 - s) * (64 - s) <= R2
    return inside & ~clash, inside & clash, other


def line_places(r, s):
    plane, rest = r // 128, r % 128
    ky = 2 * (rest % 64 - 24) + rest // 64
    here = jnp.where(plane == 0, s, 64 - s)
    away = 64 - jnp.abs(ky)
    inside = ky * ky + here * here <= R2
    clash = (away * away + (64 - s) * (64 - s) <= R2) & (plane == 0)
    place = jnp.where(plane == 0, jnp.where(ky < 0, ky + 128, ky), ky + 64)
    main = jnp.where(inside & ~clash, place, -1)
    spare = jnp.where(inside & clash, jnp.where(ky < 0, 8, 0) + (ky + 64) % 8, -1)
    return main, spare


def one_hot(condition):
    return jnp.where(condition, 1.0, 0.0).astype(BF)


def sphere_rows(plane, parity, s):
    m, lane = iota((64, 128), 0), iota((64, 128), 1)
    ky = 2 * (m - 24) + parity
    kz = jnp.where(lane < 64, lane, lane - 128)
    kx = s - 64 * plane
    return ky * ky + kz * kz + kx * kx <= R2


def kernel_z_inverse(psi, wz_in, beta, slot, tile, send, own, buf, wz, sems):
    s = lax.axis_index("fft")
    own[1024:1025, :] = slot[...].astype(F32)
    own[1025:1026, :] = ((tile[...] % 3) * 288 + tile[...] // 3).astype(F32)
    own[1026:1032, :] = jnp.zeros((6, 128), F32)
    later = [pltpu.make_async_copy(beta, own.at[pl.ds(0, 1024)], sems.at[5])]
    copies = [pltpu.make_async_copy(wz_in, wz, sems.at[4])]
    for plane in range(2):
        base = 1152 * plane
        for k, (src, dst, rows) in enumerate(((432, 0, 144), (0, 144, 152))):
            copies.append(
                pltpu.make_async_copy(
                    psi.at[pl.ds(base + src, rows)],
                    buf.at[plane, pl.ds(dst, rows)],
                    sems.at[2 * plane + k],
                )
            )
    for copy in copies[1:] + copies[:1] + later:
        copy.start()
    r = iota((1, 256), 1)
    main, spare = line_places(r, s)
    j = iota((128, 256), 0)
    pack = jnp.concatenate(
        [one_hot(j == main), one_hot((j % 32 == spare) & (j < 96))], axis=0
    )
    for copy in copies:
        copy.wait()
    lane = iota((64, 128), 1)
    rows = []
    for plane in range(2):
        lines = [[], []]
        for c in range(2):
            t = [buf[plane, pl.ds(2 * k + c, 64, stride=6), :] for k in range(3)]
            middle = pltpu.roll(t[1], 64, 1)
            even = jnp.where(lane < 64, t[0], middle)
            odd = jnp.where(lane < 64, middle, t[2])
            lines[0].append(jnp.where(sphere_rows(plane, 0, s), even, 0.0))
            lines[1].append(jnp.where(sphere_rows(plane, 1, s), odd, 0.0))
        rows += [jnp.concatenate(lines[0], 1), jnp.concatenate(lines[1], 1)]
    high, low = split(jnp.concatenate(rows, 0))
    packed = (mm(pack, high).astype(BF), mm(pack, low).astype(BF))
    out = three(mm_nt, (wz[0:384, :], wz[384:768, :]), packed)
    for c in range(2):
        block = [out[(2 * zi + c) * 64 : (2 * zi + c) * 64 + 64] for zi in range(3)]
        for zi in range(3):
            send[pl.ds(4 * c + zi, 64, stride=8), :] = block[zi][:, :128]
        send[pl.ds(4 * c + 3, 64, stride=8), :] = jnp.where(
            lane < 32, block[0][:, 128:], jnp.where(lane < 64, block[1][:, 128:], block[2][:, 128:])
        )
    for copy in later:
        copy.wait()


def block_ids(betas, row):
    return jnp.concatenate([b[1024 + row : 1025 + row, :] for b in betas], 1)


def as_column(ids):
    return jnp.broadcast_to(ids, (8, 512)).T[:, 0:1]


def slot_hot(betas):
    return one_hot(as_column(block_ids(betas, 0)).astype(jnp.int32) == iota((512, 256), 1))


def kernel_field(
    recv, ey, ix_in, u, dmat, b0, b1, b2, b3,
    field, near, far, rows_h, rows_l, field_rows, ix, sem,
):
    copy = pltpu.make_async_copy(ix_in, ix, sem)
    copy.start()
    main, spare, other = masks_sp()
    spread = []
    for c in range(2):
        high, low = split(recv[pl.ds(4 * c + 3, 64, stride=8), :])
        spread.append(mm(high, u[...]) + mm(low, u[...]))
    lines = []
    for zi in range(3):
        first, second = [], []
        for c in range(2):
            got = recv[pl.ds(4 * c + zi, 64, stride=8), :]
            extra = spread[c][:, 128 * zi : 128 * zi + 128]
            first.append(jnp.where(main, got, jnp.where(spare, extra, 0.0)))
            second.append(pltpu.roll(jnp.where(other, got, 0.0), 64, 1))
        lines += [jnp.concatenate(first, 1), jnp.concatenate(second, 1)]
    g = three(mm_nt, (ey[0:384, :], ey[384:768, :]), split(jnp.concatenate(lines, 0)))
    copy.wait()
    out = []
    for parity in range(2):
        a = 96 * parity
        table = [ix[512 * parity + 256 * i : 512 * parity + 256 * i + 256, :] for i in range(2)]
        block = jnp.concatenate(
            [
                jnp.concatenate(
                    [
                        g[a : a + 96, 128 * zi : 128 * zi + 128],
                        g[192 + a : 288 + a, 128 * zi : 128 * zi + 128],
                    ],
                    1,
                )
                for zi in range(3)
            ],
            0,
        )
        out.append(three(mm, split(block), table))
    even, odd = out
    for c in range(2):
        a = 256 * c
        kinds = (
            even[:, a : a + 128],
            even[:, a + 128 : a + 256] + odd[:, a : a + 128],
            odd[:, a + 128 : a + 256],
        )
        for k, tile in enumerate(kinds):
            span = pl.ds(288 * k, 288)
            lanes = pl.ds(128 * c, 128)
            field[span, lanes] = tile
            high, low = split(tile)
            rows_h[span, lanes] = high
            rows_l[span, lanes] = low
    rows_h[864:896, :] = jnp.zeros((32, 256), BF)
    rows_l[864:896, :] = jnp.zeros((32, 256), BF)

    betas = (b0, b1, b2, b3)
    tile_of = as_column(block_ids(betas, 1)).astype(jnp.int32)
    pick = one_hot(tile_of == iota((512, 896), 1))
    field_rows[...] = mm(pick, rows_h[...]) + mm(pick, rows_l[...])
    lane = iota((128, 128), 1)
    sums = []
    for k, beta in enumerate(betas):
        total = jnp.zeros((128, 128), F32)
        for j in range(8):
            projector = beta[pl.ds(j, 128, stride=8), :]
            for c in range(2):
                value = field_rows[128 * k : 128 * k + 128, 128 * c : 128 * c + 128] * projector
                total = jnp.where(
                    lane == 8 * c + j, jnp.sum(value, axis=1, keepdims=True), total
                )
        sums.append(total.T[:16])
    high, low = split(jnp.concatenate(sums, 1))
    slots = slot_hot(betas)
    coef = mm(high, slots) + mm(low, slots)
    coef = jnp.where(iota((16, 256), 1) < 192, coef, 0.0)
    near[0:64, :] = jnp.concatenate([dmat[...], jnp.zeros((64, 64), F32)], 1)
    near[64:80, :] = coef[:, :128]
    near[80:96, :] = coef[:, 128:]
    far[0:16, :] = coef[:, :128]
    far[16:32, :] = coef[:, 128:]


def kernel_back(
    field, near, below, above, below2, above2, b0, b1, b2, b3,
    vloc_in, fx_in, fy_in, ut_in, send, scr, rows, vloc, fx, fy, ut, sems,
):
    copies = [
        pltpu.make_async_copy(vloc_in.at[:, zi, :], vloc.at[zi], sems.at[zi]) for zi in range(3)
    ] + [
        pltpu.make_async_copy(fx_in, fx, sems.at[3]),
        pltpu.make_async_copy(fy_in, fy, sems.at[4]),
        pltpu.make_async_copy(ut_in, ut, sems.at[5]),
    ]
    for copy in copies:
        copy.start()
    lane = iota((16, 128), 1)

    def half(ref, k):
        return ref[64 + 16 * k : 80 + 16 * k, :]

    def shifted(low, high, up):
        low, high = pltpu.roll(low, 64, 1), pltpu.roll(high, 64, 1)
        if up:
            return jnp.where(lane < 64, 0.0, low), jnp.where(lane < 64, low, high)
        return jnp.where(lane < 64, low, high), jnp.where(lane < 64, high, 0.0)

    from_below = shifted(half(below, 0), half(below, 1), False)
    from_above = shifted(half(above, 0), half(above, 1), True)
    tot = [
        half(near, 0) + from_below[0] + from_above[0] + below2[16:32, :],
        half(near, 1) + from_below[1] + from_above[1] + above2[0:16, :],
    ]
    tot[1] = jnp.where(lane < 64, tot[1], 0.0)
    wide = iota((64, 128), 1)
    coupling = [
        jnp.where(wide < 64, below[0:64, :], pltpu.roll(near[0:64, :], 64, 1)),
        jnp.where(wide < 64, above[0:64, :], 0.0),
    ]
    for h in range(2):
        for c in range(2):
            coef = tot[h][8 * c : 8 * c + 8, :]
            for j in range(8):
                row = jnp.sum(coupling[h][8 * j : 8 * j + 8, :] * coef, axis=0, keepdims=True)
                scr[8 * c + j : 8 * c + j + 1, 128 * h : 128 * h + 128] = row
    betas = (b0, b1, b2, b3)
    slots = slot_hot(betas)
    high, low = split(scr[...])
    weight = mm_nt(slots, high) + mm_nt(slots, low)
    for k, beta in enumerate(betas):
        span = slice(128 * k, 128 * k + 128)
        terms = [jnp.zeros((128, 128), F32), jnp.zeros((128, 128), F32)]
        for j in range(8):
            projector = beta[pl.ds(j, 128, stride=8), :]
            for c in range(2):
                terms[c] = terms[c] + projector * weight[span, 8 * c + j : 8 * c + j + 1]
        for c in range(2):
            high, low = split(terms[c])
            rows[span, 128 * c : 128 * c + 128] = high
            rows[span, 256 + 128 * c : 384 + 128 * c] = low
    tile_of = block_ids(betas, 1).astype(jnp.int32)
    put = one_hot(iota((864, 512), 0) == tile_of)
    both = mm(put, rows[...])
    nonloc = both[:, :256] + both[:, 256:]
    for copy in copies:
        copy.wait()
    kinds = []
    for k in range(3):
        factor = jnp.concatenate([vloc[zi, pl.ds(k, 96, stride=3), :] for zi in range(3)], 0)
        at = slice(288 * k, 288 * k + 288)
        kinds.append(split(field[at, :] * jnp.concatenate([factor, factor], 1) + nonloc[at, :]))
    g = []
    for parity in range(2):
        table = [fx[1024 * parity + 512 * i : 1024 * parity + 512 * i + 512, :] for i in range(2)]
        lines = [jnp.concatenate([kinds[parity][i], kinds[parity + 1][i]], 1) for i in range(2)]
        g.append(split(three(mm, lines, table)))
    lines = [
        jnp.concatenate(
            [
                jnp.concatenate(
                    [
                        g[parity][i][96 * zi : 96 * zi + 96, 128 * c : 128 * c + 128]
                        for zi in range(3)
                    ],
                    1,
                )
                for c in range(2)
                for parity in range(2)
            ],
            0,
        )
        for i in range(2)
    ]
    h = three(mm, (fy[0:256, :], fy[256:512, :]), lines)
    main, spare, _ = masks_sp()
    spares = [jnp.zeros((64, 128), F32), jnp.zeros((64, 128), F32)]
    for zi in range(3):
        for c in range(2):
            turned = h[128 * c : 128 * c + 128, 128 * zi : 128 * zi + 128].T
            first = turned[:64]
            second = pltpu.roll(turned[64:], 64, 1)
            send[pl.ds(4 * c + zi, 64, stride=8), :] = jnp.where(main, first, second)
            high, low = split(jnp.where(spare, first, 0.0))
            move = ut[128 * zi : 128 * zi + 128, :]
            spares[c] = spares[c] + (mm(high, move) + mm(low, move))
    for c in range(2):
        send[pl.ds(4 * c + 3, 64, stride=8), :] = spares[c]


def kernel_z_forward(recv, fz, out):
    s = lax.axis_index("fft")
    out[...] = jnp.zeros((1728, 128), F32)
    r = iota((256, 1), 0)
    main, spare = line_places(r, s)
    lane = iota((256, 128), 1)
    keep = one_hot(lane == main)
    highs, lows = [], []
    for zi in range(3):
        unpack = jnp.concatenate(
            [keep, one_hot((lane == spare + 32 * zi) & (spare >= 0))], 1
        )
        lines = jnp.concatenate(
            [
                jnp.concatenate(
                    [
                        recv[pl.ds(4 * c + zi, 64, stride=8), :],
                        recv[pl.ds(4 * c + 3, 64, stride=8), :],
                    ],
                    1,
                )
                for c in range(2)
            ],
            0,
        )
        high, low = split(lines)
        columns = mm_nt(unpack, jnp.concatenate([high, low], 0))
        highs.append(columns[:, :128].astype(BF))
        lows.append(columns[:, 128:].astype(BF))
    z = three(
        mm, (jnp.concatenate(highs, 1), jnp.concatenate(lows, 1)), (fz[0:384, :], fz[384:768, :])
    )
    low_lane = iota((64, 128), 1) < 64
    for plane in range(2):
        for c in range(2):
            block = z[128 * plane : 128 * plane + 128, 128 * c : 128 * c + 128]
            even = jnp.where(sphere_rows(plane, 0, s), block[:64], 0.0)
            odd = jnp.where(sphere_rows(plane, 1, s), block[64:], 0.0)
            kinds = (
                jnp.where(low_lane, even, 0.0),
                pltpu.roll(jnp.where(low_lane, odd, even), 64, 1),
                jnp.where(low_lane, 0.0, odd),
            )
            for k, tile in enumerate(kinds):
                at = 1152 * plane + 2 * k + c
                out[pl.ds(at, 32, stride=6), :] = tile[24:56]
                out[pl.ds(at + 432, 24, stride=6), :] = tile[:24]


def call(kernel, name, out_shape, args, scratch=(), anywhere=(), limit=VMEM_LIMIT):
    specs = [
        pl.BlockSpec(memory_space=pl.ANY if k in anywhere else pltpu.VMEM)
        for k in range(len(args))
    ]
    shapes = [jax.ShapeDtypeStruct(shape, F32) for shape in out_shape]
    out = pl.pallas_call(
        kernel,
        name=name,
        out_shape=shapes,
        in_specs=specs,
        out_specs=[pl.BlockSpec(memory_space=pltpu.VMEM)] * len(shapes),
        scratch_shapes=list(scratch),
        compiler_params=pltpu.CompilerParams(vmem_limit_bytes=limit),
    )(*args)
    return out


def body(psi_g, vloc, beta, blk_slot, blk_tile, dmat):
    t = {
        name: jnp.asarray(value) for name, value in tables().items()
    }
    psi = psi_g[0].transpose(1, 0, 2).reshape(3, 2, 288, 128).transpose(0, 2, 1, 3)
    psi = psi.reshape(1728, 128)
    send, own = call(
        kernel_z_inverse,
        "z_inverse",
        [(512, 128), (1032, 128)],
        (psi, t["wz"], beta.reshape(1024, 128), blk_slot[None], blk_tile[None]),
        [
            pltpu.VMEM((2, 384, 128), F32),
            pltpu.VMEM((768, 256), BF),
            pltpu.SemaphoreType.DMA((6,)),
        ],
        anywhere=(0, 1, 2),
        limit=60 * 1024 * 1024,
    )
    betas = [own] + [
        lax.ppermute(own, "band", [(i, (i + k) % 4) for i in range(4)]) for k in (1, 3, 2)
    ]

    def exchange(x):
        x = lax.all_to_all(x.reshape(64, 8, 128), "fft", 0, 0, tiled=True)
        return x.reshape(512, 128)

    recv = exchange(send)
    vloc_tiles = vloc.reshape(3, 288, 128).transpose(1, 0, 2)
    dmat_rows = dmat.transpose(1, 2, 0).reshape(64, 64)
    field, near, far = call(
        kernel_field,
        "field",
        [(864, 256), (96, 128), (32, 128)],
        (recv, t["ey"], t["ix"], t["u"], dmat_rows, *betas),
        [
            pltpu.VMEM((896, 256), BF),
            pltpu.VMEM((896, 256), BF),
            pltpu.VMEM((512, 256), F32),
            pltpu.VMEM((1024, 512), BF),
            pltpu.SemaphoreType.DMA,
        ],
        anywhere=(2,),
    )

    def moved(x, step):
        return lax.ppermute(x, "fft", [(i, (i + step) % 64) for i in range(64)])

    sides = (moved(near, 1), moved(near, -1), moved(far, 2), moved(far, -2))
    (send,) = call(
        kernel_back,
        "back",
        [(512, 128)],
        (field, near, *sides, *betas, vloc_tiles, t["fx"], t["fy"], t["ut"]),
        [
            pltpu.VMEM((16, 256), F32),
            pltpu.VMEM((512, 512), BF),
            pltpu.VMEM((3, 288, 128), F32),
            pltpu.VMEM((2048, 256), BF),
            pltpu.VMEM((512, 384), BF),
            pltpu.VMEM((384, 128), BF),
            pltpu.SemaphoreType.DMA((6,)),
        ],
        anywhere=(10, 11, 12, 13),
    )
    (out,) = call(kernel_z_forward, "z_forward", [(1728, 128)], (exchange(send), t["fz"]))
    out = out.reshape(3, 288, 2, 128).transpose(0, 2, 1, 3).reshape(3, 2, N * N)
    return out.transpose(1, 0, 2)[None]


def solution(mesh):
    in_specs = (
        P("band", None, "fft", None),
        P("fft", None),
        P(("fft", "band"), None, None),
        P(("fft", "band")),
        P(("fft", "band")),
        P("fft", None, None),
    )
    out_specs = P("band", None, "fft", None)
    return jax.shard_map(body, mesh=mesh, in_specs=in_specs, out_specs=out_specs, check_vma=False)
```

```python
import functools

import jax
import jax.numpy as jnp
import ml_dtypes
import numpy as np
from jax import lax
from jax.experimental import pallas as pl
from jax.experimental.pallas import tpu as pltpu
from jax.sharding import PartitionSpec as P

N = 192
R2 = 48 * 48
BF = jnp.bfloat16
F32 = jnp.float32
VMEM_LIMIT = 48 * 1024 * 1024


def trig(freqs, points):
    angle = 2.0 * np.pi * (np.outer(freqs, points) % N) / N
    return np.cos(angle) / np.sqrt(N), np.sin(angle) / np.sqrt(N)


def pair_of(table):
    table = np.asarray(table, np.float32)
    high = table.astype(ml_dtypes.bfloat16)
    low = (table - high.astype(np.float32)).astype(ml_dtypes.bfloat16)
    return np.concatenate([high, low], 0)


KZ = np.concatenate([np.arange(64), np.arange(128, 192)])
SIGNED = np.concatenate([np.arange(64), np.arange(-64, 0)])
YS = [2 * np.arange(96), 2 * np.arange(96) + 1]


@functools.cache
def tables():
    t = {}
    blocks = []
    for zi in range(3):
        c, s = trig(3 * np.arange(64) + zi, KZ)
        blocks += [np.concatenate([c, -s], 1), np.concatenate([s, c], 1)]
    t["wz"] = pair_of(np.concatenate(blocks, 0))
    c, s = trig(np.concatenate(YS), SIGNED)
    t["ey"] = pair_of(
        np.concatenate([np.concatenate([c, -s], 1), np.concatenate([s, c], 1)], 0)
    )
    c, s = trig(SIGNED, np.arange(N))
    gap = np.zeros((128, 64))
    even = [np.concatenate([v, gap], 1) for v in (c, s, -s, c)]
    odd = [np.concatenate([gap, v], 1) for v in (c, s, -s, c)]
    t["ix"] = np.concatenate(
        [
            pair_of(np.block([[even[0], even[1]], [even[2], even[3]]])),
            pair_of(np.block([[odd[0], odd[1]], [odd[2], odd[3]]])),
        ],
        0,
    )
    parts = {}
    c, s = trig(np.arange(N), SIGNED)
    gap = np.zeros((64, 128))
    for name, table in (("c", c), ("s", s)):
        parts[name] = (np.concatenate([table, gap], 0), np.concatenate([gap, table], 0))

    def forward_x(which):
        cc, ss = parts["c"][which], parts["s"][which]
        first, second = np.concatenate([cc, -ss], 1), np.concatenate([ss, cc], 1)
        return np.concatenate([first[:128], second[:128], first[128:], second[128:]], 0)

    t["fx"] = np.concatenate([pair_of(forward_x(0)), pair_of(forward_x(1))], 0)
    c, s = trig(SIGNED, np.concatenate(YS))
    t["fy"] = pair_of(
        np.concatenate([np.concatenate([c, s], 1), np.concatenate([-s, c], 1)], 0)
    )
    blocks = []
    for zi in range(3):
        c, s = trig(3 * np.arange(64) + zi, KZ)
        blocks += [np.concatenate([c, -s], 1), np.concatenate([s, c], 1)]
    t["fz"] = pair_of(np.concatenate(blocks, 0))
    u = np.zeros((128, 384), np.float32)
    for zi in range(3):
        for p in range(128):
            u[32 * zi + 8 * (p >= 64) + p % 8, 128 * zi + p] = 1.0
    t["u"] = u.astype(ml_dtypes.bfloat16)
    t["ut"] = np.concatenate([u[:, 128 * zi : 128 * zi + 128].T for zi in range(3)], 0).astype(
        ml_dtypes.bfloat16
    )
    return t


def split(x):
    high = x.astype(BF)
    return high, (x - high.astype(F32)).astype(BF)


def mm(a, b):
    return jnp.dot(a, b, preferred_element_type=F32)


def mm_nt(a, b):
    return lax.dot_general(a, b, (((1,), (1,)), ((), ())), preferred_element_type=F32)


def three(product, a, b):
    return product(a[0], b[0]) + (product(a[0], b[1]) + product(a[1], b[0]))


def iota(shape, dim):
    return lax.broadcasted_iota(jnp.int32, shape, dim)


def masks_sp():
    s, p = iota((64, 128), 0), iota((64, 128), 1)
    ky = jnp.where(p < 64, p, p - 128)
    away = 64 - jnp.abs(ky)
    inside = ky * ky + s * s <= R2
    clash = away * away + (64 - s) * (64 - s) <= R2
    other = (p - 64) * (p - 64) + (64 - s) * (64 - s) <= R2
    return inside & ~clash, inside & clash, other


def line_places(r, s):
    plane, rest = r // 128, r % 128
    ky = 2 * (rest % 64 - 24) + rest // 64
    here = jnp.where(plane == 0, s, 64 - s)
    away = 64 - jnp.abs(ky)
    inside = ky * ky + here * here <= R2
    clash = (away * away + (64 - s) * (64 - s) <= R2) & (plane == 0)
    place = jnp.where(plane == 0, jnp.where(ky < 0, ky + 128, ky), ky + 64)
    main = jnp.where(inside & ~clash, place, -1)
    spare = jnp.where(inside & clash, jnp.where(ky < 0, 8, 0) + (ky + 64) % 8, -1)
    return main, spare


def one_hot(condition):
    return jnp.where(condition, 1.0, 0.0).astype(BF)


def sphere_rows(plane, parity, s):
    m, lane = iota((64, 128), 0), iota((64, 128), 1)
    ky = 2 * (m - 24) + parity
    kz = jnp.where(lane < 64, lane, lane - 128)
    kx = s - 64 * plane
    return ky * ky + kz * kz + kx * kx <= R2


def kernel_z_inverse(psi, wz_in, send, buf, wz, sems):
    s = lax.axis_index("fft")
    copies = []
    for plane in range(2):
        base = 1152 * plane
        for k, (src, dst, rows) in enumerate(((432, 0, 144), (0, 144, 152))):
            copies.append(
                pltpu.make_async_copy(
                    psi.at[pl.ds(base + src, rows)],
                    buf.at[plane, pl.ds(dst, rows)],
                    sems.at[2 * plane + k],
                )
            )
    copies.append(pltpu.make_async_copy(wz_in, wz, sems.at[4]))
    for copy in copies:
        copy.start()
    main, spare = line_places(iota((1, 256), 1), s)
    j = iota((128, 256), 0)
    pack = jnp.concatenate(
        [one_hot(j == main), one_hot((j % 32 == spare) & (j < 96))], axis=0
    )
    lane = iota((64, 128), 1)
    rows = []
    for copy in copies[:4]:
        copy.wait()
    for plane in range(2):
        lines = [[], []]
        for c in range(2):
            t = [buf[plane, pl.ds(2 * k + c, 64, stride=6), :] for k in range(3)]
            middle = pltpu.roll(t[1], 64, 1)
            even = jnp.where(lane < 64, t[0], middle)
            odd = jnp.where(lane < 64, middle, t[2])
            lines[0].append(jnp.where(sphere_rows(plane, 0, s), even, 0.0))
            lines[1].append(jnp.where(sphere_rows(plane, 1, s), odd, 0.0))
        rows += [jnp.concatenate(lines[0], 1), jnp.concatenate(lines[1], 1)]
    high, low = split(jnp.concatenate(rows, 0))
    packed = (mm(pack, high).astype(BF), mm(pack, low).astype(BF))
    copies[4].wait()
    out = three(mm_nt, (wz[0:384, :], wz[384:768, :]), packed)
    for c in range(2):
        block = [out[(2 * zi + c) * 64 : (2 * zi + c) * 64 + 64] for zi in range(3)]
        for zi in range(3):
            send[pl.ds(4 * c + zi, 64, stride=8), :] = block[zi][:, :128]
        send[pl.ds(4 * c + 3, 64, stride=8), :] = jnp.where(
            lane < 32, block[0][:, 128:], jnp.where(lane < 64, block[1][:, 128:], block[2][:, 128:])
        )


def tile_rows(tiles):
    return (tiles % 3) * 288 + tiles // 3


def as_column(ids):
    return jnp.broadcast_to(ids.astype(F32), (8, 512)).T[:, 0:1].astype(jnp.int32)


def kernel_field(
    recv, ey, ix, u, field, rows_h, rows_l,
):
    main, spare, other = masks_sp()
    spread = []
    for c in range(2):
        high, low = split(recv[pl.ds(4 * c + 3, 64, stride=8), :])
        spread.append(mm(high, u[...]) + mm(low, u[...]))
    lines = []
    for zi in range(3):
        first, second = [], []
        for c in range(2):
            got = recv[pl.ds(4 * c + zi, 64, stride=8), :]
            extra = spread[c][:, 128 * zi : 128 * zi + 128]
            first.append(jnp.where(main, got, jnp.where(spare, extra, 0.0)))
            second.append(pltpu.roll(jnp.where(other, got, 0.0), 64, 1))
        lines += [jnp.concatenate(first, 1), jnp.concatenate(second, 1)]
    g = three(mm_nt, (ey[0:384, :], ey[384:768, :]), split(jnp.concatenate(lines, 0)))
    out = []
    for parity in range(2):
        a = 96 * parity
        table = [ix[512 * parity + 256 * i : 512 * parity + 256 * i + 256, :] for i in range(2)]
        block = jnp.concatenate(
            [
                jnp.concatenate(
                    [
                        g[a : a + 96, 128 * zi : 128 * zi + 128],
                        g[192 + a : 288 + a, 128 * zi : 128 * zi + 128],
                    ],
                    1,
                )
                for zi in range(3)
            ],
            0,
        )
        out.append(three(mm, split(block), table))
    even, odd = out
    for c in range(2):
        a = 256 * c
        kinds = (
            even[:, a : a + 128],
            even[:, a + 128 : a + 256] + odd[:, a : a + 128],
            odd[:, a + 128 : a + 256],
        )
        for k, tile in enumerate(kinds):
            span = pl.ds(288 * k, 288)
            lanes = pl.ds(128 * c, 128)
            field[span, lanes] = tile
            high, low = split(tile)
            rows_h[span, lanes] = high
            rows_l[span, lanes] = low
    rows_h[864:896, :] = jnp.zeros((32, 256), BF)
    rows_l[864:896, :] = jnp.zeros((32, 256), BF)


def kernel_project(rows_h, rows_l, dmat, ids, b0, b1, b2, b3, near, far, slots_out, field_rows):
    betas = (b0, b1, b2, b3)
    tile_of = as_column(tile_rows(ids[1:2, :]))
    pick = one_hot(tile_of == iota((512, 896), 1))
    field_rows[...] = mm(pick, rows_h[...]) + mm(pick, rows_l[...])
    lane = iota((128, 128), 1)
    sums = []
    for k, beta in enumerate(betas):
        total = jnp.zeros((128, 128), F32)
        for j in range(8):
            projector = beta[pl.ds(j, 128, stride=8), :]
            for c in range(2):
                value = field_rows[128 * k : 128 * k + 128, 128 * c : 128 * c + 128] * projector
                total = jnp.where(
                    lane == 8 * c + j, jnp.sum(value, axis=1, keepdims=True), total
                )
        sums.append(total.T[:16])
    high, low = split(jnp.concatenate(sums, 1))
    slots = one_hot(as_column(ids[0:1, :]) == iota((512, 256), 1))
    slots_out[...] = slots
    coef = mm(high, slots) + mm(low, slots)
    coef = jnp.where(iota((16, 256), 1) < 192, coef, 0.0)
    near[0:64, :] = jnp.concatenate([dmat[...], jnp.zeros((64, 64), F32)], 1)
    near[64:80, :] = coef[:, :128]
    near[80:96, :] = coef[:, 128:]
    far[0:16, :] = coef[:, :128]
    far[16:32, :] = coef[:, 128:]


def kernel_put(ids, put):
    put[...] = one_hot(iota((864, 512), 0) == tile_rows(ids[1:2, :]))


def kernel_back(
    field, near, below, above, below2, above2, slots, put, b0, b1, b2, b3,
    vloc_in, fx_in, fy_in, ut_in, send, scr, rows, vloc, fx, fy, ut, sems,
):
    copies = [
        pltpu.make_async_copy(vloc_in.at[:, zi, :], vloc.at[zi], sems.at[zi]) for zi in range(3)
    ] + [
        pltpu.make_async_copy(fx_in, fx, sems.at[3]),
        pltpu.make_async_copy(fy_in, fy, sems.at[4]),
        pltpu.make_async_copy(ut_in, ut, sems.at[5]),
    ]
    for copy in copies:
        copy.start()
    lane = iota((16, 128), 1)

    def half(ref, k):
        return ref[64 + 16 * k : 80 + 16 * k, :]

    def shifted(low, high, up):
        low, high = pltpu.roll(low, 64, 1), pltpu.roll(high, 64, 1)
        if up:
            return jnp.where(lane < 64, 0.0, low), jnp.where(lane < 64, low, high)
        return jnp.where(lane < 64, low, high), jnp.where(lane < 64, high, 0.0)

    from_below = shifted(half(below, 0), half(below, 1), False)
    from_above = shifted(half(above, 0), half(above, 1), True)
    tot = [
        half(near, 0) + from_below[0] + from_above[0] + below2[16:32, :],
        half(near, 1) + from_below[1] + from_above[1] + above2[0:16, :],
    ]
    tot[1] = jnp.where(lane < 64, tot[1], 0.0)
    wide = iota((64, 128), 1)
    coupling = [
        jnp.where(wide < 64, below[0:64, :], pltpu.roll(near[0:64, :], 64, 1)),
        jnp.where(wide < 64, above[0:64, :], 0.0),
    ]
    for h in range(2):
        for c in range(2):
            coef = tot[h][8 * c : 8 * c + 8, :]
            for j in range(8):
                row = jnp.sum(coupling[h][8 * j : 8 * j + 8, :] * coef, axis=0, keepdims=True)
                scr[8 * c + j : 8 * c + j + 1, 128 * h : 128 * h + 128] = row
    betas = (b0, b1, b2, b3)
    high, low = split(scr[...])
    weight = mm_nt(slots[...], high) + mm_nt(slots[...], low)
    high, low = split(weight)
    weight = jnp.concatenate([high, low], 1)
    for k, beta in enumerate(betas):
        span = slice(128 * k, 128 * k + 128)
        terms = jnp.zeros((128, 256), F32)
        for j in range(8):
            wide = one_hot(iota((32, 256), 0) % 16 == 8 * (iota((32, 256), 1) // 128) + j)
            projector = beta[pl.ds(j, 128, stride=8), :]
            terms = terms + mm(weight[span], wide) * jnp.concatenate([projector, projector], 1)
        high, low = split(terms)
        rows[span, 0:256] = high
        rows[span, 256:512] = low
    both = mm(put[...], rows[...])
    nonloc = both[:, :256] + both[:, 256:]
    for copy in copies:
        copy.wait()
    kinds = []
    for k in range(3):
        factor = jnp.concatenate([vloc[zi, pl.ds(k, 96, stride=3), :] for zi in range(3)], 0)
        at = slice(288 * k, 288 * k + 288)
        kinds.append(split(field[at, :] * jnp.concatenate([factor, factor], 1) + nonloc[at, :]))
    g = []
    for parity in range(2):
        table = [fx[1024 * parity + 512 * i : 1024 * parity + 512 * i + 512, :] for i in range(2)]
        lines = [jnp.concatenate([kinds[parity][i], kinds[parity + 1][i]], 1) for i in range(2)]
        g.append(split(three(mm, lines, table)))
    lines = [
        jnp.concatenate(
            [
                jnp.concatenate(
                    [
                        g[parity][i][96 * zi : 96 * zi + 96, 128 * c : 128 * c + 128]
                        for zi in range(3)
                    ],
                    1,
                )
                for c in range(2)
                for parity in range(2)
            ],
            0,
        )
        for i in range(2)
    ]
    h = three(mm, (fy[0:256, :], fy[256:512, :]), lines)
    main, spare, _ = masks_sp()
    spares = [jnp.zeros((64, 128), F32), jnp.zeros((64, 128), F32)]
    for zi in range(3):
        for c in range(2):
            turned = h[128 * c : 128 * c + 128, 128 * zi : 128 * zi + 128].T
            first = turned[:64]
            second = pltpu.roll(turned[64:], 64, 1)
            send[pl.ds(4 * c + zi, 64, stride=8), :] = jnp.where(main, first, second)
            high, low = split(jnp.where(spare, first, 0.0))
            move = ut[128 * zi : 128 * zi + 128, :]
            spares[c] = spares[c] + (mm(high, move) + mm(low, move))
    for c in range(2):
        send[pl.ds(4 * c + 3, 64, stride=8), :] = spares[c]


def kernel_z_forward(recv, fz, out):
    s = lax.axis_index("fft")
    out[...] = jnp.zeros((1728, 128), F32)
    r = iota((256, 1), 0)
    main, spare = line_places(r, s)
    lane = iota((256, 128), 1)
    keep = one_hot(lane == main)
    highs, lows = [], []
    for zi in range(3):
        unpack = jnp.concatenate(
            [keep, one_hot((lane == spare + 32 * zi) & (spare >= 0))], 1
        )
        lines = jnp.concatenate(
            [
                jnp.concatenate(
                    [
                        recv[pl.ds(4 * c + zi, 64, stride=8), :],
                        recv[pl.ds(4 * c + 3, 64, stride=8), :],
                    ],
                    1,
                )
                for c in range(2)
            ],
            0,
        )
        high, low = split(lines)
        columns = mm_nt(unpack, jnp.concatenate([high, low], 0))
        highs.append(columns[:, :128].astype(BF))
        lows.append(columns[:, 128:].astype(BF))
    z = three(
        mm, (jnp.concatenate(highs, 1), jnp.concatenate(lows, 1)), (fz[0:384, :], fz[384:768, :])
    )
    low_lane = iota((64, 128), 1) < 64
    for plane in range(2):
        for c in range(2):
            block = z[128 * plane : 128 * plane + 128, 128 * c : 128 * c + 128]
            even = jnp.where(sphere_rows(plane, 0, s), block[:64], 0.0)
            odd = jnp.where(sphere_rows(plane, 1, s), block[64:], 0.0)
            kinds = (
                jnp.where(low_lane, even, 0.0),
                pltpu.roll(jnp.where(low_lane, odd, even), 64, 1),
                jnp.where(low_lane, 0.0, odd),
            )
            for k, tile in enumerate(kinds):
                at = 1152 * plane + 2 * k + c
                out[pl.ds(at, 32, stride=6), :] = tile[24:56]
                out[pl.ds(at + 432, 24, stride=6), :] = tile[:24]


def call(kernel, name, out_shape, args, scratch=(), anywhere=(), anywhere_out=(), limit=VMEM_LIMIT, cost=None):
    specs = [
        pl.BlockSpec(memory_space=pl.ANY if k in anywhere else pltpu.VMEM)
        for k in range(len(args))
    ]
    shapes = [
        jax.ShapeDtypeStruct(*shape) if isinstance(shape[0], tuple) else jax.ShapeDtypeStruct(shape, F32)
        for shape in out_shape
    ]
    out = pl.pallas_call(
        kernel,
        name=name,
        out_shape=shapes,
        in_specs=specs,
        out_specs=[
            pl.BlockSpec(memory_space=pl.ANY if k in anywhere_out else pltpu.VMEM)
            for k in range(len(shapes))
        ],
        scratch_shapes=list(scratch),
        cost_estimate=cost,
        compiler_params=pltpu.CompilerParams(vmem_limit_bytes=limit),
    )(*args)
    return out


def body(psi_g, vloc, beta, blk_slot, blk_tile, dmat):
    t = {
        name: jnp.asarray(value) for name, value in tables().items()
    }
    psi = psi_g[0].transpose(1, 0, 2).reshape(3, 2, 288, 128).transpose(0, 2, 1, 3)
    psi = psi.reshape(1728, 128)
    def gathered(x):
        return [x] + [
            lax.ppermute(x, "band", [(i, (i + k) % 4) for i in range(4)]) for k in (1, 3, 2)
        ]

    betas = gathered(beta.reshape(1024, 128))
    ids = jnp.concatenate(gathered(jnp.stack([blk_slot, blk_tile])), 1)
    (send,) = call(
        kernel_z_inverse,
        "z_inverse",
        [(512, 128)],
        (psi, t["wz"]),
        [
            pltpu.VMEM((2, 384, 128), F32),
            pltpu.VMEM((768, 256), BF),
            pltpu.SemaphoreType.DMA((5,)),
        ],
        anywhere=(0, 1),
        limit=60 * 1024 * 1024,
    )

    def exchange(x):
        x = lax.all_to_all(x.reshape(64, 8, 128), "fft", 0, 0, tiled=True)
        return x.reshape(512, 128)

    recv = exchange(send)
    vloc_tiles = vloc.reshape(3, 288, 128).transpose(1, 0, 2)
    dmat_rows = dmat.transpose(1, 2, 0).reshape(64, 64)
    field, rows_h, rows_l = call(
        kernel_field,
        "field",
        [(864, 256), ((896, 256), BF), ((896, 256), BF)],
        (recv, t["ey"], t["ix"], t["u"]),
    )
    near, far, slots = call(
        kernel_project,
        "project",
        [(96, 128), (32, 128), ((512, 256), BF)],
        (rows_h, rows_l, dmat_rows, ids, *betas),
        [pltpu.VMEM((512, 256), F32)],
    )

    def moved(x, step):
        return lax.ppermute(x, "fft", [(i, (i + step) % 64) for i in range(64)])

    sides = (moved(near, 1), moved(near, -1), moved(far, 2), moved(far, -2))
    (put,) = call(
        kernel_put,
        "put",
        [((864, 512), BF)],
        (ids,),
        cost=pl.CostEstimate(flops=2000000, bytes_accessed=3000000, transcendentals=0),
    )
    (send,) = call(
        kernel_back,
        "back",
        [(512, 128)],
        (field, near, *sides, slots, put, *betas, vloc_tiles, t["fx"], t["fy"], t["ut"]),
        [
            pltpu.VMEM((16, 256), F32),
            pltpu.VMEM((512, 512), BF),
            pltpu.VMEM((3, 288, 128), F32),
            pltpu.VMEM((2048, 256), BF),
            pltpu.VMEM((512, 384), BF),
            pltpu.VMEM((384, 128), BF),
            pltpu.SemaphoreType.DMA((6,)),
        ],
        anywhere=(12, 13, 14, 15),
    )
    (out,) = call(kernel_z_forward, "z_forward", [(1728, 128)], (exchange(send), t["fz"]))
    out = out.reshape(3, 288, 2, 128).transpose(0, 2, 1, 3).reshape(3, 2, N * N)
    return out.transpose(1, 0, 2)[None]


def solution(mesh):
    in_specs = (
        P("band", None, "fft", None),
        P("fft", None),
        P(("fft", "band"), None, None),
        P(("fft", "band")),
        P(("fft", "band")),
        P("fft", None, None),
    )
    out_specs = P("band", None, "fft", None)
    return jax.shard_map(body, mesh=mesh, in_specs=in_specs, out_specs=out_specs, check_vma=False)
```

```python
import functools

import jax
import jax.numpy as jnp
import ml_dtypes
import numpy as np
from jax import lax
from jax.experimental import pallas as pl
from jax.experimental.pallas import tpu as pltpu
from jax.sharding import PartitionSpec as P

N = 192
R2 = 48 * 48
BF = jnp.bfloat16
F32 = jnp.float32
VMEM_LIMIT = 48 * 1024 * 1024


def trig(freqs, points):
    angle = 2.0 * np.pi * (np.outer(freqs, points) % N) / N
    return np.cos(angle) / np.sqrt(N), np.sin(angle) / np.sqrt(N)


def pair_of(table):
    table = np.asarray(table, np.float32)
    high = table.astype(ml_dtypes.bfloat16)
    low = (table - high.astype(np.float32)).astype(ml_dtypes.bfloat16)
    return np.concatenate([high, low], 0)


KZ = np.concatenate([np.arange(64), np.arange(128, 192)])
SIGNED = np.concatenate([np.arange(64), np.arange(-64, 0)])
YS = [2 * np.arange(96), 2 * np.arange(96) + 1]


@functools.cache
def tables():
    t = {}
    blocks = []
    for zi in range(3):
        c, s = trig(3 * np.arange(64) + zi, KZ)
        blocks += [np.concatenate([c, -s], 1), np.concatenate([s, c], 1)]
    t["wz"] = pair_of(np.concatenate(blocks, 0))
    c, s = trig(np.concatenate(YS), SIGNED)
    t["ey"] = pair_of(
        np.concatenate([np.concatenate([c, -s], 1), np.concatenate([s, c], 1)], 0)
    )
    c, s = trig(SIGNED, np.arange(N))
    gap = np.zeros((128, 64))
    even = [np.concatenate([v, gap], 1) for v in (c, s, -s, c)]
    odd = [np.concatenate([gap, v], 1) for v in (c, s, -s, c)]
    t["ix"] = np.concatenate(
        [
            pair_of(np.block([[even[0], even[1]], [even[2], even[3]]])),
            pair_of(np.block([[odd[0], odd[1]], [odd[2], odd[3]]])),
        ],
        0,
    )
    parts = {}
    c, s = trig(np.arange(N), SIGNED)
    gap = np.zeros((64, 128))
    for name, table in (("c", c), ("s", s)):
        parts[name] = (np.concatenate([table, gap], 0), np.concatenate([gap, table], 0))

    def forward_x(which):
        cc, ss = parts["c"][which], parts["s"][which]
        first, second = np.concatenate([cc, -ss], 1), np.concatenate([ss, cc], 1)
        return np.concatenate([first[:128], second[:128], first[128:], second[128:]], 0)

    t["fx"] = np.concatenate([pair_of(forward_x(0)), pair_of(forward_x(1))], 0)
    c, s = trig(SIGNED, np.concatenate(YS))
    t["fy"] = pair_of(
        np.concatenate([np.concatenate([c, s], 1), np.concatenate([-s, c], 1)], 0)
    )
    blocks = []
    for zi in range(3):
        c, s = trig(3 * np.arange(64) + zi, KZ)
        blocks += [np.concatenate([c, -s], 1), np.concatenate([s, c], 1)]
    t["fz"] = pair_of(np.concatenate(blocks, 0))
    u = np.zeros((128, 384), np.float32)
    for zi in range(3):
        for p in range(128):
            u[32 * zi + 8 * (p >= 64) + p % 8, 128 * zi + p] = 1.0
    t["u"] = u.astype(ml_dtypes.bfloat16)
    t["ut"] = np.concatenate([u[:, 128 * zi : 128 * zi + 128].T for zi in range(3)], 0).astype(
        ml_dtypes.bfloat16
    )
    return t


def split(x):
    high = x.astype(BF)
    return high, (x - high.astype(F32)).astype(BF)


def mm(a, b):
    return jnp.dot(a, b, preferred_element_type=F32)


def mm_nt(a, b):
    return lax.dot_general(a, b, (((1,), (1,)), ((), ())), preferred_element_type=F32)


def three(product, a, b):
    return product(a[0], b[0]) + (product(a[0], b[1]) + product(a[1], b[0]))


def iota(shape, dim):
    return lax.broadcasted_iota(jnp.int32, shape, dim)


def masks_sp():
    s, p = iota((64, 128), 0), iota((64, 128), 1)
    ky = jnp.where(p < 64, p, p - 128)
    away = 64 - jnp.abs(ky)
    inside = ky * ky + s * s <= R2
    clash = away * away + (64 - s) * (64 - s) <= R2
    other = (p - 64) * (p - 64) + (64 - s) * (64 - s) <= R2
    return inside & ~clash, inside & clash, other


def line_places(r, s):
    plane, rest = r // 128, r % 128
    ky = 2 * (rest % 64 - 24) + rest // 64
    here = jnp.where(plane == 0, s, 64 - s)
    away = 64 - jnp.abs(ky)
    inside = ky * ky + here * here <= R2
    clash = (away * away + (64 - s) * (64 - s) <= R2) & (plane == 0)
    place = jnp.where(plane == 0, jnp.where(ky < 0, ky + 128, ky), ky + 64)
    main = jnp.where(inside & ~clash, place, -1)
    spare = jnp.where(inside & clash, jnp.where(ky < 0, 8, 0) + (ky + 64) % 8, -1)
    return main, spare


def one_hot(condition):
    return jnp.where(condition, 1.0, 0.0).astype(BF)


def sphere_rows(plane, parity, s):
    m, lane = iota((64, 128), 0), iota((64, 128), 1)
    ky = 2 * (m - 24) + parity
    kz = jnp.where(lane < 64, lane, lane - 128)
    kx = s - 64 * plane
    return ky * ky + kz * kz + kx * kx <= R2


def kernel_z_inverse(psi, wz_in, send, buf, wz, sems):
    s = lax.axis_index("fft")
    copies = []
    for plane in range(2):
        base = 1152 * plane
        for k, (src, dst, rows) in enumerate(((432, 0, 144), (0, 144, 152))):
            copies.append(
                pltpu.make_async_copy(
                    psi.at[pl.ds(base + src, rows)],
                    buf.at[plane, pl.ds(dst, rows)],
                    sems.at[2 * plane + k],
                )
            )
    copies.append(pltpu.make_async_copy(wz_in, wz, sems.at[4]))
    for copy in copies:
        copy.start()
    main, spare = line_places(iota((1, 256), 1), s)
    j = iota((128, 256), 0)
    pack = jnp.concatenate(
        [one_hot(j == main), one_hot((j % 32 == spare) & (j < 96))], axis=0
    )
    lane = iota((64, 128), 1)
    rows = []
    for copy in copies[:4]:
        copy.wait()
    for plane in range(2):
        lines = [[], []]
        for c in range(2):
            t = [buf[plane, pl.ds(2 * k + c, 64, stride=6), :] for k in range(3)]
            middle = pltpu.roll(t[1], 64, 1)
            even = jnp.where(lane < 64, t[0], middle)
            odd = jnp.where(lane < 64, middle, t[2])
            lines[0].append(jnp.where(sphere_rows(plane, 0, s), even, 0.0))
            lines[1].append(jnp.where(sphere_rows(plane, 1, s), odd, 0.0))
        rows += [jnp.concatenate(lines[0], 1), jnp.concatenate(lines[1], 1)]
    high, low = split(jnp.concatenate(rows, 0))
    packed = (mm(pack, high).astype(BF), mm(pack, low).astype(BF))
    copies[4].wait()
    out = three(mm_nt, (wz[0:384, :], wz[384:768, :]), packed)
    for c in range(2):
        block = [out[(2 * zi + c) * 64 : (2 * zi + c) * 64 + 64] for zi in range(3)]
        for zi in range(3):
            send[pl.ds(4 * c + zi, 64, stride=8), :] = block[zi][:, :128]
        send[pl.ds(4 * c + 3, 64, stride=8), :] = jnp.where(
            lane < 32, block[0][:, 128:], jnp.where(lane < 64, block[1][:, 128:], block[2][:, 128:])
        )


def tile_rows(tiles):
    return (tiles % 3) * 288 + tiles // 3


def as_column(ids):
    return jnp.broadcast_to(ids.astype(F32), (8, ids.shape[1])).T[:, 0:1].astype(jnp.int32)


def kernel_field(
    recv, ey, ix, u, field, rows_h, rows_l,
):
    main, spare, other = masks_sp()
    spread = []
    for c in range(2):
        high, low = split(recv[pl.ds(4 * c + 3, 64, stride=8), :])
        spread.append(mm(high, u[...]) + mm(low, u[...]))
    lines = []
    for zi in range(3):
        first, second = [], []
        for c in range(2):
            got = recv[pl.ds(4 * c + zi, 64, stride=8), :]
            extra = spread[c][:, 128 * zi : 128 * zi + 128]
            first.append(jnp.where(main, got, jnp.where(spare, extra, 0.0)))
            second.append(pltpu.roll(jnp.where(other, got, 0.0), 64, 1))
        lines += [jnp.concatenate(first, 1), jnp.concatenate(second, 1)]
    g = three(mm_nt, (ey[0:384, :], ey[384:768, :]), split(jnp.concatenate(lines, 0)))
    out = []
    for parity in range(2):
        a = 96 * parity
        table = [ix[512 * parity + 256 * i : 512 * parity + 256 * i + 256, :] for i in range(2)]
        block = jnp.concatenate(
            [
                jnp.concatenate(
                    [
                        g[a : a + 96, 128 * zi : 128 * zi + 128],
                        g[192 + a : 288 + a, 128 * zi : 128 * zi + 128],
                    ],
                    1,
                )
                for zi in range(3)
            ],
            0,
        )
        out.append(three(mm, split(block), table))
    even, odd = out
    for c in range(2):
        a = 256 * c
        kinds = (
            even[:, a : a + 128],
            even[:, a + 128 : a + 256] + odd[:, a : a + 128],
            odd[:, a + 128 : a + 256],
        )
        for k, tile in enumerate(kinds):
            span = pl.ds(288 * k, 288)
            lanes = pl.ds(128 * c, 128)
            field[span, lanes] = tile
            high, low = split(tile)
            rows_h[span, lanes] = high
            rows_l[span, lanes] = low
    rows_h[864:896, :] = jnp.zeros((32, 256), BF)
    rows_l[864:896, :] = jnp.zeros((32, 256), BF)


def project(quarters, rows_h, rows_l, tile_of, slots, betas, field_rows):
    count = 128 * quarters
    pick = one_hot(as_column(tile_of) == iota((count, 896), 1))
    field_rows[...] = mm(pick, rows_h[...]) + mm(pick, rows_l[...])
    lane = iota((128, 128), 1)
    sums = []
    for k, beta in enumerate(betas):
        total = jnp.zeros((128, 128), F32)
        for j in range(8):
            projector = beta[pl.ds(j, 128, stride=8), :]
            for c in range(2):
                value = field_rows[128 * k : 128 * k + 128, 128 * c : 128 * c + 128] * projector
                total = jnp.where(
                    lane == 8 * c + j, jnp.sum(value, axis=1, keepdims=True), total
                )
        sums.append(total.T[:16])
    high, low = split(jnp.concatenate(sums, 1))
    return mm(high, slots) + mm(low, slots)


def kernel_project(rows_h, rows_l, i0, i1, i2, i3, b0, b1, b2, coef, slots_out, tiles_out, field_rows):
    ids = jnp.concatenate([i0[...], i1[...], i2[...], i3[...]], 1)
    tile_of = tile_rows(ids[1:2, :])
    tiles_out[...] = tile_of
    slots = one_hot(as_column(ids[0:1, :]) == iota((512, 256), 1))
    slots_out[...] = slots
    coef[...] = project(3, rows_h, rows_l, tile_of[:, :384], slots[:384], (b0, b1, b2), field_rows)


def kernel_project_last(rows_h, rows_l, tiles, slots, dmat, coef_in, b3, near, far, field_rows):
    coef = coef_in[...] + project(
        1, rows_h, rows_l, tiles[:, 384:], slots[384:512, :], (b3,), field_rows
    )
    coef = jnp.where(iota((16, 256), 1) < 192, coef, 0.0)
    near[0:64, :] = jnp.concatenate([dmat[...], jnp.zeros((64, 64), F32)], 1)
    near[64:80, :] = coef[:, :128]
    near[80:96, :] = coef[:, 128:]
    far[0:16, :] = coef[:, :128]
    far[16:32, :] = coef[:, 128:]


def kernel_put(tiles, put):
    put[...] = one_hot(iota((864, 512), 0) == tiles[...])


def kernel_back(
    field, near, below, above, below2, above2, slots, put, b0, b1, b2, b3,
    vloc_in, fx_in, fy_in, ut_in, send, scr, rows, vloc, fx, fy, ut, sems,
):
    copies = [
        pltpu.make_async_copy(vloc_in.at[:, zi, :], vloc.at[zi], sems.at[zi]) for zi in range(3)
    ] + [
        pltpu.make_async_copy(fx_in, fx, sems.at[3]),
        pltpu.make_async_copy(fy_in, fy, sems.at[4]),
        pltpu.make_async_copy(ut_in, ut, sems.at[5]),
    ]
    for copy in copies:
        copy.start()
    lane = iota((16, 128), 1)

    def half(ref, k):
        return ref[64 + 16 * k : 80 + 16 * k, :]

    def shifted(low, high, up):
        low, high = pltpu.roll(low, 64, 1), pltpu.roll(high, 64, 1)
        if up:
            return jnp.where(lane < 64, 0.0, low), jnp.where(lane < 64, low, high)
        return jnp.where(lane < 64, low, high), jnp.where(lane < 64, high, 0.0)

    from_below = shifted(half(below, 0), half(below, 1), False)
    from_above = shifted(half(above, 0), half(above, 1), True)
    tot = [
        half(near, 0) + from_below[0] + from_above[0] + below2[16:32, :],
        half(near, 1) + from_below[1] + from_above[1] + above2[0:16, :],
    ]
    tot[1] = jnp.where(lane < 64, tot[1], 0.0)
    wide = iota((64, 128), 1)
    coupling = [
        jnp.where(wide < 64, below[0:64, :], pltpu.roll(near[0:64, :], 64, 1)),
        jnp.where(wide < 64, above[0:64, :], 0.0),
    ]
    for h in range(2):
        for c in range(2):
            coef = tot[h][8 * c : 8 * c + 8, :]
            for j in range(8):
                row = jnp.sum(coupling[h][8 * j : 8 * j + 8, :] * coef, axis=0, keepdims=True)
                scr[8 * c + j : 8 * c + j + 1, 128 * h : 128 * h + 128] = row
    betas = (b0, b1, b2, b3)
    high, low = split(scr[...])
    weight = mm_nt(slots[...], high) + mm_nt(slots[...], low)
    high, low = split(weight)
    weight = jnp.concatenate([high, low], 1)
    for k, beta in enumerate(betas):
        span = slice(128 * k, 128 * k + 128)
        terms = jnp.zeros((128, 256), F32)
        for j in range(8):
            wide = one_hot(iota((32, 256), 0) % 16 == 8 * (iota((32, 256), 1) // 128) + j)
            projector = beta[pl.ds(j, 128, stride=8), :]
            terms = terms + mm(weight[span], wide) * jnp.concatenate([projector, projector], 1)
        high, low = split(terms)
        rows[span, 0:256] = high
        rows[span, 256:512] = low
    both = mm(put[...], rows[...])
    nonloc = both[:, :256] + both[:, 256:]
    for copy in copies:
        copy.wait()
    kinds = []
    for k in range(3):
        factor = jnp.concatenate([vloc[zi, pl.ds(k, 96, stride=3), :] for zi in range(3)], 0)
        at = slice(288 * k, 288 * k + 288)
        kinds.append(split(field[at, :] * jnp.concatenate([factor, factor], 1) + nonloc[at, :]))
    g = []
    for parity in range(2):
        table = [fx[1024 * parity + 512 * i : 1024 * parity + 512 * i + 512, :] for i in range(2)]
        lines = [jnp.concatenate([kinds[parity][i], kinds[parity + 1][i]], 1) for i in range(2)]
        g.append(split(three(mm, lines, table)))
    lines = [
        jnp.concatenate(
            [
                jnp.concatenate(
                    [
                        g[parity][i][96 * zi : 96 * zi + 96, 128 * c : 128 * c + 128]
                        for zi in range(3)
                    ],
                    1,
                )
                for c in range(2)
                for parity in range(2)
            ],
            0,
        )
        for i in range(2)
    ]
    h = three(mm, (fy[0:256, :], fy[256:512, :]), lines)
    main, spare, _ = masks_sp()
    spares = [jnp.zeros((64, 128), F32), jnp.zeros((64, 128), F32)]
    for zi in range(3):
        for c in range(2):
            turned = h[128 * c : 128 * c + 128, 128 * zi : 128 * zi + 128].T
            first = turned[:64]
            second = pltpu.roll(turned[64:], 64, 1)
            send[pl.ds(4 * c + zi, 64, stride=8), :] = jnp.where(main, first, second)
            high, low = split(jnp.where(spare, first, 0.0))
            move = ut[128 * zi : 128 * zi + 128, :]
            spares[c] = spares[c] + (mm(high, move) + mm(low, move))
    for c in range(2):
        send[pl.ds(4 * c + 3, 64, stride=8), :] = spares[c]


def kernel_z_forward(recv, fz, result, out, sems):
    s = lax.axis_index("fft")
    out[...] = jnp.zeros((1728, 128), F32)
    spans = [(152, 280), (576, 576), (1304, 280), (0, 152), (432, 144), (1152, 152), (1584, 144)]
    copies = [
        pltpu.make_async_copy(out.at[pl.ds(*span)], result.at[pl.ds(*span)], sems.at[k])
        for k, span in enumerate(spans)
    ]
    for copy in copies[:3]:
        copy.start()
    r = iota((256, 1), 0)
    main, spare = line_places(r, s)
    lane = iota((256, 128), 1)
    keep = one_hot(lane == main)
    highs, lows = [], []
    for zi in range(3):
        unpack = jnp.concatenate(
            [keep, one_hot((lane == spare + 32 * zi) & (spare >= 0))], 1
        )
        lines = jnp.concatenate(
            [
                jnp.concatenate(
                    [
                        recv[pl.ds(4 * c + zi, 64, stride=8), :],
                        recv[pl.ds(4 * c + 3, 64, stride=8), :],
                    ],
                    1,
                )
                for c in range(2)
            ],
            0,
        )
        high, low = split(lines)
        columns = mm_nt(unpack, jnp.concatenate([high, low], 0))
        highs.append(columns[:, :128].astype(BF))
        lows.append(columns[:, 128:].astype(BF))
    z = three(
        mm, (jnp.concatenate(highs, 1), jnp.concatenate(lows, 1)), (fz[0:384, :], fz[384:768, :])
    )
    low_lane = iota((64, 128), 1) < 64
    for plane in range(2):
        for c in range(2):
            block = z[128 * plane : 128 * plane + 128, 128 * c : 128 * c + 128]
            even = jnp.where(sphere_rows(plane, 0, s), block[:64], 0.0)
            odd = jnp.where(sphere_rows(plane, 1, s), block[64:], 0.0)
            kinds = (
                jnp.where(low_lane, even, 0.0),
                pltpu.roll(jnp.where(low_lane, odd, even), 64, 1),
                jnp.where(low_lane, 0.0, odd),
            )
            for k, tile in enumerate(kinds):
                at = 1152 * plane + 2 * k + c
                out[pl.ds(at, 25, stride=6), :] = tile[24:49]
                out[pl.ds(at + 432, 24, stride=6), :] = tile[:24]
        copies[3 + 2 * plane].start()
        copies[4 + 2 * plane].start()
    for copy in copies:
        copy.wait()


def call(kernel, name, out_shape, args, scratch=(), anywhere=(), anywhere_out=(), limit=VMEM_LIMIT, cost=None):
    specs = [
        pl.BlockSpec(memory_space=pl.ANY if k in anywhere else pltpu.VMEM)
        for k in range(len(args))
    ]
    shapes = [
        jax.ShapeDtypeStruct(*shape) if isinstance(shape[0], tuple) else jax.ShapeDtypeStruct(shape, F32)
        for shape in out_shape
    ]
    out = pl.pallas_call(
        kernel,
        name=name,
        out_shape=shapes,
        in_specs=specs,
        out_specs=[
            pl.BlockSpec(memory_space=pl.ANY if k in anywhere_out else pltpu.VMEM)
            for k in range(len(shapes))
        ],
        scratch_shapes=list(scratch),
        cost_estimate=cost,
        compiler_params=pltpu.CompilerParams(vmem_limit_bytes=limit),
    )(*args)
    return out


def body(psi_g, vloc, beta, blk_slot, blk_tile, dmat):
    t = {
        name: jnp.asarray(value) for name, value in tables().items()
    }
    psi = psi_g[0].transpose(1, 0, 2).reshape(3, 2, 288, 128).transpose(0, 2, 1, 3)
    psi = psi.reshape(1728, 128)
    def gathered(x):
        return [x] + [
            lax.ppermute(x, "band", [(i, (i + k) % 4) for i in range(4)]) for k in (1, 3, 2)
        ]

    betas = gathered(beta.reshape(1024, 128))
    ids = gathered(jnp.stack([blk_slot, blk_tile]))
    (send,) = call(
        kernel_z_inverse,
        "z_inverse",
        [(512, 128)],
        (psi, t["wz"]),
        [
            pltpu.VMEM((2, 384, 128), F32),
            pltpu.VMEM((768, 256), BF),
            pltpu.SemaphoreType.DMA((5,)),
        ],
        anywhere=(0, 1),
        limit=60 * 1024 * 1024,
    )
    send, *ids = lax.optimization_barrier((send, *ids))

    def exchange(x):
        x = lax.all_to_all(x.reshape(64, 8, 128), "fft", 0, 0, tiled=True)
        return x.reshape(512, 128)

    recv = exchange(send)
    vloc_tiles = vloc.reshape(3, 288, 128).transpose(1, 0, 2)
    dmat_rows = dmat.transpose(1, 2, 0).reshape(64, 64)
    field, rows_h, rows_l = call(
        kernel_field,
        "field",
        [(864, 256), ((896, 256), BF), ((896, 256), BF)],
        (recv, t["ey"], t["ix"], t["u"]),
    )
    coef, slots, tiles = call(
        kernel_project,
        "project",
        [(16, 256), ((512, 256), BF), ((1, 512), jnp.int32)],
        (rows_h, rows_l, *ids, *betas[:3]),
        [pltpu.VMEM((384, 256), F32)],
    )
    near, far = call(
        kernel_project_last,
        "project_last",
        [(96, 128), (32, 128)],
        (rows_h, rows_l, tiles, slots, dmat_rows, coef, betas[3]),
        [pltpu.VMEM((128, 256), F32)],
    )

    def moved(x, step):
        return lax.ppermute(x, "fft", [(i, (i + step) % 64) for i in range(64)])

    sides = (moved(near, 1), moved(near, -1), moved(far, 2), moved(far, -2))
    (put,) = call(
        kernel_put,
        "put",
        [((864, 512), BF)],
        (tiles,),
        cost=pl.CostEstimate(flops=2000000, bytes_accessed=3000000, transcendentals=0),
    )
    (send,) = call(
        kernel_back,
        "back",
        [(512, 128)],
        (field, near, *sides, slots, put, *betas, vloc_tiles, t["fx"], t["fy"], t["ut"]),
        [
            pltpu.VMEM((16, 256), F32),
            pltpu.VMEM((512, 512), BF),
            pltpu.VMEM((3, 288, 128), F32),
            pltpu.VMEM((2048, 256), BF),
            pltpu.VMEM((512, 384), BF),
            pltpu.VMEM((384, 128), BF),
            pltpu.SemaphoreType.DMA((6,)),
        ],
        anywhere=(12, 13, 14, 15),
    )
    (out,) = call(kernel_z_forward, "z_forward", [(1728, 128)], (exchange(send), t["fz"]),
        [pltpu.VMEM((1728, 128), F32), pltpu.SemaphoreType.DMA((7,))], anywhere_out=(0,))
    out = out.reshape(3, 288, 2, 128).transpose(0, 2, 1, 3).reshape(3, 2, N * N)
    return out.transpose(1, 0, 2)[None]


def solution(mesh):
    in_specs = (
        P("band", None, "fft", None),
        P("fft", None),
        P(("fft", "band"), None, None),
        P(("fft", "band")),
        P(("fft", "band")),
        P("fft", None, None),
    )
    out_specs = P("band", None, "fft", None)
    return jax.shard_map(body, mesh=mesh, in_specs=in_specs, out_specs=out_specs, check_vma=False)
```

```python
import functools

import jax
import jax.numpy as jnp
import ml_dtypes
import numpy as np
from jax import lax
from jax.experimental import pallas as pl
from jax.experimental.pallas import tpu as pltpu
from jax.sharding import PartitionSpec as P

N = 192
R2 = 48 * 48
BF = jnp.bfloat16
F32 = jnp.float32
VMEM_LIMIT = 48 * 1024 * 1024


def trig(freqs, points):
    angle = 2.0 * np.pi * (np.outer(freqs, points) % N) / N
    return np.cos(angle) / np.sqrt(N), np.sin(angle) / np.sqrt(N)


def pair_of(table):
    table = np.asarray(table, np.float32)
    high = table.astype(ml_dtypes.bfloat16)
    low = (table - high.astype(np.float32)).astype(ml_dtypes.bfloat16)
    return np.concatenate([high, low], 0)


KZ = np.concatenate([np.arange(64), np.arange(128, 192)])
SIGNED = np.concatenate([np.arange(64), np.arange(-64, 0)])
YS = [2 * np.arange(96), 2 * np.arange(96) + 1]


@functools.cache
def tables():
    t = {}
    blocks = []
    for zi in range(3):
        c, s = trig(3 * np.arange(64) + zi, KZ)
        blocks += [np.concatenate([c, -s], 1), np.concatenate([s, c], 1)]
    t["wz"] = pair_of(np.concatenate(blocks, 0))
    c, s = trig(np.concatenate(YS), SIGNED)
    t["ey"] = pair_of(
        np.concatenate([np.concatenate([c, -s], 1), np.concatenate([s, c], 1)], 0)
    )
    c, s = trig(SIGNED, np.arange(N))
    gap = np.zeros((128, 64))
    even = [np.concatenate([v, gap], 1) for v in (c, s, -s, c)]
    odd = [np.concatenate([gap, v], 1) for v in (c, s, -s, c)]
    t["ix"] = np.concatenate(
        [
            pair_of(np.block([[even[0], even[1]], [even[2], even[3]]])),
            pair_of(np.block([[odd[0], odd[1]], [odd[2], odd[3]]])),
        ],
        0,
    )
    parts = {}
    c, s = trig(np.arange(N), SIGNED)
    gap = np.zeros((64, 128))
    for name, table in (("c", c), ("s", s)):
        parts[name] = (np.concatenate([table, gap], 0), np.concatenate([gap, table], 0))

    def forward_x(which):
        cc, ss = parts["c"][which], parts["s"][which]
        first, second = np.concatenate([cc, -ss], 1), np.concatenate([ss, cc], 1)
        return np.concatenate([first[:128], second[:128], first[128:], second[128:]], 0)

    t["fx"] = np.concatenate([pair_of(forward_x(0)), pair_of(forward_x(1))], 0)
    c, s = trig(SIGNED, np.concatenate(YS))
    t["fy"] = pair_of(
        np.concatenate([np.concatenate([c, s], 1), np.concatenate([-s, c], 1)], 0)
    )
    blocks = []
    for zi in range(3):
        c, s = trig(3 * np.arange(64) + zi, KZ)
        blocks += [np.concatenate([c, -s], 1), np.concatenate([s, c], 1)]
    t["fz"] = pair_of(np.concatenate(blocks, 0))
    u = np.zeros((128, 384), np.float32)
    for zi in range(3):
        for p in range(128):
            u[32 * zi + 8 * (p >= 64) + p % 8, 128 * zi + p] = 1.0
    t["u"] = u.astype(ml_dtypes.bfloat16)
    t["ut"] = np.concatenate([u[:, 128 * zi : 128 * zi + 128].T for zi in range(3)], 0).astype(
        ml_dtypes.bfloat16
    )
    return t


def split(x):
    high = x.astype(BF)
    return high, (x - high.astype(F32)).astype(BF)


def mm(a, b):
    return jnp.dot(a, b, preferred_element_type=F32)


def mm_nt(a, b):
    return lax.dot_general(a, b, (((1,), (1,)), ((), ())), preferred_element_type=F32)


def three(product, a, b):
    return product(a[0], b[0]) + (product(a[0], b[1]) + product(a[1], b[0]))


def iota(shape, dim):
    return lax.broadcasted_iota(jnp.int32, shape, dim)


def masks_sp():
    s, p = iota((64, 128), 0), iota((64, 128), 1)
    ky = jnp.where(p < 64, p, p - 128)
    away = 64 - jnp.abs(ky)
    inside = ky * ky + s * s <= R2
    clash = away * away + (64 - s) * (64 - s) <= R2
    other = (p - 64) * (p - 64) + (64 - s) * (64 - s) <= R2
    return inside & ~clash, inside & clash, other


def line_places(r, s):
    plane, rest = r // 128, r % 128
    ky = 2 * (rest % 64 - 24) + rest // 64
    here = jnp.where(plane == 0, s, 64 - s)
    away = 64 - jnp.abs(ky)
    inside = ky * ky + here * here <= R2
    clash = (away * away + (64 - s) * (64 - s) <= R2) & (plane == 0)
    place = jnp.where(plane == 0, jnp.where(ky < 0, ky + 128, ky), ky + 64)
    main = jnp.where(inside & ~clash, place, -1)
    spare = jnp.where(inside & clash, jnp.where(ky < 0, 8, 0) + (ky + 64) % 8, -1)
    return main, spare


def one_hot(condition):
    return jnp.where(condition, 1.0, 0.0).astype(BF)


def sphere_rows(plane, parity, s):
    m, lane = iota((64, 128), 0), iota((64, 128), 1)
    ky = 2 * (m - 24) + parity
    kz = jnp.where(lane < 64, lane, lane - 128)
    kx = s - 64 * plane
    return ky * ky + kz * kz + kx * kx <= R2


def kernel_z_inverse(psi, wz_in, send, buf, wz, sems):
    s = lax.axis_index("fft")
    copies = []
    for plane in range(2):
        base = 1152 * plane
        for k, (src, dst, rows) in enumerate(((432, 0, 144), (0, 144, 152))):
            copies.append(
                pltpu.make_async_copy(
                    psi.at[pl.ds(base + src, rows)],
                    buf.at[plane, pl.ds(dst, rows)],
                    sems.at[2 * plane + k],
                )
            )
    copies.append(pltpu.make_async_copy(wz_in, wz, sems.at[4]))
    for copy in copies:
        copy.start()
    main, spare = line_places(iota((1, 256), 1), s)
    j = iota((128, 256), 0)
    pack = jnp.concatenate(
        [one_hot(j == main), one_hot((j % 32 == spare) & (j < 96))], axis=0
    )
    lane = iota((64, 128), 1)
    rows = []
    for copy in copies[:4]:
        copy.wait()
    for plane in range(2):
        lines = [[], []]
        for c in range(2):
            t = [buf[plane, pl.ds(2 * k + c, 64, stride=6), :] for k in range(3)]
            middle = pltpu.roll(t[1], 64, 1)
            even = jnp.where(lane < 64, t[0], middle)
            odd = jnp.where(lane < 64, middle, t[2])
            lines[0].append(jnp.where(sphere_rows(plane, 0, s), even, 0.0))
            lines[1].append(jnp.where(sphere_rows(plane, 1, s), odd, 0.0))
        rows += [jnp.concatenate(lines[0], 1), jnp.concatenate(lines[1], 1)]
    high, low = split(jnp.concatenate(rows, 0))
    packed = (mm(pack, high).astype(BF), mm(pack, low).astype(BF))
    copies[4].wait()
    out = three(mm_nt, (wz[0:384, :], wz[384:768, :]), packed)
    for c in range(2):
        block = [out[(2 * zi + c) * 64 : (2 * zi + c) * 64 + 64] for zi in range(3)]
        for zi in range(3):
            send[pl.ds(4 * c + zi, 64, stride=8), :] = block[zi][:, :128]
        send[pl.ds(4 * c + 3, 64, stride=8), :] = jnp.where(
            lane < 32, block[0][:, 128:], jnp.where(lane < 64, block[1][:, 128:], block[2][:, 128:])
        )


def tile_rows(tiles):
    return (tiles % 3) * 288 + tiles // 3


def as_column(ids):
    return jnp.broadcast_to(ids.astype(F32), (8, ids.shape[1])).T[:, 0:1].astype(jnp.int32)


def kernel_field(
    recv, ey, ix, u, field, rows_h, rows_l,
):
    main, spare, other = masks_sp()
    spread = []
    for c in range(2):
        high, low = split(recv[pl.ds(4 * c + 3, 64, stride=8), :])
        spread.append(mm(high, u[...]) + mm(low, u[...]))
    lines = []
    for zi in range(3):
        first, second = [], []
        for c in range(2):
            got = recv[pl.ds(4 * c + zi, 64, stride=8), :]
            extra = spread[c][:, 128 * zi : 128 * zi + 128]
            first.append(jnp.where(main, got, jnp.where(spare, extra, 0.0)))
            second.append(pltpu.roll(jnp.where(other, got, 0.0), 64, 1))
        lines += [jnp.concatenate(first, 1), jnp.concatenate(second, 1)]
    g = three(mm_nt, (ey[0:384, :], ey[384:768, :]), split(jnp.concatenate(lines, 0)))
    out = []
    for parity in range(2):
        a = 96 * parity
        table = [ix[512 * parity + 256 * i : 512 * parity + 256 * i + 256, :] for i in range(2)]
        block = jnp.concatenate(
            [
                jnp.concatenate(
                    [
                        g[a : a + 96, 128 * zi : 128 * zi + 128],
                        g[192 + a : 288 + a, 128 * zi : 128 * zi + 128],
                    ],
                    1,
                )
                for zi in range(3)
            ],
            0,
        )
        out.append(three(mm, split(block), table))
    even, odd = out
    for c in range(2):
        a = 256 * c
        kinds = (
            even[:, a : a + 128],
            even[:, a + 128 : a + 256] + odd[:, a : a + 128],
            odd[:, a + 128 : a + 256],
        )
        for k, tile in enumerate(kinds):
            span = pl.ds(288 * k, 288)
            lanes = pl.ds(128 * c, 128)
            field[span, lanes] = tile
            high, low = split(tile)
            rows_h[span, lanes] = high
            rows_l[span, lanes] = low
    rows_h[864:896, :] = jnp.zeros((32, 256), BF)
    rows_l[864:896, :] = jnp.zeros((32, 256), BF)


def project(quarters, rows_h, rows_l, tile_of, slots, betas, field_rows):
    count = 128 * quarters
    pick = one_hot(as_column(tile_of) == iota((count, 896), 1))
    field_rows[...] = mm(pick, rows_h[...]) + mm(pick, rows_l[...])
    lane = iota((128, 128), 1)
    sums = []
    for k, beta in enumerate(betas):
        total = jnp.zeros((128, 128), F32)
        for j in range(8):
            projector = beta[pl.ds(j, 128, stride=8), :]
            for c in range(2):
                value = field_rows[128 * k : 128 * k + 128, 128 * c : 128 * c + 128] * projector
                total = jnp.where(
                    lane == 8 * c + j, jnp.sum(value, axis=1, keepdims=True), total
                )
        sums.append(total.T[:16])
    high, low = split(jnp.concatenate(sums, 1))
    return mm(high, slots) + mm(low, slots)


def ids_of(betas, row):
    return jnp.concatenate([b[1024 + row : 1025 + row, :] for b in betas], 1).astype(jnp.int32)


def kernel_project(rows_h, rows_l, b0, b1, b2, coef, slots_out, tiles_out, field_rows):
    betas = (b0, b1, b2)
    tile_of = tile_rows(ids_of(betas, 1))
    tiles_out[...] = tile_of
    slots = one_hot(as_column(ids_of(betas, 0)) == iota((384, 256), 1))
    slots_out[...] = slots
    coef[...] = project(3, rows_h, rows_l, tile_of, slots, betas, field_rows)


def kernel_project_last(rows_h, rows_l, dmat, coef_in, b3, near, slots_out, tiles_out, field_rows):
    tile_of = tile_rows(ids_of((b3,), 1))
    tiles_out[...] = tile_of
    slots = one_hot(as_column(ids_of((b3,), 0)) == iota((128, 256), 1))
    slots_out[...] = slots
    coef = coef_in[...] + project(1, rows_h, rows_l, tile_of, slots, (b3,), field_rows)
    coef = jnp.where(iota((16, 256), 1) < 192, coef, 0.0)
    near[0:64, :] = jnp.concatenate([dmat[...], jnp.zeros((64, 64), F32)], 1)
    near[64:80, :] = coef[:, :128]
    near[80:96, :] = coef[:, 128:]


def chip_of(own, other):
    f = lax.axis_index("fft")
    core = f % 2
    own, other = own[...], other[...]
    return (
        core,
        (f // 2) % 2 == 0,
        jnp.where(core == 0, own, other),
        jnp.where(core == 0, other, own),
    )


def kernel_merge(own, other, first, second):
    _, even, a, b = chip_of(own, other)
    low_lane = iota((16, 128), 1) < 64
    turned = pltpu.roll(b[64:80], 64, 1)
    up = jnp.where(low_lane, a[80:96] + turned, pltpu.roll(b[80:96], 64, 1))
    down = jnp.where(low_lane, a[64:80], a[64:80] + turned)
    up = jnp.concatenate([b[0:64], up], 0)
    down = jnp.concatenate([a[0:64], down], 0)
    first[...] = jnp.where(even, up, down)
    second[...] = jnp.where(even, down, up)


def kernel_put(tiles, tiles_last, put):
    tile_of = jnp.concatenate([tiles[...], tiles_last[...]], 1)
    put[...] = one_hot(iota((864, 512), 0) == tile_of)


def kernel_back(
    field, own, other, first, second, slots, slots_last, put, b0, b1, b2, b3,
    vloc_in, fx_in, fy_in, ut_in, send, scr, rows, vloc, fx, fy, ut, sems,
):
    copies = [
        pltpu.make_async_copy(vloc_in.at[:, zi, :], vloc.at[zi], sems.at[zi]) for zi in range(3)
    ] + [
        pltpu.make_async_copy(fx_in, fx, sems.at[3]),
        pltpu.make_async_copy(fy_in, fy, sems.at[4]),
        pltpu.make_async_copy(ut_in, ut, sems.at[5]),
    ]
    for copy in copies:
        copy.start()
    core, even, a, b = chip_of(own, other)
    above = jnp.where(even, first[...], second[...])
    below = jnp.where(even, second[...], first[...])
    low_lane = iota((16, 128), 1) < 64
    turned = pltpu.roll(b[64:80], 64, 1)
    tot = [
        below[64:80] + jnp.where(low_lane, a[64:80], a[64:80] + turned),
        above[64:80] + jnp.where(low_lane, a[80:96] + turned, pltpu.roll(b[80:96], 64, 1)),
    ]
    wide = iota((64, 128), 1) < 64
    coupling = [
        jnp.where(wide, below[0:64], pltpu.roll(a[0:64], 64, 1)),
        jnp.where(wide, b[0:64], pltpu.roll(above[0:64], 64, 1)),
    ]
    for h in range(2):
        for c in range(2):
            coef = tot[h][8 * c : 8 * c + 8, :]
            for j in range(8):
                row = jnp.sum(coupling[h][8 * j : 8 * j + 8, :] * coef, axis=0, keepdims=True)
                scr[8 * c + j : 8 * c + j + 1, 128 * h : 128 * h + 128] = row
    betas = (b0, b1, b2, b3)
    left, right = scr[:, :128], scr[:, 128:]
    left_turned, right_turned = pltpu.roll(left, 64, 1), pltpu.roll(right, 64, 1)
    left = jnp.where(core == 0, left, jnp.where(low_lane, left_turned, right_turned))
    right = jnp.where(low_lane, jnp.where(core == 0, right, right_turned), 0.0)
    high, low = split(jnp.concatenate([left, right], 1))
    weight = jnp.concatenate(
        [mm_nt(hot[...], high) + mm_nt(hot[...], low) for hot in (slots, slots_last)], 0
    )
    high, low = split(weight)
    weight = jnp.concatenate([high, low], 1)
    for k, beta in enumerate(betas):
        span = slice(128 * k, 128 * k + 128)
        terms = jnp.zeros((128, 256), F32)
        for j in range(8):
            wide = one_hot(iota((32, 256), 0) % 16 == 8 * (iota((32, 256), 1) // 128) + j)
            projector = beta[pl.ds(j, 128, stride=8), :]
            terms = terms + mm(weight[span], wide) * jnp.concatenate([projector, projector], 1)
        high, low = split(terms)
        rows[span, 0:256] = high
        rows[span, 256:512] = low
    both = mm(put[...], rows[...])
    nonloc = both[:, :256] + both[:, 256:]
    for copy in copies:
        copy.wait()
    kinds = []
    for k in range(3):
        factor = jnp.concatenate([vloc[zi, pl.ds(k, 96, stride=3), :] for zi in range(3)], 0)
        at = slice(288 * k, 288 * k + 288)
        kinds.append(split(field[at, :] * jnp.concatenate([factor, factor], 1) + nonloc[at, :]))
    g = []
    for parity in range(2):
        table = [fx[1024 * parity + 512 * i : 1024 * parity + 512 * i + 512, :] for i in range(2)]
        lines = [jnp.concatenate([kinds[parity][i], kinds[parity + 1][i]], 1) for i in range(2)]
        g.append(split(three(mm, lines, table)))
    lines = [
        jnp.concatenate(
            [
                jnp.concatenate(
                    [
                        g[parity][i][96 * zi : 96 * zi + 96, 128 * c : 128 * c + 128]
                        for zi in range(3)
                    ],
                    1,
                )
                for c in range(2)
                for parity in range(2)
            ],
            0,
        )
        for i in range(2)
    ]
    h = three(mm, (fy[0:256, :], fy[256:512, :]), lines)
    main, spare, _ = masks_sp()
    spares = [jnp.zeros((64, 128), F32), jnp.zeros((64, 128), F32)]
    for zi in range(3):
        for c in range(2):
            turned = h[128 * c : 128 * c + 128, 128 * zi : 128 * zi + 128].T
            first = turned[:64]
            second = pltpu.roll(turned[64:], 64, 1)
            send[pl.ds(4 * c + zi, 64, stride=8), :] = jnp.where(main, first, second)
            high, low = split(jnp.where(spare, first, 0.0))
            move = ut[128 * zi : 128 * zi + 128, :]
            spares[c] = spares[c] + (mm(high, move) + mm(low, move))
    for c in range(2):
        send[pl.ds(4 * c + 3, 64, stride=8), :] = spares[c]


def kernel_z_forward(recv, fz, result, out, sems):
    s = lax.axis_index("fft")
    out[...] = jnp.zeros((1728, 128), F32)
    spans = [(152, 280), (576, 576), (1304, 280), (0, 152), (432, 144), (1152, 152), (1584, 144)]
    copies = [
        pltpu.make_async_copy(out.at[pl.ds(*span)], result.at[pl.ds(*span)], sems.at[k])
        for k, span in enumerate(spans)
    ]
    for copy in copies[:3]:
        copy.start()
    r = iota((256, 1), 0)
    main, spare = line_places(r, s)
    lane = iota((256, 128), 1)
    keep = one_hot(lane == main)
    highs, lows = [], []
    for zi in range(3):
        unpack = jnp.concatenate(
            [keep, one_hot((lane == spare + 32 * zi) & (spare >= 0))], 1
        )
        lines = jnp.concatenate(
            [
                jnp.concatenate(
                    [
                        recv[pl.ds(4 * c + zi, 64, stride=8), :],
                        recv[pl.ds(4 * c + 3, 64, stride=8), :],
                    ],
                    1,
                )
                for c in range(2)
            ],
            0,
        )
        high, low = split(lines)
        columns = mm_nt(unpack, jnp.concatenate([high, low], 0))
        highs.append(columns[:, :128].astype(BF))
        lows.append(columns[:, 128:].astype(BF))
    z = three(
        mm, (jnp.concatenate(highs, 1), jnp.concatenate(lows, 1)), (fz[0:384, :], fz[384:768, :])
    )
    low_lane = iota((64, 128), 1) < 64
    for plane in range(2):
        for c in range(2):
            block = z[128 * plane : 128 * plane + 128, 128 * c : 128 * c + 128]
            even = jnp.where(sphere_rows(plane, 0, s), block[:64], 0.0)
            odd = jnp.where(sphere_rows(plane, 1, s), block[64:], 0.0)
            kinds = (
                jnp.where(low_lane, even, 0.0),
                pltpu.roll(jnp.where(low_lane, odd, even), 64, 1),
                jnp.where(low_lane, 0.0, odd),
            )
            for k, tile in enumerate(kinds):
                at = 1152 * plane + 2 * k + c
                out[pl.ds(at, 25, stride=6), :] = tile[24:49]
                out[pl.ds(at + 432, 24, stride=6), :] = tile[:24]
        copies[3 + 2 * plane].start()
        copies[4 + 2 * plane].start()
    for copy in copies:
        copy.wait()


def call(kernel, name, out_shape, args, scratch=(), anywhere=(), anywhere_out=(), limit=VMEM_LIMIT, cost=None):
    specs = [
        pl.BlockSpec(memory_space=pl.ANY if k in anywhere else pltpu.VMEM)
        for k in range(len(args))
    ]
    shapes = [
        jax.ShapeDtypeStruct(*shape) if isinstance(shape[0], tuple) else jax.ShapeDtypeStruct(shape, F32)
        for shape in out_shape
    ]
    out = pl.pallas_call(
        kernel,
        name=name,
        out_shape=shapes,
        in_specs=specs,
        out_specs=[
            pl.BlockSpec(memory_space=pl.ANY if k in anywhere_out else pltpu.VMEM)
            for k in range(len(shapes))
        ],
        scratch_shapes=list(scratch),
        cost_estimate=cost,
        compiler_params=pltpu.CompilerParams(vmem_limit_bytes=limit),
    )(*args)
    return out


def body(psi_g, vloc, beta, blk_slot, blk_tile, dmat):
    t = {
        name: jnp.asarray(value) for name, value in tables().items()
    }
    psi = psi_g[0].transpose(1, 0, 2).reshape(3, 2, 288, 128).transpose(0, 2, 1, 3)
    psi = psi.reshape(1728, 128)
    def gathered(x):
        return [x] + [
            lax.ppermute(x, "band", [(i, (i + k) % 4) for i in range(4)]) for k in (1, 3, 2)
        ]

    ids = jnp.concatenate([blk_slot[None], blk_tile[None], jnp.zeros((6, 128), jnp.int32)], 0)
    own = jnp.concatenate([beta, ids.astype(F32)[None]], 0).reshape(1032, 128)
    betas = gathered(own)
    (send,) = call(
        kernel_z_inverse,
        "z_inverse",
        [(512, 128)],
        (psi, t["wz"]),
        [
            pltpu.VMEM((2, 384, 128), F32),
            pltpu.VMEM((768, 256), BF),
            pltpu.SemaphoreType.DMA((5,)),
        ],
        anywhere=(0, 1),
        limit=60 * 1024 * 1024,
    )

    def exchange(x):
        x = lax.all_to_all(x.reshape(64, 8, 128), "fft", 0, 0, tiled=True)
        return x.reshape(512, 128)

    recv = exchange(send)
    vloc_tiles = vloc.reshape(3, 288, 128).transpose(1, 0, 2)
    dmat_rows = dmat.transpose(1, 2, 0).reshape(64, 64)
    field, rows_h, rows_l = call(
        kernel_field,
        "field",
        [(864, 256), ((896, 256), BF), ((896, 256), BF)],
        (recv, t["ey"], t["ix"], t["u"]),
    )
    coef, slots, tiles = call(
        kernel_project,
        "project",
        [(16, 256), ((384, 256), BF), ((1, 384), jnp.int32)],
        (rows_h, rows_l, *betas[:3]),
        [pltpu.VMEM((384, 256), F32)],
    )
    near, slots_last, tiles_last = call(
        kernel_project_last,
        "project_last",
        [(96, 128), ((128, 256), BF), ((1, 128), jnp.int32)],
        (rows_h, rows_l, dmat_rows, coef, betas[3]),
        [pltpu.VMEM((128, 256), F32)],
    )
    other = lax.ppermute(near, "fft", [(i, i ^ 1) for i in range(64)])
    first, second = call(kernel_merge, "merge", [(80, 128), (80, 128)], (near, other))
    first = lax.ppermute(first, "fft", [(i, i ^ 2) for i in range(64)])
    second = lax.ppermute(second, "fft", [(i, (((i + 2) % 64) ^ 2) - 2 & 63) for i in range(64)])
    (put,) = call(
        kernel_put,
        "put",
        [((864, 512), BF)],
        (tiles, tiles_last),
        cost=pl.CostEstimate(flops=2000000, bytes_accessed=3000000, transcendentals=0),
    )
    (send,) = call(
        kernel_back,
        "back",
        [(512, 128)],
        (field, near, other, first, second, slots, slots_last, put, *betas, vloc_tiles, t["fx"], t["fy"], t["ut"]),
        [
            pltpu.VMEM((16, 256), F32),
            pltpu.VMEM((512, 512), BF),
            pltpu.VMEM((3, 288, 128), F32),
            pltpu.VMEM((2048, 256), BF),
            pltpu.VMEM((512, 384), BF),
            pltpu.VMEM((384, 128), BF),
            pltpu.SemaphoreType.DMA((6,)),
        ],
        anywhere=(12, 13, 14, 15),
    )
    (out,) = call(kernel_z_forward, "z_forward", [(1728, 128)], (exchange(send), t["fz"]),
        [pltpu.VMEM((1728, 128), F32), pltpu.SemaphoreType.DMA((7,))], anywhere_out=(0,))
    out = out.reshape(3, 288, 2, 128).transpose(0, 2, 1, 3).reshape(3, 2, N * N)
    return out.transpose(1, 0, 2)[None]


def solution(mesh):
    in_specs = (
        P("band", None, "fft", None),
        P("fft", None),
        P(("fft", "band"), None, None),
        P(("fft", "band")),
        P(("fft", "band")),
        P("fft", None, None),
    )
    out_specs = P("band", None, "fft", None)
    return jax.shard_map(body, mesh=mesh, in_specs=in_specs, out_specs=out_specs, check_vma=False)
```

```python
import functools

import jax
import jax.numpy as jnp
import ml_dtypes
import numpy as np
from jax import lax
from jax.experimental import pallas as pl
from jax.experimental.pallas import tpu as pltpu
from jax.sharding import PartitionSpec as P

N = 192
R2 = 48 * 48
BF = jnp.bfloat16
F32 = jnp.float32
VMEM_LIMIT = 48 * 1024 * 1024


def trig(freqs, points):
    angle = 2.0 * np.pi * (np.outer(freqs, points) % N) / N
    return np.cos(angle) / np.sqrt(N), np.sin(angle) / np.sqrt(N)


def pair_of(table):
    table = np.asarray(table, np.float32)
    high = table.astype(ml_dtypes.bfloat16)
    low = (table - high.astype(np.float32)).astype(ml_dtypes.bfloat16)
    return np.concatenate([high, low], 0)


KZ = np.concatenate([np.arange(64), np.arange(128, 192)])
SIGNED = np.concatenate([np.arange(64), np.arange(-64, 0)])
YS = [2 * np.arange(96), 2 * np.arange(96) + 1]


@functools.cache
def tables():
    t = {}
    blocks = []
    for zi in range(3):
        c, s = trig(3 * np.arange(64) + zi, KZ)
        blocks += [np.concatenate([c, -s], 1), np.concatenate([s, c], 1)]
    t["wz"] = pair_of(np.concatenate(blocks, 0))
    c, s = trig(np.concatenate(YS), SIGNED)
    t["ey"] = pair_of(
        np.concatenate([np.concatenate([c, -s], 1), np.concatenate([s, c], 1)], 0)
    )
    c, s = trig(SIGNED, np.arange(N))
    gap = np.zeros((128, 64))
    even = [np.concatenate([v, gap], 1) for v in (c, s, -s, c)]
    odd = [np.concatenate([gap, v], 1) for v in (c, s, -s, c)]
    t["ix"] = np.concatenate(
        [
            pair_of(np.block([[even[0], even[1]], [even[2], even[3]]])),
            pair_of(np.block([[odd[0], odd[1]], [odd[2], odd[3]]])),
        ],
        0,
    )
    parts = {}
    c, s = trig(np.arange(N), SIGNED)
    gap = np.zeros((64, 128))
    for name, table in (("c", c), ("s", s)):
        parts[name] = (np.concatenate([table, gap], 0), np.concatenate([gap, table], 0))

    def forward_x(which):
        cc, ss = parts["c"][which], parts["s"][which]
        first, second = np.concatenate([cc, -ss], 1), np.concatenate([ss, cc], 1)
        return np.concatenate([first[:128], second[:128], first[128:], second[128:]], 0)

    t["fx"] = np.concatenate([pair_of(forward_x(0)), pair_of(forward_x(1))], 0)
    c, s = trig(SIGNED, np.concatenate(YS))
    t["fy"] = pair_of(
        np.concatenate([np.concatenate([c, s], 1), np.concatenate([-s, c], 1)], 0)
    )
    blocks = []
    for zi in range(3):
        c, s = trig(3 * np.arange(64) + zi, KZ)
        blocks += [np.concatenate([c, -s], 1), np.concatenate([s, c], 1)]
    t["fz"] = pair_of(np.concatenate(blocks, 0))
    u = np.zeros((128, 384), np.float32)
    for zi in range(3):
        for p in range(128):
            u[16 * zi + 8 * (p >= 64) + p % 8, 128 * zi + p] = 1.0
    t["u"] = u.astype(ml_dtypes.bfloat16)
    t["ut"] = np.concatenate([u[:, 128 * zi : 128 * zi + 128].T for zi in range(3)], 0).astype(
        ml_dtypes.bfloat16
    )
    return t


def split(x):
    high = x.astype(BF)
    return high, (x - high.astype(F32)).astype(BF)


def mm(a, b):
    return jnp.dot(a, b, preferred_element_type=F32)


def mm_nt(a, b):
    return lax.dot_general(a, b, (((1,), (1,)), ((), ())), preferred_element_type=F32)


def three(product, a, b):
    return product(a[0], b[0]) + (product(a[0], b[1]) + product(a[1], b[0]))


def iota(shape, dim):
    return lax.broadcasted_iota(jnp.int32, shape, dim)


def masks_sp():
    s, p = iota((64, 128), 0), iota((64, 128), 1)
    ky = jnp.where(p < 64, p, p - 128)
    away = 64 - jnp.abs(ky)
    inside = ky * ky + s * s <= R2
    clash = away * away + (64 - s) * (64 - s) <= R2
    other = (p - 64) * (p - 64) + (64 - s) * (64 - s) <= R2
    return inside & ~clash, inside & clash, other


def line_places(r, s):
    plane, rest = r // 128, r % 128
    ky = 2 * (rest % 64 - 24) + rest // 64
    here = jnp.where(plane == 0, s, 64 - s)
    away = 64 - jnp.abs(ky)
    inside = ky * ky + here * here <= R2
    clash = (away * away + (64 - s) * (64 - s) <= R2) & (plane == 0)
    place = jnp.where(plane == 0, jnp.where(ky < 0, ky + 128, ky), ky + 64)
    main = jnp.where(inside & ~clash, place, -1)
    spare = jnp.where(inside & clash, jnp.where(ky < 0, 8, 0) + (ky + 64) % 8, -1)
    return main, spare


def one_hot(condition):
    return jnp.where(condition, 1.0, 0.0).astype(BF)


def sphere_rows(plane, parity, s):
    m, lane = iota((64, 128), 0), iota((64, 128), 1)
    ky = 2 * (m - 24) + parity
    kz = jnp.where(lane < 64, lane, lane - 128)
    kx = s - 64 * plane
    return ky * ky + kz * kz + kx * kx <= R2


def kernel_z_inverse(psi, wz_in, send, buf, wz, sems):
    s = lax.axis_index("fft")
    copies = []
    for plane in range(2):
        base = 1152 * plane
        for k, (src, dst, rows) in enumerate(((432, 0, 144), (0, 144, 152))):
            copies.append(
                pltpu.make_async_copy(
                    psi.at[pl.ds(base + src, rows)],
                    buf.at[plane, pl.ds(dst, rows)],
                    sems.at[2 * plane + k],
                )
            )
    copies.append(pltpu.make_async_copy(wz_in, wz, sems.at[4]))
    for copy in copies:
        copy.start()
    main, spare = line_places(iota((1, 256), 1), s)
    j = iota((128, 256), 0)
    pack = jnp.concatenate(
        [one_hot(j == main), one_hot((j % 16 == spare) & (j % 64 < 48))], axis=0
    )
    lane = iota((64, 128), 1)
    rows = []
    for copy in copies[:4]:
        copy.wait()
    for plane in range(2):
        lines = [[], []]
        for c in range(2):
            t = [buf[plane, pl.ds(2 * k + c, 64, stride=6), :] for k in range(3)]
            middle = pltpu.roll(t[1], 64, 1)
            even = jnp.where(lane < 64, t[0], middle)
            odd = jnp.where(lane < 64, middle, t[2])
            lines[0].append(jnp.where(sphere_rows(plane, 0, s), even, 0.0))
            lines[1].append(jnp.where(sphere_rows(plane, 1, s), odd, 0.0))
        rows += [jnp.concatenate(lines[0], 1), jnp.concatenate(lines[1], 1)]
    high, low = split(jnp.concatenate(rows, 0))
    packed = (mm(pack, high).astype(BF), mm(pack, low).astype(BF))
    copies[4].wait()
    out = three(mm_nt, (wz[0:384, :], wz[384:768, :]), packed)
    spares = out[0:64, 128:]
    for c in range(2):
        for zi in range(3):
            block = out[(2 * zi + c) * 64 : (2 * zi + c) * 64 + 64]
            send[pl.ds(3 * c + zi, 64, stride=7), :] = block[:, :128]
            spares = jnp.where(lane // 16 == 4 * c + zi, block[:, 128:], spares)
    send[pl.ds(6, 64, stride=7), :] = spares


def tile_rows(tiles):
    return (tiles % 3) * 288 + tiles // 3


def as_column(ids):
    return jnp.broadcast_to(ids.astype(F32), (8, ids.shape[1])).T[:, 0:1].astype(jnp.int32)


def kernel_field(
    recv, ey, ix, u, field, rows_h, rows_l,
):
    main, spare, other = masks_sp()
    spread = []
    for c in range(2):
        got = recv[pl.ds(6, 64, stride=7), :]
        high, low = split(pltpu.roll(got, 64, 1) if c else got)
        spread.append(mm(high, u[...]) + mm(low, u[...]))
    lines = []
    for zi in range(3):
        first, second = [], []
        for c in range(2):
            got = recv[pl.ds(3 * c + zi, 64, stride=7), :]
            extra = spread[c][:, 128 * zi : 128 * zi + 128]
            first.append(jnp.where(main, got, jnp.where(spare, extra, 0.0)))
            second.append(pltpu.roll(jnp.where(other, got, 0.0), 64, 1))
        lines += [jnp.concatenate(first, 1), jnp.concatenate(second, 1)]
    g = three(mm_nt, (ey[0:384, :], ey[384:768, :]), split(jnp.concatenate(lines, 0)))
    out = []
    for parity in range(2):
        a = 96 * parity
        table = [ix[512 * parity + 256 * i : 512 * parity + 256 * i + 256, :] for i in range(2)]
        block = jnp.concatenate(
            [
                jnp.concatenate(
                    [
                        g[a : a + 96, 128 * zi : 128 * zi + 128],
                        g[192 + a : 288 + a, 128 * zi : 128 * zi + 128],
                    ],
                    1,
                )
                for zi in range(3)
            ],
            0,
        )
        out.append(three(mm, split(block), table))
    even, odd = out
    for c in range(2):
        a = 256 * c
        kinds = (
            even[:, a : a + 128],
            even[:, a + 128 : a + 256] + odd[:, a : a + 128],
            odd[:, a + 128 : a + 256],
        )
        for k, tile in enumerate(kinds):
            span = pl.ds(288 * k, 288)
            lanes = pl.ds(128 * c, 128)
            field[span, lanes] = tile
            high, low = split(tile)
            rows_h[span, lanes] = high
            rows_l[span, lanes] = low
    rows_h[864:896, :] = jnp.zeros((32, 256), BF)
    rows_l[864:896, :] = jnp.zeros((32, 256), BF)


def project(quarters, rows_h, rows_l, tile_of, slots, betas, field_rows):
    count = 128 * quarters
    pick = one_hot(as_column(tile_of) == iota((count, 896), 1))
    field_rows[...] = mm(pick, rows_h[...]) + mm(pick, rows_l[...])
    lane = iota((128, 128), 1)
    sums = []
    for k, beta in enumerate(betas):
        total = jnp.zeros((128, 128), F32)
        for j in range(8):
            projector = beta[pl.ds(j, 128, stride=8), :]
            for c in range(2):
                value = field_rows[128 * k : 128 * k + 128, 128 * c : 128 * c + 128] * projector
                total = jnp.where(
                    lane == 8 * c + j, jnp.sum(value, axis=1, keepdims=True), total
                )
        sums.append(total.T[:16])
    high, low = split(jnp.concatenate(sums, 1))
    return mm(high, slots) + mm(low, slots)


def ids_of(betas, row):
    return jnp.concatenate([b[1024 + row : 1025 + row, :] for b in betas], 1).astype(jnp.int32)


def kernel_project(rows_h, rows_l, b0, b1, b2, coef, slots_out, tiles_out, field_rows):
    betas = (b0, b1, b2)
    tile_of = tile_rows(ids_of(betas, 1))
    tiles_out[...] = tile_of
    slots = one_hot(as_column(ids_of(betas, 0)) == iota((384, 256), 1))
    slots_out[...] = slots
    coef[...] = project(3, rows_h, rows_l, tile_of, slots, betas, field_rows)


def kernel_project_last(rows_h, rows_l, dmat, coef_in, b3, near, slots_out, tiles_out, field_rows):
    tile_of = tile_rows(ids_of((b3,), 1))
    tiles_out[...] = tile_of
    slots = one_hot(as_column(ids_of((b3,), 0)) == iota((128, 256), 1))
    slots_out[...] = slots
    coef = coef_in[...] + project(1, rows_h, rows_l, tile_of, slots, (b3,), field_rows)
    coef = jnp.where(iota((16, 256), 1) < 192, coef, 0.0)
    near[0:64, :] = jnp.concatenate([dmat[...], jnp.zeros((64, 64), F32)], 1)
    near[64:80, :] = coef[:, :128]
    near[80:96, :] = coef[:, 128:]


def chip_of(own, other):
    f = lax.axis_index("fft")
    core = f % 2
    own, other = own[...], other[...]
    return (
        core,
        (f // 2) % 2 == 0,
        jnp.where(core == 0, own, other),
        jnp.where(core == 0, other, own),
    )


def kernel_merge(own, other, first, second):
    _, even, a, b = chip_of(own, other)
    low_lane = iota((16, 128), 1) < 64
    turned = pltpu.roll(b[64:80], 64, 1)
    up = jnp.where(low_lane, a[80:96] + turned, pltpu.roll(b[80:96], 64, 1))
    down = jnp.where(low_lane, a[64:80], a[64:80] + turned)
    up = jnp.concatenate([b[0:64], up], 0)
    down = jnp.concatenate([a[0:64], down], 0)
    first[...] = jnp.where(even, up, down)
    second[...] = jnp.where(even, down, up)


def kernel_put(tiles, tiles_last, put):
    tile_of = jnp.concatenate([tiles[...], tiles_last[...]], 1)
    put[...] = one_hot(iota((864, 512), 0) == tile_of)


def kernel_back(
    field, own, other, first, second, slots, slots_last, put, b0, b1, b2, b3,
    vloc_in, fx_in, fy_in, ut_in, send, scr, rows, vloc, fx, fy, ut, sems,
):
    copies = [
        pltpu.make_async_copy(vloc_in.at[:, zi, :], vloc.at[zi], sems.at[zi]) for zi in range(3)
    ] + [
        pltpu.make_async_copy(fx_in, fx, sems.at[3]),
        pltpu.make_async_copy(fy_in, fy, sems.at[4]),
        pltpu.make_async_copy(ut_in, ut, sems.at[5]),
    ]
    for copy in copies:
        copy.start()
    core, even, a, b = chip_of(own, other)
    above = jnp.where(even, first[...], second[...])
    below = jnp.where(even, second[...], first[...])
    low_lane = iota((16, 128), 1) < 64
    turned = pltpu.roll(b[64:80], 64, 1)
    tot = [
        below[64:80] + jnp.where(low_lane, a[64:80], a[64:80] + turned),
        above[64:80] + jnp.where(low_lane, a[80:96] + turned, pltpu.roll(b[80:96], 64, 1)),
    ]
    wide = iota((64, 128), 1) < 64
    coupling = [
        jnp.where(wide, below[0:64], pltpu.roll(a[0:64], 64, 1)),
        jnp.where(wide, b[0:64], pltpu.roll(above[0:64], 64, 1)),
    ]
    for h in range(2):
        for c in range(2):
            coef = tot[h][8 * c : 8 * c + 8, :]
            for j in range(8):
                row = jnp.sum(coupling[h][8 * j : 8 * j + 8, :] * coef, axis=0, keepdims=True)
                scr[8 * c + j : 8 * c + j + 1, 128 * h : 128 * h + 128] = row
    betas = (b0, b1, b2, b3)
    left, right = scr[:, :128], scr[:, 128:]
    left_turned, right_turned = pltpu.roll(left, 64, 1), pltpu.roll(right, 64, 1)
    left = jnp.where(core == 0, left, jnp.where(low_lane, left_turned, right_turned))
    right = jnp.where(low_lane, jnp.where(core == 0, right, right_turned), 0.0)
    high, low = split(jnp.concatenate([left, right], 1))
    weight = jnp.concatenate(
        [mm_nt(hot[...], high) + mm_nt(hot[...], low) for hot in (slots, slots_last)], 0
    )
    high, low = split(weight)
    weight = jnp.concatenate([high, low], 1)
    for k, beta in enumerate(betas):
        span = slice(128 * k, 128 * k + 128)
        terms = jnp.zeros((128, 256), F32)
        for j in range(8):
            wide = one_hot(iota((32, 256), 0) % 16 == 8 * (iota((32, 256), 1) // 128) + j)
            projector = beta[pl.ds(j, 128, stride=8), :]
            terms = terms + mm(weight[span], wide) * jnp.concatenate([projector, projector], 1)
        high, low = split(terms)
        rows[span, 0:256] = high
        rows[span, 256:512] = low
    both = mm(put[...], rows[...])
    nonloc = both[:, :256] + both[:, 256:]
    for copy in copies:
        copy.wait()
    kinds = []
    for k in range(3):
        factor = jnp.concatenate([vloc[zi, pl.ds(k, 96, stride=3), :] for zi in range(3)], 0)
        at = slice(288 * k, 288 * k + 288)
        kinds.append(split(field[at, :] * jnp.concatenate([factor, factor], 1) + nonloc[at, :]))
    g = []
    for parity in range(2):
        table = [fx[1024 * parity + 512 * i : 1024 * parity + 512 * i + 512, :] for i in range(2)]
        lines = [jnp.concatenate([kinds[parity][i], kinds[parity + 1][i]], 1) for i in range(2)]
        g.append(split(three(mm, lines, table)))
    lines = [
        jnp.concatenate(
            [
                jnp.concatenate(
                    [
                        g[parity][i][96 * zi : 96 * zi + 96, 128 * c : 128 * c + 128]
                        for zi in range(3)
                    ],
                    1,
                )
                for c in range(2)
                for parity in range(2)
            ],
            0,
        )
        for i in range(2)
    ]
    h = three(mm, (fy[0:256, :], fy[256:512, :]), lines)
    main, spare, _ = masks_sp()
    spares = [jnp.zeros((64, 128), F32), jnp.zeros((64, 128), F32)]
    for zi in range(3):
        for c in range(2):
            turned = h[128 * c : 128 * c + 128, 128 * zi : 128 * zi + 128].T
            first = turned[:64]
            second = pltpu.roll(turned[64:], 64, 1)
            send[pl.ds(3 * c + zi, 64, stride=7), :] = jnp.where(main, first, second)
            high, low = split(jnp.where(spare, first, 0.0))
            move = ut[128 * zi : 128 * zi + 128, :]
            spares[c] = spares[c] + (mm(high, move) + mm(low, move))
    send[pl.ds(6, 64, stride=7), :] = spares[0] + pltpu.roll(spares[1], 64, 1)


def kernel_z_forward(recv, fz, result, out, sems):
    s = lax.axis_index("fft")
    out[...] = jnp.zeros((1728, 128), F32)
    spans = [(152, 280), (576, 576), (1304, 280), (0, 152), (432, 144), (1152, 152), (1584, 144)]
    copies = [
        pltpu.make_async_copy(out.at[pl.ds(*span)], result.at[pl.ds(*span)], sems.at[k])
        for k, span in enumerate(spans)
    ]
    for copy in copies[:3]:
        copy.start()
    r = iota((256, 1), 0)
    main, spare = line_places(r, s)
    lane = iota((256, 128), 1)
    keep = one_hot(lane == main)
    spares = recv[pl.ds(6, 64, stride=7), :]
    spares = (spares, pltpu.roll(spares, 64, 1))
    highs, lows = [], []
    for zi in range(3):
        unpack = jnp.concatenate(
            [keep, one_hot((lane == spare + 16 * zi) & (spare >= 0))], 1
        )
        lines = jnp.concatenate(
            [
                jnp.concatenate(
                    [
                        recv[pl.ds(3 * c + zi, 64, stride=7), :],
                        spares[c],
                    ],
                    1,
                )
                for c in range(2)
            ],
            0,
        )
        high, low = split(lines)
        columns = mm_nt(unpack, jnp.concatenate([high, low], 0))
        highs.append(columns[:, :128].astype(BF))
        lows.append(columns[:, 128:].astype(BF))
    z = three(
        mm, (jnp.concatenate(highs, 1), jnp.concatenate(lows, 1)), (fz[0:384, :], fz[384:768, :])
    )
    low_lane = iota((64, 128), 1) < 64
    for plane in range(2):
        for c in range(2):
            block = z[128 * plane : 128 * plane + 128, 128 * c : 128 * c + 128]
            even = jnp.where(sphere_rows(plane, 0, s), block[:64], 0.0)
            odd = jnp.where(sphere_rows(plane, 1, s), block[64:], 0.0)
            kinds = (
                jnp.where(low_lane, even, 0.0),
                pltpu.roll(jnp.where(low_lane, odd, even), 64, 1),
                jnp.where(low_lane, 0.0, odd),
            )
            for k, tile in enumerate(kinds):
                at = 1152 * plane + 2 * k + c
                out[pl.ds(at, 25, stride=6), :] = tile[24:49]
                out[pl.ds(at + 432, 24, stride=6), :] = tile[:24]
        copies[3 + 2 * plane].start()
        copies[4 + 2 * plane].start()
    for copy in copies:
        copy.wait()


def call(kernel, name, out_shape, args, scratch=(), anywhere=(), anywhere_out=(), limit=VMEM_LIMIT, cost=None):
    specs = [
        pl.BlockSpec(memory_space=pl.ANY if k in anywhere else pltpu.VMEM)
        for k in range(len(args))
    ]
    shapes = [
        jax.ShapeDtypeStruct(*shape) if isinstance(shape[0], tuple) else jax.ShapeDtypeStruct(shape, F32)
        for shape in out_shape
    ]
    out = pl.pallas_call(
        kernel,
        name=name,
        out_shape=shapes,
        in_specs=specs,
        out_specs=[
            pl.BlockSpec(memory_space=pl.ANY if k in anywhere_out else pltpu.VMEM)
            for k in range(len(shapes))
        ],
        scratch_shapes=list(scratch),
        cost_estimate=cost,
        compiler_params=pltpu.CompilerParams(vmem_limit_bytes=limit),
    )(*args)
    return out


def body(psi_g, vloc, beta, blk_slot, blk_tile, dmat):
    t = {
        name: jnp.asarray(value) for name, value in tables().items()
    }
    psi = psi_g[0].transpose(1, 0, 2).reshape(3, 2, 288, 128).transpose(0, 2, 1, 3)
    psi = psi.reshape(1728, 128)
    def gathered(x):
        return [x] + [
            lax.ppermute(x, "band", [(i, (i + k) % 4) for i in range(4)]) for k in (1, 3, 2)
        ]

    ids = jnp.concatenate([blk_slot[None], blk_tile[None], jnp.zeros((6, 128), jnp.int32)], 0)
    own = jnp.concatenate([beta, ids.astype(F32)[None]], 0).reshape(1032, 128)
    (send,) = call(
        kernel_z_inverse,
        "z_inverse",
        [(448, 128)],
        (psi, t["wz"]),
        [
            pltpu.VMEM((2, 384, 128), F32),
            pltpu.VMEM((768, 256), BF),
            pltpu.SemaphoreType.DMA((5,)),
        ],
        anywhere=(0, 1),
        limit=60 * 1024 * 1024,
    )
    own, send = lax.optimization_barrier((own, send))
    betas = gathered(own)

    def exchange(x):
        x = lax.all_to_all(x.reshape(64, 1, 896), "fft", 0, 0, tiled=True)
        return x.reshape(448, 128)

    recv = exchange(send)
    vloc_tiles = vloc.reshape(3, 288, 128).transpose(1, 0, 2)
    dmat_rows = dmat.transpose(1, 2, 0).reshape(64, 64)
    field, rows_h, rows_l = call(
        kernel_field,
        "field",
        [(864, 256), ((896, 256), BF), ((896, 256), BF)],
        (recv, t["ey"], t["ix"], t["u"]),
    )
    coef, slots, tiles = call(
        kernel_project,
        "project",
        [(16, 256), ((384, 256), BF), ((1, 384), jnp.int32)],
        (rows_h, rows_l, *betas[:3]),
        [pltpu.VMEM((384, 256), F32)],
    )
    near, slots_last, tiles_last = call(
        kernel_project_last,
        "project_last",
        [(96, 128), ((128, 256), BF), ((1, 128), jnp.int32)],
        (rows_h, rows_l, dmat_rows, coef, betas[3]),
        [pltpu.VMEM((128, 256), F32)],
    )
    other = lax.ppermute(near, "fft", [(i, i ^ 1) for i in range(64)])
    first, second = call(kernel_merge, "merge", [(80, 128), (80, 128)], (near, other))
    first = lax.ppermute(first, "fft", [(i, i ^ 2) for i in range(64)])
    second = lax.ppermute(second, "fft", [(i, (((i + 2) % 64) ^ 2) - 2 & 63) for i in range(64)])
    (put,) = call(
        kernel_put,
        "put",
        [((864, 512), BF)],
        (tiles, tiles_last),
        cost=pl.CostEstimate(flops=2000000, bytes_accessed=3000000, transcendentals=0),
    )
    (send,) = call(
        kernel_back,
        "back",
        [(448, 128)],
        (field, near, other, first, second, slots, slots_last, put, *betas, vloc_tiles, t["fx"], t["fy"], t["ut"]),
        [
            pltpu.VMEM((16, 256), F32),
            pltpu.VMEM((512, 512), BF),
            pltpu.VMEM((3, 288, 128), F32),
            pltpu.VMEM((2048, 256), BF),
            pltpu.VMEM((512, 384), BF),
            pltpu.VMEM((384, 128), BF),
            pltpu.SemaphoreType.DMA((6,)),
        ],
        anywhere=(12, 13, 14, 15),
    )
    (out,) = call(kernel_z_forward, "z_forward", [(1728, 128)], (exchange(send), t["fz"]),
        [pltpu.VMEM((1728, 128), F32), pltpu.SemaphoreType.DMA((7,))], anywhere_out=(0,))
    out = out.reshape(3, 288, 2, 128).transpose(0, 2, 1, 3).reshape(3, 2, N * N)
    return out.transpose(1, 0, 2)[None]


def solution(mesh):
    in_specs = (
        P("band", None, "fft", None),
        P("fft", None),
        P(("fft", "band"), None, None),
        P(("fft", "band")),
        P(("fft", "band")),
        P("fft", None, None),
    )
    out_specs = P("band", None, "fft", None)
    return jax.shard_map(body, mesh=mesh, in_specs=in_specs, out_specs=out_specs, check_vma=False)
```

```python
import functools

import jax
import jax.numpy as jnp
import ml_dtypes
import numpy as np
from jax import lax
from jax.experimental import pallas as pl
from jax.experimental.pallas import tpu as pltpu
from jax.sharding import PartitionSpec as P

N = 192
R2 = 48 * 48
BF = jnp.bfloat16
F32 = jnp.float32
VMEM_LIMIT = 48 * 1024 * 1024


def trig(freqs, points):
    angle = 2.0 * np.pi * (np.outer(freqs, points) % N) / N
    return np.cos(angle) / np.sqrt(N), np.sin(angle) / np.sqrt(N)


def pair_of(table):
    table = np.asarray(table, np.float32)
    high = table.astype(ml_dtypes.bfloat16)
    low = (table - high.astype(np.float32)).astype(ml_dtypes.bfloat16)
    return np.concatenate([high, low], 0)


KZ = np.concatenate([np.arange(64), np.arange(128, 192)])
SIGNED = np.concatenate([np.arange(64), np.arange(-64, 0)])
YS = [2 * np.arange(96), 2 * np.arange(96) + 1]


@functools.cache
def tables():
    t = {}
    blocks = []
    for zi in range(3):
        c, s = trig(3 * np.arange(64) + zi, KZ)
        blocks += [np.concatenate([c, -s], 1), np.concatenate([s, c], 1)]
    t["wz"] = pair_of(np.concatenate(blocks, 0))
    c, s = trig(np.concatenate(YS), SIGNED)
    t["ey"] = pair_of(
        np.concatenate([np.concatenate([c, -s], 1), np.concatenate([s, c], 1)], 0)
    )
    c, s = trig(SIGNED, np.arange(N))
    gap = np.zeros((128, 64))
    even = [np.concatenate([v, gap], 1) for v in (c, s, -s, c)]
    odd = [np.concatenate([gap, v], 1) for v in (c, s, -s, c)]
    t["ix"] = np.concatenate(
        [
            pair_of(np.block([[even[0], even[1]], [even[2], even[3]]])),
            pair_of(np.block([[odd[0], odd[1]], [odd[2], odd[3]]])),
        ],
        0,
    )
    parts = {}
    c, s = trig(np.arange(N), SIGNED)
    gap = np.zeros((64, 128))
    for name, table in (("c", c), ("s", s)):
        parts[name] = (np.concatenate([table, gap], 0), np.concatenate([gap, table], 0))

    def forward_x(which):
        cc, ss = parts["c"][which], parts["s"][which]
        first, second = np.concatenate([cc, -ss], 1), np.concatenate([ss, cc], 1)
        return np.concatenate([first[:128], second[:128], first[128:], second[128:]], 0)

    t["fx"] = np.concatenate([pair_of(forward_x(0)), pair_of(forward_x(1))], 0)
    c, s = trig(SIGNED, np.concatenate(YS))
    t["fy"] = pair_of(
        np.concatenate([np.concatenate([c, s], 1), np.concatenate([-s, c], 1)], 0)
    )
    blocks = []
    for zi in range(3):
        c, s = trig(3 * np.arange(64) + zi, KZ)
        blocks += [np.concatenate([c, -s], 1), np.concatenate([s, c], 1)]
    t["fz"] = pair_of(np.concatenate(blocks, 0))
    u = np.zeros((128, 384), np.float32)
    for zi in range(3):
        for p in range(128):
            u[16 * zi + 8 * (p >= 64) + p % 8, 128 * zi + p] = 1.0
    t["u"] = u.astype(ml_dtypes.bfloat16)
    t["ut"] = np.concatenate([u[:, 128 * zi : 128 * zi + 128].T for zi in range(3)], 0).astype(
        ml_dtypes.bfloat16
    )
    return t


def split(x):
    high = x.astype(BF)
    return high, (x - high.astype(F32)).astype(BF)


def mm(a, b):
    return jnp.dot(a, b, preferred_element_type=F32)


def mm_nt(a, b):
    return lax.dot_general(a, b, (((1,), (1,)), ((), ())), preferred_element_type=F32)


def three(product, a, b):
    return product(a[0], b[0]) + (product(a[0], b[1]) + product(a[1], b[0]))


def iota(shape, dim):
    return lax.broadcasted_iota(jnp.int32, shape, dim)


def masks_sp():
    s, p = iota((64, 128), 0), iota((64, 128), 1)
    ky = jnp.where(p < 64, p, p - 128)
    away = 64 - jnp.abs(ky)
    inside = ky * ky + s * s <= R2
    clash = away * away + (64 - s) * (64 - s) <= R2
    other = (p - 64) * (p - 64) + (64 - s) * (64 - s) <= R2
    return inside & ~clash, inside & clash, other


def line_places(r, s):
    plane, rest = r // 128, r % 128
    ky = 2 * (rest % 64 - 24) + rest // 64
    here = jnp.where(plane == 0, s, 64 - s)
    away = 64 - jnp.abs(ky)
    inside = ky * ky + here * here <= R2
    clash = (away * away + (64 - s) * (64 - s) <= R2) & (plane == 0)
    place = jnp.where(plane == 0, jnp.where(ky < 0, ky + 128, ky), ky + 64)
    main = jnp.where(inside & ~clash, place, -1)
    spare = jnp.where(inside & clash, jnp.where(ky < 0, 8, 0) + (ky + 64) % 8, -1)
    return main, spare


def one_hot(condition):
    return jnp.where(condition, 1.0, 0.0).astype(BF)


def sphere_rows(plane, parity, s):
    m, lane = iota((64, 128), 0), iota((64, 128), 1)
    ky = 2 * (m - 24) + parity
    kz = jnp.where(lane < 64, lane, lane - 128)
    kx = s - 64 * plane
    return ky * ky + kz * kz + kx * kx <= R2


def kernel_z_inverse(psi, wz_in, send, buf, wz, sems):
    s = lax.axis_index("fft")
    copies = []
    for plane in range(2):
        base = 1152 * plane
        for k, (src, dst, rows) in enumerate(((432, 0, 144), (0, 144, 152))):
            copies.append(
                pltpu.make_async_copy(
                    psi.at[pl.ds(base + src, rows)],
                    buf.at[plane, pl.ds(dst, rows)],
                    sems.at[2 * plane + k],
                )
            )
    copies.append(pltpu.make_async_copy(wz_in, wz, sems.at[4]))
    for copy in copies:
        copy.start()
    main, spare = line_places(iota((1, 256), 1), s)
    j = iota((128, 256), 0)
    pack = jnp.concatenate(
        [one_hot(j == main), one_hot((j % 16 == spare) & (j % 64 < 48))], axis=0
    )
    lane = iota((64, 128), 1)
    rows = []
    for copy in copies[:4]:
        copy.wait()
    for plane in range(2):
        lines = [[], []]
        for c in range(2):
            t = [buf[plane, pl.ds(2 * k + c, 64, stride=6), :] for k in range(3)]
            middle = pltpu.roll(t[1], 64, 1)
            even = jnp.where(lane < 64, t[0], middle)
            odd = jnp.where(lane < 64, middle, t[2])
            lines[0].append(jnp.where(sphere_rows(plane, 0, s), even, 0.0))
            lines[1].append(jnp.where(sphere_rows(plane, 1, s), odd, 0.0))
        rows += [jnp.concatenate(lines[0], 1), jnp.concatenate(lines[1], 1)]
    high, low = split(jnp.concatenate(rows, 0))
    packed = (mm(pack, high).astype(BF), mm(pack, low).astype(BF))
    copies[4].wait()
    out = three(mm_nt, (wz[0:384, :], wz[384:768, :]), packed)
    spares = out[0:64, 128:]
    for c in range(2):
        for zi in range(3):
            block = out[(2 * zi + c) * 64 : (2 * zi + c) * 64 + 64]
            send[pl.ds(3 * c + zi, 64, stride=7), :] = block[:, :128]
            spares = jnp.where(lane // 16 == 4 * c + zi, block[:, 128:], spares)
    send[pl.ds(6, 64, stride=7), :] = spares


def tile_rows(tiles):
    return (tiles % 3) * 288 + tiles // 3


def as_column(ids):
    return jnp.broadcast_to(ids.astype(F32), (8, ids.shape[1])).T[:, 0:1].astype(jnp.int32)


def kernel_field(
    recv, ey, ix, u, field, rows_h, rows_l,
):
    main, spare, other = masks_sp()
    spread = []
    for c in range(2):
        got = recv[pl.ds(6, 64, stride=7), :]
        high, low = split(pltpu.roll(got, 64, 1) if c else got)
        spread.append(mm(high, u[...]) + mm(low, u[...]))
    lines = []
    for zi in range(3):
        first, second = [], []
        for c in range(2):
            got = recv[pl.ds(3 * c + zi, 64, stride=7), :]
            extra = spread[c][:, 128 * zi : 128 * zi + 128]
            first.append(jnp.where(main, got, jnp.where(spare, extra, 0.0)))
            second.append(pltpu.roll(jnp.where(other, got, 0.0), 64, 1))
        lines += [jnp.concatenate(first, 1), jnp.concatenate(second, 1)]
    g = three(mm_nt, (ey[0:384, :], ey[384:768, :]), split(jnp.concatenate(lines, 0)))
    out = []
    for parity in range(2):
        a = 96 * parity
        table = [ix[512 * parity + 256 * i : 512 * parity + 256 * i + 256, :] for i in range(2)]
        block = jnp.concatenate(
            [
                jnp.concatenate(
                    [
                        g[a : a + 96, 128 * zi : 128 * zi + 128],
                        g[192 + a : 288 + a, 128 * zi : 128 * zi + 128],
                    ],
                    1,
                )
                for zi in range(3)
            ],
            0,
        )
        out.append(three(mm, split(block), table))
    even, odd = out
    for c in range(2):
        a = 256 * c
        kinds = (
            even[:, a : a + 128],
            even[:, a + 128 : a + 256] + odd[:, a : a + 128],
            odd[:, a + 128 : a + 256],
        )
        for k, tile in enumerate(kinds):
            span = pl.ds(288 * k, 288)
            lanes = pl.ds(128 * c, 128)
            field[span, lanes] = tile
            high, low = split(tile)
            rows_h[span, lanes] = high
            rows_l[span, lanes] = low
    rows_h[864:896, :] = jnp.zeros((32, 256), BF)
    rows_l[864:896, :] = jnp.zeros((32, 256), BF)


def project(quarters, rows_h, rows_l, tile_of, slots, betas, field_rows):
    count = 128 * quarters
    pick = one_hot(as_column(tile_of) == iota((count, 896), 1))
    field_rows[...] = mm(pick, rows_h[...]) + mm(pick, rows_l[...])
    lane = iota((128, 128), 1)
    sums = []
    for k, beta in enumerate(betas):
        total = jnp.zeros((128, 128), F32)
        for j in range(8):
            projector = beta[pl.ds(j, 128, stride=8), :]
            for c in range(2):
                value = field_rows[128 * k : 128 * k + 128, 128 * c : 128 * c + 128] * projector
                total = jnp.where(
                    lane == 8 * c + j, jnp.sum(value, axis=1, keepdims=True), total
                )
        sums.append(total.T[:16])
    high, low = split(jnp.concatenate(sums, 1))
    return mm(high, slots) + mm(low, slots)


def ids_of(betas, row):
    return jnp.concatenate([b[1024 + row : 1025 + row, :] for b in betas], 1).astype(jnp.int32)


def kernel_project(rows_h, rows_l, b0, b1, b2, coef, slots_out, tiles_out, field_rows):
    betas = (b0, b1, b2)
    tile_of = tile_rows(ids_of(betas, 1))
    tiles_out[...] = tile_of
    slots = one_hot(as_column(ids_of(betas, 0)) == iota((384, 256), 1))
    slots_out[...] = slots
    coef[...] = project(3, rows_h, rows_l, tile_of, slots, betas, field_rows)


def kernel_project_last(rows_h, rows_l, dmat, coef_in, b3, near, slots_out, tiles_out, field_rows):
    tile_of = tile_rows(ids_of((b3,), 1))
    tiles_out[...] = tile_of
    slots = one_hot(as_column(ids_of((b3,), 0)) == iota((128, 256), 1))
    slots_out[...] = slots
    coef = coef_in[...] + project(1, rows_h, rows_l, tile_of, slots, (b3,), field_rows)
    coef = jnp.where(iota((16, 256), 1) < 192, coef, 0.0)
    near[0:64, :] = jnp.concatenate([dmat[...], jnp.zeros((64, 64), F32)], 1)
    near[64:80, :] = coef[:, :128]
    near[80:96, :] = coef[:, 128:]


def chip_of(own, other):
    f = lax.axis_index("fft")
    core = f % 2
    own, other = own[...], other[...]
    return (
        core,
        (f // 2) % 2 == 0,
        jnp.where(core == 0, own, other),
        jnp.where(core == 0, other, own),
    )


def kernel_merge(own, other, first, second):
    _, even, a, b = chip_of(own, other)
    low_lane = iota((16, 128), 1) < 64
    turned = pltpu.roll(b[64:80], 64, 1)
    up = jnp.where(low_lane, a[80:96] + turned, pltpu.roll(b[80:96], 64, 1))
    down = jnp.where(low_lane, a[64:80], a[64:80] + turned)
    up = jnp.concatenate([b[0:64], up], 0)
    down = jnp.concatenate([a[0:64], down], 0)
    first[...] = jnp.where(even, up, down)
    second[...] = jnp.where(even, down, up)


def kernel_put(tiles, tiles_last, put):
    tile_of = jnp.concatenate([tiles[...], tiles_last[...]], 1)
    put[...] = one_hot(iota((864, 512), 0) == tile_of)


def kernel_back(
    field, own, other, first, second, slots, slots_last, put, b0, b1, b2, b3,
    vloc_in, fx_in, fy_in, ut_in, send, scr, rows, vloc, fx, fy, ut, sems,
):
    copies = [
        pltpu.make_async_copy(vloc_in.at[:, zi, :], vloc.at[zi], sems.at[zi]) for zi in range(3)
    ] + [
        pltpu.make_async_copy(fx_in, fx, sems.at[3]),
        pltpu.make_async_copy(fy_in, fy, sems.at[4]),
        pltpu.make_async_copy(ut_in, ut, sems.at[5]),
    ]
    for copy in copies:
        copy.start()
    core, even, a, b = chip_of(own, other)
    above = jnp.where(even, first[...], second[...])
    below = jnp.where(even, second[...], first[...])
    low_lane = iota((16, 128), 1) < 64
    turned = pltpu.roll(b[64:80], 64, 1)
    tot = [
        below[64:80] + jnp.where(low_lane, a[64:80], a[64:80] + turned),
        above[64:80] + jnp.where(low_lane, a[80:96] + turned, pltpu.roll(b[80:96], 64, 1)),
    ]
    wide = iota((64, 128), 1) < 64
    coupling = [
        jnp.where(wide, below[0:64], pltpu.roll(a[0:64], 64, 1)),
        jnp.where(wide, b[0:64], pltpu.roll(above[0:64], 64, 1)),
    ]
    for h in range(2):
        for c in range(2):
            coef = tot[h][8 * c : 8 * c + 8, :]
            for j in range(8):
                row = jnp.sum(coupling[h][8 * j : 8 * j + 8, :] * coef, axis=0, keepdims=True)
                scr[8 * c + j : 8 * c + j + 1, 128 * h : 128 * h + 128] = row
    betas = (b0, b1, b2, b3)
    left, right = scr[:, :128], scr[:, 128:]
    left_turned, right_turned = pltpu.roll(left, 64, 1), pltpu.roll(right, 64, 1)
    left = jnp.where(core == 0, left, jnp.where(low_lane, left_turned, right_turned))
    right = jnp.where(low_lane, jnp.where(core == 0, right, right_turned), 0.0)
    high, low = split(jnp.concatenate([left, right], 1))
    weight = jnp.concatenate(
        [mm_nt(hot[...], high) + mm_nt(hot[...], low) for hot in (slots, slots_last)], 0
    )
    high, low = split(weight)
    weight = jnp.concatenate([high, low], 1)
    for k, beta in enumerate(betas):
        span = slice(128 * k, 128 * k + 128)
        terms = jnp.zeros((128, 256), F32)
        for j in range(8):
            wide = one_hot(iota((32, 256), 0) % 16 == 8 * (iota((32, 256), 1) // 128) + j)
            projector = beta[pl.ds(j, 128, stride=8), :]
            terms = terms + mm(weight[span], wide) * jnp.concatenate([projector, projector], 1)
        high, low = split(terms)
        rows[span, 0:256] = high
        rows[span, 256:512] = low
    both = mm(put[...], rows[...])
    nonloc = both[:, :256] + both[:, 256:]
    for copy in copies:
        copy.wait()
    kinds = []
    for k in range(3):
        factor = jnp.concatenate([vloc[zi, pl.ds(k, 96, stride=3), :] for zi in range(3)], 0)
        at = slice(288 * k, 288 * k + 288)
        kinds.append(split(field[at, :] * jnp.concatenate([factor, factor], 1) + nonloc[at, :]))
    g = []
    for parity in range(2):
        table = [fx[1024 * parity + 512 * i : 1024 * parity + 512 * i + 512, :] for i in range(2)]
        lines = [jnp.concatenate([kinds[parity][i], kinds[parity + 1][i]], 1) for i in range(2)]
        g.append(split(three(mm, lines, table)))
    lines = [
        jnp.concatenate(
            [
                jnp.concatenate(
                    [
                        g[parity][i][96 * zi : 96 * zi + 96, 128 * c : 128 * c + 128]
                        for zi in range(3)
                    ],
                    1,
                )
                for c in range(2)
                for parity in range(2)
            ],
            0,
        )
        for i in range(2)
    ]
    h = three(mm, (fy[0:256, :], fy[256:512, :]), lines)
    main, spare, _ = masks_sp()
    spares = [jnp.zeros((64, 128), F32), jnp.zeros((64, 128), F32)]
    for zi in range(3):
        for c in range(2):
            turned = h[128 * c : 128 * c + 128, 128 * zi : 128 * zi + 128].T
            first = turned[:64]
            second = pltpu.roll(turned[64:], 64, 1)
            send[pl.ds(3 * c + zi, 64, stride=7), :] = jnp.where(main, first, second)
            high, low = split(jnp.where(spare, first, 0.0))
            move = ut[128 * zi : 128 * zi + 128, :]
            spares[c] = spares[c] + (mm(high, move) + mm(low, move))
    send[pl.ds(6, 64, stride=7), :] = spares[0] + pltpu.roll(spares[1], 64, 1)


def kernel_z_forward(recv, fz, result, out, sems):
    s = lax.axis_index("fft")
    out[...] = jnp.zeros((1728, 128), F32)
    spans = [(152, 280), (576, 576), (1304, 280), (0, 152), (432, 144), (1152, 152), (1584, 144)]
    copies = [
        pltpu.make_async_copy(out.at[pl.ds(*span)], result.at[pl.ds(*span)], sems.at[k])
        for k, span in enumerate(spans)
    ]
    for copy in copies[:3]:
        copy.start()
    r = iota((256, 1), 0)
    main, spare = line_places(r, s)
    lane = iota((256, 128), 1)
    keep = one_hot(lane == main)
    spares = recv[pl.ds(6, 64, stride=7), :]
    spares = (spares, pltpu.roll(spares, 64, 1))
    highs, lows = [], []
    for zi in range(3):
        unpack = jnp.concatenate(
            [keep, one_hot((lane == spare + 16 * zi) & (spare >= 0))], 1
        )
        lines = jnp.concatenate(
            [
                jnp.concatenate(
                    [
                        recv[pl.ds(3 * c + zi, 64, stride=7), :],
                        spares[c],
                    ],
                    1,
                )
                for c in range(2)
            ],
            0,
        )
        high, low = split(lines)
        columns = mm_nt(unpack, jnp.concatenate([high, low], 0))
        highs.append(columns[:, :128].astype(BF))
        lows.append(columns[:, 128:].astype(BF))
    z = three(
        mm, (jnp.concatenate(highs, 1), jnp.concatenate(lows, 1)), (fz[0:384, :], fz[384:768, :])
    )
    low_lane = iota((64, 128), 1) < 64
    for plane in range(2):
        for c in range(2):
            block = z[128 * plane : 128 * plane + 128, 128 * c : 128 * c + 128]
            even = jnp.where(sphere_rows(plane, 0, s), block[:64], 0.0)
            odd = jnp.where(sphere_rows(plane, 1, s), block[64:], 0.0)
            kinds = (
                jnp.where(low_lane, even, 0.0),
                pltpu.roll(jnp.where(low_lane, odd, even), 64, 1),
                jnp.where(low_lane, 0.0, odd),
            )
            for k, tile in enumerate(kinds):
                at = 1152 * plane + 2 * k + c
                out[pl.ds(at, 25, stride=6), :] = tile[24:49]
                out[pl.ds(at + 432, 24, stride=6), :] = tile[:24]
        copies[3 + 2 * plane].start()
        copies[4 + 2 * plane].start()
    for copy in copies:
        copy.wait()


def call(kernel, name, out_shape, args, scratch=(), anywhere=(), anywhere_out=(), limit=VMEM_LIMIT, cost=None):
    specs = [
        pl.BlockSpec(memory_space=pl.ANY if k in anywhere else pltpu.VMEM)
        for k in range(len(args))
    ]
    shapes = [
        jax.ShapeDtypeStruct(*shape) if isinstance(shape[0], tuple) else jax.ShapeDtypeStruct(shape, F32)
        for shape in out_shape
    ]
    out = pl.pallas_call(
        kernel,
        name=name,
        out_shape=shapes,
        in_specs=specs,
        out_specs=[
            pl.BlockSpec(memory_space=pl.ANY if k in anywhere_out else pltpu.VMEM)
            for k in range(len(shapes))
        ],
        scratch_shapes=list(scratch),
        cost_estimate=cost,
        compiler_params=pltpu.CompilerParams(vmem_limit_bytes=limit),
    )(*args)
    return out


def body(psi_g, vloc, beta, blk_slot, blk_tile, dmat):
    t = {
        name: jnp.asarray(value) for name, value in tables().items()
    }
    psi = psi_g[0].transpose(1, 0, 2).reshape(3, 2, 288, 128).transpose(0, 2, 1, 3)
    psi = psi.reshape(1728, 128)
    def gathered(x):
        return [x] + [
            lax.ppermute(x, "band", [(i, (i + k) % 4) for i in range(4)]) for k in (3, 2, 1)
        ]

    ids = jnp.concatenate([blk_slot[None], blk_tile[None], jnp.zeros((6, 128), jnp.int32)], 0)
    own = jnp.concatenate([beta, ids.astype(F32)[None]], 0).reshape(1032, 128)
    (send,) = call(
        kernel_z_inverse,
        "z_inverse",
        [(448, 128)],
        (psi, t["wz"]),
        [
            pltpu.VMEM((2, 384, 128), F32),
            pltpu.VMEM((768, 256), BF),
            pltpu.SemaphoreType.DMA((5,)),
        ],
        anywhere=(0, 1),
        limit=60 * 1024 * 1024,
    )
    betas = gathered(own)

    def exchange(x):
        x = lax.all_to_all(x.reshape(64, 1, 896), "fft", 0, 0, tiled=True)
        return x.reshape(448, 128)

    recv = exchange(send)
    vloc_tiles = vloc.reshape(3, 288, 128).transpose(1, 0, 2)
    dmat_rows = dmat.transpose(1, 2, 0).reshape(64, 64)
    field, rows_h, rows_l = call(
        kernel_field,
        "field",
        [(864, 256), ((896, 256), BF), ((896, 256), BF)],
        (recv, t["ey"], t["ix"], t["u"]),
    )
    coef, slots, tiles = call(
        kernel_project,
        "project",
        [(16, 256), ((384, 256), BF), ((1, 384), jnp.int32)],
        (rows_h, rows_l, *betas[:3]),
        [pltpu.VMEM((384, 256), F32)],
    )
    near, slots_last, tiles_last = call(
        kernel_project_last,
        "project_last",
        [(96, 128), ((128, 256), BF), ((1, 128), jnp.int32)],
        (rows_h, rows_l, dmat_rows, coef, betas[3]),
        [pltpu.VMEM((128, 256), F32)],
    )
    other = lax.ppermute(near, "fft", [(i, i ^ 1) for i in range(64)])
    first, second = call(kernel_merge, "merge", [(80, 128), (80, 128)], (near, other))
    first = lax.ppermute(first, "fft", [(i, i ^ 2) for i in range(64)])
    second = lax.ppermute(second, "fft", [(i, (((i + 2) % 64) ^ 2) - 2 & 63) for i in range(64)])
    (put,) = call(
        kernel_put,
        "put",
        [((864, 512), BF)],
        (tiles, tiles_last),
        cost=pl.CostEstimate(flops=2000000, bytes_accessed=3000000, transcendentals=0),
    )
    (send,) = call(
        kernel_back,
        "back",
        [(448, 128)],
        (field, near, other, first, second, slots, slots_last, put, *betas, vloc_tiles, t["fx"], t["fy"], t["ut"]),
        [
            pltpu.VMEM((16, 256), F32),
            pltpu.VMEM((512, 512), BF),
            pltpu.VMEM((3, 288, 128), F32),
            pltpu.VMEM((2048, 256), BF),
            pltpu.VMEM((512, 384), BF),
            pltpu.VMEM((384, 128), BF),
            pltpu.SemaphoreType.DMA((6,)),
        ],
        anywhere=(12, 13, 14, 15),
    )
    (out,) = call(kernel_z_forward, "z_forward", [(1728, 128)], (exchange(send), t["fz"]),
        [pltpu.VMEM((1728, 128), F32), pltpu.SemaphoreType.DMA((7,))], anywhere_out=(0,))
    out = out.reshape(3, 288, 2, 128).transpose(0, 2, 1, 3).reshape(3, 2, N * N)
    return out.transpose(1, 0, 2)[None]


def solution(mesh):
    in_specs = (
        P("band", None, "fft", None),
        P("fft", None),
        P(("fft", "band"), None, None),
        P(("fft", "band")),
        P(("fft", "band")),
        P("fft", None, None),
    )
    out_specs = P("band", None, "fft", None)
    return jax.shard_map(body, mesh=mesh, in_specs=in_specs, out_specs=out_specs, check_vma=False)
```

```python
import functools

import jax
import jax.numpy as jnp
import ml_dtypes
import numpy as np
from jax import lax
from jax.experimental import pallas as pl
from jax.experimental.pallas import tpu as pltpu
from jax.sharding import PartitionSpec as P

N = 192
R2 = 48 * 48
BF = jnp.bfloat16
F32 = jnp.float32
VMEM_LIMIT = 48 * 1024 * 1024


def trig(freqs, points):
    angle = 2.0 * np.pi * (np.outer(freqs, points) % N) / N
    return np.cos(angle) / np.sqrt(N), np.sin(angle) / np.sqrt(N)


def pair_of(table):
    table = np.asarray(table, np.float32)
    high = table.astype(ml_dtypes.bfloat16)
    low = (table - high.astype(np.float32)).astype(ml_dtypes.bfloat16)
    return np.concatenate([high, low], 0)


KZ = np.concatenate([np.arange(64), np.arange(128, 192)])
SIGNED = np.concatenate([np.arange(64), np.arange(-64, 0)])
YS = [2 * np.arange(96), 2 * np.arange(96) + 1]


@functools.cache
def tables():
    t = {}
    blocks = []
    for zi in range(3):
        c, s = trig(3 * np.arange(64) + zi, KZ)
        blocks += [np.concatenate([c, -s], 1), np.concatenate([s, c], 1)]
    t["wz"] = pair_of(np.concatenate(blocks, 0))
    c, s = trig(np.concatenate(YS), SIGNED)
    t["ey"] = pair_of(
        np.concatenate([np.concatenate([c, -s], 1), np.concatenate([s, c], 1)], 0)
    )
    c, s = trig(SIGNED, np.arange(N))
    gap = np.zeros((128, 64))
    even = [np.concatenate([v, gap], 1) for v in (c, s, -s, c)]
    odd = [np.concatenate([gap, v], 1) for v in (c, s, -s, c)]
    t["ix"] = np.concatenate(
        [
            pair_of(np.block([[even[0], even[1]], [even[2], even[3]]])),
            pair_of(np.block([[odd[0], odd[1]], [odd[2], odd[3]]])),
        ],
        0,
    )
    parts = {}
    c, s = trig(np.arange(N), SIGNED)
    gap = np.zeros((64, 128))
    for name, table in (("c", c), ("s", s)):
        parts[name] = (np.concatenate([table, gap], 0), np.concatenate([gap, table], 0))

    def forward_x(which):
        cc, ss = parts["c"][which], parts["s"][which]
        first, second = np.concatenate([cc, -ss], 1), np.concatenate([ss, cc], 1)
        return np.concatenate([first[:128], second[:128], first[128:], second[128:]], 0)

    t["fx"] = np.concatenate([pair_of(forward_x(0)), pair_of(forward_x(1))], 0)
    c, s = trig(SIGNED, np.concatenate(YS))
    t["fy"] = pair_of(
        np.concatenate([np.concatenate([c, s], 1), np.concatenate([-s, c], 1)], 0)
    )
    blocks = []
    for zi in range(3):
        c, s = trig(3 * np.arange(64) + zi, KZ)
        blocks += [np.concatenate([c, -s], 1), np.concatenate([s, c], 1)]
    t["fz"] = pair_of(np.concatenate(blocks, 0))
    u = np.zeros((128, 384), np.float32)
    for zi in range(3):
        for p in range(128):
            u[16 * zi + 8 * (p >= 64) + p % 8, 128 * zi + p] = 1.0
    t["u"] = u.astype(ml_dtypes.bfloat16)
    t["ut"] = np.concatenate([u[:, 128 * zi : 128 * zi + 128].T for zi in range(3)], 0).astype(
        ml_dtypes.bfloat16
    )
    return t


def split(x):
    high = x.astype(BF)
    return high, (x - high.astype(F32)).astype(BF)


def mm(a, b):
    return jnp.dot(a, b, preferred_element_type=F32)


def mm_nt(a, b):
    return lax.dot_general(a, b, (((1,), (1,)), ((), ())), preferred_element_type=F32)


def three(product, a, b):
    return product(a[0], b[0]) + (product(a[0], b[1]) + product(a[1], b[0]))


def iota(shape, dim):
    return lax.broadcasted_iota(jnp.int32, shape, dim)


def masks_sp():
    s, p = iota((64, 128), 0), iota((64, 128), 1)
    ky = jnp.where(p < 64, p, p - 128)
    away = 64 - jnp.abs(ky)
    inside = ky * ky + s * s <= R2
    clash = away * away + (64 - s) * (64 - s) <= R2
    other = (p - 64) * (p - 64) + (64 - s) * (64 - s) <= R2
    return inside & ~clash, inside & clash, other


def line_places(r, s):
    plane, rest = r // 128, r % 128
    ky = 2 * (rest % 64 - 24) + rest // 64
    here = jnp.where(plane == 0, s, 64 - s)
    away = 64 - jnp.abs(ky)
    inside = ky * ky + here * here <= R2
    clash = (away * away + (64 - s) * (64 - s) <= R2) & (plane == 0)
    place = jnp.where(plane == 0, jnp.where(ky < 0, ky + 128, ky), ky + 64)
    main = jnp.where(inside & ~clash, place, -1)
    spare = jnp.where(inside & clash, jnp.where(ky < 0, 8, 0) + (ky + 64) % 8, -1)
    return main, spare


def one_hot(condition):
    return jnp.where(condition, 1.0, 0.0).astype(BF)


def sphere_rows(plane, parity, s):
    m, lane = iota((64, 128), 0), iota((64, 128), 1)
    ky = 2 * (m - 24) + parity
    kz = jnp.where(lane < 64, lane, lane - 128)
    kx = s - 64 * plane
    return ky * ky + kz * kz + kx * kx <= R2


def kernel_z_inverse(psi, wz_in, send, buf, wz, sems):
    s = lax.axis_index("fft")
    copies = []
    for plane in range(2):
        base = 1152 * plane
        for k, (src, dst, rows) in enumerate(((432, 0, 144), (0, 144, 152))):
            copies.append(
                pltpu.make_async_copy(
                    psi.at[pl.ds(base + src, rows)],
                    buf.at[plane, pl.ds(dst, rows)],
                    sems.at[2 * plane + k],
                )
            )
    copies.append(pltpu.make_async_copy(wz_in, wz, sems.at[4]))
    for copy in copies:
        copy.start()
    main, spare = line_places(iota((1, 256), 1), s)
    j = iota((128, 256), 0)
    pack = jnp.concatenate(
        [one_hot(j == main), one_hot((j % 16 == spare) & (j % 64 < 48))], axis=0
    )
    lane = iota((64, 128), 1)
    rows = []
    for copy in copies[:4]:
        copy.wait()
    for plane in range(2):
        lines = [[], []]
        for c in range(2):
            t = [buf[plane, pl.ds(2 * k + c, 64, stride=6), :] for k in range(3)]
            middle = pltpu.roll(t[1], 64, 1)
            even = jnp.where(lane < 64, t[0], middle)
            odd = jnp.where(lane < 64, middle, t[2])
            lines[0].append(jnp.where(sphere_rows(plane, 0, s), even, 0.0))
            lines[1].append(jnp.where(sphere_rows(plane, 1, s), odd, 0.0))
        rows += [jnp.concatenate(lines[0], 1), jnp.concatenate(lines[1], 1)]
    high, low = split(jnp.concatenate(rows, 0))
    packed = (mm(pack, high).astype(BF), mm(pack, low).astype(BF))
    copies[4].wait()
    out = three(mm_nt, (wz[0:384, :], wz[384:768, :]), packed)
    spares = out[0:64, 128:]
    for c in range(2):
        for zi in range(3):
            block = out[(2 * zi + c) * 64 : (2 * zi + c) * 64 + 64]
            send[pl.ds(3 * c + zi, 64, stride=7), :] = block[:, :128]
            spares = jnp.where(lane // 16 == 4 * c + zi, block[:, 128:], spares)
    send[pl.ds(6, 64, stride=7), :] = spares


def tile_rows(tiles):
    return (tiles % 3) * 288 + tiles // 3


def as_column(ids):
    return jnp.broadcast_to(ids.astype(F32), (8, ids.shape[1])).T[:, 0:1].astype(jnp.int32)


def kernel_field(
    recv, ey, ix, u, field, rows_h, rows_l,
):
    main, spare, other = masks_sp()
    spread = []
    for c in range(2):
        got = recv[pl.ds(6, 64, stride=7), :]
        high, low = split(pltpu.roll(got, 64, 1) if c else got)
        spread.append(mm(high, u[...]) + mm(low, u[...]))
    lines = []
    for zi in range(3):
        first, second = [], []
        for c in range(2):
            got = recv[pl.ds(3 * c + zi, 64, stride=7), :]
            extra = spread[c][:, 128 * zi : 128 * zi + 128]
            first.append(jnp.where(main, got, jnp.where(spare, extra, 0.0)))
            second.append(pltpu.roll(jnp.where(other, got, 0.0), 64, 1))
        lines += [jnp.concatenate(first, 1), jnp.concatenate(second, 1)]
    g = three(mm_nt, (ey[0:384, :], ey[384:768, :]), split(jnp.concatenate(lines, 0)))
    out = []
    for parity in range(2):
        a = 96 * parity
        table = [ix[512 * parity + 256 * i : 512 * parity + 256 * i + 256, :] for i in range(2)]
        block = jnp.concatenate(
            [
                jnp.concatenate(
                    [
                        g[a : a + 96, 128 * zi : 128 * zi + 128],
                        g[192 + a : 288 + a, 128 * zi : 128 * zi + 128],
                    ],
                    1,
                )
                for zi in range(3)
            ],
            0,
        )
        out.append(three(mm, split(block), table))
    even, odd = out
    for c in range(2):
        a = 256 * c
        kinds = (
            even[:, a : a + 128],
            even[:, a + 128 : a + 256] + odd[:, a : a + 128],
            odd[:, a + 128 : a + 256],
        )
        for k, tile in enumerate(kinds):
            span = pl.ds(288 * k, 288)
            lanes = pl.ds(128 * c, 128)
            field[span, lanes] = tile
            high, low = split(tile)
            rows_h[span, lanes] = high
            rows_l[span, lanes] = low
    rows_h[864:896, :] = jnp.zeros((32, 256), BF)
    rows_l[864:896, :] = jnp.zeros((32, 256), BF)


def project(quarters, rows_h, rows_l, tile_of, slots, betas, field_rows):
    count = 128 * quarters
    pick = one_hot(as_column(tile_of) == iota((count, 896), 1))
    field_rows[...] = mm(pick, rows_h[...]) + mm(pick, rows_l[...])
    lane = iota((128, 128), 1)
    sums = []
    for k, beta in enumerate(betas):
        total = jnp.zeros((128, 128), F32)
        for j in range(8):
            projector = beta[pl.ds(j, 128, stride=8), :]
            for c in range(2):
                value = field_rows[128 * k : 128 * k + 128, 128 * c : 128 * c + 128] * projector
                total = jnp.where(
                    lane == 8 * c + j, jnp.sum(value, axis=1, keepdims=True), total
                )
        sums.append(total.T[:16])
    high, low = split(jnp.concatenate(sums, 1))
    return mm(high, slots) + mm(low, slots)


def ids_of(betas, row):
    return jnp.concatenate([b[1024 + row : 1025 + row, :] for b in betas], 1).astype(jnp.int32)


def kernel_project(rows_h, rows_l, b0, b1, b2, coef, slots_out, tiles_out, field_rows):
    betas = (b0, b1, b2)
    tile_of = tile_rows(ids_of(betas, 1))
    tiles_out[...] = tile_of
    slots = one_hot(as_column(ids_of(betas, 0)) == iota((384, 256), 1))
    slots_out[...] = slots
    coef[...] = project(3, rows_h, rows_l, tile_of, slots, betas, field_rows)


def kernel_project_last(rows_h, rows_l, dmat, coef_in, b3, near, slots_out, tiles_out, field_rows):
    tile_of = tile_rows(ids_of((b3,), 1))
    tiles_out[...] = tile_of
    slots = one_hot(as_column(ids_of((b3,), 0)) == iota((128, 256), 1))
    slots_out[...] = slots
    coef = coef_in[...] + project(1, rows_h, rows_l, tile_of, slots, (b3,), field_rows)
    coef = jnp.where(iota((16, 256), 1) < 192, coef, 0.0)
    near[0:64, :] = jnp.concatenate([dmat[...], jnp.zeros((64, 64), F32)], 1)
    near[64:80, :] = coef[:, :128]
    near[80:96, :] = coef[:, 128:]


def chip_of(own, other):
    f = lax.axis_index("fft")
    core = f % 2
    own, other = own[...], other[...]
    return (
        core,
        (f // 2) % 2 == 0,
        jnp.where(core == 0, own, other),
        jnp.where(core == 0, other, own),
    )


def kernel_merge(own, other, first, second):
    _, even, a, b = chip_of(own, other)
    low_lane = iota((16, 128), 1) < 64
    turned = pltpu.roll(b[64:80], 64, 1)
    up = jnp.where(low_lane, a[80:96] + turned, pltpu.roll(b[80:96], 64, 1))
    down = jnp.where(low_lane, a[64:80], a[64:80] + turned)
    up = jnp.concatenate([b[0:64], up], 0)
    down = jnp.concatenate([a[0:64], down], 0)
    first[...] = jnp.where(even, up, down)
    second[...] = jnp.where(even, down, up)


def kernel_put(tiles, tiles_last, put):
    tile_of = jnp.concatenate([tiles[...], tiles_last[...]], 1)
    put[...] = one_hot(iota((864, 512), 0) == tile_of)


def kernel_back(
    field, own, other, second, first, slots, slots_last, put, b0, b1, b2, b3,
    vloc_in, fx_in, fy_in, ut_in, send, scr, rows, vloc, fx, fy, ut, sems,
):
    copies = [
        pltpu.make_async_copy(vloc_in.at[:, zi, :], vloc.at[zi], sems.at[zi]) for zi in range(3)
    ] + [
        pltpu.make_async_copy(fx_in, fx, sems.at[3]),
        pltpu.make_async_copy(fy_in, fy, sems.at[4]),
        pltpu.make_async_copy(ut_in, ut, sems.at[5]),
    ]
    for copy in copies:
        copy.start()
    core, even, a, b = chip_of(own, other)
    above = jnp.where(even, first[...], second[...])
    below = jnp.where(even, second[...], first[...])
    low_lane = iota((16, 128), 1) < 64
    turned = pltpu.roll(b[64:80], 64, 1)
    tot = [
        below[64:80] + jnp.where(low_lane, a[64:80], a[64:80] + turned),
        above[64:80] + jnp.where(low_lane, a[80:96] + turned, pltpu.roll(b[80:96], 64, 1)),
    ]
    wide = iota((64, 128), 1) < 64
    coupling = [
        jnp.where(wide, below[0:64], pltpu.roll(a[0:64], 64, 1)),
        jnp.where(wide, b[0:64], pltpu.roll(above[0:64], 64, 1)),
    ]
    for h in range(2):
        for c in range(2):
            coef = tot[h][8 * c : 8 * c + 8, :]
            for j in range(8):
                row = jnp.sum(coupling[h][8 * j : 8 * j + 8, :] * coef, axis=0, keepdims=True)
                scr[8 * c + j : 8 * c + j + 1, 128 * h : 128 * h + 128] = row
    betas = (b0, b1, b2, b3)
    left, right = scr[:, :128], scr[:, 128:]
    left_turned, right_turned = pltpu.roll(left, 64, 1), pltpu.roll(right, 64, 1)
    left = jnp.where(core == 0, left, jnp.where(low_lane, left_turned, right_turned))
    right = jnp.where(low_lane, jnp.where(core == 0, right, right_turned), 0.0)
    high, low = split(jnp.concatenate([left, right], 1))
    weight = jnp.concatenate(
        [mm_nt(hot[...], high) + mm_nt(hot[...], low) for hot in (slots, slots_last)], 0
    )
    high, low = split(weight)
    weight = jnp.concatenate([high, low], 1)
    for k, beta in enumerate(betas):
        span = slice(128 * k, 128 * k + 128)
        terms = jnp.zeros((128, 256), F32)
        for j in range(8):
            wide = one_hot(iota((32, 256), 0) % 16 == 8 * (iota((32, 256), 1) // 128) + j)
            projector = beta[pl.ds(j, 128, stride=8), :]
            terms = terms + mm(weight[span], wide) * jnp.concatenate([projector, projector], 1)
        high, low = split(terms)
        rows[span, 0:256] = high
        rows[span, 256:512] = low
    both = mm(put[...], rows[...])
    nonloc = both[:, :256] + both[:, 256:]
    for copy in copies:
        copy.wait()
    kinds = []
    for k in range(3):
        factor = jnp.concatenate([vloc[zi, pl.ds(k, 96, stride=3), :] for zi in range(3)], 0)
        at = slice(288 * k, 288 * k + 288)
        kinds.append(split(field[at, :] * jnp.concatenate([factor, factor], 1) + nonloc[at, :]))
    g = []
    for parity in range(2):
        table = [fx[1024 * parity + 512 * i : 1024 * parity + 512 * i + 512, :] for i in range(2)]
        lines = [jnp.concatenate([kinds[parity][i], kinds[parity + 1][i]], 1) for i in range(2)]
        g.append(split(three(mm, lines, table)))
    lines = [
        jnp.concatenate(
            [
                jnp.concatenate(
                    [
                        g[parity][i][96 * zi : 96 * zi + 96, 128 * c : 128 * c + 128]
                        for zi in range(3)
                    ],
                    1,
                )
                for c in range(2)
                for parity in range(2)
            ],
            0,
        )
        for i in range(2)
    ]
    h = three(mm, (fy[0:256, :], fy[256:512, :]), lines)
    main, spare, _ = masks_sp()
    spares = [jnp.zeros((64, 128), F32), jnp.zeros((64, 128), F32)]
    for zi in range(3):
        for c in range(2):
            turned = h[128 * c : 128 * c + 128, 128 * zi : 128 * zi + 128].T
            first = turned[:64]
            second = pltpu.roll(turned[64:], 64, 1)
            send[pl.ds(3 * c + zi, 64, stride=7), :] = jnp.where(main, first, second)
            high, low = split(jnp.where(spare, first, 0.0))
            move = ut[128 * zi : 128 * zi + 128, :]
            spares[c] = spares[c] + (mm(high, move) + mm(low, move))
    send[pl.ds(6, 64, stride=7), :] = spares[0] + pltpu.roll(spares[1], 64, 1)


def kernel_z_forward(recv, fz, result, out, sems):
    s = lax.axis_index("fft")
    out[...] = jnp.zeros((1728, 128), F32)
    spans = [(152, 280), (576, 576), (1304, 280), (0, 152), (432, 144), (1152, 152), (1584, 144)]
    copies = [
        pltpu.make_async_copy(out.at[pl.ds(*span)], result.at[pl.ds(*span)], sems.at[k])
        for k, span in enumerate(spans)
    ]
    for copy in copies[:3]:
        copy.start()
    r = iota((256, 1), 0)
    main, spare = line_places(r, s)
    lane = iota((256, 128), 1)
    keep = one_hot(lane == main)
    spares = recv[pl.ds(6, 64, stride=7), :]
    spares = (spares, pltpu.roll(spares, 64, 1))
    highs, lows = [], []
    for zi in range(3):
        unpack = jnp.concatenate(
            [keep, one_hot((lane == spare + 16 * zi) & (spare >= 0))], 1
        )
        lines = jnp.concatenate(
            [
                jnp.concatenate(
                    [
                        recv[pl.ds(3 * c + zi, 64, stride=7), :],
                        spares[c],
                    ],
                    1,
                )
                for c in range(2)
            ],
            0,
        )
        high, low = split(lines)
        columns = mm_nt(unpack, jnp.concatenate([high, low], 0))
        highs.append(columns[:, :128].astype(BF))
        lows.append(columns[:, 128:].astype(BF))
    z = three(
        mm, (jnp.concatenate(highs, 1), jnp.concatenate(lows, 1)), (fz[0:384, :], fz[384:768, :])
    )
    low_lane = iota((64, 128), 1) < 64
    for plane in range(2):
        for c in range(2):
            block = z[128 * plane : 128 * plane + 128, 128 * c : 128 * c + 128]
            even = jnp.where(sphere_rows(plane, 0, s), block[:64], 0.0)
            odd = jnp.where(sphere_rows(plane, 1, s), block[64:], 0.0)
            kinds = (
                jnp.where(low_lane, even, 0.0),
                pltpu.roll(jnp.where(low_lane, odd, even), 64, 1),
                jnp.where(low_lane, 0.0, odd),
            )
            for k, tile in enumerate(kinds):
                at = 1152 * plane + 2 * k + c
                out[pl.ds(at, 25, stride=6), :] = tile[24:49]
                out[pl.ds(at + 432, 24, stride=6), :] = tile[:24]
        copies[3 + 2 * plane].start()
        copies[4 + 2 * plane].start()
    for copy in copies:
        copy.wait()


def call(kernel, name, out_shape, args, scratch=(), anywhere=(), anywhere_out=(), limit=VMEM_LIMIT, cost=None):
    specs = [
        pl.BlockSpec(memory_space=pl.ANY if k in anywhere else pltpu.VMEM)
        for k in range(len(args))
    ]
    shapes = [
        jax.ShapeDtypeStruct(*shape) if isinstance(shape[0], tuple) else jax.ShapeDtypeStruct(shape, F32)
        for shape in out_shape
    ]
    out = pl.pallas_call(
        kernel,
        name=name,
        out_shape=shapes,
        in_specs=specs,
        out_specs=[
            pl.BlockSpec(memory_space=pl.ANY if k in anywhere_out else pltpu.VMEM)
            for k in range(len(shapes))
        ],
        scratch_shapes=list(scratch),
        cost_estimate=cost,
        compiler_params=pltpu.CompilerParams(vmem_limit_bytes=limit),
    )(*args)
    return out


def body(psi_g, vloc, beta, blk_slot, blk_tile, dmat):
    t = {
        name: jnp.asarray(value) for name, value in tables().items()
    }
    psi = psi_g[0].transpose(1, 0, 2).reshape(3, 2, 288, 128).transpose(0, 2, 1, 3)
    psi = psi.reshape(1728, 128)
    def gathered(x):
        return [x] + [
            lax.ppermute(x, "band", [(i, (i + k) % 4) for i in range(4)]) for k in (3, 2, 1)
        ]

    ids = jnp.concatenate([blk_slot[None], blk_tile[None], jnp.zeros((6, 128), jnp.int32)], 0)
    own = jnp.concatenate([beta, ids.astype(F32)[None]], 0).reshape(1032, 128)
    (send,) = call(
        kernel_z_inverse,
        "z_inverse",
        [(448, 128)],
        (psi, t["wz"]),
        [
            pltpu.VMEM((2, 384, 128), F32),
            pltpu.VMEM((768, 256), BF),
            pltpu.SemaphoreType.DMA((5,)),
        ],
        anywhere=(0, 1),
        limit=60 * 1024 * 1024,
    )
    own, send = lax.optimization_barrier((own, send))
    betas = gathered(own)

    def exchange(x):
        x = lax.all_to_all(x.reshape(64, 1, 896), "fft", 0, 0, tiled=True)
        return x.reshape(448, 128)

    recv = exchange(send)
    vloc_tiles = vloc.reshape(3, 288, 128).transpose(1, 0, 2)
    dmat_rows = dmat.transpose(1, 2, 0).reshape(64, 64)
    field, rows_h, rows_l = call(
        kernel_field,
        "field",
        [(864, 256), ((896, 256), BF), ((896, 256), BF)],
        (recv, t["ey"], t["ix"], t["u"]),
    )
    coef, slots, tiles = call(
        kernel_project,
        "project",
        [(16, 256), ((384, 256), BF), ((1, 384), jnp.int32)],
        (rows_h, rows_l, *betas[:3]),
        [pltpu.VMEM((384, 256), F32)],
    )
    near, slots_last, tiles_last = call(
        kernel_project_last,
        "project_last",
        [(96, 128), ((128, 256), BF), ((1, 128), jnp.int32)],
        (rows_h, rows_l, dmat_rows, coef, betas[3]),
        [pltpu.VMEM((128, 256), F32)],
    )
    other = lax.ppermute(near, "fft", [(i, i ^ 1) for i in range(64)])
    first, second = call(kernel_merge, "merge", [(80, 128), (80, 128)], (near, other))
    first = lax.ppermute(first, "fft", [(i, i ^ 2) for i in range(64)])
    second = lax.ppermute(second, "fft", [(i, (((i + 2) % 64) ^ 2) - 2 & 63) for i in range(64)])
    (put,) = call(
        kernel_put,
        "put",
        [((864, 512), BF)],
        (tiles, tiles_last),
        cost=pl.CostEstimate(flops=2000000, bytes_accessed=3000000, transcendentals=0),
    )
    (send,) = call(
        kernel_back,
        "back",
        [(448, 128)],
        (field, near, other, second, first, slots, slots_last, put, *betas, vloc_tiles, t["fx"], t["fy"], t["ut"]),
        [
            pltpu.VMEM((16, 256), F32),
            pltpu.VMEM((512, 512), BF),
            pltpu.VMEM((3, 288, 128), F32),
            pltpu.VMEM((2048, 256), BF),
            pltpu.VMEM((512, 384), BF),
            pltpu.VMEM((384, 128), BF),
            pltpu.SemaphoreType.DMA((6,)),
        ],
        anywhere=(12, 13, 14, 15),
    )
    (out,) = call(kernel_z_forward, "z_forward", [(1728, 128)], (exchange(send), t["fz"]),
        [pltpu.VMEM((1728, 128), F32), pltpu.SemaphoreType.DMA((7,))], anywhere_out=(0,))
    out = out.reshape(3, 288, 2, 128).transpose(0, 2, 1, 3).reshape(3, 2, N * N)
    return out.transpose(1, 0, 2)[None]


def solution(mesh):
    in_specs = (
        P("band", None, "fft", None),
        P("fft", None),
        P(("fft", "band"), None, None),
        P(("fft", "band")),
        P(("fft", "band")),
        P("fft", None, None),
    )
    out_specs = P("band", None, "fft", None)
    return jax.shard_map(body, mesh=mesh, in_specs=in_specs, out_specs=out_specs, check_vma=False)
```

```python
import functools

import jax
import jax.numpy as jnp
import ml_dtypes
import numpy as np
from jax import lax
from jax.experimental import pallas as pl
from jax.experimental.pallas import tpu as pltpu
from jax.sharding import PartitionSpec as P

N = 192
R2 = 48 * 48
BF = jnp.bfloat16
F32 = jnp.float32
VMEM_LIMIT = 48 * 1024 * 1024


def trig(freqs, points):
    angle = 2.0 * np.pi * (np.outer(freqs, points) % N) / N
    return np.cos(angle) / np.sqrt(N), np.sin(angle) / np.sqrt(N)


def pair_of(table):
    table = np.asarray(table, np.float32)
    high = table.astype(ml_dtypes.bfloat16)
    low = (table - high.astype(np.float32)).astype(ml_dtypes.bfloat16)
    return np.concatenate([high, low], 0)


KZ = np.concatenate([np.arange(64), np.arange(128, 192)])
SIGNED = np.concatenate([np.arange(64), np.arange(-64, 0)])
YS = [2 * np.arange(96), 2 * np.arange(96) + 1]


@functools.cache
def tables():
    t = {}
    blocks = []
    for zi in range(3):
        c, s = trig(3 * np.arange(64) + zi, KZ)
        blocks += [np.concatenate([c, -s], 1), np.concatenate([s, c], 1)]
    t["wz"] = pair_of(np.concatenate(blocks, 0))
    c, s = trig(np.concatenate(YS), SIGNED)
    t["ey"] = pair_of(
        np.concatenate([np.concatenate([c, -s], 1), np.concatenate([s, c], 1)], 0)
    )
    c, s = trig(SIGNED, np.arange(N))
    gap = np.zeros((128, 64))
    even = [np.concatenate([v, gap], 1) for v in (c, s, -s, c)]
    odd = [np.concatenate([gap, v], 1) for v in (c, s, -s, c)]
    t["ix"] = np.concatenate(
        [
            pair_of(np.block([[even[0], even[1]], [even[2], even[3]]])),
            pair_of(np.block([[odd[0], odd[1]], [odd[2], odd[3]]])),
        ],
        0,
    )
    parts = {}
    c, s = trig(np.arange(N), SIGNED)
    gap = np.zeros((64, 128))
    for name, table in (("c", c), ("s", s)):
        parts[name] = (np.concatenate([table, gap], 0), np.concatenate([gap, table], 0))

    def forward_x(which):
        cc, ss = parts["c"][which], parts["s"][which]
        first, second = np.concatenate([cc, -ss], 1), np.concatenate([ss, cc], 1)
        return np.concatenate([first[:128], second[:128], first[128:], second[128:]], 0)

    t["fx"] = np.concatenate([pair_of(forward_x(0)), pair_of(forward_x(1))], 0)
    c, s = trig(SIGNED, np.concatenate(YS))
    t["fy"] = pair_of(
        np.concatenate([np.concatenate([c, s], 1), np.concatenate([-s, c], 1)], 0)
    )
    blocks = []
    for zi in range(3):
        c, s = trig(3 * np.arange(64) + zi, KZ)
        blocks += [np.concatenate([c, -s], 1), np.concatenate([s, c], 1)]
    t["fz"] = pair_of(np.concatenate(blocks, 0))
    u = np.zeros((128, 384), np.float32)
    for zi in range(3):
        for p in range(128):
            u[16 * zi + 8 * (p >= 64) + p % 8, 128 * zi + p] = 1.0
    t["u"] = u.astype(ml_dtypes.bfloat16)
    t["ut"] = np.concatenate([u[:, 128 * zi : 128 * zi + 128].T for zi in range(3)], 0).astype(
        ml_dtypes.bfloat16
    )
    return t


def split(x):
    high = x.astype(BF)
    return high, (x - high.astype(F32)).astype(BF)


def mm(a, b):
    return jnp.dot(a, b, preferred_element_type=F32)


def mm_nt(a, b):
    return lax.dot_general(a, b, (((1,), (1,)), ((), ())), preferred_element_type=F32)


def three(product, a, b):
    return product(a[0], b[0]) + (product(a[0], b[1]) + product(a[1], b[0]))


def iota(shape, dim):
    return lax.broadcasted_iota(jnp.int32, shape, dim)


def masks_sp():
    s, p = iota((64, 128), 0), iota((64, 128), 1)
    ky = jnp.where(p < 64, p, p - 128)
    away = 64 - jnp.abs(ky)
    inside = ky * ky + s * s <= R2
    clash = away * away + (64 - s) * (64 - s) <= R2
    other = (p - 64) * (p - 64) + (64 - s) * (64 - s) <= R2
    return inside & ~clash, inside & clash, other


def line_places(r, s):
    plane, rest = r // 128, r % 128
    ky = 2 * (rest % 64 - 24) + rest // 64
    here = jnp.where(plane == 0, s, 64 - s)
    away = 64 - jnp.abs(ky)
    inside = ky * ky + here * here <= R2
    clash = (away * away + (64 - s) * (64 - s) <= R2) & (plane == 0)
    place = jnp.where(plane == 0, jnp.where(ky < 0, ky + 128, ky), ky + 64)
    main = jnp.where(inside & ~clash, place, -1)
    spare = jnp.where(inside & clash, jnp.where(ky < 0, 8, 0) + (ky + 64) % 8, -1)
    return main, spare


def one_hot(condition):
    return jnp.where(condition, 1.0, 0.0).astype(BF)


def sphere_rows(plane, parity, s):
    m, lane = iota((64, 128), 0), iota((64, 128), 1)
    ky = 2 * (m - 24) + parity
    kz = jnp.where(lane < 64, lane, lane - 128)
    kx = s - 64 * plane
    return ky * ky + kz * kz + kx * kx <= R2


def kernel_z_inverse(psi, wz, send):
    s = lax.axis_index("fft")
    main, spare = line_places(iota((1, 256), 1), s)
    j = iota((128, 256), 0)
    pack = jnp.concatenate(
        [one_hot(j == main), one_hot((j % 16 == spare) & (j % 64 < 48))], axis=0
    )
    lane = iota((64, 128), 1)
    rows = []
    for plane in range(2):
        lines = [[], []]
        for c in range(2):
            at = 1152 * plane + c
            t = [
                jnp.concatenate(
                    [
                        psi[pl.ds(at + 432 + 2 * k, 24, stride=6), :],
                        psi[pl.ds(at + 2 * k, 40, stride=6), :],
                    ],
                    0,
                )
                for k in range(3)
            ]
            middle = pltpu.roll(t[1], 64, 1)
            even = jnp.where(lane < 64, t[0], middle)
            odd = jnp.where(lane < 64, middle, t[2])
            lines[0].append(jnp.where(sphere_rows(plane, 0, s), even, 0.0))
            lines[1].append(jnp.where(sphere_rows(plane, 1, s), odd, 0.0))
        rows += [jnp.concatenate(lines[0], 1), jnp.concatenate(lines[1], 1)]
    high, low = split(jnp.concatenate(rows, 0))
    packed = (mm(pack, high).astype(BF), mm(pack, low).astype(BF))
    out = three(mm_nt, (wz[0:384, :], wz[384:768, :]), packed)
    spares = out[0:64, 128:]
    for c in range(2):
        for zi in range(3):
            block = out[(2 * zi + c) * 64 : (2 * zi + c) * 64 + 64]
            send[pl.ds(3 * c + zi, 64, stride=7), :] = block[:, :128]
            spares = jnp.where(lane // 16 == 4 * c + zi, block[:, 128:], spares)
    send[pl.ds(6, 64, stride=7), :] = spares


def tile_rows(tiles):
    return (tiles % 3) * 288 + tiles // 3


def as_column(ids):
    return jnp.broadcast_to(ids.astype(F32), (8, ids.shape[1])).T[:, 0:1].astype(jnp.int32)


def kernel_field(
    recv, ey, ix, u, field, rows_h, rows_l,
):
    main, spare, other = masks_sp()
    spread = []
    for c in range(2):
        got = recv[pl.ds(6, 64, stride=7), :]
        high, low = split(pltpu.roll(got, 64, 1) if c else got)
        spread.append(mm(high, u[...]) + mm(low, u[...]))
    lines = []
    for zi in range(3):
        first, second = [], []
        for c in range(2):
            got = recv[pl.ds(3 * c + zi, 64, stride=7), :]
            extra = spread[c][:, 128 * zi : 128 * zi + 128]
            first.append(jnp.where(main, got, jnp.where(spare, extra, 0.0)))
            second.append(pltpu.roll(jnp.where(other, got, 0.0), 64, 1))
        lines += [jnp.concatenate(first, 1), jnp.concatenate(second, 1)]
    g = three(mm_nt, (ey[0:384, :], ey[384:768, :]), split(jnp.concatenate(lines, 0)))
    out = []
    for parity in range(2):
        a = 96 * parity
        table = [ix[512 * parity + 256 * i : 512 * parity + 256 * i + 256, :] for i in range(2)]
        block = jnp.concatenate(
            [
                jnp.concatenate(
                    [
                        g[a : a + 96, 128 * zi : 128 * zi + 128],
                        g[192 + a : 288 + a, 128 * zi : 128 * zi + 128],
                    ],
                    1,
                )
                for zi in range(3)
            ],
            0,
        )
        out.append(three(mm, split(block), table))
    even, odd = out
    for c in range(2):
        a = 256 * c
        kinds = (
            even[:, a : a + 128],
            even[:, a + 128 : a + 256] + odd[:, a : a + 128],
            odd[:, a + 128 : a + 256],
        )
        for k, tile in enumerate(kinds):
            span = pl.ds(288 * k, 288)
            lanes = pl.ds(128 * c, 128)
            field[span, lanes] = tile
            high, low = split(tile)
            rows_h[span, lanes] = high
            rows_l[span, lanes] = low
    rows_h[864:896, :] = jnp.zeros((32, 256), BF)
    rows_l[864:896, :] = jnp.zeros((32, 256), BF)


def project(quarters, rows_h, rows_l, tile_of, slots, betas, field_rows):
    count = 128 * quarters
    pick = one_hot(as_column(tile_of) == iota((count, 896), 1))
    field_rows[...] = mm(pick, rows_h[...]) + mm(pick, rows_l[...])
    lane = iota((128, 128), 1)
    sums = []
    for k, beta in enumerate(betas):
        total = jnp.zeros((128, 128), F32)
        for j in range(8):
            projector = beta[pl.ds(j, 128, stride=8), :]
            for c in range(2):
                value = field_rows[128 * k : 128 * k + 128, 128 * c : 128 * c + 128] * projector
                total = jnp.where(
                    lane == 8 * c + j, jnp.sum(value, axis=1, keepdims=True), total
                )
        sums.append(total.T[:16])
    high, low = split(jnp.concatenate(sums, 1))
    return mm(high, slots) + mm(low, slots)


def ids_of(betas, row):
    return jnp.concatenate([b[1024 + row : 1025 + row, :] for b in betas], 1).astype(jnp.int32)


def kernel_project(rows_h, rows_l, b0, b1, b2, coef, slots_out, tiles_out, field_rows):
    betas = (b0, b1, b2)
    tile_of = tile_rows(ids_of(betas, 1))
    tiles_out[...] = tile_of
    slots = one_hot(as_column(ids_of(betas, 0)) == iota((384, 256), 1))
    slots_out[...] = slots
    coef[...] = project(3, rows_h, rows_l, tile_of, slots, betas, field_rows)


def kernel_project_last(rows_h, rows_l, dmat, coef_in, b3, near, slots_out, tiles_out, field_rows):
    tile_of = tile_rows(ids_of((b3,), 1))
    tiles_out[...] = tile_of
    slots = one_hot(as_column(ids_of((b3,), 0)) == iota((128, 256), 1))
    slots_out[...] = slots
    coef = coef_in[...] + project(1, rows_h, rows_l, tile_of, slots, (b3,), field_rows)
    coef = jnp.where(iota((16, 256), 1) < 192, coef, 0.0)
    near[0:64, :] = jnp.concatenate([dmat[...], jnp.zeros((64, 64), F32)], 1)
    near[64:80, :] = coef[:, :128]
    near[80:96, :] = coef[:, 128:]


def chip_of(own, other):
    f = lax.axis_index("fft")
    core = f % 2
    own, other = own[...], other[...]
    return (
        core,
        (f // 2) % 2 == 0,
        jnp.where(core == 0, own, other),
        jnp.where(core == 0, other, own),
    )


def kernel_merge(own, other, first, second):
    _, even, a, b = chip_of(own, other)
    low_lane = iota((16, 128), 1) < 64
    turned = pltpu.roll(b[64:80], 64, 1)
    up = jnp.where(low_lane, a[80:96] + turned, pltpu.roll(b[80:96], 64, 1))
    down = jnp.where(low_lane, a[64:80], a[64:80] + turned)
    up = jnp.concatenate([b[0:64], up], 0)
    down = jnp.concatenate([a[0:64], down], 0)
    first[...] = jnp.where(even, up, down)
    second[...] = jnp.where(even, down, up)


def kernel_put(tiles, tiles_last, put):
    tile_of = jnp.concatenate([tiles[...], tiles_last[...]], 1)
    put[...] = one_hot(iota((864, 512), 0) == tile_of)


def kernel_back(
    field, own, other, second, first, slots, slots_last, put, b0, b1, b2, b3,
    vloc_in, fx_in, fy_in, ut_in, send, scr, rows, vloc, fx, fy, ut, sems,
):
    copies = [
        pltpu.make_async_copy(vloc_in.at[:, zi, :], vloc.at[zi], sems.at[zi]) for zi in range(3)
    ] + [
        pltpu.make_async_copy(fx_in, fx, sems.at[3]),
        pltpu.make_async_copy(fy_in, fy, sems.at[4]),
        pltpu.make_async_copy(ut_in, ut, sems.at[5]),
    ]
    for copy in copies:
        copy.start()
    core, even, a, b = chip_of(own, other)
    above = jnp.where(even, first[...], second[...])
    below = jnp.where(even, second[...], first[...])
    low_lane = iota((16, 128), 1) < 64
    turned = pltpu.roll(b[64:80], 64, 1)
    tot = [
        below[64:80] + jnp.where(low_lane, a[64:80], a[64:80] + turned),
        above[64:80] + jnp.where(low_lane, a[80:96] + turned, pltpu.roll(b[80:96], 64, 1)),
    ]
    wide = iota((64, 128), 1) < 64
    coupling = [
        jnp.where(wide, below[0:64], pltpu.roll(a[0:64], 64, 1)),
        jnp.where(wide, b[0:64], pltpu.roll(above[0:64], 64, 1)),
    ]
    for h in range(2):
        for c in range(2):
            coef = tot[h][8 * c : 8 * c + 8, :]
            for j in range(8):
                row = jnp.sum(coupling[h][8 * j : 8 * j + 8, :] * coef, axis=0, keepdims=True)
                scr[8 * c + j : 8 * c + j + 1, 128 * h : 128 * h + 128] = row
    betas = (b0, b1, b2, b3)
    left, right = scr[:, :128], scr[:, 128:]
    left_turned, right_turned = pltpu.roll(left, 64, 1), pltpu.roll(right, 64, 1)
    left = jnp.where(core == 0, left, jnp.where(low_lane, left_turned, right_turned))
    right = jnp.where(low_lane, jnp.where(core == 0, right, right_turned), 0.0)
    high, low = split(jnp.concatenate([left, right], 1))
    weight = jnp.concatenate(
        [mm_nt(hot[...], high) + mm_nt(hot[...], low) for hot in (slots, slots_last)], 0
    )
    high, low = split(weight)
    weight = jnp.concatenate([high, low], 1)
    for k, beta in enumerate(betas):
        span = slice(128 * k, 128 * k + 128)
        terms = jnp.zeros((128, 256), F32)
        for j in range(8):
            wide = one_hot(iota((32, 256), 0) % 16 == 8 * (iota((32, 256), 1) // 128) + j)
            projector = beta[pl.ds(j, 128, stride=8), :]
            terms = terms + mm(weight[span], wide) * jnp.concatenate([projector, projector], 1)
        high, low = split(terms)
        rows[span, 0:256] = high
        rows[span, 256:512] = low
    both = mm(put[...], rows[...])
    nonloc = both[:, :256] + both[:, 256:]
    for copy in copies:
        copy.wait()
    kinds = []
    for k in range(3):
        factor = jnp.concatenate([vloc[zi, pl.ds(k, 96, stride=3), :] for zi in range(3)], 0)
        at = slice(288 * k, 288 * k + 288)
        kinds.append(split(field[at, :] * jnp.concatenate([factor, factor], 1) + nonloc[at, :]))
    g = []
    for parity in range(2):
        table = [fx[1024 * parity + 512 * i : 1024 * parity + 512 * i + 512, :] for i in range(2)]
        lines = [jnp.concatenate([kinds[parity][i], kinds[parity + 1][i]], 1) for i in range(2)]
        g.append(split(three(mm, lines, table)))
    lines = [
        jnp.concatenate(
            [
                jnp.concatenate(
                    [
                        g[parity][i][96 * zi : 96 * zi + 96, 128 * c : 128 * c + 128]
                        for zi in range(3)
                    ],
                    1,
                )
                for c in range(2)
                for parity in range(2)
            ],
            0,
        )
        for i in range(2)
    ]
    h = three(mm, (fy[0:256, :], fy[256:512, :]), lines)
    main, spare, _ = masks_sp()
    spares = [jnp.zeros((64, 128), F32), jnp.zeros((64, 128), F32)]
    for zi in range(3):
        for c in range(2):
            turned = h[128 * c : 128 * c + 128, 128 * zi : 128 * zi + 128].T
            first = turned[:64]
            second = pltpu.roll(turned[64:], 64, 1)
            send[pl.ds(3 * c + zi, 64, stride=7), :] = jnp.where(main, first, second)
            high, low = split(jnp.where(spare, first, 0.0))
            move = ut[128 * zi : 128 * zi + 128, :]
            spares[c] = spares[c] + (mm(high, move) + mm(low, move))
    send[pl.ds(6, 64, stride=7), :] = spares[0] + pltpu.roll(spares[1], 64, 1)


def kernel_z_forward(recv, fz, result, out, sems):
    s = lax.axis_index("fft")
    out[...] = jnp.zeros((1728, 128), F32)
    spans = [(152, 280), (576, 576), (1304, 280), (0, 152), (432, 144), (1152, 152), (1584, 144)]
    copies = [
        pltpu.make_async_copy(out.at[pl.ds(*span)], result.at[pl.ds(*span)], sems.at[k])
        for k, span in enumerate(spans)
    ]
    for copy in copies[:3]:
        copy.start()
    r = iota((256, 1), 0)
    main, spare = line_places(r, s)
    lane = iota((256, 128), 1)
    keep = one_hot(lane == main)
    spares = recv[pl.ds(6, 64, stride=7), :]
    spares = (spares, pltpu.roll(spares, 64, 1))
    highs, lows = [], []
    for zi in range(3):
        unpack = jnp.concatenate(
            [keep, one_hot((lane == spare + 16 * zi) & (spare >= 0))], 1
        )
        lines = jnp.concatenate(
            [
                jnp.concatenate(
                    [
                        recv[pl.ds(3 * c + zi, 64, stride=7), :],
                        spares[c],
                    ],
                    1,
                )
                for c in range(2)
            ],
            0,
        )
        high, low = split(lines)
        columns = mm_nt(unpack, jnp.concatenate([high, low], 0))
        highs.append(columns[:, :128].astype(BF))
        lows.append(columns[:, 128:].astype(BF))
    z = three(
        mm, (jnp.concatenate(highs, 1), jnp.concatenate(lows, 1)), (fz[0:384, :], fz[384:768, :])
    )
    low_lane = iota((64, 128), 1) < 64
    for plane in range(2):
        for c in range(2):
            block = z[128 * plane : 128 * plane + 128, 128 * c : 128 * c + 128]
            even = jnp.where(sphere_rows(plane, 0, s), block[:64], 0.0)
            odd = jnp.where(sphere_rows(plane, 1, s), block[64:], 0.0)
            kinds = (
                jnp.where(low_lane, even, 0.0),
                pltpu.roll(jnp.where(low_lane, odd, even), 64, 1),
                jnp.where(low_lane, 0.0, odd),
            )
            for k, tile in enumerate(kinds):
                at = 1152 * plane + 2 * k + c
                out[pl.ds(at, 25, stride=6), :] = tile[24:49]
                out[pl.ds(at + 432, 24, stride=6), :] = tile[:24]
        copies[3 + 2 * plane].start()
        copies[4 + 2 * plane].start()
    for copy in copies:
        copy.wait()


def call(kernel, name, out_shape, args, scratch=(), anywhere=(), anywhere_out=(), limit=VMEM_LIMIT, cost=None):
    specs = [
        pl.BlockSpec(memory_space=pl.ANY if k in anywhere else pltpu.VMEM)
        for k in range(len(args))
    ]
    shapes = [
        jax.ShapeDtypeStruct(*shape) if isinstance(shape[0], tuple) else jax.ShapeDtypeStruct(shape, F32)
        for shape in out_shape
    ]
    out = pl.pallas_call(
        kernel,
        name=name,
        out_shape=shapes,
        in_specs=specs,
        out_specs=[
            pl.BlockSpec(memory_space=pl.ANY if k in anywhere_out else pltpu.VMEM)
            for k in range(len(shapes))
        ],
        scratch_shapes=list(scratch),
        cost_estimate=cost,
        compiler_params=pltpu.CompilerParams(vmem_limit_bytes=limit),
    )(*args)
    return out


def body(psi_g, vloc, beta, blk_slot, blk_tile, dmat):
    t = {
        name: jnp.asarray(value) for name, value in tables().items()
    }
    psi = psi_g[0].transpose(1, 0, 2).reshape(3, 2, 288, 128).transpose(0, 2, 1, 3)
    psi = psi.reshape(1728, 128)
    def gathered(x):
        return [x] + [
            lax.ppermute(x, "band", [(i, (i + k) % 4) for i in range(4)]) for k in (3, 2, 1)
        ]

    ids = jnp.concatenate([blk_slot[None], blk_tile[None], jnp.zeros((6, 128), jnp.int32)], 0)
    own = jnp.concatenate([beta, ids.astype(F32)[None]], 0).reshape(1032, 128)
    (send,) = call(kernel_z_inverse, "z_inverse", [(448, 128)], (psi, t["wz"]))
    betas = gathered(own)

    def exchange(x):
        x = lax.all_to_all(x.reshape(64, 1, 896), "fft", 0, 0, tiled=True)
        return x.reshape(448, 128)

    recv = exchange(send)
    vloc_tiles = vloc.reshape(3, 288, 128).transpose(1, 0, 2)
    dmat_rows = dmat.transpose(1, 2, 0).reshape(64, 64)
    field, rows_h, rows_l = call(
        kernel_field,
        "field",
        [(864, 256), ((896, 256), BF), ((896, 256), BF)],
        (recv, t["ey"], t["ix"], t["u"]),
    )
    coef, slots, tiles = call(
        kernel_project,
        "project",
        [(16, 256), ((384, 256), BF), ((1, 384), jnp.int32)],
        (rows_h, rows_l, *betas[:3]),
        [pltpu.VMEM((384, 256), F32)],
    )
    near, slots_last, tiles_last = call(
        kernel_project_last,
        "project_last",
        [(96, 128), ((128, 256), BF), ((1, 128), jnp.int32)],
        (rows_h, rows_l, dmat_rows, coef, betas[3]),
        [pltpu.VMEM((128, 256), F32)],
    )
    other = lax.ppermute(near, "fft", [(i, i ^ 1) for i in range(64)])
    first, second = call(kernel_merge, "merge", [(80, 128), (80, 128)], (near, other))
    first = lax.ppermute(first, "fft", [(i, i ^ 2) for i in range(64)])
    second = lax.ppermute(second, "fft", [(i, (((i + 2) % 64) ^ 2) - 2 & 63) for i in range(64)])
    (put,) = call(
        kernel_put,
        "put",
        [((864, 512), BF)],
        (tiles, tiles_last),
        cost=pl.CostEstimate(flops=2000000, bytes_accessed=3000000, transcendentals=0),
    )
    (send,) = call(
        kernel_back,
        "back",
        [(448, 128)],
        (field, near, other, second, first, slots, slots_last, put, *betas, vloc_tiles, t["fx"], t["fy"], t["ut"]),
        [
            pltpu.VMEM((16, 256), F32),
            pltpu.VMEM((512, 512), BF),
            pltpu.VMEM((3, 288, 128), F32),
            pltpu.VMEM((2048, 256), BF),
            pltpu.VMEM((512, 384), BF),
            pltpu.VMEM((384, 128), BF),
            pltpu.SemaphoreType.DMA((6,)),
        ],
        anywhere=(12, 13, 14, 15),
    )
    (out,) = call(kernel_z_forward, "z_forward", [(1728, 128)], (exchange(send), t["fz"]),
        [pltpu.VMEM((1728, 128), F32), pltpu.SemaphoreType.DMA((7,))], anywhere_out=(0,))
    out = out.reshape(3, 288, 2, 128).transpose(0, 2, 1, 3).reshape(3, 2, N * N)
    return out.transpose(1, 0, 2)[None]


def solution(mesh):
    in_specs = (
        P("band", None, "fft", None),
        P("fft", None),
        P(("fft", "band"), None, None),
        P(("fft", "band")),
        P(("fft", "band")),
        P("fft", None, None),
    )
    out_specs = P("band", None, "fft", None)
    return jax.shard_map(body, mesh=mesh, in_specs=in_specs, out_specs=out_specs, check_vma=False)
```

```python
import functools

import jax
import jax.numpy as jnp
import ml_dtypes
import numpy as np
from jax import lax
from jax.experimental import pallas as pl
from jax.experimental.pallas import tpu as pltpu
from jax.sharding import PartitionSpec as P

N = 192
R2 = 48 * 48
BF = jnp.bfloat16
F32 = jnp.float32
VMEM_LIMIT = 32 * 1024 * 1024


def trig(freqs, points):
    angle = 2.0 * np.pi * (np.outer(freqs, points) % N) / N
    return np.cos(angle) / np.sqrt(N), np.sin(angle) / np.sqrt(N)


def pair_of(table):
    table = np.asarray(table, np.float32)
    high = table.astype(ml_dtypes.bfloat16)
    low = (table - high.astype(np.float32)).astype(ml_dtypes.bfloat16)
    return np.concatenate([high, low], 0)


KZ = np.concatenate([np.arange(64), np.arange(128, 192)])
SIGNED = np.concatenate([np.arange(64), np.arange(-64, 0)])
YS = [2 * np.arange(96), 2 * np.arange(96) + 1]


@functools.cache
def tables():
    t = {}
    blocks = []
    for zi in range(3):
        c, s = trig(3 * np.arange(64) + zi, KZ)
        blocks += [np.concatenate([c, -s], 1), np.concatenate([s, c], 1)]
    t["wz"] = pair_of(np.concatenate(blocks, 0))
    c, s = trig(np.concatenate(YS), SIGNED)
    t["ey"] = pair_of(
        np.concatenate([np.concatenate([c, -s], 1), np.concatenate([s, c], 1)], 0)
    )
    c, s = trig(SIGNED, np.arange(N))
    gap = np.zeros((128, 64))
    even = [np.concatenate([v, gap], 1) for v in (c, s, -s, c)]
    odd = [np.concatenate([gap, v], 1) for v in (c, s, -s, c)]
    t["ix"] = np.concatenate(
        [
            pair_of(np.block([[even[0], even[1]], [even[2], even[3]]])),
            pair_of(np.block([[odd[0], odd[1]], [odd[2], odd[3]]])),
        ],
        0,
    )
    parts = {}
    c, s = trig(np.arange(N), SIGNED)
    gap = np.zeros((64, 128))
    for name, table in (("c", c), ("s", s)):
        parts[name] = (np.concatenate([table, gap], 0), np.concatenate([gap, table], 0))

    def forward_x(which):
        cc, ss = parts["c"][which], parts["s"][which]
        first, second = np.concatenate([cc, -ss], 1), np.concatenate([ss, cc], 1)
        return np.concatenate([first[:128], second[:128], first[128:], second[128:]], 0)

    t["fx"] = np.concatenate([pair_of(forward_x(0)), pair_of(forward_x(1))], 0)
    c, s = trig(SIGNED, np.concatenate(YS))
    t["fy"] = pair_of(
        np.concatenate([np.concatenate([c, s], 1), np.concatenate([-s, c], 1)], 0)
    )
    blocks = []
    for zi in range(3):
        c, s = trig(3 * np.arange(64) + zi, KZ)
        blocks += [np.concatenate([c, -s], 1), np.concatenate([s, c], 1)]
    t["fz"] = pair_of(np.concatenate(blocks, 0))
    u = np.zeros((128, 384), np.float32)
    for zi in range(3):
        for p in range(128):
            u[16 * zi + 8 * (p >= 64) + p % 8, 128 * zi + p] = 1.0
    t["u"] = u.astype(ml_dtypes.bfloat16)
    t["ut"] = np.concatenate([u[:, 128 * zi : 128 * zi + 128].T for zi in range(3)], 0).astype(
        ml_dtypes.bfloat16
    )
    return t


def split(x):
    high = x.astype(BF)
    return high, (x - high.astype(F32)).astype(BF)


def mm(a, b):
    return jnp.dot(a, b, preferred_element_type=F32)


def mm_nt(a, b):
    return lax.dot_general(a, b, (((1,), (1,)), ((), ())), preferred_element_type=F32)


def three(product, a, b):
    return product(a[0], b[0]) + (product(a[0], b[1]) + product(a[1], b[0]))


def iota(shape, dim):
    return lax.broadcasted_iota(jnp.int32, shape, dim)


def masks_sp():
    s, p = iota((64, 128), 0), iota((64, 128), 1)
    ky = jnp.where(p < 64, p, p - 128)
    away = 64 - jnp.abs(ky)
    inside = ky * ky + s * s <= R2
    clash = away * away + (64 - s) * (64 - s) <= R2
    other = (p - 64) * (p - 64) + (64 - s) * (64 - s) <= R2
    return inside & ~clash, inside & clash, other


def line_places(r, s):
    plane, rest = r // 128, r % 128
    ky = 2 * (rest % 64 - 24) + rest // 64
    here = jnp.where(plane == 0, s, 64 - s)
    away = 64 - jnp.abs(ky)
    inside = ky * ky + here * here <= R2
    clash = (away * away + (64 - s) * (64 - s) <= R2) & (plane == 0)
    place = jnp.where(plane == 0, jnp.where(ky < 0, ky + 128, ky), ky + 64)
    main = jnp.where(inside & ~clash, place, -1)
    spare = jnp.where(inside & clash, jnp.where(ky < 0, 8, 0) + (ky + 64) % 8, -1)
    return main, spare


def one_hot(condition):
    return jnp.where(condition, 1.0, 0.0).astype(BF)


def sphere_rows(plane, parity, s):
    m, lane = iota((64, 128), 0), iota((64, 128), 1)
    ky = 2 * (m - 24) + parity
    kz = jnp.where(lane < 64, lane, lane - 128)
    kx = s - 64 * plane
    return ky * ky + kz * kz + kx * kx <= R2


def kernel_z_inverse(psi, wz, send):
    s = lax.axis_index("fft")
    main, spare = line_places(iota((1, 256), 1), s)
    j = iota((128, 256), 0)
    pack = jnp.concatenate(
        [one_hot(j == main), one_hot((j % 16 == spare) & (j % 64 < 48))], axis=0
    )
    lane = iota((64, 128), 1)
    rows = []
    for plane in range(2):
        lines = [[], []]
        for c in range(2):
            at = 1152 * plane + c
            t = [
                jnp.concatenate(
                    [
                        psi[pl.ds(at + 432 + 2 * k, 24, stride=6), :],
                        psi[pl.ds(at + 2 * k, 40, stride=6), :],
                    ],
                    0,
                )
                for k in range(3)
            ]
            middle = pltpu.roll(t[1], 64, 1)
            even = jnp.where(lane < 64, t[0], middle)
            odd = jnp.where(lane < 64, middle, t[2])
            lines[0].append(jnp.where(sphere_rows(plane, 0, s), even, 0.0))
            lines[1].append(jnp.where(sphere_rows(plane, 1, s), odd, 0.0))
        rows += [jnp.concatenate(lines[0], 1), jnp.concatenate(lines[1], 1)]
    high, low = split(jnp.concatenate(rows, 0))
    packed = (mm(pack, high).astype(BF), mm(pack, low).astype(BF))
    out = three(mm_nt, (wz[0:384, :], wz[384:768, :]), packed)
    spares = out[0:64, 128:]
    for c in range(2):
        for zi in range(3):
            block = out[(2 * zi + c) * 64 : (2 * zi + c) * 64 + 64]
            send[pl.ds(3 * c + zi, 64, stride=7), :] = block[:, :128]
            spares = jnp.where(lane // 16 == 4 * c + zi, block[:, 128:], spares)
    send[pl.ds(6, 64, stride=7), :] = spares


def tile_rows(tiles):
    return (tiles % 3) * 288 + tiles // 3


def as_column(ids):
    return jnp.broadcast_to(ids.astype(F32), (8, ids.shape[1])).T[:, 0:1].astype(jnp.int32)


def kernel_field(
    recv, ey, ix, u, field, rows_h, rows_l,
):
    main, spare, other = masks_sp()
    spread = []
    for c in range(2):
        got = recv[pl.ds(6, 64, stride=7), :]
        high, low = split(pltpu.roll(got, 64, 1) if c else got)
        spread.append(mm(high, u[...]) + mm(low, u[...]))
    lines = []
    for zi in range(3):
        first, second = [], []
        for c in range(2):
            got = recv[pl.ds(3 * c + zi, 64, stride=7), :]
            extra = spread[c][:, 128 * zi : 128 * zi + 128]
            first.append(jnp.where(main, got, jnp.where(spare, extra, 0.0)))
            second.append(pltpu.roll(jnp.where(other, got, 0.0), 64, 1))
        lines += [jnp.concatenate(first, 1), jnp.concatenate(second, 1)]
    g = three(mm_nt, (ey[0:384, :], ey[384:768, :]), split(jnp.concatenate(lines, 0)))
    out = []
    for parity in range(2):
        a = 96 * parity
        table = [ix[512 * parity + 256 * i : 512 * parity + 256 * i + 256, :] for i in range(2)]
        block = jnp.concatenate(
            [
                jnp.concatenate(
                    [
                        g[a : a + 96, 128 * zi : 128 * zi + 128],
                        g[192 + a : 288 + a, 128 * zi : 128 * zi + 128],
                    ],
                    1,
                )
                for zi in range(3)
            ],
            0,
        )
        out.append(three(mm, split(block), table))
    even, odd = out
    for c in range(2):
        a = 256 * c
        kinds = (
            even[:, a : a + 128],
            even[:, a + 128 : a + 256] + odd[:, a : a + 128],
            odd[:, a + 128 : a + 256],
        )
        for k, tile in enumerate(kinds):
            span = pl.ds(288 * k, 288)
            lanes = pl.ds(128 * c, 128)
            field[span, lanes] = tile
            high, low = split(tile)
            rows_h[span, lanes] = high
            rows_l[span, lanes] = low
    rows_h[864:896, :] = jnp.zeros((32, 256), BF)
    rows_l[864:896, :] = jnp.zeros((32, 256), BF)


def project(quarters, rows_h, rows_l, tile_of, slots, betas, field_rows):
    count = 128 * quarters
    pick = one_hot(as_column(tile_of) == iota((count, 896), 1))
    field_rows[...] = mm(pick, rows_h[...]) + mm(pick, rows_l[...])
    lane = iota((128, 128), 1)
    sums = []
    for k, beta in enumerate(betas):
        total = jnp.zeros((128, 128), F32)
        for j in range(8):
            projector = beta[pl.ds(j, 128, stride=8), :]
            for c in range(2):
                value = field_rows[128 * k : 128 * k + 128, 128 * c : 128 * c + 128] * projector
                total = jnp.where(
                    lane == 8 * c + j, jnp.sum(value, axis=1, keepdims=True), total
                )
        sums.append(total.T[:16])
    high, low = split(jnp.concatenate(sums, 1))
    return mm(high, slots) + mm(low, slots)


def ids_of(betas, row):
    return jnp.concatenate([b[1024 + row : 1025 + row, :] for b in betas], 1).astype(jnp.int32)


def kernel_project(rows_h, rows_l, b0, b1, b2, coef, slots_out, tiles_out, field_rows):
    betas = (b0, b1, b2)
    tile_of = tile_rows(ids_of(betas, 1))
    tiles_out[...] = tile_of
    slots = one_hot(as_column(ids_of(betas, 0)) == iota((384, 256), 1))
    slots_out[...] = slots
    coef[...] = project(3, rows_h, rows_l, tile_of, slots, betas, field_rows)


def kernel_project_last(rows_h, rows_l, dmat, coef_in, b3, near, slots_out, tiles_out, field_rows):
    tile_of = tile_rows(ids_of((b3,), 1))
    tiles_out[...] = tile_of
    slots = one_hot(as_column(ids_of((b3,), 0)) == iota((128, 256), 1))
    slots_out[...] = slots
    coef = coef_in[...] + project(1, rows_h, rows_l, tile_of, slots, (b3,), field_rows)
    coef = jnp.where(iota((16, 256), 1) < 192, coef, 0.0)
    near[0:64, :] = jnp.concatenate([dmat[...], jnp.zeros((64, 64), F32)], 1)
    near[64:80, :] = coef[:, :128]
    near[80:96, :] = coef[:, 128:]


def chip_of(own, other):
    f = lax.axis_index("fft")
    core = f % 2
    own, other = own[...], other[...]
    return (
        core,
        (f // 2) % 2 == 0,
        jnp.where(core == 0, own, other),
        jnp.where(core == 0, other, own),
    )


def kernel_merge(own, other, first, second):
    _, even, a, b = chip_of(own, other)
    low_lane = iota((16, 128), 1) < 64
    turned = pltpu.roll(b[64:80], 64, 1)
    up = jnp.where(low_lane, a[80:96] + turned, pltpu.roll(b[80:96], 64, 1))
    down = jnp.where(low_lane, a[64:80], a[64:80] + turned)
    up = jnp.concatenate([b[0:64], up], 0)
    down = jnp.concatenate([a[0:64], down], 0)
    first[...] = jnp.where(even, up, down)
    second[...] = jnp.where(even, down, up)


def kernel_put(tiles, tiles_last, vloc_in, put, vloc_out, vloc, sems):
    copies = [
        pltpu.make_async_copy(vloc_in.at[:, zi, :], vloc.at[zi], sems.at[zi]) for zi in range(3)
    ]
    for copy in copies:
        copy.start()
    tile_of = jnp.concatenate([tiles[...], tiles_last[...]], 1)
    put[...] = one_hot(iota((864, 512), 0) == tile_of)
    for copy in copies:
        copy.wait()
    for k in range(3):
        for zi in range(3):
            at = 288 * k + 96 * zi
            vloc_out[at : at + 96, :] = vloc[zi, pl.ds(k, 96, stride=3), :]


def kernel_back(
    field, own, other, second, first, slots, slots_last, put, b0, b1, b2, b3,
    vloc, fx, fy, ut, send, scr, rows,
):
    core, even, a, b = chip_of(own, other)
    above = jnp.where(even, first[...], second[...])
    below = jnp.where(even, second[...], first[...])
    low_lane = iota((16, 128), 1) < 64
    turned = pltpu.roll(b[64:80], 64, 1)
    tot = [
        below[64:80] + jnp.where(low_lane, a[64:80], a[64:80] + turned),
        above[64:80] + jnp.where(low_lane, a[80:96] + turned, pltpu.roll(b[80:96], 64, 1)),
    ]
    wide = iota((64, 128), 1) < 64
    coupling = [
        jnp.where(wide, below[0:64], pltpu.roll(a[0:64], 64, 1)),
        jnp.where(wide, b[0:64], pltpu.roll(above[0:64], 64, 1)),
    ]
    for h in range(2):
        for c in range(2):
            coef = tot[h][8 * c : 8 * c + 8, :]
            for j in range(8):
                row = jnp.sum(coupling[h][8 * j : 8 * j + 8, :] * coef, axis=0, keepdims=True)
                scr[8 * c + j : 8 * c + j + 1, 128 * h : 128 * h + 128] = row
    betas = (b0, b1, b2, b3)
    left, right = scr[:, :128], scr[:, 128:]
    left_turned, right_turned = pltpu.roll(left, 64, 1), pltpu.roll(right, 64, 1)
    left = jnp.where(core == 0, left, jnp.where(low_lane, left_turned, right_turned))
    right = jnp.where(low_lane, jnp.where(core == 0, right, right_turned), 0.0)
    high, low = split(jnp.concatenate([left, right], 1))
    weight = jnp.concatenate(
        [mm_nt(hot[...], high) + mm_nt(hot[...], low) for hot in (slots, slots_last)], 0
    )
    high, low = split(weight)
    weight = jnp.concatenate([high, low], 1)
    for k, beta in enumerate(betas):
        span = slice(128 * k, 128 * k + 128)
        terms = jnp.zeros((128, 256), F32)
        for j in range(8):
            wide = one_hot(iota((32, 256), 0) % 16 == 8 * (iota((32, 256), 1) // 128) + j)
            projector = beta[pl.ds(j, 128, stride=8), :]
            terms = terms + mm(weight[span], wide) * jnp.concatenate([projector, projector], 1)
        high, low = split(terms)
        rows[span, 0:256] = high
        rows[span, 256:512] = low
    both = mm(put[...], rows[...])
    nonloc = both[:, :256] + both[:, 256:]
    kinds = []
    for k in range(3):
        at = slice(288 * k, 288 * k + 288)
        factor = vloc[at, :]
        kinds.append(split(field[at, :] * jnp.concatenate([factor, factor], 1) + nonloc[at, :]))
    g = []
    for parity in range(2):
        table = [fx[1024 * parity + 512 * i : 1024 * parity + 512 * i + 512, :] for i in range(2)]
        lines = [jnp.concatenate([kinds[parity][i], kinds[parity + 1][i]], 1) for i in range(2)]
        g.append(split(three(mm, lines, table)))
    lines = [
        jnp.concatenate(
            [
                jnp.concatenate(
                    [
                        g[parity][i][96 * zi : 96 * zi + 96, 128 * c : 128 * c + 128]
                        for zi in range(3)
                    ],
                    1,
                )
                for c in range(2)
                for parity in range(2)
            ],
            0,
        )
        for i in range(2)
    ]
    h = three(mm, (fy[0:256, :], fy[256:512, :]), lines)
    main, spare, _ = masks_sp()
    spares = [jnp.zeros((64, 128), F32), jnp.zeros((64, 128), F32)]
    for zi in range(3):
        for c in range(2):
            turned = h[128 * c : 128 * c + 128, 128 * zi : 128 * zi + 128].T
            first = turned[:64]
            second = pltpu.roll(turned[64:], 64, 1)
            send[pl.ds(3 * c + zi, 64, stride=7), :] = jnp.where(main, first, second)
            high, low = split(jnp.where(spare, first, 0.0))
            move = ut[128 * zi : 128 * zi + 128, :]
            spares[c] = spares[c] + (mm(high, move) + mm(low, move))
    send[pl.ds(6, 64, stride=7), :] = spares[0] + pltpu.roll(spares[1], 64, 1)


def kernel_z_forward(recv, fz, result, out, sems):
    s = lax.axis_index("fft")
    out[...] = jnp.zeros((1728, 128), F32)
    spans = [(152, 280), (576, 576), (1304, 280), (0, 152), (432, 144), (1152, 152), (1584, 144)]
    copies = [
        pltpu.make_async_copy(out.at[pl.ds(*span)], result.at[pl.ds(*span)], sems.at[k])
        for k, span in enumerate(spans)
    ]
    for copy in copies[:3]:
        copy.start()
    r = iota((256, 1), 0)
    main, spare = line_places(r, s)
    lane = iota((256, 128), 1)
    keep = one_hot(lane == main)
    spares = recv[pl.ds(6, 64, stride=7), :]
    spares = (spares, pltpu.roll(spares, 64, 1))
    highs, lows = [], []
    for zi in range(3):
        unpack = jnp.concatenate(
            [keep, one_hot((lane == spare + 16 * zi) & (spare >= 0))], 1
        )
        lines = jnp.concatenate(
            [
                jnp.concatenate(
                    [
                        recv[pl.ds(3 * c + zi, 64, stride=7), :],
                        spares[c],
                    ],
                    1,
                )
                for c in range(2)
            ],
            0,
        )
        high, low = split(lines)
        columns = mm_nt(unpack, jnp.concatenate([high, low], 0))
        highs.append(columns[:, :128].astype(BF))
        lows.append(columns[:, 128:].astype(BF))
    z = three(
        mm, (jnp.concatenate(highs, 1), jnp.concatenate(lows, 1)), (fz[0:384, :], fz[384:768, :])
    )
    low_lane = iota((64, 128), 1) < 64
    for plane in range(2):
        for c in range(2):
            block = z[128 * plane : 128 * plane + 128, 128 * c : 128 * c + 128]
            even = jnp.where(sphere_rows(plane, 0, s), block[:64], 0.0)
            odd = jnp.where(sphere_rows(plane, 1, s), block[64:], 0.0)
            kinds = (
                jnp.where(low_lane, even, 0.0),
                pltpu.roll(jnp.where(low_lane, odd, even), 64, 1),
                jnp.where(low_lane, 0.0, odd),
            )
            for k, tile in enumerate(kinds):
                at = 1152 * plane + 2 * k + c
                out[pl.ds(at, 25, stride=6), :] = tile[24:49]
                out[pl.ds(at + 432, 24, stride=6), :] = tile[:24]
        copies[3 + 2 * plane].start()
        copies[4 + 2 * plane].start()
    for copy in copies:
        copy.wait()


def call(kernel, name, out_shape, args, scratch=(), anywhere=(), anywhere_out=(), limit=VMEM_LIMIT, cost=None):
    specs = [
        pl.BlockSpec(memory_space=pl.ANY if k in anywhere else pltpu.VMEM)
        for k in range(len(args))
    ]
    shapes = [
        jax.ShapeDtypeStruct(*shape) if isinstance(shape[0], tuple) else jax.ShapeDtypeStruct(shape, F32)
        for shape in out_shape
    ]
    out = pl.pallas_call(
        kernel,
        name=name,
        out_shape=shapes,
        in_specs=specs,
        out_specs=[
            pl.BlockSpec(memory_space=pl.ANY if k in anywhere_out else pltpu.VMEM)
            for k in range(len(shapes))
        ],
        scratch_shapes=list(scratch),
        cost_estimate=cost,
        compiler_params=pltpu.CompilerParams(vmem_limit_bytes=limit),
    )(*args)
    return out


def body(psi_g, vloc, beta, blk_slot, blk_tile, dmat):
    t = {
        name: jnp.asarray(value) for name, value in tables().items()
    }
    psi = psi_g[0].transpose(1, 0, 2).reshape(3, 2, 288, 128).transpose(0, 2, 1, 3)
    psi = psi.reshape(1728, 128)
    def gathered(x):
        return [x] + [
            lax.ppermute(x, "band", [(i, (i + k) % 4) for i in range(4)]) for k in (3, 2, 1)
        ]

    ids = jnp.concatenate([blk_slot[None], blk_tile[None], jnp.zeros((6, 128), jnp.int32)], 0)
    own = jnp.concatenate([beta, ids.astype(F32)[None]], 0).reshape(1032, 128)
    (send,) = call(kernel_z_inverse, "z_inverse", [(448, 128)], (psi, t["wz"]))
    betas = gathered(own)

    def exchange(x):
        x = lax.all_to_all(x.reshape(64, 1, 896), "fft", 0, 0, tiled=True)
        return x.reshape(448, 128)

    recv = exchange(send)
    vloc_tiles = vloc.reshape(3, 288, 128).transpose(1, 0, 2)
    dmat_rows = dmat.transpose(1, 2, 0).reshape(64, 64)
    field, rows_h, rows_l = call(
        kernel_field,
        "field",
        [(864, 256), ((896, 256), BF), ((896, 256), BF)],
        (recv, t["ey"], t["ix"], t["u"]),
    )
    coef, slots, tiles = call(
        kernel_project,
        "project",
        [(16, 256), ((384, 256), BF), ((1, 384), jnp.int32)],
        (rows_h, rows_l, *betas[:3]),
        [pltpu.VMEM((384, 256), F32)],
    )
    near, slots_last, tiles_last = call(
        kernel_project_last,
        "project_last",
        [(96, 128), ((128, 256), BF), ((1, 128), jnp.int32)],
        (rows_h, rows_l, dmat_rows, coef, betas[3]),
        [pltpu.VMEM((128, 256), F32)],
    )
    other = lax.ppermute(near, "fft", [(i, i ^ 1) for i in range(64)])
    first, second = call(kernel_merge, "merge", [(80, 128), (80, 128)], (near, other))
    first = lax.ppermute(first, "fft", [(i, i ^ 2) for i in range(64)])
    second = lax.ppermute(second, "fft", [(i, (((i + 2) % 64) ^ 2) - 2 & 63) for i in range(64)])
    put, vloc_rows = call(
        kernel_put,
        "put",
        [((864, 512), BF), (864, 128)],
        (tiles, tiles_last, vloc_tiles),
        [pltpu.VMEM((3, 288, 128), F32), pltpu.SemaphoreType.DMA((3,))],
        anywhere=(2,),
        cost=pl.CostEstimate(flops=2000000, bytes_accessed=3000000, transcendentals=0),
    )
    (send,) = call(
        kernel_back,
        "back",
        [(448, 128)],
        (field, near, other, second, first, slots, slots_last, put, *betas, vloc_rows, t["fx"], t["fy"], t["ut"]),
        [
            pltpu.VMEM((16, 256), F32),
            pltpu.VMEM((512, 512), BF),
        ],
    )
    (out,) = call(kernel_z_forward, "z_forward", [(1728, 128)], (exchange(send), t["fz"]),
        [pltpu.VMEM((1728, 128), F32), pltpu.SemaphoreType.DMA((7,))], anywhere_out=(0,))
    out = out.reshape(3, 288, 2, 128).transpose(0, 2, 1, 3).reshape(3, 2, N * N)
    return out.transpose(1, 0, 2)[None]


def solution(mesh):
    in_specs = (
        P("band", None, "fft", None),
        P("fft", None),
        P(("fft", "band"), None, None),
        P(("fft", "band")),
        P(("fft", "band")),
        P("fft", None, None),
    )
    out_specs = P("band", None, "fft", None)
    return jax.shard_map(body, mesh=mesh, in_specs=in_specs, out_specs=out_specs, check_vma=False)
```

```python
import functools

import jax
import jax.numpy as jnp
import ml_dtypes
import numpy as np
from jax import lax
from jax.experimental import pallas as pl
from jax.experimental.pallas import tpu as pltpu
from jax.sharding import PartitionSpec as P

N = 192
R2 = 48 * 48
BF = jnp.bfloat16
F32 = jnp.float32
VMEM_LIMIT = 32 * 1024 * 1024


def trig(freqs, points):
    angle = 2.0 * np.pi * (np.outer(freqs, points) % N) / N
    return np.cos(angle) / np.sqrt(N), np.sin(angle) / np.sqrt(N)


def pair_of(table):
    table = np.asarray(table, np.float32)
    high = table.astype(ml_dtypes.bfloat16)
    low = (table - high.astype(np.float32)).astype(ml_dtypes.bfloat16)
    return np.concatenate([high, low], 0)


KZ = np.concatenate([np.arange(64), np.arange(128, 192)])
SIGNED = np.concatenate([np.arange(64), np.arange(-64, 0)])
YS = [2 * np.arange(96), 2 * np.arange(96) + 1]


@functools.cache
def tables():
    t = {}
    blocks = []
    for zi in range(3):
        c, s = trig(3 * np.arange(64) + zi, KZ)
        blocks += [np.concatenate([c, -s], 1), np.concatenate([s, c], 1)]
    t["wz"] = pair_of(np.concatenate(blocks, 0))
    c, s = trig(np.concatenate(YS), SIGNED)
    t["ey"] = pair_of(
        np.concatenate([np.concatenate([c, -s], 1), np.concatenate([s, c], 1)], 0)
    )
    c, s = trig(SIGNED, np.arange(N))
    gap = np.zeros((128, 64))
    even = [np.concatenate([v, gap], 1) for v in (c, s, -s, c)]
    odd = [np.concatenate([gap, v], 1) for v in (c, s, -s, c)]
    t["ix"] = np.concatenate(
        [
            pair_of(np.block([[even[0], even[1]], [even[2], even[3]]])),
            pair_of(np.block([[odd[0], odd[1]], [odd[2], odd[3]]])),
        ],
        0,
    )
    parts = {}
    c, s = trig(np.arange(N), SIGNED)
    gap = np.zeros((64, 128))
    for name, table in (("c", c), ("s", s)):
        parts[name] = (np.concatenate([table, gap], 0), np.concatenate([gap, table], 0))

    def forward_x(which):
        cc, ss = parts["c"][which], parts["s"][which]
        first, second = np.concatenate([cc, -ss], 1), np.concatenate([ss, cc], 1)
        return np.concatenate([first[:128], second[:128], first[128:], second[128:]], 0)

    t["fx"] = np.concatenate([pair_of(forward_x(0)), pair_of(forward_x(1))], 0)
    c, s = trig(SIGNED, np.concatenate(YS))
    t["fy"] = pair_of(
        np.concatenate([np.concatenate([c, s], 1), np.concatenate([-s, c], 1)], 0)
    )
    blocks = []
    for zi in range(3):
        c, s = trig(3 * np.arange(64) + zi, KZ)
        blocks += [np.concatenate([c, -s], 1), np.concatenate([s, c], 1)]
    t["fz"] = pair_of(np.concatenate(blocks, 0))
    u = np.zeros((128, 384), np.float32)
    for zi in range(3):
        for p in range(128):
            u[16 * zi + 8 * (p >= 64) + p % 8, 128 * zi + p] = 1.0
    t["u"] = u.astype(ml_dtypes.bfloat16)
    t["ut"] = np.concatenate([u[:, 128 * zi : 128 * zi + 128].T for zi in range(3)], 0).astype(
        ml_dtypes.bfloat16
    )
    return t


def split(x):
    high = x.astype(BF)
    return high, (x - high.astype(F32)).astype(BF)


def mm(a, b):
    return jnp.dot(a, b, preferred_element_type=F32)


def mm_nt(a, b):
    return lax.dot_general(a, b, (((1,), (1,)), ((), ())), preferred_element_type=F32)


def three(product, a, b):
    return product(a[0], b[0]) + (product(a[0], b[1]) + product(a[1], b[0]))


def iota(shape, dim):
    return lax.broadcasted_iota(jnp.int32, shape, dim)


def masks_sp():
    s, p = iota((64, 128), 0), iota((64, 128), 1)
    ky = jnp.where(p < 64, p, p - 128)
    away = 64 - jnp.abs(ky)
    inside = ky * ky + s * s <= R2
    clash = away * away + (64 - s) * (64 - s) <= R2
    other = (p - 64) * (p - 64) + (64 - s) * (64 - s) <= R2
    return inside & ~clash, inside & clash, other


def line_places(r, s):
    plane, rest = r // 128, r % 128
    ky = 2 * (rest % 64 - 24) + rest // 64
    here = jnp.where(plane == 0, s, 64 - s)
    away = 64 - jnp.abs(ky)
    inside = ky * ky + here * here <= R2
    clash = (away * away + (64 - s) * (64 - s) <= R2) & (plane == 0)
    place = jnp.where(plane == 0, jnp.where(ky < 0, ky + 128, ky), ky + 64)
    main = jnp.where(inside & ~clash, place, -1)
    spare = jnp.where(inside & clash, jnp.where(ky < 0, 8, 0) + (ky + 64) % 8, -1)
    return main, spare


def one_hot(condition):
    return jnp.where(condition, 1.0, 0.0).astype(BF)


def sphere_rows(plane, parity, s):
    m, lane = iota((64, 128), 0), iota((64, 128), 1)
    ky = 2 * (m - 24) + parity
    kz = jnp.where(lane < 64, lane, lane - 128)
    kx = s - 64 * plane
    return ky * ky + kz * kz + kx * kx <= R2


def kernel_z_inverse(psi, wz, send):
    s = lax.axis_index("fft")
    main, spare = line_places(iota((1, 256), 1), s)
    j = iota((128, 256), 0)
    pack = jnp.concatenate(
        [one_hot(j == main), one_hot((j % 16 == spare) & (j % 64 < 48))], axis=0
    )
    lane = iota((64, 128), 1)
    rows = []
    for plane in range(2):
        lines = [[], []]
        for c in range(2):
            at = 1152 * plane + c
            t = [
                jnp.concatenate(
                    [
                        psi[pl.ds(at + 432 + 2 * k, 24, stride=6), :],
                        psi[pl.ds(at + 2 * k, 40, stride=6), :],
                    ],
                    0,
                )
                for k in range(3)
            ]
            middle = pltpu.roll(t[1], 64, 1)
            even = jnp.where(lane < 64, t[0], middle)
            odd = jnp.where(lane < 64, middle, t[2])
            lines[0].append(jnp.where(sphere_rows(plane, 0, s), even, 0.0))
            lines[1].append(jnp.where(sphere_rows(plane, 1, s), odd, 0.0))
        rows += [jnp.concatenate(lines[0], 1), jnp.concatenate(lines[1], 1)]
    high, low = split(jnp.concatenate(rows, 0))
    packed = (mm(pack, high).astype(BF), mm(pack, low).astype(BF))
    out = three(mm_nt, (wz[0:384, :], wz[384:768, :]), packed)
    spares = out[0:64, 128:]
    for c in range(2):
        for zi in range(3):
            block = out[(2 * zi + c) * 64 : (2 * zi + c) * 64 + 64]
            send[pl.ds(3 * c + zi, 64, stride=7), :] = block[:, :128]
            spares = jnp.where(lane // 16 == 4 * c + zi, block[:, 128:], spares)
    send[pl.ds(6, 64, stride=7), :] = spares


def tile_rows(tiles):
    return (tiles % 3) * 288 + tiles // 3


def as_column(ids):
    return jnp.broadcast_to(ids.astype(F32), (8, ids.shape[1])).T[:, 0:1].astype(jnp.int32)


def kernel_field(
    recv, ey, ix, u, field, rows_h, rows_l,
):
    main, spare, other = masks_sp()
    spread = []
    for c in range(2):
        got = recv[pl.ds(6, 64, stride=7), :]
        high, low = split(pltpu.roll(got, 64, 1) if c else got)
        spread.append(mm(high, u[...]) + mm(low, u[...]))
    lines = []
    for zi in range(3):
        first, second = [], []
        for c in range(2):
            got = recv[pl.ds(3 * c + zi, 64, stride=7), :]
            extra = spread[c][:, 128 * zi : 128 * zi + 128]
            first.append(jnp.where(main, got, jnp.where(spare, extra, 0.0)))
            second.append(pltpu.roll(jnp.where(other, got, 0.0), 64, 1))
        lines += [jnp.concatenate(first, 1), jnp.concatenate(second, 1)]
    g = three(mm_nt, (ey[0:384, :], ey[384:768, :]), split(jnp.concatenate(lines, 0)))
    out = []
    for parity in range(2):
        a = 96 * parity
        table = [ix[512 * parity + 256 * i : 512 * parity + 256 * i + 256, :] for i in range(2)]
        block = jnp.concatenate(
            [
                jnp.concatenate(
                    [
                        g[a : a + 96, 128 * zi : 128 * zi + 128],
                        g[192 + a : 288 + a, 128 * zi : 128 * zi + 128],
                    ],
                    1,
                )
                for zi in range(3)
            ],
            0,
        )
        out.append(three(mm, split(block), table))
    even, odd = out
    for c in range(2):
        a = 256 * c
        kinds = (
            even[:, a : a + 128],
            even[:, a + 128 : a + 256] + odd[:, a : a + 128],
            odd[:, a + 128 : a + 256],
        )
        for k, tile in enumerate(kinds):
            span = pl.ds(288 * k, 288)
            lanes = pl.ds(128 * c, 128)
            field[span, lanes] = tile
            high, low = split(tile)
            rows_h[span, lanes] = high
            rows_l[span, lanes] = low
    rows_h[864:896, :] = jnp.zeros((32, 256), BF)
    rows_l[864:896, :] = jnp.zeros((32, 256), BF)


def project(quarters, rows_h, rows_l, tile_of, slots, betas, field_rows):
    count = 128 * quarters
    pick = one_hot(as_column(tile_of) == iota((count, 896), 1))
    field_rows[...] = mm(pick, rows_h[...]) + mm(pick, rows_l[...])
    lane = iota((128, 128), 1)
    sums = []
    for k, beta in enumerate(betas):
        total = jnp.zeros((128, 128), F32)
        for j in range(8):
            projector = beta[pl.ds(j, 128, stride=8), :]
            for c in range(2):
                value = field_rows[128 * k : 128 * k + 128, 128 * c : 128 * c + 128] * projector
                total = jnp.where(
                    lane == 8 * c + j, jnp.sum(value, axis=1, keepdims=True), total
                )
        sums.append(total.T[:16])
    high, low = split(jnp.concatenate(sums, 1))
    return mm(high, slots) + mm(low, slots)


def ids_of(betas, row):
    return jnp.concatenate([b[1024 + row : 1025 + row, :] for b in betas], 1).astype(jnp.int32)


def kernel_project(rows_h, rows_l, b0, b1, b2, coef, slots_out, tiles_out, field_rows):
    betas = (b0, b1, b2)
    tile_of = tile_rows(ids_of(betas, 1))
    tiles_out[...] = tile_of
    slots = one_hot(as_column(ids_of(betas, 0)) == iota((384, 256), 1))
    slots_out[...] = slots
    coef[...] = project(3, rows_h, rows_l, tile_of, slots, betas, field_rows)


def kernel_project_last(rows_h, rows_l, dmat, coef_in, b3, near, slots_out, tiles_out, field_rows):
    tile_of = tile_rows(ids_of((b3,), 1))
    tiles_out[...] = tile_of
    slots = one_hot(as_column(ids_of((b3,), 0)) == iota((128, 256), 1))
    slots_out[...] = slots
    coef = coef_in[...] + project(1, rows_h, rows_l, tile_of, slots, (b3,), field_rows)
    coef = jnp.where(iota((16, 256), 1) < 192, coef, 0.0)
    near[0:64, :] = jnp.concatenate([dmat[...], jnp.zeros((64, 64), F32)], 1)
    near[64:80, :] = coef[:, :128]
    near[80:96, :] = coef[:, 128:]


def chip_of(own, other):
    f = lax.axis_index("fft")
    core = f % 2
    own, other = own[...], other[...]
    return (
        core,
        (f // 2) % 2 == 0,
        jnp.where(core == 0, own, other),
        jnp.where(core == 0, other, own),
    )


def kernel_merge(own, other, first, second):
    _, even, a, b = chip_of(own, other)
    low_lane = iota((16, 128), 1) < 64
    turned = pltpu.roll(b[64:80], 64, 1)
    up = jnp.where(low_lane, a[80:96] + turned, pltpu.roll(b[80:96], 64, 1))
    down = jnp.where(low_lane, a[64:80], a[64:80] + turned)
    up = jnp.concatenate([b[0:64], up], 0)
    down = jnp.concatenate([a[0:64], down], 0)
    first[...] = jnp.where(even, up, down)
    second[...] = jnp.where(even, down, up)


def kernel_put(tiles, tiles_last, vloc_in, put, vloc_out, vloc, sems):
    copies = [
        pltpu.make_async_copy(vloc_in.at[:, zi, :], vloc.at[zi], sems.at[zi]) for zi in range(3)
    ]
    for copy in copies:
        copy.start()
    tile_of = jnp.concatenate([tiles[...], tiles_last[...]], 1)
    put[...] = one_hot(iota((864, 512), 0) == tile_of)
    for copy in copies:
        copy.wait()
    for k in range(3):
        for zi in range(3):
            at = 288 * k + 96 * zi
            vloc_out[at : at + 96, :] = vloc[zi, pl.ds(k, 96, stride=3), :]


def kernel_back(
    field, own, other, second, first, slots, slots_last, put, b0, b1, b2, b3,
    vloc, fx, fy, ut, send, scr, rows,
):
    core, even, a, b = chip_of(own, other)
    above = jnp.where(even, first[...], second[...])
    below = jnp.where(even, second[...], first[...])
    low_lane = iota((16, 128), 1) < 64
    turned = pltpu.roll(b[64:80], 64, 1)
    tot = [
        below[64:80] + jnp.where(low_lane, a[64:80], a[64:80] + turned),
        above[64:80] + jnp.where(low_lane, a[80:96] + turned, pltpu.roll(b[80:96], 64, 1)),
    ]
    wide = iota((64, 128), 1) < 64
    coupling = [
        jnp.where(wide, below[0:64], pltpu.roll(a[0:64], 64, 1)),
        jnp.where(wide, b[0:64], pltpu.roll(above[0:64], 64, 1)),
    ]
    for h in range(2):
        for c in range(2):
            coef = tot[h][8 * c : 8 * c + 8, :]
            for j in range(8):
                row = jnp.sum(coupling[h][8 * j : 8 * j + 8, :] * coef, axis=0, keepdims=True)
                scr[8 * c + j : 8 * c + j + 1, 128 * h : 128 * h + 128] = row
    betas = (b0, b1, b2, b3)
    left, right = scr[:, :128], scr[:, 128:]
    left_turned, right_turned = pltpu.roll(left, 64, 1), pltpu.roll(right, 64, 1)
    left = jnp.where(core == 0, left, jnp.where(low_lane, left_turned, right_turned))
    right = jnp.where(low_lane, jnp.where(core == 0, right, right_turned), 0.0)
    high, low = split(jnp.concatenate([left, right], 1))
    weight = jnp.concatenate(
        [mm_nt(hot[...], high) + mm_nt(hot[...], low) for hot in (slots, slots_last)], 0
    )
    high, low = split(weight)
    weight = jnp.concatenate([high, low], 1)
    for k, beta in enumerate(betas):
        span = slice(128 * k, 128 * k + 128)
        terms = jnp.zeros((128, 256), F32)
        for j in range(8):
            wide = one_hot(iota((32, 256), 0) % 16 == 8 * (iota((32, 256), 1) // 128) + j)
            projector = beta[pl.ds(j, 128, stride=8), :]
            terms = terms + mm(weight[span], wide) * jnp.concatenate([projector, projector], 1)
        high, low = split(terms)
        rows[span, 0:256] = high
        rows[span, 256:512] = low
    both = mm(put[...], rows[...])
    nonloc = both[:, :256] + both[:, 256:]
    kinds = []
    for k in range(3):
        at = slice(288 * k, 288 * k + 288)
        factor = vloc[at, :]
        kinds.append(split(field[at, :] * jnp.concatenate([factor, factor], 1) + nonloc[at, :]))
    g = []
    for parity in range(2):
        table = [fx[1024 * parity + 512 * i : 1024 * parity + 512 * i + 512, :] for i in range(2)]
        lines = [jnp.concatenate([kinds[parity][i], kinds[parity + 1][i]], 1) for i in range(2)]
        g.append(split(three(mm, lines, table)))
    lines = [
        jnp.concatenate(
            [
                jnp.concatenate(
                    [
                        g[parity][i][96 * zi : 96 * zi + 96, 128 * c : 128 * c + 128]
                        for zi in range(3)
                    ],
                    1,
                )
                for c in range(2)
                for parity in range(2)
            ],
            0,
        )
        for i in range(2)
    ]
    h = three(mm, (fy[0:256, :], fy[256:512, :]), lines)
    main, spare, _ = masks_sp()
    spares = [jnp.zeros((64, 128), F32), jnp.zeros((64, 128), F32)]
    for zi in range(3):
        for c in range(2):
            turned = h[128 * c : 128 * c + 128, 128 * zi : 128 * zi + 128].T
            first = turned[:64]
            second = pltpu.roll(turned[64:], 64, 1)
            send[pl.ds(3 * c + zi, 64, stride=7), :] = jnp.where(main, first, second)
            high, low = split(jnp.where(spare, first, 0.0))
            move = ut[128 * zi : 128 * zi + 128, :]
            spares[c] = spares[c] + (mm(high, move) + mm(low, move))
    send[pl.ds(6, 64, stride=7), :] = spares[0] + pltpu.roll(spares[1], 64, 1)


def kernel_z_forward(recv, fz, result, out, sems):
    s = lax.axis_index("fft")
    out[...] = jnp.zeros((1728, 128), F32)
    spans = [(152, 280), (576, 576), (1304, 280), (0, 152), (432, 144), (1152, 152), (1584, 144)]
    copies = [
        pltpu.make_async_copy(out.at[pl.ds(*span)], result.at[pl.ds(*span)], sems.at[k])
        for k, span in enumerate(spans)
    ]
    for copy in copies[:3]:
        copy.start()
    r = iota((256, 1), 0)
    main, spare = line_places(r, s)
    lane = iota((256, 128), 1)
    keep = one_hot(lane == main)
    spares = recv[pl.ds(6, 64, stride=7), :]
    spares = (spares, pltpu.roll(spares, 64, 1))
    highs, lows = [], []
    for zi in range(3):
        unpack = jnp.concatenate(
            [keep, one_hot((lane == spare + 16 * zi) & (spare >= 0))], 1
        )
        lines = jnp.concatenate(
            [
                jnp.concatenate(
                    [
                        recv[pl.ds(3 * c + zi, 64, stride=7), :],
                        spares[c],
                    ],
                    1,
                )
                for c in range(2)
            ],
            0,
        )
        high, low = split(lines)
        columns = mm_nt(unpack, jnp.concatenate([high, low], 0))
        highs.append(columns[:, :128].astype(BF))
        lows.append(columns[:, 128:].astype(BF))
    z = three(
        mm, (jnp.concatenate(highs, 1), jnp.concatenate(lows, 1)), (fz[0:384, :], fz[384:768, :])
    )
    low_lane = iota((64, 128), 1) < 64
    for plane in range(2):
        for c in range(2):
            block = z[128 * plane : 128 * plane + 128, 128 * c : 128 * c + 128]
            even = jnp.where(sphere_rows(plane, 0, s), block[:64], 0.0)
            odd = jnp.where(sphere_rows(plane, 1, s), block[64:], 0.0)
            kinds = (
                jnp.where(low_lane, even, 0.0),
                pltpu.roll(jnp.where(low_lane, odd, even), 64, 1),
                jnp.where(low_lane, 0.0, odd),
            )
            for k, tile in enumerate(kinds):
                at = 1152 * plane + 2 * k + c
                out[pl.ds(at, 25, stride=6), :] = tile[24:49]
                out[pl.ds(at + 432, 24, stride=6), :] = tile[:24]
        copies[3 + 2 * plane].start()
        copies[4 + 2 * plane].start()
    for copy in copies:
        copy.wait()


def call(kernel, name, out_shape, args, scratch=(), anywhere=(), anywhere_out=(), limit=VMEM_LIMIT, cost=None):
    specs = [
        pl.BlockSpec(memory_space=pl.ANY if k in anywhere else pltpu.VMEM)
        for k in range(len(args))
    ]
    shapes = [
        jax.ShapeDtypeStruct(*shape) if isinstance(shape[0], tuple) else jax.ShapeDtypeStruct(shape, F32)
        for shape in out_shape
    ]
    out = pl.pallas_call(
        kernel,
        name=name,
        out_shape=shapes,
        in_specs=specs,
        out_specs=[
            pl.BlockSpec(memory_space=pl.ANY if k in anywhere_out else pltpu.VMEM)
            for k in range(len(shapes))
        ],
        scratch_shapes=list(scratch),
        cost_estimate=cost,
        compiler_params=pltpu.CompilerParams(vmem_limit_bytes=limit),
    )(*args)
    return out


def body(psi_g, vloc, beta, blk_slot, blk_tile, dmat):
    t = {
        name: jnp.asarray(value) for name, value in tables().items()
    }
    psi = psi_g[0].transpose(1, 0, 2).reshape(3, 2, 288, 128).transpose(0, 2, 1, 3)
    psi = psi.reshape(1728, 128)
    def from_band(x, k):
        return lax.ppermute(x, "band", [(i, (i + k) % 4) for i in range(4)])

    ids = jnp.concatenate([blk_slot[None], blk_tile[None], jnp.zeros((6, 128), jnp.int32)], 0)
    own = jnp.concatenate([beta, ids.astype(F32)[None]], 0).reshape(1032, 128)
    (send,) = call(kernel_z_inverse, "z_inverse", [(448, 128)], (psi, t["wz"]))
    own_later, send = lax.optimization_barrier((own, send))
    betas = [own, from_band(own, 3), from_band(own, 2), from_band(own_later, 1)]

    def exchange(x):
        x = lax.all_to_all(x.reshape(64, 1, 896), "fft", 0, 0, tiled=True)
        return x.reshape(448, 128)

    recv = exchange(send)
    vloc_tiles = vloc.reshape(3, 288, 128).transpose(1, 0, 2)
    dmat_rows = dmat.transpose(1, 2, 0).reshape(64, 64)
    field, rows_h, rows_l = call(
        kernel_field,
        "field",
        [(864, 256), ((896, 256), BF), ((896, 256), BF)],
        (recv, t["ey"], t["ix"], t["u"]),
    )
    coef, slots, tiles = call(
        kernel_project,
        "project",
        [(16, 256), ((384, 256), BF), ((1, 384), jnp.int32)],
        (rows_h, rows_l, *betas[:3]),
        [pltpu.VMEM((384, 256), F32)],
    )
    near, slots_last, tiles_last = call(
        kernel_project_last,
        "project_last",
        [(96, 128), ((128, 256), BF), ((1, 128), jnp.int32)],
        (rows_h, rows_l, dmat_rows, coef, betas[3]),
        [pltpu.VMEM((128, 256), F32)],
    )
    other = lax.ppermute(near, "fft", [(i, i ^ 1) for i in range(64)])
    first, second = call(kernel_merge, "merge", [(80, 128), (80, 128)], (near, other))
    first = lax.ppermute(first, "fft", [(i, i ^ 2) for i in range(64)])
    second = lax.ppermute(second, "fft", [(i, (((i + 2) % 64) ^ 2) - 2 & 63) for i in range(64)])
    put, vloc_rows = call(
        kernel_put,
        "put",
        [((864, 512), BF), (864, 128)],
        (tiles, tiles_last, vloc_tiles),
        [pltpu.VMEM((3, 288, 128), F32), pltpu.SemaphoreType.DMA((3,))],
        anywhere=(2,),
        cost=pl.CostEstimate(flops=2000000, bytes_accessed=3000000, transcendentals=0),
    )
    (send,) = call(
        kernel_back,
        "back",
        [(448, 128)],
        (field, near, other, second, first, slots, slots_last, put, *betas, vloc_rows, t["fx"], t["fy"], t["ut"]),
        [
            pltpu.VMEM((16, 256), F32),
            pltpu.VMEM((512, 512), BF),
        ],
    )
    (out,) = call(kernel_z_forward, "z_forward", [(1728, 128)], (exchange(send), t["fz"]),
        [pltpu.VMEM((1728, 128), F32), pltpu.SemaphoreType.DMA((7,))], anywhere_out=(0,))
    out = out.reshape(3, 288, 2, 128).transpose(0, 2, 1, 3).reshape(3, 2, N * N)
    return out.transpose(1, 0, 2)[None]


def solution(mesh):
    in_specs = (
        P("band", None, "fft", None),
        P("fft", None),
        P(("fft", "band"), None, None),
        P(("fft", "band")),
        P(("fft", "band")),
        P("fft", None, None),
    )
    out_specs = P("band", None, "fft", None)
    return jax.shard_map(body, mesh=mesh, in_specs=in_specs, out_specs=out_specs, check_vma=False)
```

```python
import functools

import jax
import jax.numpy as jnp
import ml_dtypes
import numpy as np
from jax import lax
from jax.experimental import pallas as pl
from jax.experimental.pallas import tpu as pltpu
from jax.sharding import PartitionSpec as P

N = 192
R2 = 48 * 48
BF = jnp.bfloat16
F32 = jnp.float32
VMEM_LIMIT = 32 * 1024 * 1024


def trig(freqs, points):
    angle = 2.0 * np.pi * (np.outer(freqs, points) % N) / N
    return np.cos(angle) / np.sqrt(N), np.sin(angle) / np.sqrt(N)


def pair_of(table):
    table = np.asarray(table, np.float32)
    high = table.astype(ml_dtypes.bfloat16)
    low = (table - high.astype(np.float32)).astype(ml_dtypes.bfloat16)
    return np.concatenate([high, low], 0)


KZ = np.concatenate([np.arange(64), np.arange(128, 192)])
SIGNED = np.concatenate([np.arange(64), np.arange(-64, 0)])
YS = [2 * np.arange(96), 2 * np.arange(96) + 1]


@functools.cache
def tables():
    t = {}
    blocks = []
    for zi in range(3):
        c, s = trig(3 * np.arange(64) + zi, KZ)
        blocks += [np.concatenate([c, -s], 1), np.concatenate([s, c], 1)]
    t["wz"] = pair_of(np.concatenate(blocks, 0))
    c, s = trig(np.concatenate(YS), SIGNED)
    t["ey"] = pair_of(
        np.concatenate([np.concatenate([c, -s], 1), np.concatenate([s, c], 1)], 0)
    )
    c, s = trig(SIGNED, np.arange(N))
    gap = np.zeros((128, 64))
    even = [np.concatenate([v, gap], 1) for v in (c, s, -s, c)]
    odd = [np.concatenate([gap, v], 1) for v in (c, s, -s, c)]
    t["ix"] = np.concatenate(
        [
            pair_of(np.block([[even[0], even[1]], [even[2], even[3]]])),
            pair_of(np.block([[odd[0], odd[1]], [odd[2], odd[3]]])),
        ],
        0,
    )
    parts = {}
    c, s = trig(np.arange(N), SIGNED)
    gap = np.zeros((64, 128))
    for name, table in (("c", c), ("s", s)):
        parts[name] = (np.concatenate([table, gap], 0), np.concatenate([gap, table], 0))

    def forward_x(which):
        cc, ss = parts["c"][which], parts["s"][which]
        first, second = np.concatenate([cc, -ss], 1), np.concatenate([ss, cc], 1)
        return np.concatenate([first[:128], second[:128], first[128:], second[128:]], 0)

    t["fx"] = np.concatenate([pair_of(forward_x(0)), pair_of(forward_x(1))], 0)
    c, s = trig(SIGNED, np.concatenate(YS))
    t["fy"] = pair_of(
        np.concatenate([np.concatenate([c, s], 1), np.concatenate([-s, c], 1)], 0)
    )
    blocks = []
    for zi in range(3):
        c, s = trig(3 * np.arange(64) + zi, KZ)
        blocks += [np.concatenate([c, -s], 1), np.concatenate([s, c], 1)]
    t["fz"] = pair_of(np.concatenate(blocks, 0))
    u = np.zeros((128, 384), np.float32)
    for zi in range(3):
        for p in range(128):
            u[16 * zi + 8 * (p >= 64) + p % 8, 128 * zi + p] = 1.0
    t["u"] = u.astype(ml_dtypes.bfloat16)
    t["ut"] = np.concatenate([u[:, 128 * zi : 128 * zi + 128].T for zi in range(3)], 0).astype(
        ml_dtypes.bfloat16
    )
    return t


def split(x):
    high = x.astype(BF)
    return high, (x - high.astype(F32)).astype(BF)


def mm(a, b):
    return jnp.dot(a, b, preferred_element_type=F32)


def mm_nt(a, b):
    return lax.dot_general(a, b, (((1,), (1,)), ((), ())), preferred_element_type=F32)


def three(product, a, b):
    return product(a[0], b[0]) + (product(a[0], b[1]) + product(a[1], b[0]))


def iota(shape, dim):
    return lax.broadcasted_iota(jnp.int32, shape, dim)


def masks_sp():
    s, p = iota((64, 128), 0), iota((64, 128), 1)
    ky = jnp.where(p < 64, p, p - 128)
    away = 64 - jnp.abs(ky)
    inside = ky * ky + s * s <= R2
    clash = away * away + (64 - s) * (64 - s) <= R2
    other = (p - 64) * (p - 64) + (64 - s) * (64 - s) <= R2
    return inside & ~clash, inside & clash, other


def line_places(r, s):
    plane, rest = r // 128, r % 128
    ky = 2 * (rest % 64 - 24) + rest // 64
    here = jnp.where(plane == 0, s, 64 - s)
    away = 64 - jnp.abs(ky)
    inside = ky * ky + here * here <= R2
    clash = (away * away + (64 - s) * (64 - s) <= R2) & (plane == 0)
    place = jnp.where(plane == 0, jnp.where(ky < 0, ky + 128, ky), ky + 64)
    main = jnp.where(inside & ~clash, place, -1)
    spare = jnp.where(inside & clash, jnp.where(ky < 0, 8, 0) + (ky + 64) % 8, -1)
    return main, spare


def one_hot(condition):
    return jnp.where(condition, 1.0, 0.0).astype(BF)


def sphere_rows(plane, parity, s):
    m, lane = iota((64, 128), 0), iota((64, 128), 1)
    ky = 2 * (m - 24) + parity
    kz = jnp.where(lane < 64, lane, lane - 128)
    kx = s - 64 * plane
    return ky * ky + kz * kz + kx * kx <= R2


def kernel_z_inverse(psi, wz, send):
    s = lax.axis_index("fft")
    main, spare = line_places(iota((1, 256), 1), s)
    j = iota((128, 256), 0)
    pack = jnp.concatenate(
        [one_hot(j == main), one_hot((j % 16 == spare) & (j % 64 < 48))], axis=0
    )
    lane = iota((64, 128), 1)
    rows = []
    for plane in range(2):
        lines = [[], []]
        for c in range(2):
            at = 1152 * plane + c
            t = [
                jnp.concatenate(
                    [
                        psi[pl.ds(at + 432 + 2 * k, 24, stride=6), :],
                        psi[pl.ds(at + 2 * k, 40, stride=6), :],
                    ],
                    0,
                )
                for k in range(3)
            ]
            middle = pltpu.roll(t[1], 64, 1)
            even = jnp.where(lane < 64, t[0], middle)
            odd = jnp.where(lane < 64, middle, t[2])
            lines[0].append(jnp.where(sphere_rows(plane, 0, s), even, 0.0))
            lines[1].append(jnp.where(sphere_rows(plane, 1, s), odd, 0.0))
        rows += [jnp.concatenate(lines[0], 1), jnp.concatenate(lines[1], 1)]
    high, low = split(jnp.concatenate(rows, 0))
    packed = (mm(pack, high).astype(BF), mm(pack, low).astype(BF))
    out = three(mm_nt, (wz[0:384, :], wz[384:768, :]), packed)
    spares = out[0:64, 128:]
    for c in range(2):
        for zi in range(3):
            block = out[(2 * zi + c) * 64 : (2 * zi + c) * 64 + 64]
            send[pl.ds(3 * c + zi, 64, stride=7), :] = block[:, :128]
            spares = jnp.where(lane // 16 == 4 * c + zi, block[:, 128:], spares)
    send[pl.ds(6, 64, stride=7), :] = spares


def tile_rows(tiles):
    return (tiles % 3) * 288 + tiles // 3


def as_column(ids):
    return jnp.broadcast_to(ids.astype(F32), (8, ids.shape[1])).T[:, 0:1].astype(jnp.int32)


def kernel_field(
    recv, ey, ix, u, field, rows_h, rows_l,
):
    main, spare, other = masks_sp()
    spread = []
    for c in range(2):
        got = recv[pl.ds(6, 64, stride=7), :]
        high, low = split(pltpu.roll(got, 64, 1) if c else got)
        spread.append(mm(high, u[...]) + mm(low, u[...]))
    lines = []
    for zi in range(3):
        first, second = [], []
        for c in range(2):
            got = recv[pl.ds(3 * c + zi, 64, stride=7), :]
            extra = spread[c][:, 128 * zi : 128 * zi + 128]
            first.append(jnp.where(main, got, jnp.where(spare, extra, 0.0)))
            second.append(pltpu.roll(jnp.where(other, got, 0.0), 64, 1))
        lines += [jnp.concatenate(first, 1), jnp.concatenate(second, 1)]
    g = three(mm_nt, (ey[0:384, :], ey[384:768, :]), split(jnp.concatenate(lines, 0)))
    out = []
    for parity in range(2):
        a = 96 * parity
        table = [ix[512 * parity + 256 * i : 512 * parity + 256 * i + 256, :] for i in range(2)]
        block = jnp.concatenate(
            [
                jnp.concatenate(
                    [
                        g[a : a + 96, 128 * zi : 128 * zi + 128],
                        g[192 + a : 288 + a, 128 * zi : 128 * zi + 128],
                    ],
                    1,
                )
                for zi in range(3)
            ],
            0,
        )
        out.append(three(mm, split(block), table))
    even, odd = out
    for c in range(2):
        a = 256 * c
        kinds = (
            even[:, a : a + 128],
            even[:, a + 128 : a + 256] + odd[:, a : a + 128],
            odd[:, a + 128 : a + 256],
        )
        for k, tile in enumerate(kinds):
            span = pl.ds(288 * k, 288)
            lanes = pl.ds(128 * c, 128)
            field[span, lanes] = tile
            high, low = split(tile)
            rows_h[span, lanes] = high
            rows_l[span, lanes] = low
    rows_h[864:896, :] = jnp.zeros((32, 256), BF)
    rows_l[864:896, :] = jnp.zeros((32, 256), BF)


def project(quarters, rows_h, rows_l, tile_of, slots, betas, field_rows):
    count = 128 * quarters
    pick = one_hot(as_column(tile_of) == iota((count, 896), 1))
    field_rows[...] = mm(pick, rows_h[...]) + mm(pick, rows_l[...])
    lane = iota((128, 128), 1)
    sums = []
    for k, beta in enumerate(betas):
        total = jnp.zeros((128, 128), F32)
        for j in range(8):
            projector = beta[pl.ds(j, 128, stride=8), :]
            for c in range(2):
                value = field_rows[128 * k : 128 * k + 128, 128 * c : 128 * c + 128] * projector
                total = jnp.where(
                    lane == 8 * c + j, jnp.sum(value, axis=1, keepdims=True), total
                )
        sums.append(total.T[:16])
    high, low = split(jnp.concatenate(sums, 1))
    return mm(high, slots) + mm(low, slots)


def ids_of(betas, row):
    return jnp.concatenate([b[1024 + row : 1025 + row, :] for b in betas], 1).astype(jnp.int32)


def kernel_project(rows_h, rows_l, b0, b1, b2, coef, slots_out, tiles_out, field_rows):
    betas = (b0, b1, b2)
    tile_of = tile_rows(ids_of(betas, 1))
    tiles_out[...] = tile_of
    slots = one_hot(as_column(ids_of(betas, 0)) == iota((384, 256), 1))
    slots_out[...] = slots
    coef[...] = project(3, rows_h, rows_l, tile_of, slots, betas, field_rows)


def kernel_project_last(rows_h, rows_l, dmat, coef_in, b3, near, slots_out, tiles_out, field_rows):
    tile_of = tile_rows(ids_of((b3,), 1))
    tiles_out[...] = tile_of
    slots = one_hot(as_column(ids_of((b3,), 0)) == iota((128, 256), 1))
    slots_out[...] = slots
    coef = coef_in[...] + project(1, rows_h, rows_l, tile_of, slots, (b3,), field_rows)
    coef = jnp.where(iota((16, 256), 1) < 192, coef, 0.0)
    near[0:64, :] = jnp.concatenate([dmat[...], jnp.zeros((64, 64), F32)], 1)
    near[64:80, :] = coef[:, :128]
    near[80:96, :] = coef[:, 128:]


def chip_of(own, other):
    f = lax.axis_index("fft")
    core = f % 2
    own, other = own[...], other[...]
    return (
        core,
        (f // 2) % 2 == 0,
        jnp.where(core == 0, own, other),
        jnp.where(core == 0, other, own),
    )


def kernel_merge(own, other, first, second):
    _, even, a, b = chip_of(own, other)
    low_lane = iota((16, 128), 1) < 64
    turned = pltpu.roll(b[64:80], 64, 1)
    up = jnp.where(low_lane, a[80:96] + turned, pltpu.roll(b[80:96], 64, 1))
    down = jnp.where(low_lane, a[64:80], a[64:80] + turned)
    up = jnp.concatenate([b[0:64], up], 0)
    down = jnp.concatenate([a[0:64], down], 0)
    first[...] = jnp.where(even, up, down)
    second[...] = jnp.where(even, down, up)


def kernel_put(tiles, tiles_last, vloc_in, put, vloc_out, vloc, sems):
    copies = [
        pltpu.make_async_copy(vloc_in.at[:, zi, :], vloc.at[zi], sems.at[zi]) for zi in range(3)
    ]
    for copy in copies:
        copy.start()
    tile_of = jnp.concatenate([tiles[...], tiles_last[...]], 1)
    put[...] = one_hot(iota((864, 512), 0) == tile_of)
    for copy in copies:
        copy.wait()
    for k in range(3):
        for zi in range(3):
            at = 288 * k + 96 * zi
            vloc_out[at : at + 96, :] = vloc[zi, pl.ds(k, 96, stride=3), :]


def kernel_back(
    field, own, other, second, first, slots, slots_last, put, b0, b1, b2, b3,
    vloc, fx, fy, ut, send, scr, rows,
):
    core, even, a, b = chip_of(own, other)
    above = jnp.where(even, first[...], second[...])
    below = jnp.where(even, second[...], first[...])
    low_lane = iota((16, 128), 1) < 64
    turned = pltpu.roll(b[64:80], 64, 1)
    tot = [
        below[64:80] + jnp.where(low_lane, a[64:80], a[64:80] + turned),
        above[64:80] + jnp.where(low_lane, a[80:96] + turned, pltpu.roll(b[80:96], 64, 1)),
    ]
    wide = iota((64, 128), 1) < 64
    coupling = [
        jnp.where(wide, below[0:64], pltpu.roll(a[0:64], 64, 1)),
        jnp.where(wide, b[0:64], pltpu.roll(above[0:64], 64, 1)),
    ]
    for h in range(2):
        for c in range(2):
            coef = tot[h][8 * c : 8 * c + 8, :]
            for j in range(8):
                row = jnp.sum(coupling[h][8 * j : 8 * j + 8, :] * coef, axis=0, keepdims=True)
                scr[8 * c + j : 8 * c + j + 1, 128 * h : 128 * h + 128] = row
    betas = (b0, b1, b2, b3)
    left, right = scr[:, :128], scr[:, 128:]
    left_turned, right_turned = pltpu.roll(left, 64, 1), pltpu.roll(right, 64, 1)
    left = jnp.where(core == 0, left, jnp.where(low_lane, left_turned, right_turned))
    right = jnp.where(low_lane, jnp.where(core == 0, right, right_turned), 0.0)
    high, low = split(jnp.concatenate([left, right], 1))
    weight = jnp.concatenate(
        [mm_nt(hot[...], high) + mm_nt(hot[...], low) for hot in (slots, slots_last)], 0
    )
    high, low = split(weight)
    weight = jnp.concatenate([high, low], 1)
    for k, beta in enumerate(betas):
        span = slice(128 * k, 128 * k + 128)
        terms = jnp.zeros((128, 256), F32)
        for j in range(8):
            wide = one_hot(iota((32, 256), 0) % 16 == 8 * (iota((32, 256), 1) // 128) + j)
            projector = beta[pl.ds(j, 128, stride=8), :]
            terms = terms + mm(weight[span], wide) * jnp.concatenate([projector, projector], 1)
        high, low = split(terms)
        rows[span, 0:256] = high
        rows[span, 256:512] = low
    both = mm(put[...], rows[...])
    nonloc = both[:, :256] + both[:, 256:]
    kinds = []
    for k in range(3):
        at = slice(288 * k, 288 * k + 288)
        factor = vloc[at, :]
        kinds.append(split(field[at, :] * jnp.concatenate([factor, factor], 1) + nonloc[at, :]))
    g = []
    for parity in range(2):
        table = [fx[1024 * parity + 512 * i : 1024 * parity + 512 * i + 512, :] for i in range(2)]
        lines = [jnp.concatenate([kinds[parity][i], kinds[parity + 1][i]], 1) for i in range(2)]
        g.append(split(three(mm, lines, table)))
    lines = [
        jnp.concatenate(
            [
                jnp.concatenate(
                    [
                        g[parity][i][96 * zi : 96 * zi + 96, 128 * c : 128 * c + 128]
                        for zi in range(3)
                    ],
                    1,
                )
                for c in range(2)
                for parity in range(2)
            ],
            0,
        )
        for i in range(2)
    ]
    h = three(mm, (fy[0:256, :], fy[256:512, :]), lines)
    main, spare, _ = masks_sp()
    spares = [jnp.zeros((64, 128), F32), jnp.zeros((64, 128), F32)]
    for zi in range(3):
        for c in range(2):
            turned = h[128 * c : 128 * c + 128, 128 * zi : 128 * zi + 128].T
            first = turned[:64]
            second = pltpu.roll(turned[64:], 64, 1)
            send[pl.ds(3 * c + zi, 64, stride=7), :] = jnp.where(main, first, second)
            high, low = split(jnp.where(spare, first, 0.0))
            move = ut[128 * zi : 128 * zi + 128, :]
            spares[c] = spares[c] + (mm(high, move) + mm(low, move))
    send[pl.ds(6, 64, stride=7), :] = spares[0] + pltpu.roll(spares[1], 64, 1)


def kernel_z_forward(recv, fz, result, out, sems):
    s = lax.axis_index("fft")
    out[...] = jnp.zeros((1728, 128), F32)
    spans = [(152, 280), (576, 576), (1304, 280), (0, 152), (432, 144), (1152, 152), (1584, 144)]
    copies = [
        pltpu.make_async_copy(out.at[pl.ds(*span)], result.at[pl.ds(*span)], sems.at[k])
        for k, span in enumerate(spans)
    ]
    for copy in copies[:3]:
        copy.start()
    r = iota((256, 1), 0)
    main, spare = line_places(r, s)
    lane = iota((256, 128), 1)
    keep = one_hot(lane == main)
    spares = recv[pl.ds(6, 64, stride=7), :]
    spares = (spares, pltpu.roll(spares, 64, 1))
    highs, lows = [], []
    for zi in range(3):
        unpack = jnp.concatenate(
            [keep, one_hot((lane == spare + 16 * zi) & (spare >= 0))], 1
        )
        lines = jnp.concatenate(
            [
                jnp.concatenate(
                    [
                        recv[pl.ds(3 * c + zi, 64, stride=7), :],
                        spares[c],
                    ],
                    1,
                )
                for c in range(2)
            ],
            0,
        )
        high, low = split(lines)
        columns = mm_nt(unpack, jnp.concatenate([high, low], 0))
        highs.append(columns[:, :128].astype(BF))
        lows.append(columns[:, 128:].astype(BF))
    z = three(
        mm, (jnp.concatenate(highs, 1), jnp.concatenate(lows, 1)), (fz[0:384, :], fz[384:768, :])
    )
    low_lane = iota((64, 128), 1) < 64
    for plane in range(2):
        for c in range(2):
            block = z[128 * plane : 128 * plane + 128, 128 * c : 128 * c + 128]
            even = jnp.where(sphere_rows(plane, 0, s), block[:64], 0.0)
            odd = jnp.where(sphere_rows(plane, 1, s), block[64:], 0.0)
            kinds = (
                jnp.where(low_lane, even, 0.0),
                pltpu.roll(jnp.where(low_lane, odd, even), 64, 1),
                jnp.where(low_lane, 0.0, odd),
            )
            for k, tile in enumerate(kinds):
                at = 1152 * plane + 2 * k + c
                out[pl.ds(at, 25, stride=6), :] = tile[24:49]
                out[pl.ds(at + 432, 24, stride=6), :] = tile[:24]
        copies[3 + 2 * plane].start()
        copies[4 + 2 * plane].start()
    for copy in copies:
        copy.wait()


def call(kernel, name, out_shape, args, scratch=(), anywhere=(), anywhere_out=(), limit=VMEM_LIMIT, cost=None):
    specs = [
        pl.BlockSpec(memory_space=pl.ANY if k in anywhere else pltpu.VMEM)
        for k in range(len(args))
    ]
    shapes = [
        jax.ShapeDtypeStruct(*shape) if isinstance(shape[0], tuple) else jax.ShapeDtypeStruct(shape, F32)
        for shape in out_shape
    ]
    out = pl.pallas_call(
        kernel,
        name=name,
        out_shape=shapes,
        in_specs=specs,
        out_specs=[
            pl.BlockSpec(memory_space=pl.ANY if k in anywhere_out else pltpu.VMEM)
            for k in range(len(shapes))
        ],
        scratch_shapes=list(scratch),
        cost_estimate=cost,
        compiler_params=pltpu.CompilerParams(vmem_limit_bytes=limit),
    )(*args)
    return out


def body(psi_g, vloc, beta, blk_slot, blk_tile, dmat):
    t = {
        name: jnp.asarray(value) for name, value in tables().items()
    }
    psi = psi_g[0].transpose(1, 0, 2).reshape(3, 2, 288, 128).transpose(0, 2, 1, 3)
    psi = psi.reshape(1728, 128)
    def from_band(x, k):
        return lax.ppermute(x, "band", [(i, (i + k) % 4) for i in range(4)])

    ids = jnp.concatenate([blk_slot[None], blk_tile[None], jnp.zeros((6, 128), jnp.int32)], 0)
    own = jnp.concatenate([beta, ids.astype(F32)[None]], 0).reshape(1032, 128)
    (send,) = call(kernel_z_inverse, "z_inverse", [(448, 128)], (psi, t["wz"]))
    own_later, send = lax.optimization_barrier((own, send))
    betas = [own, from_band(own, 2), from_band(own, 3), from_band(own_later, 1)]

    def exchange(x):
        x = lax.all_to_all(x.reshape(64, 1, 896), "fft", 0, 0, tiled=True)
        return x.reshape(448, 128)

    recv = exchange(send)
    vloc_tiles = vloc.reshape(3, 288, 128).transpose(1, 0, 2)
    dmat_rows = dmat.transpose(1, 2, 0).reshape(64, 64)
    field, rows_h, rows_l = call(
        kernel_field,
        "field",
        [(864, 256), ((896, 256), BF), ((896, 256), BF)],
        (recv, t["ey"], t["ix"], t["u"]),
    )
    coef, slots, tiles = call(
        kernel_project,
        "project",
        [(16, 256), ((384, 256), BF), ((1, 384), jnp.int32)],
        (rows_h, rows_l, *betas[:3]),
        [pltpu.VMEM((384, 256), F32)],
    )
    near, slots_last, tiles_last = call(
        kernel_project_last,
        "project_last",
        [(96, 128), ((128, 256), BF), ((1, 128), jnp.int32)],
        (rows_h, rows_l, dmat_rows, coef, betas[3]),
        [pltpu.VMEM((128, 256), F32)],
    )
    other = lax.ppermute(near, "fft", [(i, i ^ 1) for i in range(64)])
    first, second = call(kernel_merge, "merge", [(80, 128), (80, 128)], (near, other))
    first = lax.ppermute(first, "fft", [(i, i ^ 2) for i in range(64)])
    second = lax.ppermute(second, "fft", [(i, (((i + 2) % 64) ^ 2) - 2 & 63) for i in range(64)])
    put, vloc_rows = call(
        kernel_put,
        "put",
        [((864, 512), BF), (864, 128)],
        (tiles, tiles_last, vloc_tiles),
        [pltpu.VMEM((3, 288, 128), F32), pltpu.SemaphoreType.DMA((3,))],
        anywhere=(2,),
        cost=pl.CostEstimate(flops=2000000, bytes_accessed=3000000, transcendentals=0),
    )
    (send,) = call(
        kernel_back,
        "back",
        [(448, 128)],
        (field, near, other, second, first, slots, slots_last, put, *betas, vloc_rows, t["fx"], t["fy"], t["ut"]),
        [
            pltpu.VMEM((16, 256), F32),
            pltpu.VMEM((512, 512), BF),
        ],
    )
    (out,) = call(kernel_z_forward, "z_forward", [(1728, 128)], (exchange(send), t["fz"]),
        [pltpu.VMEM((1728, 128), F32), pltpu.SemaphoreType.DMA((7,))], anywhere_out=(0,))
    out = out.reshape(3, 288, 2, 128).transpose(0, 2, 1, 3).reshape(3, 2, N * N)
    return out.transpose(1, 0, 2)[None]


def solution(mesh):
    in_specs = (
        P("band", None, "fft", None),
        P("fft", None),
        P(("fft", "band"), None, None),
        P(("fft", "band")),
        P(("fft", "band")),
        P("fft", None, None),
    )
    out_specs = P("band", None, "fft", None)
    return jax.shard_map(body, mesh=mesh, in_specs=in_specs, out_specs=out_specs, check_vma=False)
```

```python
import functools

import jax
import jax.numpy as jnp
import ml_dtypes
import numpy as np
from jax import lax
from jax.experimental import pallas as pl
from jax.experimental.pallas import tpu as pltpu
from jax.sharding import PartitionSpec as P

N = 192
R2 = 48 * 48
BF = jnp.bfloat16
F32 = jnp.float32
VMEM_LIMIT = 32 * 1024 * 1024


def trig(freqs, points):
    angle = 2.0 * np.pi * (np.outer(freqs, points) % N) / N
    return np.cos(angle) / np.sqrt(N), np.sin(angle) / np.sqrt(N)


def pair_of(table):
    table = np.asarray(table, np.float32)
    high = table.astype(ml_dtypes.bfloat16)
    low = (table - high.astype(np.float32)).astype(ml_dtypes.bfloat16)
    return np.concatenate([high, low], 0)


KZ = np.concatenate([np.arange(64), np.arange(128, 192)])
SIGNED = np.concatenate([np.arange(64), np.arange(-64, 0)])
YS = [2 * np.arange(96), 2 * np.arange(96) + 1]


@functools.cache
def tables():
    t = {}
    blocks = []
    for zi in range(3):
        c, s = trig(3 * np.arange(64) + zi, KZ)
        blocks += [np.concatenate([c, -s], 1), np.concatenate([s, c], 1)]
    t["wz"] = pair_of(np.concatenate(blocks, 0))
    c, s = trig(np.concatenate(YS), SIGNED)
    t["ey"] = pair_of(
        np.concatenate([np.concatenate([c, -s], 1), np.concatenate([s, c], 1)], 0)
    )
    c, s = trig(SIGNED, np.arange(N))
    gap = np.zeros((128, 64))
    even = [np.concatenate([v, gap], 1) for v in (c, s, -s, c)]
    odd = [np.concatenate([gap, v], 1) for v in (c, s, -s, c)]
    t["ix"] = np.concatenate(
        [
            pair_of(np.block([[even[0], even[1]], [even[2], even[3]]])),
            pair_of(np.block([[odd[0], odd[1]], [odd[2], odd[3]]])),
        ],
        0,
    )
    parts = {}
    c, s = trig(np.arange(N), SIGNED)
    gap = np.zeros((64, 128))
    for name, table in (("c", c), ("s", s)):
        parts[name] = (np.concatenate([table, gap], 0), np.concatenate([gap, table], 0))

    def forward_x(which):
        cc, ss = parts["c"][which], parts["s"][which]
        first, second = np.concatenate([cc, -ss], 1), np.concatenate([ss, cc], 1)
        return np.concatenate([first[:128], second[:128], first[128:], second[128:]], 0)

    t["fx"] = np.concatenate([pair_of(forward_x(0)), pair_of(forward_x(1))], 0)
    c, s = trig(SIGNED, np.concatenate(YS))
    t["fy"] = pair_of(
        np.concatenate([np.concatenate([c, s], 1), np.concatenate([-s, c], 1)], 0)
    )
    blocks = []
    for zi in range(3):
        c, s = trig(3 * np.arange(64) + zi, KZ)
        blocks += [np.concatenate([c, -s], 1), np.concatenate([s, c], 1)]
    t["fz"] = pair_of(np.concatenate(blocks, 0))
    u = np.zeros((128, 384), np.float32)
    for zi in range(3):
        for p in range(128):
            u[16 * zi + 8 * (p >= 64) + p % 8, 128 * zi + p] = 1.0
    t["u"] = u.astype(ml_dtypes.bfloat16)
    t["ut"] = np.concatenate([u[:, 128 * zi : 128 * zi + 128].T for zi in range(3)], 0).astype(
        ml_dtypes.bfloat16
    )
    return t


def split(x):
    high = x.astype(BF)
    return high, (x - high.astype(F32)).astype(BF)


def mm(a, b):
    return jnp.dot(a, b, preferred_element_type=F32)


def mm_nt(a, b):
    return lax.dot_general(a, b, (((1,), (1,)), ((), ())), preferred_element_type=F32)


def three(product, a, b):
    return product(a[0], b[0]) + (product(a[0], b[1]) + product(a[1], b[0]))


def iota(shape, dim):
    return lax.broadcasted_iota(jnp.int32, shape, dim)


def masks_sp():
    s, p = iota((64, 128), 0), iota((64, 128), 1)
    ky = jnp.where(p < 64, p, p - 128)
    away = 64 - jnp.abs(ky)
    inside = ky * ky + s * s <= R2
    clash = away * away + (64 - s) * (64 - s) <= R2
    other = (p - 64) * (p - 64) + (64 - s) * (64 - s) <= R2
    return inside & ~clash, inside & clash, other


def line_places(r, s):
    plane, rest = r // 128, r % 128
    ky = 2 * (rest % 64 - 24) + rest // 64
    here = jnp.where(plane == 0, s, 64 - s)
    away = 64 - jnp.abs(ky)
    inside = ky * ky + here * here <= R2
    clash = (away * away + (64 - s) * (64 - s) <= R2) & (plane == 0)
    place = jnp.where(plane == 0, jnp.where(ky < 0, ky + 128, ky), ky + 64)
    main = jnp.where(inside & ~clash, place, -1)
    spare = jnp.where(inside & clash, jnp.where(ky < 0, 8, 0) + (ky + 64) % 8, -1)
    return main, spare


def one_hot(condition):
    return jnp.where(condition, 1.0, 0.0).astype(BF)


def sphere_rows(plane, parity, s):
    m, lane = iota((64, 128), 0), iota((64, 128), 1)
    ky = 2 * (m - 24) + parity
    kz = jnp.where(lane < 64, lane, lane - 128)
    kx = s - 64 * plane
    return ky * ky + kz * kz + kx * kx <= R2


def kernel_z_inverse(psi, wz, send):
    s = lax.axis_index("fft")
    main, spare = line_places(iota((1, 256), 1), s)
    j = iota((128, 256), 0)
    pack = jnp.concatenate(
        [one_hot(j == main), one_hot((j % 16 == spare) & (j % 64 < 48))], axis=0
    )
    lane = iota((64, 128), 1)
    rows = []
    for plane in range(2):
        lines = [[], []]
        for c in range(2):
            at = 1152 * plane + c
            t = [
                jnp.concatenate(
                    [
                        psi[pl.ds(at + 432 + 2 * k, 24, stride=6), :],
                        psi[pl.ds(at + 2 * k, 40, stride=6), :],
                    ],
                    0,
                )
                for k in range(3)
            ]
            middle = pltpu.roll(t[1], 64, 1)
            even = jnp.where(lane < 64, t[0], middle)
            odd = jnp.where(lane < 64, middle, t[2])
            lines[0].append(jnp.where(sphere_rows(plane, 0, s), even, 0.0))
            lines[1].append(jnp.where(sphere_rows(plane, 1, s), odd, 0.0))
        rows += [jnp.concatenate(lines[0], 1), jnp.concatenate(lines[1], 1)]
    high, low = split(jnp.concatenate(rows, 0))
    packed = (mm(pack, high).astype(BF), mm(pack, low).astype(BF))
    out = three(mm_nt, (wz[0:384, :], wz[384:768, :]), packed)
    spares = out[0:64, 128:]
    for c in range(2):
        for zi in range(3):
            block = out[(2 * zi + c) * 64 : (2 * zi + c) * 64 + 64]
            send[pl.ds(3 * c + zi, 64, stride=7), :] = block[:, :128]
            spares = jnp.where(lane // 16 == 4 * c + zi, block[:, 128:], spares)
    send[pl.ds(6, 64, stride=7), :] = spares


def tile_rows(tiles):
    return (tiles % 3) * 288 + tiles // 3


def as_column(ids):
    return jnp.broadcast_to(ids.astype(F32), (8, ids.shape[1])).T[:, 0:1].astype(jnp.int32)


def kernel_field(
    recv, ey, ix, u, field, rows_h, rows_l,
):
    main, spare, other = masks_sp()
    spread = []
    for c in range(2):
        got = recv[pl.ds(6, 64, stride=7), :]
        high, low = split(pltpu.roll(got, 64, 1) if c else got)
        spread.append(mm(high, u[...]) + mm(low, u[...]))
    lines = []
    for zi in range(3):
        first, second = [], []
        for c in range(2):
            got = recv[pl.ds(3 * c + zi, 64, stride=7), :]
            extra = spread[c][:, 128 * zi : 128 * zi + 128]
            first.append(jnp.where(main, got, jnp.where(spare, extra, 0.0)))
            second.append(pltpu.roll(jnp.where(other, got, 0.0), 64, 1))
        lines += [jnp.concatenate(first, 1), jnp.concatenate(second, 1)]
    g = three(mm_nt, (ey[0:384, :], ey[384:768, :]), split(jnp.concatenate(lines, 0)))
    out = []
    for parity in range(2):
        a = 96 * parity
        table = [ix[512 * parity + 256 * i : 512 * parity + 256 * i + 256, :] for i in range(2)]
        block = jnp.concatenate(
            [
                jnp.concatenate(
                    [
                        g[a : a + 96, 128 * zi : 128 * zi + 128],
                        g[192 + a : 288 + a, 128 * zi : 128 * zi + 128],
                    ],
                    1,
                )
                for zi in range(3)
            ],
            0,
        )
        out.append(three(mm, split(block), table))
    even, odd = out
    for c in range(2):
        a = 256 * c
        kinds = (
            even[:, a : a + 128],
            even[:, a + 128 : a + 256] + odd[:, a : a + 128],
            odd[:, a + 128 : a + 256],
        )
        for k, tile in enumerate(kinds):
            span = pl.ds(288 * k, 288)
            lanes = pl.ds(128 * c, 128)
            field[span, lanes] = tile
            high, low = split(tile)
            rows_h[span, lanes] = high
            rows_l[span, lanes] = low
    rows_h[864:896, :] = jnp.zeros((32, 256), BF)
    rows_l[864:896, :] = jnp.zeros((32, 256), BF)


def project(quarters, rows_h, rows_l, tile_of, slots, betas, field_rows):
    count = 128 * quarters
    pick = one_hot(as_column(tile_of) == iota((count, 896), 1))
    field_rows[...] = mm(pick, rows_h[...]) + mm(pick, rows_l[...])
    lane = iota((128, 128), 1)
    sums = []
    for k, beta in enumerate(betas):
        total = jnp.zeros((128, 128), F32)
        for j in range(8):
            projector = beta[pl.ds(j, 128, stride=8), :]
            for c in range(2):
                value = field_rows[128 * k : 128 * k + 128, 128 * c : 128 * c + 128] * projector
                total = jnp.where(
                    lane == 8 * c + j, jnp.sum(value, axis=1, keepdims=True), total
                )
        sums.append(total.T[:16])
    high, low = split(jnp.concatenate(sums, 1))
    return mm(high, slots) + mm(low, slots)


def ids_of(betas, row):
    return jnp.concatenate([b[1024 + row : 1025 + row, :] for b in betas], 1).astype(jnp.int32)


def kernel_project(rows_h, rows_l, b0, b1, b2, coef, slots_out, tiles_out, field_rows):
    betas = (b0, b1, b2)
    tile_of = tile_rows(ids_of(betas, 1))
    tiles_out[...] = tile_of
    slots = one_hot(as_column(ids_of(betas, 0)) == iota((384, 256), 1))
    slots_out[...] = slots
    coef[...] = project(3, rows_h, rows_l, tile_of, slots, betas, field_rows)


def kernel_project_last(rows_h, rows_l, dmat, coef_in, b3, near, slots_out, tiles_out, field_rows):
    tile_of = tile_rows(ids_of((b3,), 1))
    tiles_out[...] = tile_of
    slots = one_hot(as_column(ids_of((b3,), 0)) == iota((128, 256), 1))
    slots_out[...] = slots
    coef = coef_in[...] + project(1, rows_h, rows_l, tile_of, slots, (b3,), field_rows)
    coef = jnp.where(iota((16, 256), 1) < 192, coef, 0.0)
    near[0:64, :] = jnp.concatenate([dmat[...], jnp.zeros((64, 64), F32)], 1)
    near[64:80, :] = coef[:, :128]
    near[80:96, :] = coef[:, 128:]


def chip_of(own, other):
    f = lax.axis_index("fft")
    core = f % 2
    own, other = own[...], other[...]
    return (
        core,
        (f // 2) % 2 == 0,
        jnp.where(core == 0, own, other),
        jnp.where(core == 0, other, own),
    )


def kernel_merge(own, other, first, second):
    _, even, a, b = chip_of(own, other)
    low_lane = iota((16, 128), 1) < 64
    turned = pltpu.roll(b[64:80], 64, 1)
    up = jnp.where(low_lane, a[80:96] + turned, pltpu.roll(b[80:96], 64, 1))
    down = jnp.where(low_lane, a[64:80], a[64:80] + turned)
    up = jnp.concatenate([b[0:64], up], 0)
    down = jnp.concatenate([a[0:64], down], 0)
    first[...] = jnp.where(even, up, down)
    second[...] = jnp.where(even, down, up)


def kernel_put(tiles, tiles_last, vloc_in, put, vloc_out, vloc, sems):
    copies = [
        pltpu.make_async_copy(vloc_in.at[:, zi, :], vloc.at[zi], sems.at[zi]) for zi in range(3)
    ]
    for copy in copies:
        copy.start()
    tile_of = jnp.concatenate([tiles[...], tiles_last[...]], 1)
    put[...] = one_hot(iota((864, 512), 0) == tile_of)
    for copy in copies:
        copy.wait()
    for k in range(3):
        for zi in range(3):
            at = 288 * k + 96 * zi
            vloc_out[at : at + 96, :] = vloc[zi, pl.ds(k, 96, stride=3), :]


def kernel_back(
    field, own, other, second, first, slots, slots_last, put, b0, b1, b2, b3,
    vloc, fx, fy, ut, send, scr, rows,
):
    core, even, a, b = chip_of(own, other)
    above = jnp.where(even, first[...], second[...])
    below = jnp.where(even, second[...], first[...])
    low_lane = iota((16, 128), 1) < 64
    turned = pltpu.roll(b[64:80], 64, 1)
    tot = [
        below[64:80] + jnp.where(low_lane, a[64:80], a[64:80] + turned),
        above[64:80] + jnp.where(low_lane, a[80:96] + turned, pltpu.roll(b[80:96], 64, 1)),
    ]
    wide = iota((64, 128), 1) < 64
    coupling = [
        jnp.where(wide, below[0:64], pltpu.roll(a[0:64], 64, 1)),
        jnp.where(wide, b[0:64], pltpu.roll(above[0:64], 64, 1)),
    ]
    for h in range(2):
        for c in range(2):
            coef = tot[h][8 * c : 8 * c + 8, :]
            for j in range(8):
                row = jnp.sum(coupling[h][8 * j : 8 * j + 8, :] * coef, axis=0, keepdims=True)
                scr[8 * c + j : 8 * c + j + 1, 128 * h : 128 * h + 128] = row
    betas = (b0, b1, b2, b3)
    left, right = scr[:, :128], scr[:, 128:]
    left_turned, right_turned = pltpu.roll(left, 64, 1), pltpu.roll(right, 64, 1)
    left = jnp.where(core == 0, left, jnp.where(low_lane, left_turned, right_turned))
    right = jnp.where(low_lane, jnp.where(core == 0, right, right_turned), 0.0)
    high, low = split(jnp.concatenate([left, right], 1))
    weight = jnp.concatenate(
        [mm_nt(hot[...], high) + mm_nt(hot[...], low) for hot in (slots, slots_last)], 0
    )
    high, low = split(weight)
    weight = jnp.concatenate([high, low], 1)
    for k, beta in enumerate(betas):
        span = slice(128 * k, 128 * k + 128)
        terms = jnp.zeros((128, 256), F32)
        for j in range(8):
            wide = one_hot(iota((32, 256), 0) % 16 == 8 * (iota((32, 256), 1) // 128) + j)
            projector = beta[pl.ds(j, 128, stride=8), :]
            terms = terms + mm(weight[span], wide) * jnp.concatenate([projector, projector], 1)
        high, low = split(terms)
        rows[span, 0:256] = high
        rows[span, 256:512] = low
    both = mm(put[...], rows[...])
    nonloc = both[:, :256] + both[:, 256:]
    kinds = []
    for k in range(3):
        at = slice(288 * k, 288 * k + 288)
        factor = vloc[at, :]
        kinds.append(split(field[at, :] * jnp.concatenate([factor, factor], 1) + nonloc[at, :]))
    g = []
    for parity in range(2):
        table = [fx[1024 * parity + 512 * i : 1024 * parity + 512 * i + 512, :] for i in range(2)]
        lines = [jnp.concatenate([kinds[parity][i], kinds[parity + 1][i]], 1) for i in range(2)]
        g.append(split(three(mm, lines, table)))
    lines = [
        jnp.concatenate(
            [
                jnp.concatenate(
                    [
                        g[parity][i][96 * zi : 96 * zi + 96, 128 * c : 128 * c + 128]
                        for zi in range(3)
                    ],
                    1,
                )
                for c in range(2)
                for parity in range(2)
            ],
            0,
        )
        for i in range(2)
    ]
    h = three(mm, (fy[0:256, :], fy[256:512, :]), lines)
    main, spare, _ = masks_sp()
    spares = [jnp.zeros((64, 128), F32), jnp.zeros((64, 128), F32)]
    for zi in range(3):
        for c in range(2):
            turned = h[128 * c : 128 * c + 128, 128 * zi : 128 * zi + 128].T
            first = turned[:64]
            second = pltpu.roll(turned[64:], 64, 1)
            send[pl.ds(3 * c + zi, 64, stride=7), :] = jnp.where(main, first, second)
            high, low = split(jnp.where(spare, first, 0.0))
            move = ut[128 * zi : 128 * zi + 128, :]
            spares[c] = spares[c] + (mm(high, move) + mm(low, move))
    send[pl.ds(6, 64, stride=7), :] = spares[0] + pltpu.roll(spares[1], 64, 1)


def kernel_z_forward(recv, fz, result, out, sems):
    s = lax.axis_index("fft")
    out[...] = jnp.zeros((1728, 128), F32)
    spans = [(152, 280), (576, 576), (1304, 280), (0, 152), (432, 144), (1152, 152), (1584, 144)]
    copies = [
        pltpu.make_async_copy(out.at[pl.ds(*span)], result.at[pl.ds(*span)], sems.at[k])
        for k, span in enumerate(spans)
    ]
    for copy in copies[:3]:
        copy.start()
    r = iota((256, 1), 0)
    main, spare = line_places(r, s)
    lane = iota((256, 128), 1)
    keep = one_hot(lane == main)
    spares = recv[pl.ds(6, 64, stride=7), :]
    spares = (spares, pltpu.roll(spares, 64, 1))
    highs, lows = [], []
    for zi in range(3):
        unpack = jnp.concatenate(
            [keep, one_hot((lane == spare + 16 * zi) & (spare >= 0))], 1
        )
        lines = jnp.concatenate(
            [
                jnp.concatenate(
                    [
                        recv[pl.ds(3 * c + zi, 64, stride=7), :],
                        spares[c],
                    ],
                    1,
                )
                for c in range(2)
            ],
            0,
        )
        high, low = split(lines)
        columns = mm_nt(unpack, jnp.concatenate([high, low], 0))
        highs.append(columns[:, :128].astype(BF))
        lows.append(columns[:, 128:].astype(BF))
    z = three(
        mm, (jnp.concatenate(highs, 1), jnp.concatenate(lows, 1)), (fz[0:384, :], fz[384:768, :])
    )
    low_lane = iota((64, 128), 1) < 64
    for plane in range(2):
        for c in range(2):
            block = z[128 * plane : 128 * plane + 128, 128 * c : 128 * c + 128]
            even = jnp.where(sphere_rows(plane, 0, s), block[:64], 0.0)
            odd = jnp.where(sphere_rows(plane, 1, s), block[64:], 0.0)
            kinds = (
                jnp.where(low_lane, even, 0.0),
                pltpu.roll(jnp.where(low_lane, odd, even), 64, 1),
                jnp.where(low_lane, 0.0, odd),
            )
            for k, tile in enumerate(kinds):
                at = 1152 * plane + 2 * k + c
                out[pl.ds(at, 25, stride=6), :] = tile[24:49]
                out[pl.ds(at + 432, 24, stride=6), :] = tile[:24]
        copies[3 + 2 * plane].start()
        copies[4 + 2 * plane].start()
    for copy in copies:
        copy.wait()


def call(kernel, name, out_shape, args, scratch=(), anywhere=(), anywhere_out=(), limit=VMEM_LIMIT, cost=None):
    specs = [
        pl.BlockSpec(memory_space=pl.ANY if k in anywhere else pltpu.VMEM)
        for k in range(len(args))
    ]
    shapes = [
        jax.ShapeDtypeStruct(*shape) if isinstance(shape[0], tuple) else jax.ShapeDtypeStruct(shape, F32)
        for shape in out_shape
    ]
    out = pl.pallas_call(
        kernel,
        name=name,
        out_shape=shapes,
        in_specs=specs,
        out_specs=[
            pl.BlockSpec(memory_space=pl.ANY if k in anywhere_out else pltpu.VMEM)
            for k in range(len(shapes))
        ],
        scratch_shapes=list(scratch),
        cost_estimate=cost,
        compiler_params=pltpu.CompilerParams(vmem_limit_bytes=limit),
    )(*args)
    return out


def body(psi_g, vloc, beta, blk_slot, blk_tile, dmat):
    t = {
        name: jnp.asarray(value) for name, value in tables().items()
    }
    psi = psi_g[0].transpose(1, 0, 2).reshape(3, 2, 288, 128).transpose(0, 2, 1, 3)
    psi = psi.reshape(1728, 128)
    def from_band(x, k):
        return lax.ppermute(x, "band", [(i, (i + k) % 4) for i in range(4)])

    ids = jnp.concatenate([blk_slot[None], blk_tile[None], jnp.zeros((6, 128), jnp.int32)], 0)
    own = jnp.concatenate([beta, ids.astype(F32)[None]], 0).reshape(1032, 128)
    (send,) = call(kernel_z_inverse, "z_inverse", [(448, 128)], (psi, t["wz"]))
    betas = [own, from_band(own, 2), from_band(own, 3), from_band(own, 1)]

    def exchange(x):
        x = lax.all_to_all(x.reshape(64, 1, 896), "fft", 0, 0, tiled=True)
        return x.reshape(448, 128)

    recv = exchange(send)
    vloc_tiles = vloc.reshape(3, 288, 128).transpose(1, 0, 2)
    dmat_rows = dmat.transpose(1, 2, 0).reshape(64, 64)
    field, rows_h, rows_l = call(
        kernel_field,
        "field",
        [(864, 256), ((896, 256), BF), ((896, 256), BF)],
        (recv, t["ey"], t["ix"], t["u"]),
    )
    coef, slots, tiles = call(
        kernel_project,
        "project",
        [(16, 256), ((384, 256), BF), ((1, 384), jnp.int32)],
        (rows_h, rows_l, *betas[:3]),
        [pltpu.VMEM((384, 256), F32)],
    )
    near, slots_last, tiles_last = call(
        kernel_project_last,
        "project_last",
        [(96, 128), ((128, 256), BF), ((1, 128), jnp.int32)],
        (rows_h, rows_l, dmat_rows, coef, betas[3]),
        [pltpu.VMEM((128, 256), F32)],
    )
    other = lax.ppermute(near, "fft", [(i, i ^ 1) for i in range(64)])
    first, second = call(kernel_merge, "merge", [(80, 128), (80, 128)], (near, other))
    first = lax.ppermute(first, "fft", [(i, i ^ 2) for i in range(64)])
    second = lax.ppermute(second, "fft", [(i, (((i + 2) % 64) ^ 2) - 2 & 63) for i in range(64)])
    put, vloc_rows = call(
        kernel_put,
        "put",
        [((864, 512), BF), (864, 128)],
        (tiles, tiles_last, vloc_tiles),
        [pltpu.VMEM((3, 288, 128), F32), pltpu.SemaphoreType.DMA((3,))],
        anywhere=(2,),
        cost=pl.CostEstimate(flops=2000000, bytes_accessed=3000000, transcendentals=0),
    )
    (send,) = call(
        kernel_back,
        "back",
        [(448, 128)],
        (field, near, other, second, first, slots, slots_last, put, *betas, vloc_rows, t["fx"], t["fy"], t["ut"]),
        [
            pltpu.VMEM((16, 256), F32),
            pltpu.VMEM((512, 512), BF),
        ],
    )
    (out,) = call(kernel_z_forward, "z_forward", [(1728, 128)], (exchange(send), t["fz"]),
        [pltpu.VMEM((1728, 128), F32), pltpu.SemaphoreType.DMA((7,))], anywhere_out=(0,))
    out = out.reshape(3, 288, 2, 128).transpose(0, 2, 1, 3).reshape(3, 2, N * N)
    return out.transpose(1, 0, 2)[None]


def solution(mesh):
    in_specs = (
        P("band", None, "fft", None),
        P("fft", None),
        P(("fft", "band"), None, None),
        P(("fft", "band")),
        P(("fft", "band")),
        P("fft", None, None),
    )
    out_specs = P("band", None, "fft", None)
    return jax.shard_map(body, mesh=mesh, in_specs=in_specs, out_specs=out_specs, check_vma=False)
```

```python
import functools

import jax
import jax.numpy as jnp
import ml_dtypes
import numpy as np
from jax import lax
from jax.experimental import pallas as pl
from jax.experimental.pallas import tpu as pltpu
from jax.sharding import PartitionSpec as P

N = 192
R2 = 48 * 48
BF = jnp.bfloat16
F32 = jnp.float32
VMEM_LIMIT = 32 * 1024 * 1024


def trig(freqs, points):
    angle = 2.0 * np.pi * (np.outer(freqs, points) % N) / N
    return np.cos(angle) / np.sqrt(N), np.sin(angle) / np.sqrt(N)


def pair_of(table):
    table = np.asarray(table, np.float32)
    high = table.astype(ml_dtypes.bfloat16)
    low = (table - high.astype(np.float32)).astype(ml_dtypes.bfloat16)
    return np.concatenate([high, low], 0)


KZ = np.concatenate([np.arange(64), np.arange(128, 192)])
SIGNED = np.concatenate([np.arange(64), np.arange(-64, 0)])
YS = [2 * np.arange(96), 2 * np.arange(96) + 1]


@functools.cache
def tables():
    t = {}
    blocks = []
    for zi in range(3):
        c, s = trig(3 * np.arange(64) + zi, KZ)
        blocks += [np.concatenate([c, -s], 1), np.concatenate([s, c], 1)]
    t["wz"] = pair_of(np.concatenate(blocks, 0))
    c, s = trig(np.concatenate(YS), SIGNED)
    t["ey"] = pair_of(
        np.concatenate([np.concatenate([c, -s], 1), np.concatenate([s, c], 1)], 0)
    )
    c, s = trig(SIGNED, np.arange(N))
    gap = np.zeros((128, 64))
    even = [np.concatenate([v, gap], 1) for v in (c, s, -s, c)]
    odd = [np.concatenate([gap, v], 1) for v in (c, s, -s, c)]
    t["ix"] = np.concatenate(
        [
            pair_of(np.block([[even[0], even[1]], [even[2], even[3]]])),
            pair_of(np.block([[odd[0], odd[1]], [odd[2], odd[3]]])),
        ],
        0,
    )
    parts = {}
    c, s = trig(np.arange(N), SIGNED)
    gap = np.zeros((64, 128))
    for name, table in (("c", c), ("s", s)):
        parts[name] = (np.concatenate([table, gap], 0), np.concatenate([gap, table], 0))

    def forward_x(which):
        cc, ss = parts["c"][which], parts["s"][which]
        first, second = np.concatenate([cc, -ss], 1), np.concatenate([ss, cc], 1)
        return np.concatenate([first[:128], second[:128], first[128:], second[128:]], 0)

    t["fx"] = np.concatenate([pair_of(forward_x(0)), pair_of(forward_x(1))], 0)
    c, s = trig(SIGNED, np.concatenate(YS))
    t["fy"] = pair_of(
        np.concatenate([np.concatenate([c, s], 1), np.concatenate([-s, c], 1)], 0)
    )
    blocks = []
    for zi in range(3):
        c, s = trig(3 * np.arange(64) + zi, KZ)
        blocks += [np.concatenate([c, -s], 1), np.concatenate([s, c], 1)]
    t["fz"] = pair_of(np.concatenate(blocks, 0))
    u = np.zeros((128, 384), np.float32)
    for zi in range(3):
        for p in range(128):
            u[16 * zi + 8 * (p >= 64) + p % 8, 128 * zi + p] = 1.0
    t["u"] = u.astype(ml_dtypes.bfloat16)
    t["ut"] = np.concatenate([u[:, 128 * zi : 128 * zi + 128].T for zi in range(3)], 0).astype(
        ml_dtypes.bfloat16
    )
    return t


def split(x):
    high = x.astype(BF)
    return high, (x - high.astype(F32)).astype(BF)


def mm(a, b):
    return jnp.dot(a, b, preferred_element_type=F32)


def mm_nt(a, b):
    return lax.dot_general(a, b, (((1,), (1,)), ((), ())), preferred_element_type=F32)


def three(product, a, b):
    return product(a[0], b[0]) + (product(a[0], b[1]) + product(a[1], b[0]))


def iota(shape, dim):
    return lax.broadcasted_iota(jnp.int32, shape, dim)


def masks_sp():
    s, p = iota((64, 128), 0), iota((64, 128), 1)
    ky = jnp.where(p < 64, p, p - 128)
    away = 64 - jnp.abs(ky)
    inside = ky * ky + s * s <= R2
    clash = away * away + (64 - s) * (64 - s) <= R2
    other = (p - 64) * (p - 64) + (64 - s) * (64 - s) <= R2
    return inside & ~clash, inside & clash, other


def line_places(r, s):
    plane, rest = r // 128, r % 128
    ky = 2 * (rest % 64 - 24) + rest // 64
    here = jnp.where(plane == 0, s, 64 - s)
    away = 64 - jnp.abs(ky)
    inside = ky * ky + here * here <= R2
    clash = (away * away + (64 - s) * (64 - s) <= R2) & (plane == 0)
    place = jnp.where(plane == 0, jnp.where(ky < 0, ky + 128, ky), ky + 64)
    main = jnp.where(inside & ~clash, place, -1)
    spare = jnp.where(inside & clash, jnp.where(ky < 0, 8, 0) + (ky + 64) % 8, -1)
    return main, spare


def one_hot(condition):
    return jnp.where(condition, 1.0, 0.0).astype(BF)


def sphere_rows(plane, parity, s):
    m, lane = iota((64, 128), 0), iota((64, 128), 1)
    ky = 2 * (m - 24) + parity
    kz = jnp.where(lane < 64, lane, lane - 128)
    kx = s - 64 * plane
    return ky * ky + kz * kz + kx * kx <= R2


def kernel_z_inverse(psi, wz, send):
    s = lax.axis_index("fft")
    main, spare = line_places(iota((1, 256), 1), s)
    j = iota((128, 256), 0)
    pack = jnp.concatenate(
        [one_hot(j == main), one_hot((j % 16 == spare) & (j % 64 < 48))], axis=0
    )
    lane = iota((64, 128), 1)
    rows = []
    for plane in range(2):
        lines = [[], []]
        for c in range(2):
            at = 1152 * plane + c
            t = [
                jnp.concatenate(
                    [
                        psi[pl.ds(at + 432 + 2 * k, 24, stride=6), :],
                        psi[pl.ds(at + 2 * k, 40, stride=6), :],
                    ],
                    0,
                )
                for k in range(3)
            ]
            middle = pltpu.roll(t[1], 64, 1)
            even = jnp.where(lane < 64, t[0], middle)
            odd = jnp.where(lane < 64, middle, t[2])
            lines[0].append(jnp.where(sphere_rows(plane, 0, s), even, 0.0))
            lines[1].append(jnp.where(sphere_rows(plane, 1, s), odd, 0.0))
        rows += [jnp.concatenate(lines[0], 1), jnp.concatenate(lines[1], 1)]
    high, low = split(jnp.concatenate(rows, 0))
    packed = (mm(pack, high).astype(BF), mm(pack, low).astype(BF))
    out = three(mm_nt, (wz[0:384, :], wz[384:768, :]), packed)
    spares = out[0:64, 128:]
    for c in range(2):
        for zi in range(3):
            block = out[(2 * zi + c) * 64 : (2 * zi + c) * 64 + 64]
            send[pl.ds(3 * c + zi, 64, stride=7), :] = block[:, :128]
            spares = jnp.where(lane // 16 == 4 * c + zi, block[:, 128:], spares)
    send[pl.ds(6, 64, stride=7), :] = spares


def tile_rows(tiles):
    return (tiles % 3) * 288 + tiles // 3


def as_column(ids):
    return jnp.broadcast_to(ids.astype(F32), (8, ids.shape[1])).T[:, 0:1].astype(jnp.int32)


def kernel_field(
    recv, ey, ix, u, field, rows_h, rows_l,
):
    main, spare, other = masks_sp()
    spread = []
    for c in range(2):
        got = recv[pl.ds(6, 64, stride=7), :]
        high, low = split(pltpu.roll(got, 64, 1) if c else got)
        spread.append(mm(high, u[...]) + mm(low, u[...]))
    lines = []
    for zi in range(3):
        first, second = [], []
        for c in range(2):
            got = recv[pl.ds(3 * c + zi, 64, stride=7), :]
            extra = spread[c][:, 128 * zi : 128 * zi + 128]
            first.append(jnp.where(main, got, jnp.where(spare, extra, 0.0)))
            second.append(pltpu.roll(jnp.where(other, got, 0.0), 64, 1))
        lines += [jnp.concatenate(first, 1), jnp.concatenate(second, 1)]
    g = three(mm_nt, (ey[0:384, :], ey[384:768, :]), split(jnp.concatenate(lines, 0)))
    out = []
    for parity in range(2):
        a = 96 * parity
        table = [ix[512 * parity + 256 * i : 512 * parity + 256 * i + 256, :] for i in range(2)]
        block = jnp.concatenate(
            [
                jnp.concatenate(
                    [
                        g[a : a + 96, 128 * zi : 128 * zi + 128],
                        g[192 + a : 288 + a, 128 * zi : 128 * zi + 128],
                    ],
                    1,
                )
                for zi in range(3)
            ],
            0,
        )
        out.append(three(mm, split(block), table))
    even, odd = out
    for c in range(2):
        a = 256 * c
        kinds = (
            even[:, a : a + 128],
            even[:, a + 128 : a + 256] + odd[:, a : a + 128],
            odd[:, a + 128 : a + 256],
        )
        for k, tile in enumerate(kinds):
            span = pl.ds(288 * k, 288)
            lanes = pl.ds(128 * c, 128)
            field[span, lanes] = tile
            high, low = split(tile)
            rows_h[span, lanes] = high
            rows_l[span, lanes] = low
    rows_h[864:896, :] = jnp.zeros((32, 256), BF)
    rows_l[864:896, :] = jnp.zeros((32, 256), BF)


def project(quarters, rows_h, rows_l, tile_of, slots, betas, field_rows):
    count = 128 * quarters
    pick = one_hot(as_column(tile_of) == iota((count, 896), 1))
    field_rows[...] = mm(pick, rows_h[...]) + mm(pick, rows_l[...])
    lane = iota((128, 128), 1)
    sums = []
    for k, beta in enumerate(betas):
        total = jnp.zeros((128, 128), F32)
        for j in range(8):
            projector = beta[pl.ds(j, 128, stride=8), :]
            for c in range(2):
                value = field_rows[128 * k : 128 * k + 128, 128 * c : 128 * c + 128] * projector
                total = jnp.where(
                    lane == 8 * c + j, jnp.sum(value, axis=1, keepdims=True), total
                )
        sums.append(total.T[:16])
    high, low = split(jnp.concatenate(sums, 1))
    return mm(high, slots) + mm(low, slots)


def ids_of(betas, row):
    return jnp.concatenate([b[1024 + row : 1025 + row, :] for b in betas], 1).astype(jnp.int32)


def kernel_project(rows_h, rows_l, b0, b1, b2, coef, slots_out, tiles_out, field_rows):
    betas = (b0, b1, b2)
    tile_of = tile_rows(ids_of(betas, 1))
    tiles_out[...] = tile_of
    slots = one_hot(as_column(ids_of(betas, 0)) == iota((384, 256), 1))
    slots_out[...] = slots
    coef[...] = project(3, rows_h, rows_l, tile_of, slots, betas, field_rows)


def kernel_project_last(rows_h, rows_l, dmat, coef_in, b3, near, slots_out, tiles_out, field_rows):
    tile_of = tile_rows(ids_of((b3,), 1))
    tiles_out[...] = tile_of
    slots = one_hot(as_column(ids_of((b3,), 0)) == iota((128, 256), 1))
    slots_out[...] = slots
    coef = coef_in[...] + project(1, rows_h, rows_l, tile_of, slots, (b3,), field_rows)
    coef = jnp.where(iota((16, 256), 1) < 192, coef, 0.0)
    near[0:64, :] = jnp.concatenate([dmat[...], jnp.zeros((64, 64), F32)], 1)
    near[64:80, :] = coef[:, :128]
    near[80:96, :] = coef[:, 128:]


def chip_of(own, other):
    f = lax.axis_index("fft")
    core = f % 2
    own, other = own[...], other[...]
    return (
        core,
        (f // 2) % 2 == 0,
        jnp.where(core == 0, own, other),
        jnp.where(core == 0, other, own),
    )


def kernel_merge(own, other, first, second):
    _, even, a, b = chip_of(own, other)
    low_lane = iota((16, 128), 1) < 64
    turned = pltpu.roll(b[64:80], 64, 1)
    up = jnp.where(low_lane, a[80:96] + turned, pltpu.roll(b[80:96], 64, 1))
    down = jnp.where(low_lane, a[64:80], a[64:80] + turned)
    up = jnp.concatenate([b[0:64], up], 0)
    down = jnp.concatenate([a[0:64], down], 0)
    first[...] = jnp.where(even, up, down)
    second[...] = jnp.where(even, down, up)


def kernel_put(tiles, tiles_last, vloc_in, put, vloc_out, vloc, sems):
    copies = [
        pltpu.make_async_copy(vloc_in.at[:, zi, :], vloc.at[zi], sems.at[zi]) for zi in range(3)
    ]
    for copy in copies:
        copy.start()
    tile_of = jnp.concatenate([tiles[...], tiles_last[...]], 1)
    put[...] = one_hot(iota((864, 512), 0) == tile_of)
    for copy in copies:
        copy.wait()
    for k in range(3):
        for zi in range(3):
            at = 288 * k + 96 * zi
            vloc_out[at : at + 96, :] = vloc[zi, pl.ds(k, 96, stride=3), :]


def kernel_back(
    field, own, other, second, first, slots, slots_last, put, b0, b1, b2, b3,
    vloc, fx, fy, ut, send, scr, rows,
):
    core, even, a, b = chip_of(own, other)
    above = jnp.where(even, first[...], second[...])
    below = jnp.where(even, second[...], first[...])
    low_lane = iota((16, 128), 1) < 64
    turned = pltpu.roll(b[64:80], 64, 1)
    tot = [
        below[64:80] + jnp.where(low_lane, a[64:80], a[64:80] + turned),
        above[64:80] + jnp.where(low_lane, a[80:96] + turned, pltpu.roll(b[80:96], 64, 1)),
    ]
    wide = iota((64, 128), 1) < 64
    coupling = [
        jnp.where(wide, below[0:64], pltpu.roll(a[0:64], 64, 1)),
        jnp.where(wide, b[0:64], pltpu.roll(above[0:64], 64, 1)),
    ]
    for h in range(2):
        for c in range(2):
            coef = tot[h][8 * c : 8 * c + 8, :]
            for j in range(8):
                row = jnp.sum(coupling[h][8 * j : 8 * j + 8, :] * coef, axis=0, keepdims=True)
                scr[8 * c + j : 8 * c + j + 1, 128 * h : 128 * h + 128] = row
    betas = (b0, b1, b2, b3)
    left, right = scr[:, :128], scr[:, 128:]
    left_turned, right_turned = pltpu.roll(left, 64, 1), pltpu.roll(right, 64, 1)
    left = jnp.where(core == 0, left, jnp.where(low_lane, left_turned, right_turned))
    right = jnp.where(low_lane, jnp.where(core == 0, right, right_turned), 0.0)
    high, low = split(jnp.concatenate([left, right], 1))
    weight = jnp.concatenate(
        [mm_nt(hot[...], high) + mm_nt(hot[...], low) for hot in (slots, slots_last)], 0
    )
    high, low = split(weight)
    weight = jnp.concatenate([high, low], 1)
    for k, beta in enumerate(betas):
        span = slice(128 * k, 128 * k + 128)
        terms = jnp.zeros((128, 256), F32)
        for j in range(8):
            wide = one_hot(iota((32, 256), 0) % 16 == 8 * (iota((32, 256), 1) // 128) + j)
            projector = beta[pl.ds(j, 128, stride=8), :]
            terms = terms + mm(weight[span], wide) * jnp.concatenate([projector, projector], 1)
        high, low = split(terms)
        rows[span, 0:256] = high
        rows[span, 256:512] = low
    both = mm(put[...], rows[...])
    nonloc = both[:, :256] + both[:, 256:]
    kinds = []
    for k in range(3):
        at = slice(288 * k, 288 * k + 288)
        factor = vloc[at, :]
        kinds.append(split(field[at, :] * jnp.concatenate([factor, factor], 1) + nonloc[at, :]))
    g = []
    for parity in range(2):
        table = [fx[1024 * parity + 512 * i : 1024 * parity + 512 * i + 512, :] for i in range(2)]
        lines = [jnp.concatenate([kinds[parity][i], kinds[parity + 1][i]], 1) for i in range(2)]
        g.append(split(three(mm, lines, table)))
    lines = [
        jnp.concatenate(
            [
                jnp.concatenate(
                    [
                        g[parity][i][96 * zi : 96 * zi + 96, 128 * c : 128 * c + 128]
                        for zi in range(3)
                    ],
                    1,
                )
                for c in range(2)
                for parity in range(2)
            ],
            0,
        )
        for i in range(2)
    ]
    h = three(mm, (fy[0:256, :], fy[256:512, :]), lines)
    main, spare, _ = masks_sp()
    spares = [jnp.zeros((64, 128), F32), jnp.zeros((64, 128), F32)]
    for zi in range(3):
        for c in range(2):
            turned = h[128 * c : 128 * c + 128, 128 * zi : 128 * zi + 128].T
            first = turned[:64]
            second = pltpu.roll(turned[64:], 64, 1)
            send[pl.ds(3 * c + zi, 64, stride=7), :] = jnp.where(main, first, second)
            high, low = split(jnp.where(spare, first, 0.0))
            move = ut[128 * zi : 128 * zi + 128, :]
            spares[c] = spares[c] + (mm(high, move) + mm(low, move))
    send[pl.ds(6, 64, stride=7), :] = spares[0] + pltpu.roll(spares[1], 64, 1)


def kernel_z_forward(recv, fz, result, out, sems):
    s = lax.axis_index("fft")
    out[...] = jnp.zeros((1728, 128), F32)
    spans = [(152, 280), (576, 576), (1304, 280), (0, 152), (432, 144), (1152, 152), (1584, 144)]
    copies = [
        pltpu.make_async_copy(out.at[pl.ds(*span)], result.at[pl.ds(*span)], sems.at[k])
        for k, span in enumerate(spans)
    ]
    for copy in copies[:3]:
        copy.start()
    r = iota((256, 1), 0)
    main, spare = line_places(r, s)
    lane = iota((256, 128), 1)
    keep = one_hot(lane == main)
    spares = recv[pl.ds(6, 64, stride=7), :]
    spares = (spares, pltpu.roll(spares, 64, 1))
    highs, lows = [], []
    for zi in range(3):
        unpack = jnp.concatenate(
            [keep, one_hot((lane == spare + 16 * zi) & (spare >= 0))], 1
        )
        lines = jnp.concatenate(
            [
                jnp.concatenate(
                    [
                        recv[pl.ds(3 * c + zi, 64, stride=7), :],
                        spares[c],
                    ],
                    1,
                )
                for c in range(2)
            ],
            0,
        )
        high, low = split(lines)
        columns = mm_nt(unpack, jnp.concatenate([high, low], 0))
        highs.append(columns[:, :128].astype(BF))
        lows.append(columns[:, 128:].astype(BF))
    z = three(
        mm, (jnp.concatenate(highs, 1), jnp.concatenate(lows, 1)), (fz[0:384, :], fz[384:768, :])
    )
    low_lane = iota((64, 128), 1) < 64
    for plane in range(2):
        for c in range(2):
            block = z[128 * plane : 128 * plane + 128, 128 * c : 128 * c + 128]
            even = jnp.where(sphere_rows(plane, 0, s), block[:64], 0.0)
            odd = jnp.where(sphere_rows(plane, 1, s), block[64:], 0.0)
            kinds = (
                jnp.where(low_lane, even, 0.0),
                pltpu.roll(jnp.where(low_lane, odd, even), 64, 1),
                jnp.where(low_lane, 0.0, odd),
            )
            for k, tile in enumerate(kinds):
                at = 1152 * plane + 2 * k + c
                out[pl.ds(at, 25, stride=6), :] = tile[24:49]
                out[pl.ds(at + 432, 24, stride=6), :] = tile[:24]
        copies[3 + 2 * plane].start()
        copies[4 + 2 * plane].start()
    for copy in copies:
        copy.wait()


def call(kernel, name, out_shape, args, scratch=(), anywhere=(), anywhere_out=(), limit=VMEM_LIMIT, cost=None):
    specs = [
        pl.BlockSpec(memory_space=pl.ANY if k in anywhere else pltpu.VMEM)
        for k in range(len(args))
    ]
    shapes = [
        jax.ShapeDtypeStruct(*shape) if isinstance(shape[0], tuple) else jax.ShapeDtypeStruct(shape, F32)
        for shape in out_shape
    ]
    out = pl.pallas_call(
        kernel,
        name=name,
        out_shape=shapes,
        in_specs=specs,
        out_specs=[
            pl.BlockSpec(memory_space=pl.ANY if k in anywhere_out else pltpu.VMEM)
            for k in range(len(shapes))
        ],
        scratch_shapes=list(scratch),
        cost_estimate=cost,
        compiler_params=pltpu.CompilerParams(vmem_limit_bytes=limit),
    )(*args)
    return out


def body(psi_g, vloc, beta, blk_slot, blk_tile, dmat):
    t = {
        name: jnp.asarray(value) for name, value in tables().items()
    }
    psi = psi_g[0].transpose(1, 0, 2).reshape(3, 2, 288, 128).transpose(0, 2, 1, 3)
    psi = psi.reshape(1728, 128)
    def from_band(x, k):
        return lax.ppermute(x, "band", [(i, (i + k) % 4) for i in range(4)])

    ids = jnp.concatenate([blk_slot[None], blk_tile[None], jnp.zeros((6, 128), jnp.int32)], 0)
    own = jnp.concatenate([beta, ids.astype(F32)[None]], 0).reshape(1032, 128)
    (send,) = call(kernel_z_inverse, "z_inverse", [(448, 128)], (psi, t["wz"]))
    betas = [own, from_band(own, 2), from_band(own, 1), from_band(own, 3)]

    def exchange(x):
        x = lax.all_to_all(x.reshape(64, 1, 896), "fft", 0, 0, tiled=True)
        return x.reshape(448, 128)

    recv = exchange(send)
    vloc_tiles = vloc.reshape(3, 288, 128).transpose(1, 0, 2)
    dmat_rows = dmat.transpose(1, 2, 0).reshape(64, 64)
    field, rows_h, rows_l = call(
        kernel_field,
        "field",
        [(864, 256), ((896, 256), BF), ((896, 256), BF)],
        (recv, t["ey"], t["ix"], t["u"]),
    )
    coef, slots, tiles = call(
        kernel_project,
        "project",
        [(16, 256), ((384, 256), BF), ((1, 384), jnp.int32)],
        (rows_h, rows_l, *betas[:3]),
        [pltpu.VMEM((384, 256), F32)],
    )
    near, slots_last, tiles_last = call(
        kernel_project_last,
        "project_last",
        [(96, 128), ((128, 256), BF), ((1, 128), jnp.int32)],
        (rows_h, rows_l, dmat_rows, coef, betas[3]),
        [pltpu.VMEM((128, 256), F32)],
    )
    other = lax.ppermute(near, "fft", [(i, i ^ 1) for i in range(64)])
    first, second = call(kernel_merge, "merge", [(80, 128), (80, 128)], (near, other))
    first = lax.ppermute(first, "fft", [(i, i ^ 2) for i in range(64)])
    second = lax.ppermute(second, "fft", [(i, (((i + 2) % 64) ^ 2) - 2 & 63) for i in range(64)])
    put, vloc_rows = call(
        kernel_put,
        "put",
        [((864, 512), BF), (864, 128)],
        (tiles, tiles_last, vloc_tiles),
        [pltpu.VMEM((3, 288, 128), F32), pltpu.SemaphoreType.DMA((3,))],
        anywhere=(2,),
        cost=pl.CostEstimate(flops=2000000, bytes_accessed=3000000, transcendentals=0),
    )
    (send,) = call(
        kernel_back,
        "back",
        [(448, 128)],
        (field, near, other, second, first, slots, slots_last, put, *betas, vloc_rows, t["fx"], t["fy"], t["ut"]),
        [
            pltpu.VMEM((16, 256), F32),
            pltpu.VMEM((512, 512), BF),
        ],
    )
    (out,) = call(kernel_z_forward, "z_forward", [(1728, 128)], (exchange(send), t["fz"]),
        [pltpu.VMEM((1728, 128), F32), pltpu.SemaphoreType.DMA((7,))], anywhere_out=(0,))
    out = out.reshape(3, 288, 2, 128).transpose(0, 2, 1, 3).reshape(3, 2, N * N)
    return out.transpose(1, 0, 2)[None]


def solution(mesh):
    in_specs = (
        P("band", None, "fft", None),
        P("fft", None),
        P(("fft", "band"), None, None),
        P(("fft", "band")),
        P(("fft", "band")),
        P("fft", None, None),
    )
    out_specs = P("band", None, "fft", None)
    return jax.shard_map(body, mesh=mesh, in_specs=in_specs, out_specs=out_specs, check_vma=False)
```

```python
import functools

import jax
import jax.numpy as jnp
import ml_dtypes
import numpy as np
from jax import lax
from jax.experimental import pallas as pl
from jax.experimental.pallas import tpu as pltpu
from jax.sharding import PartitionSpec as P

N = 192
R2 = 48 * 48
BF = jnp.bfloat16
F32 = jnp.float32
VMEM_LIMIT = 32 * 1024 * 1024


def trig(freqs, points):
    angle = 2.0 * np.pi * (np.outer(freqs, points) % N) / N
    return np.cos(angle) / np.sqrt(N), np.sin(angle) / np.sqrt(N)


def pair_of(table):
    table = np.asarray(table, np.float32)
    high = table.astype(ml_dtypes.bfloat16)
    low = (table - high.astype(np.float32)).astype(ml_dtypes.bfloat16)
    return np.concatenate([high, low], 0)


KZ = np.concatenate([np.arange(64), np.arange(128, 192)])
SIGNED = np.concatenate([np.arange(64), np.arange(-64, 0)])
YS = [2 * np.arange(96), 2 * np.arange(96) + 1]


@functools.cache
def tables():
    t = {}
    blocks = []
    for zi in range(3):
        c, s = trig(3 * np.arange(64) + zi, KZ)
        blocks += [np.concatenate([c, -s], 1), np.concatenate([s, c], 1)]
    t["wz"] = pair_of(np.concatenate(blocks, 0))
    c, s = trig(np.concatenate(YS), SIGNED)
    t["ey"] = pair_of(
        np.concatenate([np.concatenate([c, -s], 1), np.concatenate([s, c], 1)], 0)
    )
    c, s = trig(SIGNED, np.arange(N))
    gap = np.zeros((128, 64))
    even = [np.concatenate([v, gap], 1) for v in (c, s, -s, c)]
    odd = [np.concatenate([gap, v], 1) for v in (c, s, -s, c)]
    t["ix"] = np.concatenate(
        [
            pair_of(np.block([[even[0], even[1]], [even[2], even[3]]])),
            pair_of(np.block([[odd[0], odd[1]], [odd[2], odd[3]]])),
        ],
        0,
    )
    parts = {}
    c, s = trig(np.arange(N), SIGNED)
    gap = np.zeros((64, 128))
    for name, table in (("c", c), ("s", s)):
        parts[name] = (np.concatenate([table, gap], 0), np.concatenate([gap, table], 0))

    def forward_x(which):
        cc, ss = parts["c"][which], parts["s"][which]
        first, second = np.concatenate([cc, -ss], 1), np.concatenate([ss, cc], 1)
        return np.concatenate([first[:128], second[:128], first[128:], second[128:]], 0)

    t["fx"] = np.concatenate([pair_of(forward_x(0)), pair_of(forward_x(1))], 0)
    c, s = trig(SIGNED, np.concatenate(YS))
    t["fy"] = pair_of(
        np.concatenate([np.concatenate([c, s], 1), np.concatenate([-s, c], 1)], 0)
    )
    blocks = []
    for zi in range(3):
        c, s = trig(3 * np.arange(64) + zi, KZ)
        blocks += [np.concatenate([c, -s], 1), np.concatenate([s, c], 1)]
    t["fz"] = pair_of(np.concatenate(blocks, 0))
    u = np.zeros((128, 384), np.float32)
    for zi in range(3):
        for p in range(128):
            u[16 * zi + 8 * (p >= 64) + p % 8, 128 * zi + p] = 1.0
    t["u"] = u.astype(ml_dtypes.bfloat16)
    t["ut"] = np.concatenate([u[:, 128 * zi : 128 * zi + 128].T for zi in range(3)], 0).astype(
        ml_dtypes.bfloat16
    )
    return t


def split(x):
    high = x.astype(BF)
    return high, (x - high.astype(F32)).astype(BF)


def mm(a, b):
    return jnp.dot(a, b, preferred_element_type=F32)


def mm_nt(a, b):
    return lax.dot_general(a, b, (((1,), (1,)), ((), ())), preferred_element_type=F32)


def three(product, a, b):
    return product(a[0], b[0]) + (product(a[0], b[1]) + product(a[1], b[0]))


def iota(shape, dim):
    return lax.broadcasted_iota(jnp.int32, shape, dim)


def masks_sp():
    s, p = iota((64, 128), 0), iota((64, 128), 1)
    ky = jnp.where(p < 64, p, p - 128)
    away = 64 - jnp.abs(ky)
    inside = ky * ky + s * s <= R2
    clash = away * away + (64 - s) * (64 - s) <= R2
    other = (p - 64) * (p - 64) + (64 - s) * (64 - s) <= R2
    return inside & ~clash, inside & clash, other


def line_places(r, s):
    plane, rest = r // 128, r % 128
    ky = 2 * (rest % 64 - 24) + rest // 64
    here = jnp.where(plane == 0, s, 64 - s)
    away = 64 - jnp.abs(ky)
    inside = ky * ky + here * here <= R2
    clash = (away * away + (64 - s) * (64 - s) <= R2) & (plane == 0)
    place = jnp.where(plane == 0, jnp.where(ky < 0, ky + 128, ky), ky + 64)
    main = jnp.where(inside & ~clash, place, -1)
    spare = jnp.where(inside & clash, jnp.where(ky < 0, 8, 0) + (ky + 64) % 8, -1)
    return main, spare


def one_hot(condition):
    return jnp.where(condition, 1.0, 0.0).astype(BF)


def sphere_rows(plane, parity, s):
    m, lane = iota((64, 128), 0), iota((64, 128), 1)
    ky = 2 * (m - 24) + parity
    kz = jnp.where(lane < 64, lane, lane - 128)
    kx = s - 64 * plane
    return ky * ky + kz * kz + kx * kx <= R2


def kernel_z_inverse(psi, wz, send):
    s = lax.axis_index("fft")
    main, spare = line_places(iota((1, 256), 1), s)
    j = iota((128, 256), 0)
    pack = jnp.concatenate(
        [one_hot(j == main), one_hot((j % 16 == spare) & (j % 64 < 48))], axis=0
    )
    lane = iota((64, 128), 1)
    rows = []
    for plane in range(2):
        lines = [[], []]
        for c in range(2):
            at = 1152 * plane + c
            t = [
                jnp.concatenate(
                    [
                        psi[pl.ds(at + 432 + 2 * k, 24, stride=6), :],
                        psi[pl.ds(at + 2 * k, 40, stride=6), :],
                    ],
                    0,
                )
                for k in range(3)
            ]
            middle = pltpu.roll(t[1], 64, 1)
            even = jnp.where(lane < 64, t[0], middle)
            odd = jnp.where(lane < 64, middle, t[2])
            lines[0].append(jnp.where(sphere_rows(plane, 0, s), even, 0.0))
            lines[1].append(jnp.where(sphere_rows(plane, 1, s), odd, 0.0))
        rows += [jnp.concatenate(lines[0], 1), jnp.concatenate(lines[1], 1)]
    high, low = split(jnp.concatenate(rows, 0))
    packed = (mm(pack, high).astype(BF), mm(pack, low).astype(BF))
    out = three(mm_nt, (wz[0:384, :], wz[384:768, :]), packed)
    spares = out[0:64, 128:]
    for c in range(2):
        for zi in range(3):
            block = out[(2 * zi + c) * 64 : (2 * zi + c) * 64 + 64]
            send[pl.ds(3 * c + zi, 64, stride=7), :] = block[:, :128]
            spares = jnp.where(lane // 16 == 4 * c + zi, block[:, 128:], spares)
    send[pl.ds(6, 64, stride=7), :] = spares


def tile_rows(tiles):
    return (tiles % 3) * 288 + tiles // 3


def as_column(ids):
    return jnp.broadcast_to(ids.astype(F32), (8, ids.shape[1])).T[:, 0:1].astype(jnp.int32)


def kernel_field(
    recv, ey, ix, u, field, rows_h, rows_l,
):
    main, spare, other = masks_sp()
    spread = []
    for c in range(2):
        got = recv[pl.ds(6, 64, stride=7), :]
        high, low = split(pltpu.roll(got, 64, 1) if c else got)
        spread.append(mm(high, u[...]) + mm(low, u[...]))
    lines = []
    for zi in range(3):
        first, second = [], []
        for c in range(2):
            got = recv[pl.ds(3 * c + zi, 64, stride=7), :]
            extra = spread[c][:, 128 * zi : 128 * zi + 128]
            first.append(jnp.where(main, got, jnp.where(spare, extra, 0.0)))
            second.append(pltpu.roll(jnp.where(other, got, 0.0), 64, 1))
        lines += [jnp.concatenate(first, 1), jnp.concatenate(second, 1)]
    g = three(mm_nt, (ey[0:384, :], ey[384:768, :]), split(jnp.concatenate(lines, 0)))
    out = []
    for parity in range(2):
        a = 96 * parity
        table = [ix[512 * parity + 256 * i : 512 * parity + 256 * i + 256, :] for i in range(2)]
        block = jnp.concatenate(
            [
                jnp.concatenate(
                    [
                        g[a : a + 96, 128 * zi : 128 * zi + 128],
                        g[192 + a : 288 + a, 128 * zi : 128 * zi + 128],
                    ],
                    1,
                )
                for zi in range(3)
            ],
            0,
        )
        out.append(three(mm, split(block), table))
    even, odd = out
    for c in range(2):
        a = 256 * c
        kinds = (
            even[:, a : a + 128],
            even[:, a + 128 : a + 256] + odd[:, a : a + 128],
            odd[:, a + 128 : a + 256],
        )
        for k, tile in enumerate(kinds):
            span = pl.ds(288 * k, 288)
            lanes = pl.ds(128 * c, 128)
            field[span, lanes] = tile
            high, low = split(tile)
            rows_h[span, lanes] = high
            rows_l[span, lanes] = low
    rows_h[864:896, :] = jnp.zeros((32, 256), BF)
    rows_l[864:896, :] = jnp.zeros((32, 256), BF)


def project(quarters, rows_h, rows_l, tile_of, slots, betas, field_rows):
    count = 128 * quarters
    pick = one_hot(as_column(tile_of) == iota((count, 896), 1))
    field_rows[...] = mm(pick, rows_h[...]) + mm(pick, rows_l[...])
    lane = iota((128, 128), 1)
    sums = []
    for k, beta in enumerate(betas):
        total = jnp.zeros((128, 128), F32)
        for j in range(8):
            projector = beta[pl.ds(j, 128, stride=8), :]
            for c in range(2):
                value = field_rows[128 * k : 128 * k + 128, 128 * c : 128 * c + 128] * projector
                total = jnp.where(
                    lane == 8 * c + j, jnp.sum(value, axis=1, keepdims=True), total
                )
        sums.append(total.T[:16])
    high, low = split(jnp.concatenate(sums, 1))
    return mm(high, slots) + mm(low, slots)


def ids_of(betas, row):
    return jnp.concatenate([b[1024 + row : 1025 + row, :] for b in betas], 1).astype(jnp.int32)


def kernel_project(rows_h, rows_l, b0, b1, b2, coef, slots_out, tiles_out, field_rows):
    betas = (b0, b1, b2)
    tile_of = tile_rows(ids_of(betas, 1))
    tiles_out[...] = tile_of
    slots = one_hot(as_column(ids_of(betas, 0)) == iota((384, 256), 1))
    slots_out[...] = slots
    coef[...] = project(3, rows_h, rows_l, tile_of, slots, betas, field_rows)


def kernel_project_last(rows_h, rows_l, dmat, coef_in, b3, near, slots_out, tiles_out, field_rows):
    tile_of = tile_rows(ids_of((b3,), 1))
    tiles_out[...] = tile_of
    slots = one_hot(as_column(ids_of((b3,), 0)) == iota((128, 256), 1))
    slots_out[...] = slots
    coef = coef_in[...] + project(1, rows_h, rows_l, tile_of, slots, (b3,), field_rows)
    coef = jnp.where(iota((16, 256), 1) < 192, coef, 0.0)
    near[0:64, :] = jnp.concatenate([dmat[...], jnp.zeros((64, 64), F32)], 1)
    near[64:80, :] = coef[:, :128]
    near[80:96, :] = coef[:, 128:]


def chip_of(own, other):
    f = lax.axis_index("fft")
    core = f % 2
    own, other = own[...], other[...]
    return (
        core,
        (f // 2) % 2 == 0,
        jnp.where(core == 0, own, other),
        jnp.where(core == 0, other, own),
    )


def kernel_merge(own, other, first, second):
    _, even, a, b = chip_of(own, other)
    low_lane = iota((16, 128), 1) < 64
    turned = pltpu.roll(b[64:80], 64, 1)
    up = jnp.where(low_lane, a[80:96] + turned, pltpu.roll(b[80:96], 64, 1))
    down = jnp.where(low_lane, a[64:80], a[64:80] + turned)
    up = jnp.concatenate([b[0:64], up], 0)
    down = jnp.concatenate([a[0:64], down], 0)
    first[...] = jnp.where(even, up, down)
    second[...] = jnp.where(even, down, up)


def kernel_put(tiles, tiles_last, field, vloc_in, put, local, vloc, sems):
    copies = [
        pltpu.make_async_copy(vloc_in.at[:, zi, :], vloc.at[zi], sems.at[zi]) for zi in range(3)
    ]
    for copy in copies:
        copy.start()
    tile_of = jnp.concatenate([tiles[...], tiles_last[...]], 1)
    put[...] = one_hot(iota((864, 512), 0) == tile_of)
    for copy in copies:
        copy.wait()
    for k in range(3):
        for zi in range(3):
            at = 288 * k + 96 * zi
            factor = vloc[zi, pl.ds(k, 96, stride=3), :]
            local[at : at + 96, :] = field[at : at + 96, :] * jnp.concatenate([factor, factor], 1)


def kernel_back(
    local, own, other, second, first, slots, slots_last, put, b0, b1, b2, b3,
    fx, fy, ut, send, scr, rows,
):
    core, even, a, b = chip_of(own, other)
    above = jnp.where(even, first[...], second[...])
    below = jnp.where(even, second[...], first[...])
    low_lane = iota((16, 128), 1) < 64
    turned = pltpu.roll(b[64:80], 64, 1)
    tot = [
        below[64:80] + jnp.where(low_lane, a[64:80], a[64:80] + turned),
        above[64:80] + jnp.where(low_lane, a[80:96] + turned, pltpu.roll(b[80:96], 64, 1)),
    ]
    wide = iota((64, 128), 1) < 64
    coupling = [
        jnp.where(wide, below[0:64], pltpu.roll(a[0:64], 64, 1)),
        jnp.where(wide, b[0:64], pltpu.roll(above[0:64], 64, 1)),
    ]
    for h in range(2):
        for c in range(2):
            coef = tot[h][8 * c : 8 * c + 8, :]
            for j in range(8):
                row = jnp.sum(coupling[h][8 * j : 8 * j + 8, :] * coef, axis=0, keepdims=True)
                scr[8 * c + j : 8 * c + j + 1, 128 * h : 128 * h + 128] = row
    betas = (b0, b1, b2, b3)
    left, right = scr[:, :128], scr[:, 128:]
    left_turned, right_turned = pltpu.roll(left, 64, 1), pltpu.roll(right, 64, 1)
    left = jnp.where(core == 0, left, jnp.where(low_lane, left_turned, right_turned))
    right = jnp.where(low_lane, jnp.where(core == 0, right, right_turned), 0.0)
    high, low = split(jnp.concatenate([left, right], 1))
    parts = jnp.concatenate([high, low], 0)
    weight = jnp.concatenate([mm_nt(hot[...], parts) for hot in (slots, slots_last)], 0).astype(BF)
    for k, beta in enumerate(betas):
        span = slice(128 * k, 128 * k + 128)
        terms = jnp.zeros((128, 256), F32)
        for j in range(8):
            wide = one_hot(iota((32, 256), 0) % 16 == 8 * (iota((32, 256), 1) // 128) + j)
            projector = beta[pl.ds(j, 128, stride=8), :]
            terms = terms + mm(weight[span], wide) * jnp.concatenate([projector, projector], 1)
        high, low = split(terms)
        rows[span, 0:256] = high
        rows[span, 256:512] = low
    both = mm(put[...], rows[...])
    nonloc = both[:, :256] + both[:, 256:]
    kinds = []
    for k in range(3):
        at = slice(288 * k, 288 * k + 288)
        kinds.append(split(local[at, :] + nonloc[at, :]))
    g = []
    for parity in range(2):
        table = [fx[1024 * parity + 512 * i : 1024 * parity + 512 * i + 512, :] for i in range(2)]
        lines = [jnp.concatenate([kinds[parity][i], kinds[parity + 1][i]], 1) for i in range(2)]
        g.append(split(three(mm, lines, table)))
    lines = [
        jnp.concatenate(
            [
                jnp.concatenate(
                    [
                        g[parity][i][96 * zi : 96 * zi + 96, 128 * c : 128 * c + 128]
                        for zi in range(3)
                    ],
                    1,
                )
                for c in range(2)
                for parity in range(2)
            ],
            0,
        )
        for i in range(2)
    ]
    h = three(mm, (fy[0:256, :], fy[256:512, :]), lines)
    main, spare, _ = masks_sp()
    spares = [jnp.zeros((64, 128), F32), jnp.zeros((64, 128), F32)]
    for zi in range(3):
        for c in range(2):
            turned = h[128 * c : 128 * c + 128, 128 * zi : 128 * zi + 128].T
            first = turned[:64]
            second = pltpu.roll(turned[64:], 64, 1)
            send[pl.ds(3 * c + zi, 64, stride=7), :] = jnp.where(main, first, second)
            high, low = split(jnp.where(spare, first, 0.0))
            move = ut[128 * zi : 128 * zi + 128, :]
            spares[c] = spares[c] + (mm(high, move) + mm(low, move))
    send[pl.ds(6, 64, stride=7), :] = spares[0] + pltpu.roll(spares[1], 64, 1)


def kernel_z_forward(recv, fz, result, out, sems):
    s = lax.axis_index("fft")
    out[...] = jnp.zeros((1728, 128), F32)
    spans = [(152, 280), (576, 576), (1304, 280), (0, 152), (432, 144), (1152, 152), (1584, 144)]
    copies = [
        pltpu.make_async_copy(out.at[pl.ds(*span)], result.at[pl.ds(*span)], sems.at[k])
        for k, span in enumerate(spans)
    ]
    for copy in copies[:3]:
        copy.start()
    r = iota((256, 1), 0)
    main, spare = line_places(r, s)
    lane = iota((256, 128), 1)
    keep = one_hot(lane == main)
    spares = recv[pl.ds(6, 64, stride=7), :]
    spares = (spares, pltpu.roll(spares, 64, 1))
    highs, lows = [], []
    for zi in range(3):
        unpack = jnp.concatenate(
            [keep, one_hot((lane == spare + 16 * zi) & (spare >= 0))], 1
        )
        lines = jnp.concatenate(
            [
                jnp.concatenate(
                    [
                        recv[pl.ds(3 * c + zi, 64, stride=7), :],
                        spares[c],
                    ],
                    1,
                )
                for c in range(2)
            ],
            0,
        )
        high, low = split(lines)
        columns = mm_nt(unpack, jnp.concatenate([high, low], 0))
        highs.append(columns[:, :128].astype(BF))
        lows.append(columns[:, 128:].astype(BF))
    z = three(
        mm, (jnp.concatenate(highs, 1), jnp.concatenate(lows, 1)), (fz[0:384, :], fz[384:768, :])
    )
    low_lane = iota((64, 128), 1) < 64
    for plane in range(2):
        for c in range(2):
            block = z[128 * plane : 128 * plane + 128, 128 * c : 128 * c + 128]
            even = jnp.where(sphere_rows(plane, 0, s), block[:64], 0.0)
            odd = jnp.where(sphere_rows(plane, 1, s), block[64:], 0.0)
            kinds = (
                jnp.where(low_lane, even, 0.0),
                pltpu.roll(jnp.where(low_lane, odd, even), 64, 1),
                jnp.where(low_lane, 0.0, odd),
            )
            for k, tile in enumerate(kinds):
                at = 1152 * plane + 2 * k + c
                out[pl.ds(at, 25, stride=6), :] = tile[24:49]
                out[pl.ds(at + 432, 24, stride=6), :] = tile[:24]
        copies[3 + 2 * plane].start()
        copies[4 + 2 * plane].start()
    for copy in copies:
        copy.wait()


def call(kernel, name, out_shape, args, scratch=(), anywhere=(), anywhere_out=(), limit=VMEM_LIMIT, cost=None):
    specs = [
        pl.BlockSpec(memory_space=pl.ANY if k in anywhere else pltpu.VMEM)
        for k in range(len(args))
    ]
    shapes = [
        jax.ShapeDtypeStruct(*shape) if isinstance(shape[0], tuple) else jax.ShapeDtypeStruct(shape, F32)
        for shape in out_shape
    ]
    out = pl.pallas_call(
        kernel,
        name=name,
        out_shape=shapes,
        in_specs=specs,
        out_specs=[
            pl.BlockSpec(memory_space=pl.ANY if k in anywhere_out else pltpu.VMEM)
            for k in range(len(shapes))
        ],
        scratch_shapes=list(scratch),
        cost_estimate=cost,
        compiler_params=pltpu.CompilerParams(vmem_limit_bytes=limit),
    )(*args)
    return out


def body(psi_g, vloc, beta, blk_slot, blk_tile, dmat):
    t = {
        name: jnp.asarray(value) for name, value in tables().items()
    }
    psi = psi_g[0].transpose(1, 0, 2).reshape(3, 2, 288, 128).transpose(0, 2, 1, 3)
    psi = psi.reshape(1728, 128)
    def from_band(x, k):
        return lax.ppermute(x, "band", [(i, (i + k) % 4) for i in range(4)])

    ids = jnp.concatenate([blk_slot[None], blk_tile[None], jnp.zeros((6, 128), jnp.int32)], 0)
    own = jnp.concatenate([beta, ids.astype(F32)[None]], 0).reshape(1032, 128)
    (send,) = call(kernel_z_inverse, "z_inverse", [(448, 128)], (psi, t["wz"]))
    own_later, send = lax.optimization_barrier((own, send))
    betas = [own, from_band(own, 3), from_band(own, 2), from_band(own_later, 1)]

    def exchange(x):
        x = lax.all_to_all(x.reshape(64, 1, 896), "fft", 0, 0, tiled=True)
        return x.reshape(448, 128)

    recv = exchange(send)
    vloc_tiles = vloc.reshape(3, 288, 128).transpose(1, 0, 2)
    dmat_rows = dmat.transpose(1, 2, 0).reshape(64, 64)
    field, rows_h, rows_l = call(
        kernel_field,
        "field",
        [(864, 256), ((896, 256), BF), ((896, 256), BF)],
        (recv, t["ey"], t["ix"], t["u"]),
    )
    coef, slots, tiles = call(
        kernel_project,
        "project",
        [(16, 256), ((384, 256), BF), ((1, 384), jnp.int32)],
        (rows_h, rows_l, *betas[:3]),
        [pltpu.VMEM((384, 256), F32)],
    )
    near, slots_last, tiles_last = call(
        kernel_project_last,
        "project_last",
        [(96, 128), ((128, 256), BF), ((1, 128), jnp.int32)],
        (rows_h, rows_l, dmat_rows, coef, betas[3]),
        [pltpu.VMEM((128, 256), F32)],
    )
    other = lax.ppermute(near, "fft", [(i, i ^ 1) for i in range(64)])
    first, second = call(kernel_merge, "merge", [(80, 128), (80, 128)], (near, other))
    first = lax.ppermute(first, "fft", [(i, i ^ 2) for i in range(64)])
    second = lax.ppermute(second, "fft", [(i, (((i + 2) % 64) ^ 2) - 2 & 63) for i in range(64)])
    put, local = call(
        kernel_put,
        "put",
        [((864, 512), BF), (864, 256)],
        (tiles, tiles_last, field, vloc_tiles),
        [pltpu.VMEM((3, 288, 128), F32), pltpu.SemaphoreType.DMA((3,))],
        anywhere=(3,),
        cost=pl.CostEstimate(flops=2000000, bytes_accessed=3000000, transcendentals=0),
    )
    (send,) = call(
        kernel_back,
        "back",
        [(448, 128)],
        (local, near, other, second, first, slots, slots_last, put, *betas, t["fx"], t["fy"], t["ut"]),
        [
            pltpu.VMEM((16, 256), F32),
            pltpu.VMEM((512, 512), BF),
        ],
    )
    (out,) = call(kernel_z_forward, "z_forward", [(1728, 128)], (exchange(send), t["fz"]),
        [pltpu.VMEM((1728, 128), F32), pltpu.SemaphoreType.DMA((7,))], anywhere_out=(0,))
    out = out.reshape(3, 288, 2, 128).transpose(0, 2, 1, 3).reshape(3, 2, N * N)
    return out.transpose(1, 0, 2)[None]


def solution(mesh):
    in_specs = (
        P("band", None, "fft", None),
        P("fft", None),
        P(("fft", "band"), None, None),
        P(("fft", "band")),
        P(("fft", "band")),
        P("fft", None, None),
    )
    out_specs = P("band", None, "fft", None)
    return jax.shard_map(body, mesh=mesh, in_specs=in_specs, out_specs=out_specs, check_vma=False)
```

```python
import functools

import jax
import jax.numpy as jnp
import ml_dtypes
import numpy as np
from jax import lax
from jax.experimental import pallas as pl
from jax.experimental.pallas import tpu as pltpu
from jax.sharding import PartitionSpec as P

N = 192
R2 = 48 * 48
BF = jnp.bfloat16
F32 = jnp.float32
VMEM_LIMIT = 32 * 1024 * 1024


def trig(freqs, points):
    angle = 2.0 * np.pi * (np.outer(freqs, points) % N) / N
    return np.cos(angle) / np.sqrt(N), np.sin(angle) / np.sqrt(N)


def pair_of(table):
    table = np.asarray(table, np.float32)
    high = table.astype(ml_dtypes.bfloat16)
    low = (table - high.astype(np.float32)).astype(ml_dtypes.bfloat16)
    return np.concatenate([high, low], 0)


KZ = np.concatenate([np.arange(64), np.arange(128, 192)])
SIGNED = np.concatenate([np.arange(64), np.arange(-64, 0)])
YS = [2 * np.arange(96), 2 * np.arange(96) + 1]


@functools.cache
def tables():
    t = {}
    blocks = []
    for zi in range(3):
        c, s = trig(3 * np.arange(64) + zi, KZ)
        blocks += [np.concatenate([c, -s], 1), np.concatenate([s, c], 1)]
    t["wz"] = pair_of(np.concatenate(blocks, 0))
    c, s = trig(np.concatenate(YS), SIGNED)
    t["ey"] = pair_of(
        np.concatenate([np.concatenate([c, -s], 1), np.concatenate([s, c], 1)], 0)
    )
    c, s = trig(SIGNED, np.arange(N))
    gap = np.zeros((128, 64))
    even = [np.concatenate([v, gap], 1) for v in (c, s, -s, c)]
    odd = [np.concatenate([gap, v], 1) for v in (c, s, -s, c)]
    t["ix"] = np.concatenate(
        [
            pair_of(np.block([[even[0], even[1]], [even[2], even[3]]])),
            pair_of(np.block([[odd[0], odd[1]], [odd[2], odd[3]]])),
        ],
        0,
    )
    parts = {}
    c, s = trig(np.arange(N), SIGNED)
    gap = np.zeros((64, 128))
    for name, table in (("c", c), ("s", s)):
        parts[name] = (np.concatenate([table, gap], 0), np.concatenate([gap, table], 0))

    def forward_x(which):
        cc, ss = parts["c"][which], parts["s"][which]
        first, second = np.concatenate([cc, -ss], 1), np.concatenate([ss, cc], 1)
        return np.concatenate([first[:128], second[:128], first[128:], second[128:]], 0)

    t["fx"] = np.concatenate([pair_of(forward_x(0)), pair_of(forward_x(1))], 0)
    c, s = trig(SIGNED, np.concatenate(YS))
    t["fy"] = pair_of(
        np.concatenate([np.concatenate([c, s], 1), np.concatenate([-s, c], 1)], 0)
    )
    blocks = []
    for zi in range(3):
        c, s = trig(3 * np.arange(64) + zi, KZ)
        blocks += [np.concatenate([c, -s], 1), np.concatenate([s, c], 1)]
    t["fz"] = pair_of(np.concatenate(blocks, 0))
    u = np.zeros((128, 384), np.float32)
    for zi in range(3):
        for p in range(128):
            u[16 * zi + 8 * (p >= 64) + p % 8, 128 * zi + p] = 1.0
    t["u"] = u.astype(ml_dtypes.bfloat16)
    t["ut"] = np.concatenate([u[:, 128 * zi : 128 * zi + 128].T for zi in range(3)], 0).astype(
        ml_dtypes.bfloat16
    )
    return t


def split(x):
    high = x.astype(BF)
    return high, (x - high.astype(F32)).astype(BF)


def mm(a, b):
    return jnp.dot(a, b, preferred_element_type=F32)


def mm_nt(a, b):
    return lax.dot_general(a, b, (((1,), (1,)), ((), ())), preferred_element_type=F32)


def three(product, a, b):
    return product(a[0], b[0]) + (product(a[0], b[1]) + product(a[1], b[0]))


def iota(shape, dim):
    return lax.broadcasted_iota(jnp.int32, shape, dim)


def masks_sp():
    s, p = iota((64, 128), 0), iota((64, 128), 1)
    ky = jnp.where(p < 64, p, p - 128)
    away = 64 - jnp.abs(ky)
    inside = ky * ky + s * s <= R2
    clash = away * away + (64 - s) * (64 - s) <= R2
    other = (p - 64) * (p - 64) + (64 - s) * (64 - s) <= R2
    return inside & ~clash, inside & clash, other


def line_places(r, s):
    plane, rest = r // 128, r % 128
    ky = 2 * (rest % 64 - 24) + rest // 64
    here = jnp.where(plane == 0, s, 64 - s)
    away = 64 - jnp.abs(ky)
    inside = ky * ky + here * here <= R2
    clash = (away * away + (64 - s) * (64 - s) <= R2) & (plane == 0)
    place = jnp.where(plane == 0, jnp.where(ky < 0, ky + 128, ky), ky + 64)
    main = jnp.where(inside & ~clash, place, -1)
    spare = jnp.where(inside & clash, jnp.where(ky < 0, 8, 0) + (ky + 64) % 8, -1)
    return main, spare


def one_hot(condition):
    return jnp.where(condition, 1.0, 0.0).astype(BF)


def sphere_rows(plane, parity, s):
    m, lane = iota((64, 128), 0), iota((64, 128), 1)
    ky = 2 * (m - 24) + parity
    kz = jnp.where(lane < 64, lane, lane - 128)
    kx = s - 64 * plane
    return ky * ky + kz * kz + kx * kx <= R2


def kernel_z_inverse(psi, wz, send):
    s = lax.axis_index("fft")
    main, spare = line_places(iota((1, 256), 1), s)
    j = iota((128, 256), 0)
    pack = jnp.concatenate(
        [one_hot(j == main), one_hot((j % 16 == spare) & (j % 64 < 48))], axis=0
    )
    lane = iota((64, 128), 1)
    rows = []
    for plane in range(2):
        lines = [[], []]
        for c in range(2):
            at = 1152 * plane + c
            t = [
                jnp.concatenate(
                    [
                        psi[pl.ds(at + 432 + 2 * k, 24, stride=6), :],
                        psi[pl.ds(at + 2 * k, 40, stride=6), :],
                    ],
                    0,
                )
                for k in range(3)
            ]
            middle = pltpu.roll(t[1], 64, 1)
            even = jnp.where(lane < 64, t[0], middle)
            odd = jnp.where(lane < 64, middle, t[2])
            lines[0].append(jnp.where(sphere_rows(plane, 0, s), even, 0.0))
            lines[1].append(jnp.where(sphere_rows(plane, 1, s), odd, 0.0))
        rows += [jnp.concatenate(lines[0], 1), jnp.concatenate(lines[1], 1)]
    high, low = split(jnp.concatenate(rows, 0))
    packed = (mm(pack, high).astype(BF), mm(pack, low).astype(BF))
    out = three(mm_nt, (wz[0:384, :], wz[384:768, :]), packed)
    spares = out[0:64, 128:]
    for c in range(2):
        for zi in range(3):
            block = out[(2 * zi + c) * 64 : (2 * zi + c) * 64 + 64]
            send[pl.ds(3 * c + zi, 64, stride=7), :] = block[:, :128]
            spares = jnp.where(lane // 16 == 4 * c + zi, block[:, 128:], spares)
    send[pl.ds(6, 64, stride=7), :] = spares


def tile_rows(tiles):
    return (tiles % 3) * 288 + tiles // 3


def as_column(ids):
    return jnp.broadcast_to(ids.astype(F32), (8, ids.shape[1])).T[:, 0:1].astype(jnp.int32)


def kernel_field(
    recv, ey, ix, u, field, rows_h, rows_l,
):
    main, spare, other = masks_sp()
    spread = []
    for c in range(2):
        got = recv[pl.ds(6, 64, stride=7), :]
        high, low = split(pltpu.roll(got, 64, 1) if c else got)
        spread.append(mm(high, u[...]) + mm(low, u[...]))
    lines = []
    for zi in range(3):
        first, second = [], []
        for c in range(2):
            got = recv[pl.ds(3 * c + zi, 64, stride=7), :]
            extra = spread[c][:, 128 * zi : 128 * zi + 128]
            first.append(jnp.where(main, got, jnp.where(spare, extra, 0.0)))
            second.append(pltpu.roll(jnp.where(other, got, 0.0), 64, 1))
        lines += [jnp.concatenate(first, 1), jnp.concatenate(second, 1)]
    g = three(mm_nt, (ey[0:384, :], ey[384:768, :]), split(jnp.concatenate(lines, 0)))
    out = []
    for parity in range(2):
        a = 96 * parity
        table = [ix[512 * parity + 256 * i : 512 * parity + 256 * i + 256, :] for i in range(2)]
        block = jnp.concatenate(
            [
                jnp.concatenate(
                    [
                        g[a : a + 96, 128 * zi : 128 * zi + 128],
                        g[192 + a : 288 + a, 128 * zi : 128 * zi + 128],
                    ],
                    1,
                )
                for zi in range(3)
            ],
            0,
        )
        out.append(three(mm, split(block), table))
    even, odd = out
    for c in range(2):
        a = 256 * c
        kinds = (
            even[:, a : a + 128],
            even[:, a + 128 : a + 256] + odd[:, a : a + 128],
            odd[:, a + 128 : a + 256],
        )
        for k, tile in enumerate(kinds):
            span = pl.ds(288 * k, 288)
            lanes = pl.ds(128 * c, 128)
            field[span, lanes] = tile
            high, low = split(tile)
            rows_h[span, lanes] = high
            rows_l[span, lanes] = low
    rows_h[864:896, :] = jnp.zeros((32, 256), BF)
    rows_l[864:896, :] = jnp.zeros((32, 256), BF)


def project(quarters, rows_h, rows_l, tile_of, slots, betas, field_rows):
    count = 128 * quarters
    pick = one_hot(as_column(tile_of) == iota((count, 896), 1))
    field_rows[...] = mm(pick, rows_h[...]) + mm(pick, rows_l[...])
    lane = iota((128, 128), 1)
    sums = []
    for k, beta in enumerate(betas):
        total = jnp.zeros((128, 128), F32)
        for j in range(8):
            projector = beta[pl.ds(j, 128, stride=8), :]
            for c in range(2):
                value = field_rows[128 * k : 128 * k + 128, 128 * c : 128 * c + 128] * projector
                total = jnp.where(
                    lane == 8 * c + j, jnp.sum(value, axis=1, keepdims=True), total
                )
        sums.append(total.T[:16])
    high, low = split(jnp.concatenate(sums, 1))
    return mm(high, slots) + mm(low, slots)


def ids_of(betas, row):
    return jnp.concatenate([b[1024 + row : 1025 + row, :] for b in betas], 1).astype(jnp.int32)


def kernel_project(rows_h, rows_l, b0, b1, b2, coef, slots_out, tiles_out, field_rows):
    betas = (b0, b1, b2)
    tile_of = tile_rows(ids_of(betas, 1))
    tiles_out[...] = tile_of
    slots = one_hot(as_column(ids_of(betas, 0)) == iota((384, 256), 1))
    slots_out[...] = slots
    coef[...] = project(3, rows_h, rows_l, tile_of, slots, betas, field_rows)


def kernel_project_last(rows_h, rows_l, dmat, coef_in, b3, near, slots_out, tiles_out, field_rows):
    tile_of = tile_rows(ids_of((b3,), 1))
    tiles_out[...] = tile_of
    slots = one_hot(as_column(ids_of((b3,), 0)) == iota((128, 256), 1))
    slots_out[...] = slots
    coef = coef_in[...] + project(1, rows_h, rows_l, tile_of, slots, (b3,), field_rows)
    coef = jnp.where(iota((16, 256), 1) < 192, coef, 0.0)
    near[0:64, :] = jnp.concatenate([dmat[...], jnp.zeros((64, 64), F32)], 1)
    near[64:80, :] = coef[:, :128]
    near[80:96, :] = coef[:, 128:]


def chip_of(own, other):
    f = lax.axis_index("fft")
    core = f % 2
    own, other = own[...], other[...]
    return (
        core,
        (f // 2) % 2 == 0,
        jnp.where(core == 0, own, other),
        jnp.where(core == 0, other, own),
    )


def kernel_merge(own, other, first, second):
    _, even, a, b = chip_of(own, other)
    low_lane = iota((16, 128), 1) < 64
    turned = pltpu.roll(b[64:80], 64, 1)
    up = jnp.where(low_lane, a[80:96] + turned, pltpu.roll(b[80:96], 64, 1))
    down = jnp.where(low_lane, a[64:80], a[64:80] + turned)
    up = jnp.concatenate([b[0:64], up], 0)
    down = jnp.concatenate([a[0:64], down], 0)
    first[...] = jnp.where(even, up, down)
    second[...] = jnp.where(even, down, up)


def kernel_put(tiles, tiles_last, field, vloc_in, put, local, vloc, sems):
    copies = [
        pltpu.make_async_copy(vloc_in.at[:, zi, :], vloc.at[zi], sems.at[zi]) for zi in range(3)
    ]
    for copy in copies:
        copy.start()
    tile_of = jnp.concatenate([tiles[...], tiles_last[...]], 1)
    put[...] = one_hot(iota((864, 512), 0) == tile_of)
    for copy in copies:
        copy.wait()
    for k in range(3):
        for zi in range(3):
            at = 288 * k + 96 * zi
            factor = vloc[zi, pl.ds(k, 96, stride=3), :]
            local[at : at + 96, :] = field[at : at + 96, :] * jnp.concatenate([factor, factor], 1)


def kernel_back(
    local, own, other, second, first, slots, slots_last, put, b0, b1, b2, b3,
    fx, fy, ut, send, scr, rows,
):
    core, even, a, b = chip_of(own, other)
    above = jnp.where(even, first[...], second[...])
    below = jnp.where(even, second[...], first[...])
    low_lane = iota((16, 128), 1) < 64
    turned = pltpu.roll(b[64:80], 64, 1)
    tot = [
        below[64:80] + jnp.where(low_lane, a[64:80], a[64:80] + turned),
        above[64:80] + jnp.where(low_lane, a[80:96] + turned, pltpu.roll(b[80:96], 64, 1)),
    ]
    wide = iota((64, 128), 1) < 64
    coupling = [
        jnp.where(wide, below[0:64], pltpu.roll(a[0:64], 64, 1)),
        jnp.where(wide, b[0:64], pltpu.roll(above[0:64], 64, 1)),
    ]
    for h in range(2):
        for c in range(2):
            coef = tot[h][8 * c : 8 * c + 8, :]
            for j in range(8):
                row = jnp.sum(coupling[h][8 * j : 8 * j + 8, :] * coef, axis=0, keepdims=True)
                scr[8 * c + j : 8 * c + j + 1, 128 * h : 128 * h + 128] = row
    betas = (b0, b1, b2, b3)
    left, right = scr[:, :128], scr[:, 128:]
    left_turned, right_turned = pltpu.roll(left, 64, 1), pltpu.roll(right, 64, 1)
    left = jnp.where(core == 0, left, jnp.where(low_lane, left_turned, right_turned))
    right = jnp.where(low_lane, jnp.where(core == 0, right, right_turned), 0.0)
    high, low = split(jnp.concatenate([left, right], 1))
    parts = jnp.concatenate([high, low], 0)
    weight = jnp.concatenate([mm_nt(hot[...], parts) for hot in (slots, slots_last)], 0).astype(BF)
    for k, beta in enumerate(betas):
        span = slice(128 * k, 128 * k + 128)
        terms = jnp.zeros((128, 256), F32)
        for j in range(8):
            wide = one_hot(iota((32, 256), 0) % 16 == 8 * (iota((32, 256), 1) // 128) + j)
            projector = beta[pl.ds(j, 128, stride=8), :]
            terms = terms + mm(weight[span], wide) * jnp.concatenate([projector, projector], 1)
        high, low = split(terms)
        rows[span, 0:256] = high
        rows[span, 256:512] = low
    both = mm(put[...], rows[...])
    nonloc = both[:, :256] + both[:, 256:]
    kinds = []
    for k in range(3):
        at = slice(288 * k, 288 * k + 288)
        kinds.append(split(local[at, :] + nonloc[at, :]))
    g = []
    for parity in range(2):
        table = [fx[1024 * parity + 512 * i : 1024 * parity + 512 * i + 512, :] for i in range(2)]
        lines = [jnp.concatenate([kinds[parity][i], kinds[parity + 1][i]], 1) for i in range(2)]
        g.append(split(three(mm, lines, table)))
    lines = [
        jnp.concatenate(
            [
                jnp.concatenate(
                    [
                        g[parity][i][96 * zi : 96 * zi + 96, 128 * c : 128 * c + 128]
                        for zi in range(3)
                    ],
                    1,
                )
                for c in range(2)
                for parity in range(2)
            ],
            0,
        )
        for i in range(2)
    ]
    h = three(mm, (fy[0:256, :], fy[256:512, :]), lines)
    main, spare, _ = masks_sp()
    spares = [jnp.zeros((64, 128), F32), jnp.zeros((64, 128), F32)]
    for zi in range(3):
        for c in range(2):
            turned = h[128 * c : 128 * c + 128, 128 * zi : 128 * zi + 128].T
            first = turned[:64]
            second = pltpu.roll(turned[64:], 64, 1)
            send[pl.ds(3 * c + zi, 64, stride=7), :] = jnp.where(main, first, second)
            high, low = split(jnp.where(spare, first, 0.0))
            move = ut[128 * zi : 128 * zi + 128, :]
            spares[c] = spares[c] + (mm(high, move) + mm(low, move))
    send[pl.ds(6, 64, stride=7), :] = spares[0] + pltpu.roll(spares[1], 64, 1)


def kernel_z_forward(recv, fz, result, out, sems):
    s = lax.axis_index("fft")
    out[...] = jnp.zeros((1728, 128), F32)
    spans = [(152, 280), (576, 576), (1304, 280), (0, 152), (432, 144), (1152, 152), (1584, 144)]
    copies = [
        pltpu.make_async_copy(out.at[pl.ds(*span)], result.at[pl.ds(*span)], sems.at[k])
        for k, span in enumerate(spans)
    ]
    for copy in copies[:3]:
        copy.start()
    r = iota((256, 1), 0)
    main, spare = line_places(r, s)
    lane = iota((256, 128), 1)
    keep = one_hot(lane == main)
    spares = recv[pl.ds(6, 64, stride=7), :]
    spares = (spares, pltpu.roll(spares, 64, 1))
    highs, lows = [], []
    for zi in range(3):
        unpack = jnp.concatenate(
            [keep, one_hot((lane == spare + 16 * zi) & (spare >= 0))], 1
        )
        lines = jnp.concatenate(
            [
                jnp.concatenate(
                    [
                        recv[pl.ds(3 * c + zi, 64, stride=7), :],
                        spares[c],
                    ],
                    1,
                )
                for c in range(2)
            ],
            0,
        )
        high, low = split(lines)
        columns = mm_nt(unpack, jnp.concatenate([high, low], 0))
        highs.append(columns[:, :128].astype(BF))
        lows.append(columns[:, 128:].astype(BF))
    z = three(
        mm, (jnp.concatenate(highs, 1), jnp.concatenate(lows, 1)), (fz[0:384, :], fz[384:768, :])
    )
    low_lane = iota((64, 128), 1) < 64
    for plane in range(2):
        for c in range(2):
            block = z[128 * plane : 128 * plane + 128, 128 * c : 128 * c + 128]
            even = jnp.where(sphere_rows(plane, 0, s), block[:64], 0.0)
            odd = jnp.where(sphere_rows(plane, 1, s), block[64:], 0.0)
            kinds = (
                jnp.where(low_lane, even, 0.0),
                pltpu.roll(jnp.where(low_lane, odd, even), 64, 1),
                jnp.where(low_lane, 0.0, odd),
            )
            for k, tile in enumerate(kinds):
                at = 1152 * plane + 2 * k + c
                out[pl.ds(at, 25, stride=6), :] = tile[24:49]
                out[pl.ds(at + 432, 24, stride=6), :] = tile[:24]
        copies[3 + 2 * plane].start()
        copies[4 + 2 * plane].start()
    for copy in copies:
        copy.wait()


def call(kernel, name, out_shape, args, scratch=(), anywhere=(), anywhere_out=(), limit=VMEM_LIMIT, cost=None):
    specs = [
        pl.BlockSpec(memory_space=pl.ANY if k in anywhere else pltpu.VMEM)
        for k in range(len(args))
    ]
    shapes = [
        jax.ShapeDtypeStruct(*shape) if isinstance(shape[0], tuple) else jax.ShapeDtypeStruct(shape, F32)
        for shape in out_shape
    ]
    out = pl.pallas_call(
        kernel,
        name=name,
        out_shape=shapes,
        in_specs=specs,
        out_specs=[
            pl.BlockSpec(memory_space=pl.ANY if k in anywhere_out else pltpu.VMEM)
            for k in range(len(shapes))
        ],
        scratch_shapes=list(scratch),
        cost_estimate=cost,
        compiler_params=pltpu.CompilerParams(vmem_limit_bytes=limit),
    )(*args)
    return out


def body(psi_g, vloc, beta, blk_slot, blk_tile, dmat):
    t = {
        name: jnp.asarray(value) for name, value in tables().items()
    }
    psi = psi_g[0].transpose(1, 0, 2).reshape(3, 2, 288, 128).transpose(0, 2, 1, 3)
    psi = psi.reshape(1728, 128)
    def from_band(x, k):
        return lax.ppermute(x, "band", [(i, (i + k) % 4) for i in range(4)])

    ids = jnp.concatenate([blk_slot[None], blk_tile[None], jnp.zeros((6, 128), jnp.int32)], 0)
    own = jnp.concatenate([beta, ids.astype(F32)[None]], 0).reshape(1032, 128)
    (send,) = call(kernel_z_inverse, "z_inverse", [(448, 128)], (psi, t["wz"]))
    betas = [own, from_band(own, 2), from_band(own, 3), from_band(own, 1)]

    def exchange(x):
        x = lax.all_to_all(x.reshape(64, 1, 896), "fft", 0, 0, tiled=True)
        return x.reshape(448, 128)

    recv = exchange(send)
    vloc_tiles = vloc.reshape(3, 288, 128).transpose(1, 0, 2)
    dmat_rows = dmat.transpose(1, 2, 0).reshape(64, 64)
    field, rows_h, rows_l = call(
        kernel_field,
        "field",
        [(864, 256), ((896, 256), BF), ((896, 256), BF)],
        (recv, t["ey"], t["ix"], t["u"]),
    )
    coef, slots, tiles = call(
        kernel_project,
        "project",
        [(16, 256), ((384, 256), BF), ((1, 384), jnp.int32)],
        (rows_h, rows_l, *betas[:3]),
        [pltpu.VMEM((384, 256), F32)],
    )
    near, slots_last, tiles_last = call(
        kernel_project_last,
        "project_last",
        [(96, 128), ((128, 256), BF), ((1, 128), jnp.int32)],
        (rows_h, rows_l, dmat_rows, coef, betas[3]),
        [pltpu.VMEM((128, 256), F32)],
    )
    other = lax.ppermute(near, "fft", [(i, i ^ 1) for i in range(64)])
    first, second = call(kernel_merge, "merge", [(80, 128), (80, 128)], (near, other))
    first = lax.ppermute(first, "fft", [(i, i ^ 2) for i in range(64)])
    second = lax.ppermute(second, "fft", [(i, (((i + 2) % 64) ^ 2) - 2 & 63) for i in range(64)])
    put, local = call(
        kernel_put,
        "put",
        [((864, 512), BF), (864, 256)],
        (tiles, tiles_last, field, vloc_tiles),
        [pltpu.VMEM((3, 288, 128), F32), pltpu.SemaphoreType.DMA((3,))],
        anywhere=(3,),
        cost=pl.CostEstimate(flops=2000000, bytes_accessed=3000000, transcendentals=0),
    )
    (send,) = call(
        kernel_back,
        "back",
        [(448, 128)],
        (local, near, other, second, first, slots, slots_last, put, *betas, t["fx"], t["fy"], t["ut"]),
        [
            pltpu.VMEM((16, 256), F32),
            pltpu.VMEM((512, 512), BF),
        ],
    )
    (out,) = call(kernel_z_forward, "z_forward", [(1728, 128)], (exchange(send), t["fz"]),
        [pltpu.VMEM((1728, 128), F32), pltpu.SemaphoreType.DMA((7,))], anywhere_out=(0,))
    out = out.reshape(3, 288, 2, 128).transpose(0, 2, 1, 3).reshape(3, 2, N * N)
    return out.transpose(1, 0, 2)[None]


def solution(mesh):
    in_specs = (
        P("band", None, "fft", None),
        P("fft", None),
        P(("fft", "band"), None, None),
        P(("fft", "band")),
        P(("fft", "band")),
        P("fft", None, None),
    )
    out_specs = P("band", None, "fft", None)
    return jax.shard_map(body, mesh=mesh, in_specs=in_specs, out_specs=out_specs, check_vma=False)
```

```python
import functools

import jax
import jax.numpy as jnp
import ml_dtypes
import numpy as np
from jax import lax
from jax.experimental import pallas as pl
from jax.experimental.pallas import tpu as pltpu
from jax.sharding import PartitionSpec as P

N = 192
R2 = 48 * 48
BF = jnp.bfloat16
F32 = jnp.float32
VMEM_LIMIT = 32 * 1024 * 1024


def trig(freqs, points):
    angle = 2.0 * np.pi * (np.outer(freqs, points) % N) / N
    return np.cos(angle) / np.sqrt(N), np.sin(angle) / np.sqrt(N)


def pair_of(table):
    table = np.asarray(table, np.float32)
    high = table.astype(ml_dtypes.bfloat16)
    low = (table - high.astype(np.float32)).astype(ml_dtypes.bfloat16)
    return np.concatenate([high, low], 0)


KZ = np.concatenate([np.arange(64), np.arange(128, 192)])
SIGNED = np.concatenate([np.arange(64), np.arange(-64, 0)])
YS = [2 * np.arange(96), 2 * np.arange(96) + 1]


@functools.cache
def tables():
    t = {}
    blocks = []
    for zi in range(3):
        c, s = trig(3 * np.arange(64) + zi, KZ)
        blocks += [np.concatenate([c, -s], 1), np.concatenate([s, c], 1)]
    t["wz"] = pair_of(np.concatenate(blocks, 0))
    c, s = trig(np.concatenate(YS), SIGNED)
    t["ey"] = pair_of(
        np.concatenate([np.concatenate([c, -s], 1), np.concatenate([s, c], 1)], 0)
    )
    c, s = trig(SIGNED, np.arange(N))
    gap = np.zeros((128, 64))
    even = [np.concatenate([v, gap], 1) for v in (c, s, -s, c)]
    odd = [np.concatenate([gap, v], 1) for v in (c, s, -s, c)]
    t["ix"] = np.concatenate(
        [
            pair_of(np.block([[even[0], even[1]], [even[2], even[3]]])),
            pair_of(np.block([[odd[0], odd[1]], [odd[2], odd[3]]])),
        ],
        0,
    )
    parts = {}
    c, s = trig(np.arange(N), SIGNED)
    gap = np.zeros((64, 128))
    for name, table in (("c", c), ("s", s)):
        parts[name] = (np.concatenate([table, gap], 0), np.concatenate([gap, table], 0))

    def forward_x(which):
        cc, ss = parts["c"][which], parts["s"][which]
        first, second = np.concatenate([cc, -ss], 1), np.concatenate([ss, cc], 1)
        return np.concatenate([first[:128], second[:128], first[128:], second[128:]], 0)

    t["fx"] = np.concatenate([pair_of(forward_x(0)), pair_of(forward_x(1))], 0)
    c, s = trig(SIGNED, np.concatenate(YS))
    t["fy"] = pair_of(
        np.concatenate([np.concatenate([c, s], 1), np.concatenate([-s, c], 1)], 0)
    )
    blocks = []
    for zi in range(3):
        c, s = trig(3 * np.arange(64) + zi, KZ)
        blocks += [np.concatenate([c, -s], 1), np.concatenate([s, c], 1)]
    t["fz"] = pair_of(np.concatenate(blocks, 0))
    u = np.zeros((128, 384), np.float32)
    for zi in range(3):
        for p in range(128):
            u[16 * zi + 8 * (p >= 64) + p % 8, 128 * zi + p] = 1.0
    t["u"] = u.astype(ml_dtypes.bfloat16)
    t["ut"] = np.concatenate([u[:, 128 * zi : 128 * zi + 128].T for zi in range(3)], 0).astype(
        ml_dtypes.bfloat16
    )
    return t


def split(x):
    high = x.astype(BF)
    return high, (x - high.astype(F32)).astype(BF)


def mm(a, b):
    return jnp.dot(a, b, preferred_element_type=F32)


def mm_nt(a, b):
    return lax.dot_general(a, b, (((1,), (1,)), ((), ())), preferred_element_type=F32)


def three(product, a, b):
    return product(a[0], b[0]) + (product(a[0], b[1]) + product(a[1], b[0]))


def iota(shape, dim):
    return lax.broadcasted_iota(jnp.int32, shape, dim)


def masks_sp():
    s, p = iota((64, 128), 0), iota((64, 128), 1)
    ky = jnp.where(p < 64, p, p - 128)
    away = 64 - jnp.abs(ky)
    inside = ky * ky + s * s <= R2
    clash = away * away + (64 - s) * (64 - s) <= R2
    other = (p - 64) * (p - 64) + (64 - s) * (64 - s) <= R2
    return inside & ~clash, inside & clash, other


def line_places(r, s):
    plane, rest = r // 128, r % 128
    ky = 2 * (rest % 64 - 24) + rest // 64
    here = jnp.where(plane == 0, s, 64 - s)
    away = 64 - jnp.abs(ky)
    inside = ky * ky + here * here <= R2
    clash = (away * away + (64 - s) * (64 - s) <= R2) & (plane == 0)
    place = jnp.where(plane == 0, jnp.where(ky < 0, ky + 128, ky), ky + 64)
    main = jnp.where(inside & ~clash, place, -1)
    spare = jnp.where(inside & clash, jnp.where(ky < 0, 8, 0) + (ky + 64) % 8, -1)
    return main, spare


def one_hot(condition):
    return jnp.where(condition, 1.0, 0.0).astype(BF)


def sphere_rows(plane, parity, s):
    m, lane = iota((64, 128), 0), iota((64, 128), 1)
    ky = 2 * (m - 24) + parity
    kz = jnp.where(lane < 64, lane, lane - 128)
    kx = s - 64 * plane
    return ky * ky + kz * kz + kx * kx <= R2


def kernel_z_inverse(psi, wz, send):
    s = lax.axis_index("fft")
    main, spare = line_places(iota((1, 256), 1), s)
    j = iota((128, 256), 0)
    pack = jnp.concatenate(
        [one_hot(j == main), one_hot((j % 16 == spare) & (j % 64 < 48))], axis=0
    )
    lane = iota((64, 128), 1)
    rows = []
    for plane in range(2):
        lines = [[], []]
        for c in range(2):
            at = 1152 * plane + c
            t = [
                jnp.concatenate(
                    [
                        psi[pl.ds(at + 432 + 2 * k, 24, stride=6), :],
                        psi[pl.ds(at + 2 * k, 40, stride=6), :],
                    ],
                    0,
                )
                for k in range(3)
            ]
            middle = pltpu.roll(t[1], 64, 1)
            even = jnp.where(lane < 64, t[0], middle)
            odd = jnp.where(lane < 64, middle, t[2])
            lines[0].append(jnp.where(sphere_rows(plane, 0, s), even, 0.0))
            lines[1].append(jnp.where(sphere_rows(plane, 1, s), odd, 0.0))
        rows += [jnp.concatenate(lines[0], 1), jnp.concatenate(lines[1], 1)]
    high, low = split(jnp.concatenate(rows, 0))
    packed = (mm(pack, high).astype(BF), mm(pack, low).astype(BF))
    out = three(mm_nt, (wz[0:384, :], wz[384:768, :]), packed)
    spares = out[0:64, 128:]
    for c in range(2):
        for zi in range(3):
            block = out[(2 * zi + c) * 64 : (2 * zi + c) * 64 + 64]
            send[pl.ds(3 * c + zi, 64, stride=7), :] = block[:, :128]
            spares = jnp.where(lane // 16 == 4 * c + zi, block[:, 128:], spares)
    send[pl.ds(6, 64, stride=7), :] = spares


def tile_rows(tiles):
    return (tiles % 3) * 288 + tiles // 3


def as_column(ids):
    return jnp.broadcast_to(ids.astype(F32), (8, ids.shape[1])).T[:, 0:1].astype(jnp.int32)


def kernel_field(
    recv, ey, ix, u, field, rows_h, rows_l,
):
    main, spare, other = masks_sp()
    spread = []
    for c in range(2):
        got = recv[pl.ds(6, 64, stride=7), :]
        high, low = split(pltpu.roll(got, 64, 1) if c else got)
        spread.append(mm(high, u[...]) + mm(low, u[...]))
    lines = []
    for zi in range(3):
        first, second = [], []
        for c in range(2):
            got = recv[pl.ds(3 * c + zi, 64, stride=7), :]
            extra = spread[c][:, 128 * zi : 128 * zi + 128]
            first.append(jnp.where(main, got, jnp.where(spare, extra, 0.0)))
            second.append(pltpu.roll(jnp.where(other, got, 0.0), 64, 1))
        lines += [jnp.concatenate(first, 1), jnp.concatenate(second, 1)]
    g = three(mm_nt, (ey[0:384, :], ey[384:768, :]), split(jnp.concatenate(lines, 0)))
    out = []
    for parity in range(2):
        a = 96 * parity
        table = [ix[512 * parity + 256 * i : 512 * parity + 256 * i + 256, :] for i in range(2)]
        block = jnp.concatenate(
            [
                jnp.concatenate(
                    [
                        g[a : a + 96, 128 * zi : 128 * zi + 128],
                        g[192 + a : 288 + a, 128 * zi : 128 * zi + 128],
                    ],
                    1,
                )
                for zi in range(3)
            ],
            0,
        )
        out.append(three(mm, split(block), table))
    even, odd = out
    for c in range(2):
        a = 256 * c
        kinds = (
            even[:, a : a + 128],
            even[:, a + 128 : a + 256] + odd[:, a : a + 128],
            odd[:, a + 128 : a + 256],
        )
        for k, tile in enumerate(kinds):
            span = pl.ds(288 * k, 288)
            lanes = pl.ds(128 * c, 128)
            field[span, lanes] = tile
            high, low = split(tile)
            rows_h[span, lanes] = high
            rows_l[span, lanes] = low
    rows_h[864:896, :] = jnp.zeros((32, 256), BF)
    rows_l[864:896, :] = jnp.zeros((32, 256), BF)


def project(quarters, rows_h, rows_l, tile_of, slots, betas, field_rows):
    count = 128 * quarters
    pick = one_hot(as_column(tile_of) == iota((count, 896), 1))
    field_rows[...] = mm(pick, rows_h[...]) + mm(pick, rows_l[...])
    lane = iota((128, 128), 1)
    sums = []
    for k, beta in enumerate(betas):
        total = jnp.zeros((128, 128), F32)
        for j in range(8):
            projector = beta[pl.ds(j, 128, stride=8), :]
            for c in range(2):
                value = field_rows[128 * k : 128 * k + 128, 128 * c : 128 * c + 128] * projector
                total = jnp.where(
                    lane == 8 * c + j, jnp.sum(value, axis=1, keepdims=True), total
                )
        sums.append(total.T[:16])
    high, low = split(jnp.concatenate(sums, 1))
    return mm(high, slots) + mm(low, slots)


def ids_of(betas, row):
    return jnp.concatenate([b[1024 + row : 1025 + row, :] for b in betas], 1).astype(jnp.int32)


def kernel_project(rows_h, rows_l, b0, b1, b2, coef, slots_out, tiles_out, field_rows):
    betas = (b0, b1, b2)
    tile_of = tile_rows(ids_of(betas, 1))
    tiles_out[...] = tile_of
    slots = one_hot(as_column(ids_of(betas, 0)) == iota((384, 256), 1))
    slots_out[...] = slots
    coef[...] = project(3, rows_h, rows_l, tile_of, slots, betas, field_rows)


def kernel_project_last(rows_h, rows_l, dmat, coef_in, b3, near, slots_out, tiles_out, field_rows):
    tile_of = tile_rows(ids_of((b3,), 1))
    tiles_out[...] = tile_of
    slots = one_hot(as_column(ids_of((b3,), 0)) == iota((128, 256), 1))
    slots_out[...] = slots
    coef = coef_in[...] + project(1, rows_h, rows_l, tile_of, slots, (b3,), field_rows)
    coef = jnp.where(iota((16, 256), 1) < 192, coef, 0.0)
    near[0:64, :] = jnp.concatenate([dmat[...], jnp.zeros((64, 64), F32)], 1)
    near[64:80, :] = coef[:, :128]
    near[80:96, :] = coef[:, 128:]


def chip_of(own, other):
    f = lax.axis_index("fft")
    core = f % 2
    own, other = own[...], other[...]
    return (
        core,
        (f // 2) % 2 == 0,
        jnp.where(core == 0, own, other),
        jnp.where(core == 0, other, own),
    )


def kernel_merge(own, other, first, second):
    _, even, a, b = chip_of(own, other)
    low_lane = iota((16, 128), 1) < 64
    turned = pltpu.roll(b[64:80], 64, 1)
    up = jnp.where(low_lane, a[80:96] + turned, pltpu.roll(b[80:96], 64, 1))
    down = jnp.where(low_lane, a[64:80], a[64:80] + turned)
    up = jnp.concatenate([b[0:64], up], 0)
    down = jnp.concatenate([a[0:64], down], 0)
    first[...] = jnp.where(even, up, down)
    second[...] = jnp.where(even, down, up)


def kernel_put(tiles, tiles_last, field, vloc_in, put, local, vloc, sems):
    copies = [
        pltpu.make_async_copy(vloc_in.at[:, zi, :], vloc.at[zi], sems.at[zi]) for zi in range(3)
    ]
    for copy in copies:
        copy.start()
    tile_of = jnp.concatenate([tiles[...], tiles_last[...]], 1)
    put[...] = one_hot(iota((864, 512), 0) == tile_of)
    for copy in copies:
        copy.wait()
    for k in range(3):
        for zi in range(3):
            at = 288 * k + 96 * zi
            factor = vloc[zi, pl.ds(k, 96, stride=3), :]
            local[at : at + 96, :] = field[at : at + 96, :] * jnp.concatenate([factor, factor], 1)


def kernel_back(
    local, own, other, second, first, slots, slots_last, put, b0, b1, b2, b3,
    fx, fy, ut, send, scr, rows,
):
    core, even, a, b = chip_of(own, other)
    above = jnp.where(even, first[...], second[...])
    below = jnp.where(even, second[...], first[...])
    low_lane = iota((16, 128), 1) < 64
    turned = pltpu.roll(b[64:80], 64, 1)
    tot = [
        below[64:80] + jnp.where(low_lane, a[64:80], a[64:80] + turned),
        above[64:80] + jnp.where(low_lane, a[80:96] + turned, pltpu.roll(b[80:96], 64, 1)),
    ]
    wide = iota((64, 128), 1) < 64
    coupling = [
        jnp.where(wide, below[0:64], pltpu.roll(a[0:64], 64, 1)),
        jnp.where(wide, b[0:64], pltpu.roll(above[0:64], 64, 1)),
    ]
    for h in range(2):
        for c in range(2):
            coef = tot[h][8 * c : 8 * c + 8, :]
            for j in range(8):
                row = jnp.sum(coupling[h][8 * j : 8 * j + 8, :] * coef, axis=0, keepdims=True)
                scr[8 * c + j : 8 * c + j + 1, 128 * h : 128 * h + 128] = row
    betas = (b0, b1, b2, b3)
    left, right = scr[:, :128], scr[:, 128:]
    left_turned, right_turned = pltpu.roll(left, 64, 1), pltpu.roll(right, 64, 1)
    left = jnp.where(core == 0, left, jnp.where(low_lane, left_turned, right_turned))
    right = jnp.where(low_lane, jnp.where(core == 0, right, right_turned), 0.0)
    high, low = split(jnp.concatenate([left, right], 1))
    parts = jnp.concatenate([high, low], 0)
    weight = jnp.concatenate([mm_nt(hot[...], parts) for hot in (slots, slots_last)], 0).astype(BF)
    for k, beta in enumerate(betas):
        span = slice(128 * k, 128 * k + 128)
        terms = jnp.zeros((128, 256), F32)
        for j in range(8):
            wide = one_hot(iota((32, 256), 0) % 16 == 8 * (iota((32, 256), 1) // 128) + j)
            projector = beta[pl.ds(j, 128, stride=8), :]
            terms = terms + mm(weight[span], wide) * jnp.concatenate([projector, projector], 1)
        high, low = split(terms)
        rows[span, 0:256] = high
        rows[span, 256:512] = low
    both = mm(put[...], rows[...])
    nonloc = both[:, :256] + both[:, 256:]
    kinds = []
    for k in range(3):
        at = slice(288 * k, 288 * k + 288)
        kinds.append(split(local[at, :] + nonloc[at, :]))
    g = []
    for parity in range(2):
        table = [fx[1024 * parity + 512 * i : 1024 * parity + 512 * i + 512, :] for i in range(2)]
        lines = [jnp.concatenate([kinds[parity][i], kinds[parity + 1][i]], 1) for i in range(2)]
        g.append(split(three(mm, lines, table)))
    lines = [
        jnp.concatenate(
            [
                jnp.concatenate(
                    [
                        g[parity][i][96 * zi : 96 * zi + 96, 128 * c : 128 * c + 128]
                        for zi in range(3)
                    ],
                    1,
                )
                for c in range(2)
                for parity in range(2)
            ],
            0,
        )
        for i in range(2)
    ]
    h = three(mm, (fy[0:256, :], fy[256:512, :]), lines)
    main, spare, _ = masks_sp()
    spares = [jnp.zeros((64, 128), F32), jnp.zeros((64, 128), F32)]
    for zi in range(3):
        for c in range(2):
            turned = h[128 * c : 128 * c + 128, 128 * zi : 128 * zi + 128].T
            first = turned[:64]
            second = pltpu.roll(turned[64:], 64, 1)
            send[pl.ds(3 * c + zi, 64, stride=7), :] = jnp.where(main, first, second)
            high, low = split(jnp.where(spare, first, 0.0))
            move = ut[128 * zi : 128 * zi + 128, :]
            spares[c] = spares[c] + (mm(high, move) + mm(low, move))
    send[pl.ds(6, 64, stride=7), :] = spares[0] + pltpu.roll(spares[1], 64, 1)


def kernel_z_forward(recv, fz, result, out, sems):
    s = lax.axis_index("fft")
    out[...] = jnp.zeros((1728, 128), F32)
    spans = [(152, 280), (576, 576), (1304, 280), (0, 152), (432, 144), (1152, 152), (1584, 144)]
    copies = [
        pltpu.make_async_copy(out.at[pl.ds(*span)], result.at[pl.ds(*span)], sems.at[k])
        for k, span in enumerate(spans)
    ]
    for copy in copies[:3]:
        copy.start()
    r = iota((256, 1), 0)
    main, spare = line_places(r, s)
    lane = iota((256, 128), 1)
    keep = one_hot(lane == main)
    spares = recv[pl.ds(6, 64, stride=7), :]
    spares = (spares, pltpu.roll(spares, 64, 1))
    highs, lows = [], []
    for zi in range(3):
        unpack = jnp.concatenate(
            [keep, one_hot((lane == spare + 16 * zi) & (spare >= 0))], 1
        )
        lines = jnp.concatenate(
            [
                jnp.concatenate(
                    [
                        recv[pl.ds(3 * c + zi, 64, stride=7), :],
                        spares[c],
                    ],
                    1,
                )
                for c in range(2)
            ],
            0,
        )
        high, low = split(lines)
        columns = mm_nt(unpack, jnp.concatenate([high, low], 0))
        highs.append(columns[:, :128].astype(BF))
        lows.append(columns[:, 128:].astype(BF))
    z = three(
        mm, (jnp.concatenate(highs, 1), jnp.concatenate(lows, 1)), (fz[0:384, :], fz[384:768, :])
    )
    low_lane = iota((64, 128), 1) < 64
    for plane in range(2):
        for c in range(2):
            block = z[128 * plane : 128 * plane + 128, 128 * c : 128 * c + 128]
            even = jnp.where(sphere_rows(plane, 0, s), block[:64], 0.0)
            odd = jnp.where(sphere_rows(plane, 1, s), block[64:], 0.0)
            kinds = (
                jnp.where(low_lane, even, 0.0),
                pltpu.roll(jnp.where(low_lane, odd, even), 64, 1),
                jnp.where(low_lane, 0.0, odd),
            )
            for k, tile in enumerate(kinds):
                at = 1152 * plane + 2 * k + c
                out[pl.ds(at, 25, stride=6), :] = tile[24:49]
                out[pl.ds(at + 432, 24, stride=6), :] = tile[:24]
        copies[3 + 2 * plane].start()
        copies[4 + 2 * plane].start()
    for copy in copies:
        copy.wait()


def call(kernel, name, out_shape, args, scratch=(), anywhere=(), anywhere_out=(), limit=VMEM_LIMIT, cost=None):
    specs = [
        pl.BlockSpec(memory_space=pl.ANY if k in anywhere else pltpu.VMEM)
        for k in range(len(args))
    ]
    shapes = [
        jax.ShapeDtypeStruct(*shape) if isinstance(shape[0], tuple) else jax.ShapeDtypeStruct(shape, F32)
        for shape in out_shape
    ]
    out = pl.pallas_call(
        kernel,
        name=name,
        out_shape=shapes,
        in_specs=specs,
        out_specs=[
            pl.BlockSpec(memory_space=pl.ANY if k in anywhere_out else pltpu.VMEM)
            for k in range(len(shapes))
        ],
        scratch_shapes=list(scratch),
        cost_estimate=cost,
        compiler_params=pltpu.CompilerParams(vmem_limit_bytes=limit),
    )(*args)
    return out


def body(psi_g, vloc, beta, blk_slot, blk_tile, dmat):
    t = {
        name: jnp.asarray(value) for name, value in tables().items()
    }
    psi = psi_g[0].transpose(1, 0, 2).reshape(3, 2, 288, 128).transpose(0, 2, 1, 3)
    psi = psi.reshape(1728, 128)
    def from_band(x, k):
        return lax.ppermute(x, "band", [(i, (i + k) % 4) for i in range(4)])

    ids = jnp.concatenate([blk_slot[None], blk_tile[None], jnp.zeros((6, 128), jnp.int32)], 0)
    own = jnp.concatenate([beta, ids.astype(F32)[None]], 0).reshape(1032, 128)
    (send,) = call(kernel_z_inverse, "z_inverse", [(448, 128)], (psi, t["wz"]))
    own_later, send = lax.optimization_barrier((own, send))
    betas = [own, from_band(own, 2), from_band(own, 3), from_band(own_later, 1)]

    def exchange(x):
        x = lax.all_to_all(x.reshape(64, 1, 896), "fft", 0, 0, tiled=True)
        return x.reshape(448, 128)

    recv = exchange(send)
    vloc_tiles = vloc.reshape(3, 288, 128).transpose(1, 0, 2)
    dmat_rows = dmat.transpose(1, 2, 0).reshape(64, 64)
    field, rows_h, rows_l = call(
        kernel_field,
        "field",
        [(864, 256), ((896, 256), BF), ((896, 256), BF)],
        (recv, t["ey"], t["ix"], t["u"]),
    )
    coef, slots, tiles = call(
        kernel_project,
        "project",
        [(16, 256), ((384, 256), BF), ((1, 384), jnp.int32)],
        (rows_h, rows_l, *betas[:3]),
        [pltpu.VMEM((384, 256), F32)],
    )
    near, slots_last, tiles_last = call(
        kernel_project_last,
        "project_last",
        [(96, 128), ((128, 256), BF), ((1, 128), jnp.int32)],
        (rows_h, rows_l, dmat_rows, coef, betas[3]),
        [pltpu.VMEM((128, 256), F32)],
    )
    other = lax.ppermute(near, "fft", [(i, i ^ 1) for i in range(64)])
    first, second = call(kernel_merge, "merge", [(80, 128), (80, 128)], (near, other))
    first = lax.ppermute(first, "fft", [(i, i ^ 2) for i in range(64)])
    second = lax.ppermute(second, "fft", [(i, (((i + 2) % 64) ^ 2) - 2 & 63) for i in range(64)])
    put, local = call(
        kernel_put,
        "put",
        [((864, 512), BF), (864, 256)],
        (tiles, tiles_last, field, vloc_tiles),
        [pltpu.VMEM((3, 288, 128), F32), pltpu.SemaphoreType.DMA((3,))],
        anywhere=(3,),
        cost=pl.CostEstimate(flops=2000000, bytes_accessed=3000000, transcendentals=0),
    )
    (send,) = call(
        kernel_back,
        "back",
        [(448, 128)],
        (local, near, other, second, first, slots, slots_last, put, *betas, t["fx"], t["fy"], t["ut"]),
        [
            pltpu.VMEM((16, 256), F32),
            pltpu.VMEM((512, 512), BF),
        ],
    )
    (out,) = call(kernel_z_forward, "z_forward", [(1728, 128)], (exchange(send), t["fz"]),
        [pltpu.VMEM((1728, 128), F32), pltpu.SemaphoreType.DMA((7,))], anywhere_out=(0,))
    out = out.reshape(3, 288, 2, 128).transpose(0, 2, 1, 3).reshape(3, 2, N * N)
    return out.transpose(1, 0, 2)[None]


def solution(mesh):
    in_specs = (
        P("band", None, "fft", None),
        P("fft", None),
        P(("fft", "band"), None, None),
        P(("fft", "band")),
        P(("fft", "band")),
        P("fft", None, None),
    )
    out_specs = P("band", None, "fft", None)
    return jax.shard_map(body, mesh=mesh, in_specs=in_specs, out_specs=out_specs, check_vma=False)
```

```python
import functools

import jax
import jax.numpy as jnp
import ml_dtypes
import numpy as np
from jax import lax
from jax.experimental import pallas as pl
from jax.experimental.pallas import tpu as pltpu
from jax.sharding import PartitionSpec as P

N = 192
R2 = 48 * 48
BF = jnp.bfloat16
F32 = jnp.float32
VMEM_LIMIT = 32 * 1024 * 1024


def trig(freqs, points):
    angle = 2.0 * np.pi * (np.outer(freqs, points) % N) / N
    return np.cos(angle) / np.sqrt(N), np.sin(angle) / np.sqrt(N)


def pair_of(table):
    table = np.asarray(table, np.float32)
    high = table.astype(ml_dtypes.bfloat16)
    low = (table - high.astype(np.float32)).astype(ml_dtypes.bfloat16)
    return np.concatenate([high, low], 0)


KZ = np.concatenate([np.arange(64), np.arange(128, 192)])
SIGNED = np.concatenate([np.arange(64), np.arange(-64, 0)])
YS = [2 * np.arange(96), 2 * np.arange(96) + 1]


@functools.cache
def tables():
    t = {}
    blocks = []
    for zi in range(3):
        c, s = trig(3 * np.arange(64) + zi, KZ)
        blocks += [np.concatenate([c, -s], 1), np.concatenate([s, c], 1)]
    t["wz"] = pair_of(np.concatenate(blocks, 0))
    c, s = trig(np.concatenate(YS), SIGNED)
    t["ey"] = pair_of(
        np.concatenate([np.concatenate([c, -s], 1), np.concatenate([s, c], 1)], 0)
    )
    c, s = trig(SIGNED, np.arange(N))
    gap = np.zeros((128, 64))
    even = [np.concatenate([v, gap], 1) for v in (c, s, -s, c)]
    odd = [np.concatenate([gap, v], 1) for v in (c, s, -s, c)]
    t["ix"] = np.concatenate(
        [
            pair_of(np.block([[even[0], even[1]], [even[2], even[3]]])),
            pair_of(np.block([[odd[0], odd[1]], [odd[2], odd[3]]])),
        ],
        0,
    )
    parts = {}
    c, s = trig(np.arange(N), SIGNED)
    gap = np.zeros((64, 128))
    for name, table in (("c", c), ("s", s)):
        parts[name] = (np.concatenate([table, gap], 0), np.concatenate([gap, table], 0))

    def forward_x(which):
        cc, ss = parts["c"][which], parts["s"][which]
        first, second = np.concatenate([cc, -ss], 1), np.concatenate([ss, cc], 1)
        return np.concatenate([first[:128], second[:128], first[128:], second[128:]], 0)

    t["fx"] = np.concatenate([pair_of(forward_x(0)), pair_of(forward_x(1))], 0)
    c, s = trig(SIGNED, np.concatenate(YS))
    t["fy"] = pair_of(
        np.concatenate([np.concatenate([c, s], 1), np.concatenate([-s, c], 1)], 0)
    )
    blocks = []
    for zi in range(3):
        c, s = trig(3 * np.arange(64) + zi, KZ)
        blocks += [np.concatenate([c, -s], 1), np.concatenate([s, c], 1)]
    t["fz"] = pair_of(np.concatenate(blocks, 0))
    u = np.zeros((128, 384), np.float32)
    for zi in range(3):
        for p in range(128):
            u[16 * zi + 8 * (p >= 64) + p % 8, 128 * zi + p] = 1.0
    t["u"] = u.astype(ml_dtypes.bfloat16)
    t["ut"] = np.concatenate([u[:, 128 * zi : 128 * zi + 128].T for zi in range(3)], 0).astype(
        ml_dtypes.bfloat16
    )
    return t


def split(x):
    high = x.astype(BF)
    return high, (x - high.astype(F32)).astype(BF)


def mm(a, b):
    return jnp.dot(a, b, preferred_element_type=F32)


def mm_nt(a, b):
    return lax.dot_general(a, b, (((1,), (1,)), ((), ())), preferred_element_type=F32)


def three(product, a, b):
    return product(a[0], b[0]) + (product(a[0], b[1]) + product(a[1], b[0]))


def iota(shape, dim):
    return lax.broadcasted_iota(jnp.int32, shape, dim)


def masks_sp():
    s, p = iota((64, 128), 0), iota((64, 128), 1)
    ky = jnp.where(p < 64, p, p - 128)
    away = 64 - jnp.abs(ky)
    inside = ky * ky + s * s <= R2
    clash = away * away + (64 - s) * (64 - s) <= R2
    other = (p - 64) * (p - 64) + (64 - s) * (64 - s) <= R2
    return inside & ~clash, inside & clash, other


def line_places(r, s):
    plane, rest = r // 128, r % 128
    ky = 2 * (rest % 64 - 24) + rest // 64
    here = jnp.where(plane == 0, s, 64 - s)
    away = 64 - jnp.abs(ky)
    inside = ky * ky + here * here <= R2
    clash = (away * away + (64 - s) * (64 - s) <= R2) & (plane == 0)
    place = jnp.where(plane == 0, jnp.where(ky < 0, ky + 128, ky), ky + 64)
    main = jnp.where(inside & ~clash, place, -1)
    spare = jnp.where(inside & clash, jnp.where(ky < 0, 8, 0) + (ky + 64) % 8, -1)
    return main, spare


def one_hot(condition):
    return jnp.where(condition, 1.0, 0.0).astype(BF)


def sphere_rows(plane, parity, s):
    m, lane = iota((64, 128), 0), iota((64, 128), 1)
    ky = 2 * (m - 24) + parity
    kz = jnp.where(lane < 64, lane, lane - 128)
    kx = s - 64 * plane
    return ky * ky + kz * kz + kx * kx <= R2


def kernel_z_inverse(psi, wz, send):
    s = lax.axis_index("fft")
    main, spare = line_places(iota((1, 256), 1), s)
    j = iota((128, 256), 0)
    pack = jnp.concatenate(
        [one_hot(j == main), one_hot((j % 16 == spare) & (j % 64 < 48))], axis=0
    )
    lane = iota((64, 128), 1)
    rows = []
    for plane in range(2):
        lines = [[], []]
        for c in range(2):
            at = 1152 * plane + c
            t = [
                jnp.concatenate(
                    [
                        psi[pl.ds(at + 432 + 2 * k, 24, stride=6), :],
                        psi[pl.ds(at + 2 * k, 40, stride=6), :],
                    ],
                    0,
                )
                for k in range(3)
            ]
            middle = pltpu.roll(t[1], 64, 1)
            even = jnp.where(lane < 64, t[0], middle)
            odd = jnp.where(lane < 64, middle, t[2])
            lines[0].append(jnp.where(sphere_rows(plane, 0, s), even, 0.0))
            lines[1].append(jnp.where(sphere_rows(plane, 1, s), odd, 0.0))
        rows += [jnp.concatenate(lines[0], 1), jnp.concatenate(lines[1], 1)]
    high, low = split(jnp.concatenate(rows, 0))
    packed = (mm(pack, high).astype(BF), mm(pack, low).astype(BF))
    out = three(mm_nt, (wz[0:384, :], wz[384:768, :]), packed)
    spares = out[0:64, 128:]
    for c in range(2):
        for zi in range(3):
            block = out[(2 * zi + c) * 64 : (2 * zi + c) * 64 + 64]
            send[pl.ds(3 * c + zi, 64, stride=7), :] = block[:, :128]
            spares = jnp.where(lane // 16 == 4 * c + zi, block[:, 128:], spares)
    send[pl.ds(6, 64, stride=7), :] = spares


def tile_rows(tiles):
    return (tiles % 3) * 288 + tiles // 3


def as_column(ids):
    return jnp.broadcast_to(ids.astype(F32), (8, ids.shape[1])).T[:, 0:1].astype(jnp.int32)


def kernel_field(
    recv, ey, ix, u, field, rows_h, rows_l,
):
    main, spare, other = masks_sp()
    spread = []
    for c in range(2):
        got = recv[pl.ds(6, 64, stride=7), :]
        high, low = split(pltpu.roll(got, 64, 1) if c else got)
        spread.append(mm(high, u[...]) + mm(low, u[...]))
    lines = []
    for zi in range(3):
        first, second = [], []
        for c in range(2):
            got = recv[pl.ds(3 * c + zi, 64, stride=7), :]
            extra = spread[c][:, 128 * zi : 128 * zi + 128]
            first.append(jnp.where(main, got, jnp.where(spare, extra, 0.0)))
            second.append(pltpu.roll(jnp.where(other, got, 0.0), 64, 1))
        lines += [jnp.concatenate(first, 1), jnp.concatenate(second, 1)]
    g = three(mm_nt, (ey[0:384, :], ey[384:768, :]), split(jnp.concatenate(lines, 0)))
    out = []
    for parity in range(2):
        a = 96 * parity
        table = [ix[512 * parity + 256 * i : 512 * parity + 256 * i + 256, :] for i in range(2)]
        block = jnp.concatenate(
            [
                jnp.concatenate(
                    [
                        g[a : a + 96, 128 * zi : 128 * zi + 128],
                        g[192 + a : 288 + a, 128 * zi : 128 * zi + 128],
                    ],
                    1,
                )
                for zi in range(3)
            ],
            0,
        )
        out.append(three(mm, split(block), table))
    even, odd = out
    for c in range(2):
        a = 256 * c
        kinds = (
            even[:, a : a + 128],
            even[:, a + 128 : a + 256] + odd[:, a : a + 128],
            odd[:, a + 128 : a + 256],
        )
        for k, tile in enumerate(kinds):
            span = pl.ds(288 * k, 288)
            lanes = pl.ds(128 * c, 128)
            field[span, lanes] = tile
            high, low = split(tile)
            rows_h[span, lanes] = high
            rows_l[span, lanes] = low
    rows_h[864:896, :] = jnp.zeros((32, 256), BF)
    rows_l[864:896, :] = jnp.zeros((32, 256), BF)


def project(quarters, rows_h, rows_l, tile_of, slots, betas, field_rows):
    count = 128 * quarters
    pick = one_hot(as_column(tile_of) == iota((count, 896), 1))
    field_rows[...] = mm(pick, rows_h[...]) + mm(pick, rows_l[...])
    lane = iota((128, 128), 1)
    sums = []
    for k, beta in enumerate(betas):
        total = jnp.zeros((128, 128), F32)
        for j in range(8):
            projector = beta[pl.ds(j, 128, stride=8), :]
            for c in range(2):
                value = field_rows[128 * k : 128 * k + 128, 128 * c : 128 * c + 128] * projector
                total = jnp.where(
                    lane == 8 * c + j, jnp.sum(value, axis=1, keepdims=True), total
                )
        sums.append(total.T[:16])
    high, low = split(jnp.concatenate(sums, 1))
    return mm(high, slots) + mm(low, slots)


def ids_of(betas, row):
    return jnp.concatenate([b[1024 + row : 1025 + row, :] for b in betas], 1).astype(jnp.int32)


def kernel_project(rows_h, rows_l, b0, b1, b2, coef, slots_out, tiles_out, field_rows):
    betas = (b0, b1, b2)
    tile_of = tile_rows(ids_of(betas, 1))
    tiles_out[...] = tile_of
    slots = one_hot(as_column(ids_of(betas, 0)) == iota((384, 256), 1))
    slots_out[...] = slots
    coef[...] = project(3, rows_h, rows_l, tile_of, slots, betas, field_rows)


def kernel_project_last(rows_h, rows_l, dmat, coef_in, b3, near, slots_out, tiles_out, field_rows):
    tile_of = tile_rows(ids_of((b3,), 1))
    tiles_out[...] = tile_of
    slots = one_hot(as_column(ids_of((b3,), 0)) == iota((128, 256), 1))
    slots_out[...] = slots
    coef = coef_in[...] + project(1, rows_h, rows_l, tile_of, slots, (b3,), field_rows)
    coef = jnp.where(iota((16, 256), 1) < 192, coef, 0.0)
    near[0:64, :] = jnp.concatenate([dmat[...], jnp.zeros((64, 64), F32)], 1)
    near[64:80, :] = coef[:, :128]
    near[80:96, :] = coef[:, 128:]


def chip_of(own, other):
    f = lax.axis_index("fft")
    core = f % 2
    own, other = own[...], other[...]
    return (
        core,
        (f // 2) % 2 == 0,
        jnp.where(core == 0, own, other),
        jnp.where(core == 0, other, own),
    )


def kernel_merge(own, other, first, second):
    _, even, a, b = chip_of(own, other)
    low_lane = iota((16, 128), 1) < 64
    turned = pltpu.roll(b[64:80], 64, 1)
    up = jnp.where(low_lane, a[80:96] + turned, pltpu.roll(b[80:96], 64, 1))
    down = jnp.where(low_lane, a[64:80], a[64:80] + turned)
    up = jnp.concatenate([b[0:64], up], 0)
    down = jnp.concatenate([a[0:64], down], 0)
    first[...] = jnp.where(even, up, down)
    second[...] = jnp.where(even, down, up)


def kernel_put(tiles, tiles_last, field, vloc_in, put, local, vloc, sems):
    copies = [
        pltpu.make_async_copy(vloc_in.at[:, zi, :], vloc.at[zi], sems.at[zi]) for zi in range(3)
    ]
    for copy in copies:
        copy.start()
    tile_of = jnp.concatenate([tiles[...], tiles_last[...]], 1)
    put[...] = one_hot(iota((864, 512), 0) == tile_of)
    for copy in copies:
        copy.wait()
    for k in range(3):
        for zi in range(3):
            at = 288 * k + 96 * zi
            factor = vloc[zi, pl.ds(k, 96, stride=3), :]
            local[at : at + 96, :] = field[at : at + 96, :] * jnp.concatenate([factor, factor], 1)


def kernel_back(
    local, own, other, second, first, slots, slots_last, put, b0, b1, b2, b3,
    fx, fy, ut, send, scr, rows,
):
    core, even, a, b = chip_of(own, other)
    above = jnp.where(even, first[...], second[...])
    below = jnp.where(even, second[...], first[...])
    low_lane = iota((16, 128), 1) < 64
    turned = pltpu.roll(b[64:80], 64, 1)
    tot = [
        below[64:80] + jnp.where(low_lane, a[64:80], a[64:80] + turned),
        above[64:80] + jnp.where(low_lane, a[80:96] + turned, pltpu.roll(b[80:96], 64, 1)),
    ]
    wide = iota((64, 128), 1) < 64
    coupling = [
        jnp.where(wide, below[0:64], pltpu.roll(a[0:64], 64, 1)),
        jnp.where(wide, b[0:64], pltpu.roll(above[0:64], 64, 1)),
    ]
    for h in range(2):
        for c in range(2):
            coef = tot[h][8 * c : 8 * c + 8, :]
            for j in range(8):
                row = jnp.sum(coupling[h][8 * j : 8 * j + 8, :] * coef, axis=0, keepdims=True)
                scr[8 * c + j : 8 * c + j + 1, 128 * h : 128 * h + 128] = row
    betas = (b0, b1, b2, b3)
    left, right = scr[:, :128], scr[:, 128:]
    left_turned, right_turned = pltpu.roll(left, 64, 1), pltpu.roll(right, 64, 1)
    left = jnp.where(core == 0, left, jnp.where(low_lane, left_turned, right_turned))
    right = jnp.where(low_lane, jnp.where(core == 0, right, right_turned), 0.0)
    high, low = split(jnp.concatenate([left, right], 1))
    parts = jnp.concatenate([high, low], 0)
    weight = jnp.concatenate([mm_nt(hot[...], parts) for hot in (slots, slots_last)], 0).astype(BF)
    for k, beta in enumerate(betas):
        span = slice(128 * k, 128 * k + 128)
        terms = jnp.zeros((128, 256), F32)
        for j in range(8):
            wide = one_hot(iota((32, 256), 0) % 16 == 8 * (iota((32, 256), 1) // 128) + j)
            projector = beta[pl.ds(j, 128, stride=8), :]
            terms = terms + mm(weight[span], wide) * jnp.concatenate([projector, projector], 1)
        high, low = split(terms)
        rows[span, 0:256] = high
        rows[span, 256:512] = low
    both = mm(put[...], rows[...])
    nonloc = both[:, :256] + both[:, 256:]
    kinds = []
    for k in range(3):
        at = slice(288 * k, 288 * k + 288)
        kinds.append(split(local[at, :] + nonloc[at, :]))
    g = []
    for parity in range(2):
        table = [fx[1024 * parity + 512 * i : 1024 * parity + 512 * i + 512, :] for i in range(2)]
        lines = [jnp.concatenate([kinds[parity][i], kinds[parity + 1][i]], 1) for i in range(2)]
        g.append(split(three(mm, lines, table)))
    lines = [
        jnp.concatenate(
            [
                jnp.concatenate(
                    [
                        g[parity][i][96 * zi : 96 * zi + 96, 128 * c : 128 * c + 128]
                        for zi in range(3)
                    ],
                    1,
                )
                for c in range(2)
                for parity in range(2)
            ],
            0,
        )
        for i in range(2)
    ]
    h = three(mm, (fy[0:256, :], fy[256:512, :]), lines)
    main, spare, _ = masks_sp()
    spares = [jnp.zeros((64, 128), F32), jnp.zeros((64, 128), F32)]
    for zi in range(3):
        for c in range(2):
            turned = h[128 * c : 128 * c + 128, 128 * zi : 128 * zi + 128].T
            first = turned[:64]
            second = pltpu.roll(turned[64:], 64, 1)
            send[pl.ds(3 * c + zi, 64, stride=7), :] = jnp.where(main, first, second)
            high, low = split(jnp.where(spare, first, 0.0))
            move = ut[128 * zi : 128 * zi + 128, :]
            spares[c] = spares[c] + (mm(high, move) + mm(low, move))
    send[pl.ds(6, 64, stride=7), :] = spares[0] + pltpu.roll(spares[1], 64, 1)


def kernel_z_forward(recv, fz, result, out, sems):
    s = lax.axis_index("fft")
    out[...] = jnp.zeros((1728, 128), F32)
    spans = [(152, 280), (576, 576), (1304, 280), (0, 152), (432, 144), (1152, 152), (1584, 144)]
    copies = [
        pltpu.make_async_copy(out.at[pl.ds(*span)], result.at[pl.ds(*span)], sems.at[k])
        for k, span in enumerate(spans)
    ]
    for copy in copies[:3]:
        copy.start()
    r = iota((256, 1), 0)
    main, spare = line_places(r, s)
    lane = iota((256, 128), 1)
    keep = one_hot(lane == main)
    spares = recv[pl.ds(6, 64, stride=7), :]
    spares = (spares, pltpu.roll(spares, 64, 1))
    highs, lows = [], []
    for zi in range(3):
        unpack = jnp.concatenate(
            [keep, one_hot((lane == spare + 16 * zi) & (spare >= 0))], 1
        )
        lines = jnp.concatenate(
            [
                jnp.concatenate(
                    [
                        recv[pl.ds(3 * c + zi, 64, stride=7), :],
                        spares[c],
                    ],
                    1,
                )
                for c in range(2)
            ],
            0,
        )
        high, low = split(lines)
        columns = mm_nt(unpack, jnp.concatenate([high, low], 0))
        highs.append(columns[:, :128].astype(BF))
        lows.append(columns[:, 128:].astype(BF))
    z = three(
        mm, (jnp.concatenate(highs, 1), jnp.concatenate(lows, 1)), (fz[0:384, :], fz[384:768, :])
    )
    low_lane = iota((64, 128), 1) < 64
    for plane in range(2):
        for c in range(2):
            block = z[128 * plane : 128 * plane + 128, 128 * c : 128 * c + 128]
            even = jnp.where(sphere_rows(plane, 0, s), block[:64], 0.0)
            odd = jnp.where(sphere_rows(plane, 1, s), block[64:], 0.0)
            kinds = (
                jnp.where(low_lane, even, 0.0),
                pltpu.roll(jnp.where(low_lane, odd, even), 64, 1),
                jnp.where(low_lane, 0.0, odd),
            )
            for k, tile in enumerate(kinds):
                at = 1152 * plane + 2 * k + c
                out[pl.ds(at, 25, stride=6), :] = tile[24:49]
                out[pl.ds(at + 432, 24, stride=6), :] = tile[:24]
        copies[3 + 2 * plane].start()
        copies[4 + 2 * plane].start()
    for copy in copies:
        copy.wait()


def call(kernel, name, out_shape, args, scratch=(), anywhere=(), anywhere_out=(), limit=VMEM_LIMIT, cost=None):
    specs = [
        pl.BlockSpec(memory_space=pl.ANY if k in anywhere else pltpu.VMEM)
        for k in range(len(args))
    ]
    shapes = [
        jax.ShapeDtypeStruct(*shape) if isinstance(shape[0], tuple) else jax.ShapeDtypeStruct(shape, F32)
        for shape in out_shape
    ]
    out = pl.pallas_call(
        kernel,
        name=name,
        out_shape=shapes,
        in_specs=specs,
        out_specs=[
            pl.BlockSpec(memory_space=pl.ANY if k in anywhere_out else pltpu.VMEM)
            for k in range(len(shapes))
        ],
        scratch_shapes=list(scratch),
        cost_estimate=cost,
        compiler_params=pltpu.CompilerParams(vmem_limit_bytes=limit),
    )(*args)
    return out


def body(psi_g, vloc, beta, blk_slot, blk_tile, dmat):
    t = {
        name: jnp.asarray(value) for name, value in tables().items()
    }
    psi = psi_g[0].transpose(1, 0, 2).reshape(3, 2, 288, 128).transpose(0, 2, 1, 3)
    psi = psi.reshape(1728, 128)
    def from_band(x, k):
        return lax.ppermute(x, "band", [(i, (i + k) % 4) for i in range(4)])

    ids = jnp.concatenate([blk_slot[None], blk_tile[None], jnp.zeros((6, 128), jnp.int32)], 0)
    own = jnp.concatenate([beta, ids.astype(F32)[None]], 0).reshape(1032, 128)
    (send,) = call(kernel_z_inverse, "z_inverse", [(448, 128)], (psi, t["wz"]))
    betas = [own, from_band(own, 2), from_band(own, 1), from_band(own, 3)]

    def exchange(x):
        x = lax.all_to_all(x.reshape(64, 1, 896), "fft", 0, 0, tiled=True)
        return x.reshape(448, 128)

    recv = exchange(send)
    vloc_tiles = vloc.reshape(3, 288, 128).transpose(1, 0, 2)
    dmat_rows = dmat.transpose(1, 2, 0).reshape(64, 64)
    field, rows_h, rows_l = call(
        kernel_field,
        "field",
        [(864, 256), ((896, 256), BF), ((896, 256), BF)],
        (recv, t["ey"], t["ix"], t["u"]),
    )
    coef, slots, tiles = call(
        kernel_project,
        "project",
        [(16, 256), ((384, 256), BF), ((1, 384), jnp.int32)],
        (rows_h, rows_l, *betas[:3]),
        [pltpu.VMEM((384, 256), F32)],
    )
    near, slots_last, tiles_last = call(
        kernel_project_last,
        "project_last",
        [(96, 128), ((128, 256), BF), ((1, 128), jnp.int32)],
        (rows_h, rows_l, dmat_rows, coef, betas[3]),
        [pltpu.VMEM((128, 256), F32)],
    )
    other = lax.ppermute(near, "fft", [(i, i ^ 1) for i in range(64)])
    first, second = call(kernel_merge, "merge", [(80, 128), (80, 128)], (near, other))
    first = lax.ppermute(first, "fft", [(i, i ^ 2) for i in range(64)])
    second = lax.ppermute(second, "fft", [(i, (((i + 2) % 64) ^ 2) - 2 & 63) for i in range(64)])
    put, local = call(
        kernel_put,
        "put",
        [((864, 512), BF), (864, 256)],
        (tiles, tiles_last, field, vloc_tiles),
        [pltpu.VMEM((3, 288, 128), F32), pltpu.SemaphoreType.DMA((3,))],
        anywhere=(3,),
        cost=pl.CostEstimate(flops=2000000, bytes_accessed=3000000, transcendentals=0),
    )
    (send,) = call(
        kernel_back,
        "back",
        [(448, 128)],
        (local, near, other, second, first, slots, slots_last, put, *betas, t["fx"], t["fy"], t["ut"]),
        [
            pltpu.VMEM((16, 256), F32),
            pltpu.VMEM((512, 512), BF),
        ],
    )
    (out,) = call(kernel_z_forward, "z_forward", [(1728, 128)], (exchange(send), t["fz"]),
        [pltpu.VMEM((1728, 128), F32), pltpu.SemaphoreType.DMA((7,))], anywhere_out=(0,))
    out = out.reshape(3, 288, 2, 128).transpose(0, 2, 1, 3).reshape(3, 2, N * N)
    return out.transpose(1, 0, 2)[None]


def solution(mesh):
    in_specs = (
        P("band", None, "fft", None),
        P("fft", None),
        P(("fft", "band"), None, None),
        P(("fft", "band")),
        P(("fft", "band")),
        P("fft", None, None),
    )
    out_specs = P("band", None, "fft", None)
    return jax.shard_map(body, mesh=mesh, in_specs=in_specs, out_specs=out_specs, check_vma=False)
```
